32 devices in a mesh: grp: 4 (over x, core), ep: 8 (over z, y).
Axes of the slice: x: 2, y: 2, z: 4, core: 2. Of those that a mesh axis runs over, the one named last changes fastest.
Arguments:
- tokens: bfloat16 [16384, 1536], P(('grp', 'ep')), may hold values from -6 to 6
- segment_ids: int32 [32, 512], P(('grp', 'ep')), may hold values from 0 to 15, never falling along the last dimension, each value on 1 to 256 neighbouring positions
- routes: int32 [16384, 4], P(('grp', 'ep')), may hold values from 0 to 7, all different within a row; in each aligned block of 512 rows (0 to 511, 512 to 1023, ...) at most 384 rows name the same one
- route_gates: float32 [16384, 4], P(('grp', 'ep')), may hold values from 0.125 to 0.5
- attn_gain: float32 [1536], replicated, may hold values from 0.25 to 1.75
- ffn_gain: float32 [1536], replicated, may hold values from 0.25 to 1.75
- query_weight: bfloat16 [1536, 1536], replicated, may hold values from -0.15625 to 0.15625
- key_matrix: bfloat16 [1536, 256], replicated, may hold values from -0.15625 to 0.15625
- value_matrix: bfloat16 [1536, 256], replicated, may hold values from -0.15625 to 0.15625
- output_weight: bfloat16 [1536, 1536], replicated, may hold values from -0.625 to 0.625
- expert_gate: bfloat16 [8, 1536, 768], P('ep'), may hold values from -0.15625 to 0.15625
- expert_up: bfloat16 [8, 1536, 768], P('ep'), may hold values from -0.15625 to 0.15625
- expert_down: bfloat16 [8, 768, 1536], P('ep'), may hold values from -0.21875 to 0.21875
- cotangent: bfloat16 [16384, 1536], P(('grp', 'ep')), may hold values from -6 to 6
Outputs:
- layer_out: bfloat16 [16384, 1536], P(('grp', 'ep'))
- tokens_grad: float32 [16384, 1536], P(('grp', 'ep'))
- query_grad: float32 [1536, 1536], P(('grp', 'ep'))
- key_grad: float32 [1536, 256], P(('grp', 'ep'))
- value_grad: float32 [1536, 256], P(('grp', 'ep'))
- output_grad: float32 [1536, 1536], P(None, ('grp', 'ep'))
- attn_gain_grad: float32 [1536], P(('grp', 'ep'))
- ffn_gain_grad: float32 [1536], P(('grp', 'ep'))
- expert_gate_grad: float32 [8, 1536, 768], P('ep', 'grp')
- expert_up_grad: float32 [8, 1536, 768], P('ep', 'grp')
- expert_down_grad: float32 [8, 768, 1536], P('ep', None, 'grp')
The draws below stay inside these ranges and needn't reach their ends.
Inputs may be any that keep to these rules, and one draw needn't show every extreme that they name: `routes`: the 4 numbers of a row differ. Among the rows of one device (512 aligned rows) no expert is named more than 384 times, a bound that some block reaches. `segment_ids`: each row never falls; each segment holds 1 to 256 positions, one exactly that many. The positions of a row's largest number are padding.
All inputs are finite; a program needn't handle non-finite values.
Results may differ from the reference program's by a relative error of at most 0.013.
Values may be sent and summed in bfloat16 or wider, within the bound.
A program may use at most 256 MiB of HBM per device.

```python
import math
from functools import partial
import jax
import jax.numpy as jnp
import numpy as np
from jax import lax

MODEL_WIDTH = 1536
QUERY_HEADS = 12
KEY_VALUE_HEADS = 2
HEAD_SIZE = 128
FF_E = 768
TOP = 4
DOCS = 16
TOK_DEV = 512
EXPERTS = 8
SEQS = 32
TOKENS = 16384
CAP = 384
N_GRP = 4
N_EP = 8


def spiked(values, rng, source, target, parts, factor):
    owner, partner = [(jnp.arange(values.shape[dim]) // (values.shape[dim] // parts)).reshape([-1 if axis == dim else 1 for axis in range(values.ndim)]) for dim in (source, target)]
    chosen = jax.random.permutation(rng, parts)[partner]
    strong = (owner == chosen) | (owner == (partner + parts // 2) % parts)
    return jnp.where(strong, factor * values, values)


def block_scale(rng, dims, shards, smallest, high):
    level = 1.0
    for dim, parts in shards:
        heights = jax.random.uniform(jax.random.fold_in(jax.random.fold_in(rng, 6), dim), (parts,), jnp.float32, smallest / len(shards), high / len(shards))
        level = level * jnp.repeat(jnp.exp(heights), dims[dim] // parts).reshape((-1,) + (1,) * (len(dims) - 1 - dim))
    return level


def length_profile(number_of, total, limit, slope):
    weights = [(1 << 20) // math.isqrt(standing ** slope) + 1 for standing in range(2, number_of + 1)]
    spare, given = total - limit - (number_of - 1), [1] * (number_of - 1)
    while spare > 0:
        free = [i for i in range(number_of - 1) if given[i] < limit]
        mass, left = sum([weights[i] for i in free]), spare
        for i in free:
            extra = min(limit - given[i], max(1, left * weights[i] // mass), spare)
            given[i] = given[i] + extra
            spare = spare - extra
    return np.array([limit] + given)


def uneven(stream_key, amount, total, most, lean):
    if amount == 2:
        one = jax.random.randint(stream_key, (), max(1, total - most), min(most, total - 1) + 1)
        return jnp.stack([one, total - one])
    lengths = jnp.asarray(length_profile(amount, total, most, lean), jnp.int32)
    twos = (amount - 1) // 2
    giver, sink = lengths[1:1 + 2 * twos:2], lengths[2:2 + 2 * twos:2]
    margin = jnp.minimum(giver - 1, most - sink)
    moved = jax.random.randint(jax.random.fold_in(stream_key, 1), (twos,), 0, 1 << 20) % (margin + 1)
    lengths = lengths.at[1:1 + 2 * twos:2].set(giver - moved).at[2:2 + 2 * twos:2].set(sink + moved)
    return lengths[jax.random.permutation(jax.random.fold_in(stream_key, 2), amount)]


def routed_block(stream_key, own, number, rows, amount, top, reach, lean):
    ranking = jax.random.permutation(stream_key, amount)
    packed, ordinary = shares(amount, rows * top, reach, lean, True), shares(amount, rows * top, reach, lean, False)
    places = jnp.arange(amount)

    def named(sizes, rotation):
        used = int((sizes > 0).sum())
        fixed = max(1, used // 4)
        passed = fixed + (places - fixed + rotation * (used - fixed)) % max(1, amount - fixed)
        return jnp.zeros((amount,), jnp.int32).at[ranking[jnp.where(places < fixed, places, passed)]].set(jnp.asarray(sizes, jnp.int32))

    sizes = jnp.where(number % 4 == 0, named(packed, number // 4), named(ordinary, number - number // 4 - 1))
    mixed = jax.random.permutation(jax.random.fold_in(own, 3), amount)
    donor, sink = mixed[0:amount // 2 * 2:2], mixed[1:amount // 2 * 2:2]
    room = jnp.minimum(sizes[donor] - 1, reach - sizes[sink]) // 2
    room = jnp.where((donor == ranking[0]) | (sink == ranking[0]) | (sizes[sink] == 0), 0, jnp.maximum(room, 0))
    passed = jax.random.randint(jax.random.fold_in(own, 4), (amount // 2,), 0, 1 << 20) % (room + 1)
    sizes = sizes.at[donor].add(-passed).at[sink].add(passed)
    labels = jnp.searchsorted(jnp.cumsum(sizes), jnp.arange(rows * top), side="right").astype(jnp.int32)
    grid = labels.reshape(top, rows).T
    grid = grid[jax.random.permutation(jax.random.fold_in(own, 1), rows)]
    rotation = jax.random.randint(jax.random.fold_in(own, 2), (rows, 1), 0, top)
    return jnp.take_along_axis(grid, (jnp.arange(top)[None, :] + rotation) % top, axis=1)


def shares(count, total, limit, lean, full):
    weights = [(1 << 20) // math.isqrt(standing ** lean) + 1 for standing in range(1, count + 1)]
    largest = limit if full else min(limit, max(-(-total // count), total * weights[0] // sum(weights)))
    least = 1 if total - largest >= count - 1 else 0
    holding, surplus = [largest] + [least] * (count - 1), total - largest - least * (count - 1)
    while surplus > 0:
        candidates = [i for i in range(1, count) if holding[i] < largest] or [i for i in range(1, count) if holding[i] < limit]
        whole, remaining = sum([weights[i] for i in candidates]), surplus
        for i in candidates:
            more = min(limit - holding[i], max(1, remaining * weights[i] // whole), surplus)
            holding[i] = holding[i] + more
            surplus = surplus - more
    return np.array(holding)


def scatter_about(rng, shape, scale, bound, cuts=(), kind=jnp.bfloat16):
    entries = jax.random.normal(rng, shape, jnp.float32) * scale
    if len(cuts) > 0:
        entries = block_scale(rng, shape, cuts, -0.22, 0.18) * entries
    return jnp.clip(entries, min=-bound, max=bound).astype(kind)


def heavy_noise(stream_key, dims, width, limit, pieces, heavy, held_as=jnp.bfloat16):
    drawn = width * jax.random.normal(stream_key, dims, jnp.float32)
    if pieces:
        drawn = drawn * block_scale(stream_key, dims, pieces, -0.22, 0.18)
    return jnp.clip(spiked(drawn, jax.random.fold_in(stream_key, 3), *heavy), -limit, limit).astype(held_as)


def setup_inputs(seed: int = 0) -> dict:
    splits = jax.random.split(jax.random.key(seed), 15)
    tokens = heavy_noise(splits[0], (TOKENS, MODEL_WIDTH), 1.0, 6.0, ((0, 32),), (0, 1, 32, 2.75))
    segment_ids = jax.vmap(lambda own: jnp.searchsorted(jnp.cumsum(uneven(own, DOCS, TOK_DEV, TOK_DEV // 2, 2)), jnp.arange(TOK_DEV), side="right"))(jax.random.split(splits[1], SEQS)).reshape((SEQS, TOK_DEV)).astype(jnp.int32)
    routes_keys = jax.random.split(jax.random.fold_in(splits[2], 1), TOKENS // TOK_DEV)
    routes_turns = jax.random.permutation(jax.random.fold_in(splits[2], 3), TOKENS // TOK_DEV)
    routes = jax.vmap(lambda own, number: routed_block(jax.random.fold_in(splits[2], 2), own, number, TOK_DEV, EXPERTS, TOP, CAP, 1))(routes_keys, routes_turns).reshape((TOKENS, TOP))
    route_gates = jnp.clip(jnp.exp(math.log(0.5) - 1.3862944 * jax.random.uniform(splits[3], (TOKENS, TOP), jnp.float32) ** block_scale(splits[3], (TOKENS, TOP), ((0, 32),), -0.2, 0.2)), 0.125, 0.5)
    attn_gain = jnp.clip(1.0 + 0.15 * jax.random.normal(splits[4], (MODEL_WIDTH,), jnp.float32), 0.25, 1.75)
    ffn_gain = jnp.clip(1.0 + 0.15 * jax.random.normal(splits[5], (MODEL_WIDTH,), jnp.float32), 0.25, 1.75)
    query_weight = scatter_about(splits[6], (MODEL_WIDTH, QUERY_HEADS * HEAD_SIZE), MODEL_WIDTH ** -0.5, 0.15625)
    key_matrix = scatter_about(splits[7], (MODEL_WIDTH, KEY_VALUE_HEADS * HEAD_SIZE), MODEL_WIDTH ** -0.5, 0.15625)
    value_matrix = scatter_about(splits[8], (MODEL_WIDTH, KEY_VALUE_HEADS * HEAD_SIZE), MODEL_WIDTH ** -0.5, 0.15625)
    output_weight = scatter_about(splits[9], (QUERY_HEADS * HEAD_SIZE, MODEL_WIDTH), (QUERY_HEADS * HEAD_SIZE // 16) ** -0.5, 0.625)
    expert_gate = scatter_about(splits[10], (EXPERTS, MODEL_WIDTH, FF_E), MODEL_WIDTH ** -0.5, 0.15625, ((0, 8),))
    expert_up = scatter_about(splits[11], (EXPERTS, MODEL_WIDTH, FF_E), MODEL_WIDTH ** -0.5, 0.15625, ((0, 8),))
    expert_down = scatter_about(splits[12], (EXPERTS, FF_E, MODEL_WIDTH), FF_E ** -0.5, 0.21875, ((0, 8),))
    cotangent = heavy_noise(splits[13], (TOKENS, MODEL_WIDTH), 1.0, 6.0, ((0, 32),), (0, 1, 32, 2.75))
    return {"tokens": tokens, "segment_ids": segment_ids, "routes": routes, "route_gates": route_gates, "attn_gain": attn_gain, "ffn_gain": ffn_gain, "query_weight": query_weight, "key_matrix": key_matrix, "value_matrix": value_matrix, "output_weight": output_weight, "expert_gate": expert_gate, "expert_up": expert_up, "expert_down": expert_down, "cotangent": cotangent}


@jax.custom_vjp
def lower_precision(v):
    return lax.optimization_barrier(v.astype(jnp.bfloat16)).astype(jnp.float32)

@jax.custom_vjp
def lower_precision_backward(v):
    return v

def low_keep(v):
    return (lower_precision(v), None)

def low_pass(kept, grad):
    return (grad,)

def back_keep(v):
    return (v, None)

def back_low(kept, grad):
    return (lower_precision(grad),)
lower_precision.defvjp(low_keep, low_pass)
lower_precision_backward.defvjp(back_keep, back_low)
EPS = 1e-06
BASE = 10000.0

def matrix_product_highest(left, right):
    return jnp.dot(left, right, precision=lax.Precision.HIGHEST, preferred_element_type=jnp.float32)

def rms_scale(value_rows, gain):
    factor = lax.rsqrt(lax.optimization_barrier(jnp.mean(value_rows * value_rows, axis=-1, keepdims=True)) + EPS)
    return value_rows * factor * gain

def apply_rotary(value_rows, cosine_table, sine_table):
    half = value_rows.shape[-1] // 2
    first = value_rows[..., :half]
    second = value_rows[..., half:]
    return jnp.concatenate([first * cosine_table - second * sine_table, second * cosine_table + first * sine_table], axis=-1)

def attend_one(inputs, query_weight, key_matrix, value_matrix):
    row_entries, segment = inputs
    length_total = row_entries.shape[0]
    position = jnp.arange(length_total, dtype=jnp.float32)
    inverse = BASE ** (-jnp.arange(HEAD_SIZE // 2, dtype=jnp.float32) * 2.0 / HEAD_SIZE)
    angle = position[:, None] * inverse[None, :]
    cosine_table = jnp.cos(angle)[:, None, :]
    sine_table = jnp.sin(angle)[:, None, :]
    query_rows = lower_precision_backward(matrix_product_highest(row_entries, query_weight)).reshape(length_total, QUERY_HEADS, HEAD_SIZE)
    key_rows = lower_precision_backward(matrix_product_highest(row_entries, key_matrix)).reshape(length_total, KEY_VALUE_HEADS, HEAD_SIZE)
    value_rows = lower_precision(lower_precision_backward(matrix_product_highest(row_entries, value_matrix))).reshape(length_total, KEY_VALUE_HEADS, HEAD_SIZE)
    query_rows = lower_precision(apply_rotary(query_rows, cosine_table, sine_table)).reshape(length_total, KEY_VALUE_HEADS, QUERY_HEADS // KEY_VALUE_HEADS, HEAD_SIZE)
    key_rows = lower_precision(apply_rotary(key_rows, cosine_table, sine_table))
    score = jnp.einsum('tkgd,skd->kgts', query_rows, key_rows, precision=lax.Precision.HIGHEST) * HEAD_SIZE ** (-0.5)
    score = lower_precision_backward(score)
    padding = segment == jnp.max(segment)
    later = jnp.arange(length_total)[:, None] >= jnp.arange(length_total)[None, :]
    diagonal = jnp.arange(length_total)[:, None] == jnp.arange(length_total)[None, :]
    allowed = later & (segment[:, None] == segment[None, :]) & (jnp.logical_not(padding)[None, :] | diagonal)
    score = jnp.where(allowed, score, -1e+30)
    probs = lower_precision(jax.nn.softmax(score, axis=-1))
    attended = jnp.einsum('kgts,skd->tkgd', probs, value_rows, precision=lax.Precision.HIGHEST)
    return lower_precision(lower_precision_backward(attended.reshape(length_total, QUERY_HEADS * HEAD_SIZE)))

def forward(tokens, attn_gain, ffn_gain, query_weight, key_matrix, value_matrix, output_weight, expert_gate, expert_up, expert_down, segment_ids, routes, route_gates):
    h_first = lower_precision(rms_scale(tokens, attn_gain))
    attend = jax.checkpoint(partial(attend_one, query_weight=query_weight, key_matrix=key_matrix, value_matrix=value_matrix))
    attended = lax.map(attend, (h_first.reshape(SEQS, TOK_DEV, MODEL_WIDTH), segment_ids))
    attended = attended.reshape(TOKENS, QUERY_HEADS * HEAD_SIZE)
    mixed = tokens + lower_precision_backward(matrix_product_highest(attended, output_weight))
    h_second = lower_precision(rms_scale(mixed, ffn_gain))
    padded = jnp.concatenate([h_second, jnp.zeros((1, MODEL_WIDTH), jnp.float32)], axis=0)
    flat_routes = routes.reshape(-1)
    flat_gates = jnp.concatenate([route_gates.reshape(-1), jnp.zeros((1,), jnp.float32)])
    row_bound = N_GRP * N_EP * CAP

    def expert_step(total, inputs):
        expert, gate_w, up_w, down_w = inputs
        index = jnp.nonzero(flat_routes == expert, size=row_bound, fill_value=TOKENS * TOP)[0].astype(jnp.int32)
        token_row = index // TOP
        row_entries = lower_precision_backward(padded[token_row])
        gate_val = lower_precision_backward(matrix_product_highest(row_entries, gate_w))
        up_val = lower_precision_backward(matrix_product_highest(row_entries, up_w))
        act = lower_precision(jax.nn.gelu(gate_val, approximate=True) * up_val)
        result = lower_precision(lower_precision_backward(matrix_product_highest(act, down_w)))
        return (total.at[token_row].add(result * flat_gates[index][:, None]), None)
    start = jnp.zeros((TOKENS + 1, MODEL_WIDTH), jnp.float32)
    total, _ = lax.scan(jax.checkpoint(expert_step), start, (jnp.arange(EXPERTS, dtype=jnp.int32), expert_gate, expert_up, expert_down))
    return mixed + total[:TOKENS]

def reference(tokens, segment_ids, routes, route_gates, attn_gain, ffn_gain, query_weight, key_matrix, value_matrix, output_weight, expert_gate, expert_up, expert_down, cotangent):
    floats = (tokens.astype(jnp.float32), attn_gain, ffn_gain, query_weight.astype(jnp.float32), key_matrix.astype(jnp.float32), value_matrix.astype(jnp.float32), output_weight.astype(jnp.float32), expert_gate.astype(jnp.float32), expert_up.astype(jnp.float32), expert_down.astype(jnp.float32))
    layer, pullback = jax.vjp(partial(forward, segment_ids=segment_ids, routes=routes, route_gates=route_gates), *floats)
    grads = pullback(cotangent.astype(jnp.float32))
    return (layer.astype(jnp.bfloat16), grads[0], grads[3], grads[4], grads[5], grads[6], grads[1], grads[2], grads[7], grads[8], grads[9])
```

```python
import jax
import jax.numpy as jnp
from jax import lax
from jax.sharding import PartitionSpec as P

HEAD_SIZE = 128


EPS = 1e-06
BASE = 10000.0


def apply_rotary(value_rows, cosine_table, sine_table):
    half = value_rows.shape[-1] // 2
    first = value_rows[..., :half]
    second = value_rows[..., half:]
    return jnp.concatenate(
        [first * cosine_table - second * sine_table, second * cosine_table + first * sine_table],
        axis=-1,
    )


def unrotate(value_rows, cosine_table, sine_table):
    half = value_rows.shape[-1] // 2
    first = value_rows[..., :half]
    second = value_rows[..., half:]
    return jnp.concatenate(
        [first * cosine_table + second * sine_table, second * cosine_table - first * sine_table],
        axis=-1,
    )


def glu_value(gate_val, up_val):
    return jax.nn.gelu(gate_val, approximate=True) * up_val


def scores_of(query_rot, key_rot, allowed):
    score = jnp.einsum(
        "tkgd,skd->kgts", query_rot, key_rot, preferred_element_type=jnp.float32
    ) * HEAD_SIZE ** (-0.5)
    return jnp.where(allowed, score, -1e30)


def local_routed(
    tokens,
    segment_ids,
    routes,
    route_gates,
    attn_gain,
    ffn_gain,
    query_weight,
    key_matrix,
    value_matrix,
    output_weight,
    expert_gate,
    expert_up,
    expert_down,
    cotangent,
):
    length_total, width = tokens.shape
    choose = routes.shape[1]
    local_experts = expert_gate.shape[0]
    owners = lax.axis_size("ep")
    experts = owners * local_experts
    capacity = 3 * length_total * choose // (2 * experts)
    query_heads = query_weight.shape[1] // HEAD_SIZE
    key_heads = key_matrix.shape[1] // HEAD_SIZE
    q_per_kv = query_heads // key_heads
    segment = segment_ids[0]
    padding = segment == jnp.max(segment)
    later = jnp.arange(length_total)[:, None] >= jnp.arange(length_total)[None, :]
    diagonal = jnp.arange(length_total)[:, None] == jnp.arange(length_total)[None, :]
    allowed = (
        later
        & (segment[:, None] == segment[None, :])
        & (jnp.logical_not(padding)[None, :] | diagonal)
    )
    position = jnp.arange(length_total, dtype=jnp.float32)
    inverse = BASE ** (-jnp.arange(HEAD_SIZE // 2, dtype=jnp.float32) * 2.0 / HEAD_SIZE)
    angle = position[:, None] * inverse[None, :]
    cosine_table = jnp.cos(angle)[:, None, :]
    sine_table = jnp.sin(angle)[:, None, :]
    tok_float = tokens.astype(jnp.float32)
    scale_first = lax.rsqrt(jnp.mean(tok_float * tok_float, axis=-1, keepdims=True) + EPS)
    normed_first = tok_float * scale_first
    h_first = (normed_first * attn_gain).astype(jnp.bfloat16)
    query_rows = jnp.dot(h_first, query_weight, preferred_element_type=jnp.float32).reshape(
        length_total, query_heads, HEAD_SIZE
    )
    key_rows = jnp.dot(h_first, key_matrix, preferred_element_type=jnp.float32).reshape(
        length_total, key_heads, HEAD_SIZE
    )
    value_low = jnp.dot(h_first, value_matrix, preferred_element_type=jnp.float32).astype(
        jnp.bfloat16
    )
    value_low = value_low.reshape(length_total, key_heads, HEAD_SIZE)
    query_rot = (
        apply_rotary(query_rows, cosine_table, sine_table)
        .astype(jnp.bfloat16)
        .reshape(length_total, key_heads, q_per_kv, HEAD_SIZE)
    )
    key_rot = apply_rotary(key_rows, cosine_table, sine_table).astype(jnp.bfloat16)
    score = scores_of(query_rot, key_rot, allowed)
    row_max = jnp.max(score, axis=-1, keepdims=True)
    expo = jnp.exp(score - row_max)
    row_sum = jnp.sum(expo, axis=-1, keepdims=True)
    log_total = row_max + jnp.log(row_sum)
    probs_low = (expo / row_sum).astype(jnp.bfloat16)
    attended = jnp.einsum(
        "kgts,skd->tkgd", probs_low, value_low, preferred_element_type=jnp.float32
    )
    attended = attended.reshape(length_total, query_heads * HEAD_SIZE).astype(jnp.bfloat16)
    mixed = tok_float + jnp.dot(attended, output_weight, preferred_element_type=jnp.float32)
    scale_second = lax.rsqrt(jnp.mean(mixed * mixed, axis=-1, keepdims=True) + EPS)
    normed_second = mixed * scale_second
    h_second = (normed_second * ffn_gain).astype(jnp.bfloat16)
    flat_routes = routes.reshape(-1)
    assigns = flat_routes.shape[0]
    onehot = (flat_routes[:, None] == jnp.arange(experts, dtype=jnp.int32)[None, :]).astype(
        jnp.int32
    )
    position_in = jnp.sum(jnp.cumsum(onehot, axis=0) * onehot, axis=1) - 1
    slot_index = flat_routes * capacity + position_in
    source = (
        jnp.full((experts * capacity,), assigns, jnp.int32)
        .at[slot_index]
        .set(jnp.arange(assigns, dtype=jnp.int32))
    )
    token_of = source // choose
    h_ext = jnp.concatenate([h_second, jnp.zeros((1, width), jnp.bfloat16)], axis=0)
    send_rows = h_ext[token_of].reshape(owners, local_experts, capacity, width)
    row_entries = lax.all_to_all(send_rows, "ep", split_axis=0, concat_axis=0, tiled=True)
    gate_val = jnp.einsum(
        "secd,edf->secf", row_entries, expert_gate, preferred_element_type=jnp.float32
    )
    up_val = jnp.einsum(
        "secd,edf->secf", row_entries, expert_up, preferred_element_type=jnp.float32
    )
    act = glu_value(gate_val, up_val).astype(jnp.bfloat16)
    result = jnp.einsum("secf,efd->secd", act, expert_down, preferred_element_type=jnp.float32)
    outputs = (result.astype(jnp.bfloat16), row_entries, gate_val, up_val)
    returned = lax.all_to_all(outputs[0], "ep", split_axis=0, concat_axis=0, tiled=True).reshape(
        experts * capacity, width
    )
    picked = returned[slot_index].reshape(length_total, choose, width).astype(jnp.float32)
    layer_out = (mixed + jnp.sum(route_gates[:, :, None] * picked, axis=1)).astype(jnp.bfloat16)
    grad_out = cotangent.astype(jnp.float32)
    slot_grads = (
        (route_gates[:, :, None] * grad_out[:, None, :])
        .astype(jnp.bfloat16)
        .reshape(assigns, width)
    )
    slot_ext = jnp.concatenate([slot_grads, jnp.zeros((1, width), jnp.bfloat16)], axis=0)
    grad_send = slot_ext[source].reshape(owners, local_experts, capacity, width)
    grad_recv = lax.all_to_all(grad_send, "ep", split_axis=0, concat_axis=0, tiled=True)
    recv_rows = outputs[1]
    gate_val = outputs[2]
    up_val = outputs[3]
    act, act_back = jax.vjp(glu_value, gate_val, up_val)
    act_low = act.astype(jnp.bfloat16)
    down_part = jnp.einsum("secf,secd->efd", act_low, grad_recv, preferred_element_type=jnp.float32)
    act_grad = jnp.einsum(
        "secd,efd->secf", grad_recv, expert_down, preferred_element_type=jnp.float32
    )
    gate_grad_val, up_grad_val = act_back(act_grad)
    gate_low = gate_grad_val.astype(jnp.bfloat16)
    up_low = up_grad_val.astype(jnp.bfloat16)
    gate_part = jnp.einsum(
        "secd,secf->edf", recv_rows, gate_low, preferred_element_type=jnp.float32
    )
    up_part = jnp.einsum("secd,secf->edf", recv_rows, up_low, preferred_element_type=jnp.float32)
    rows_grad = jnp.einsum(
        "secf,edf->secd", gate_low, expert_gate, preferred_element_type=jnp.float32
    )
    rows_grad = rows_grad + jnp.einsum(
        "secf,edf->secd", up_low, expert_up, preferred_element_type=jnp.float32
    )
    rows_back = lax.all_to_all(
        rows_grad.astype(jnp.bfloat16), "ep", split_axis=0, concat_axis=0, tiled=True
    )
    rows_back = rows_back.reshape(experts * capacity, width)
    expert_sums = (
        lax.psum_scatter(
            gate_part.astype(jnp.bfloat16), "grp", scatter_dimension=1, tiled=True
        ).astype(jnp.float32),
        lax.psum_scatter(
            up_part.astype(jnp.bfloat16), "grp", scatter_dimension=1, tiled=True
        ).astype(jnp.float32),
        lax.psum_scatter(
            down_part.astype(jnp.bfloat16), "grp", scatter_dimension=2, tiled=True
        ).astype(jnp.float32),
    )
    second_grad = jnp.sum(
        rows_back[slot_index].reshape(length_total, choose, width).astype(jnp.float32), axis=1
    )
    ffn_gain_part = jnp.sum(second_grad * normed_second, axis=0)
    normed_grad = second_grad * ffn_gain
    mixed_grad = grad_out + scale_second * (
        normed_grad - normed_second * jnp.mean(normed_grad * normed_second, axis=-1, keepdims=True)
    )
    mixed_low = mixed_grad.astype(jnp.bfloat16)
    output_part = jnp.einsum("ti,td->id", attended, mixed_low, preferred_element_type=jnp.float32)
    attended_grad = jnp.einsum(
        "td,id->ti", mixed_low, output_weight, preferred_element_type=jnp.float32
    )
    attended_grad = attended_grad.astype(jnp.bfloat16).reshape(
        length_total, key_heads, q_per_kv, HEAD_SIZE
    )
    probs = jnp.exp(scores_of(query_rot, key_rot, allowed) - log_total)
    probs_again = probs.astype(jnp.bfloat16)
    value_part_grad = jnp.einsum(
        "kgts,tkgd->skd", probs_again, attended_grad, preferred_element_type=jnp.float32
    )
    prob_grad = jnp.einsum(
        "tkgd,skd->kgts", attended_grad, value_low, preferred_element_type=jnp.float32
    )
    inner = jnp.sum(probs * prob_grad, axis=-1, keepdims=True)
    score_grad = (probs * (prob_grad - inner)).astype(jnp.bfloat16)
    qrot_grad = jnp.einsum(
        "kgts,skd->tkgd", score_grad, key_rot, preferred_element_type=jnp.float32
    ) * HEAD_SIZE ** (-0.5)
    krot_grad = jnp.einsum(
        "kgts,tkgd->skd", score_grad, query_rot, preferred_element_type=jnp.float32
    ) * HEAD_SIZE ** (-0.5)
    query_grad_low = unrotate(
        qrot_grad.reshape(length_total, query_heads, HEAD_SIZE), cosine_table, sine_table
    )
    query_grad_low = query_grad_low.astype(jnp.bfloat16).reshape(
        length_total, query_heads * HEAD_SIZE
    )
    key_grad_low = (
        unrotate(krot_grad, cosine_table, sine_table)
        .astype(jnp.bfloat16)
        .reshape(length_total, key_heads * HEAD_SIZE)
    )
    value_grad_low = value_part_grad.astype(jnp.bfloat16).reshape(
        length_total, key_heads * HEAD_SIZE
    )
    query_part = jnp.einsum(
        "td,ti->di", h_first, query_grad_low, preferred_element_type=jnp.float32
    )
    key_part = jnp.einsum("td,ti->di", h_first, key_grad_low, preferred_element_type=jnp.float32)
    value_part = jnp.einsum(
        "td,ti->di", h_first, value_grad_low, preferred_element_type=jnp.float32
    )
    first_grad = jnp.einsum(
        "ti,di->td", query_grad_low, query_weight, preferred_element_type=jnp.float32
    )
    first_grad = first_grad + jnp.einsum(
        "ti,di->td", key_grad_low, key_matrix, preferred_element_type=jnp.float32
    )
    first_grad = first_grad + jnp.einsum(
        "ti,di->td", value_grad_low, value_matrix, preferred_element_type=jnp.float32
    )
    attn_gain_part = jnp.sum(first_grad * normed_first, axis=0)
    normed_first_grad = first_grad * attn_gain
    tokens_grad = mixed_grad + scale_first * (
        normed_first_grad
        - normed_first * jnp.mean(normed_first_grad * normed_first, axis=-1, keepdims=True)
    )
    shared = (
        lax.psum_scatter(query_part, ("grp", "ep"), scatter_dimension=0, tiled=True),
        lax.psum_scatter(key_part, ("grp", "ep"), scatter_dimension=0, tiled=True),
        lax.psum_scatter(value_part, ("grp", "ep"), scatter_dimension=0, tiled=True),
        lax.psum_scatter(output_part, ("grp", "ep"), scatter_dimension=1, tiled=True),
        lax.psum_scatter(attn_gain_part, ("grp", "ep"), scatter_dimension=0, tiled=True),
        lax.psum_scatter(ffn_gain_part, ("grp", "ep"), scatter_dimension=0, tiled=True),
    )
    return (
        layer_out,
        tokens_grad,
        shared[0],
        shared[1],
        shared[2],
        shared[3],
        shared[4],
        shared[5],
        expert_sums[0],
        expert_sums[1],
        expert_sums[2],
    )


def local_dense(
    tokens,
    segment_ids,
    routes,
    route_gates,
    attn_gain,
    ffn_gain,
    query_weight,
    key_matrix,
    value_matrix,
    output_weight,
    expert_gate,
    expert_up,
    expert_down,
    cotangent,
):
    f32, bf16 = jnp.float32, jnp.bfloat16
    length_total, width = tokens.shape
    owners = lax.axis_size("ep")
    experts = owners
    bit_y, bit_z, bit_far, bit_core, bit_x = 1, 2, owners // 2, owners, 2 * owners
    names = ("grp", "ep")
    count = lax.axis_size("grp") * owners
    me = lax.axis_index("grp") * owners + lax.axis_index("ep")
    core = (me // bit_core) % 2
    side = (me // bit_x) % 2
    on_core1 = core == 1

    def swap(value, mask):
        return lax.ppermute(value, names, [(i, i ^ mask) for i in range(count)])

    def swap_mixed(value, mask0, mask1):
        return lax.ppermute(
            value, names, [(i, i ^ (mask1 if i & bit_core else mask0)) for i in range(count)]
        )

    def swap_core1(value, mask):
        return lax.ppermute(value, names, [(i, i ^ mask) for i in range(count) if i & bit_core])

    def gather_group(chunk):
        from_y = swap(chunk, bit_y)
        from_z = swap(chunk, bit_z)
        far = swap_mixed(jnp.where(on_core1, from_y, from_z), bit_y, bit_z)
        mine = [chunk, from_y, from_z, far]
        return mine + [swap(part, bit_core) for part in mine]

    def reduce_group(parts):
        own, to_y, to_z, far = [
            parts[i].astype(f32) + swap(parts[4 + i], bit_core).astype(f32) for i in range(4)
        ]
        passed = swap_mixed(far.astype(bf16), bit_y, bit_z).astype(f32)
        to_y = to_y + jnp.where(on_core1, passed, 0.0)
        to_z = to_z + jnp.where(on_core1, 0.0, passed)
        return own + swap(to_y.astype(bf16), bit_y).astype(f32) + swap(
            to_z.astype(bf16), bit_z
        ).astype(f32)

    def fetch(weight):
        rows = weight.shape[0] // 2
        half = lax.dynamic_slice_in_dim(weight, side * rows, rows, 0)
        here = swap_core1(half, bit_far)
        there = swap_core1(here, bit_x)
        low = jnp.where(side == 0, here, there)
        high = jnp.where(side == 0, there, here)
        return jnp.where(on_core1, jnp.concatenate([low, high], axis=0), weight)

    def give(grad, dim):
        size = grad.shape[dim] // 2
        sent = lax.dynamic_slice_in_dim(grad, (1 - side) * size, size, dim).astype(bf16)
        kept = lax.dynamic_slice_in_dim(grad, side * size, size, dim)
        half = kept + swap(sent, bit_x).astype(f32)
        foreign = swap_core1(half.astype(bf16), bit_far).astype(f32)
        base = jnp.where(on_core1, foreign, half)
        size = size // 2
        sent = lax.dynamic_slice_in_dim(base, (1 - core) * size, size, dim).astype(bf16)
        kept = lax.dynamic_slice_in_dim(base, core * size, size, dim)
        return kept + swap(sent, bit_core).astype(f32)

    def reduce_all(value):
        order = [bit_core, bit_x, bit_y, bit_z, bit_far]
        bits = [bit_x, bit_core, bit_far, bit_z, bit_y]
        rows, columns = value.shape
        block = value.reshape((2,) * 5 + (rows // count, columns))
        for mask in order:
            axis = bits.index(mask)
            mine = (me // mask) % 2
            sent = lax.dynamic_slice_in_dim(block, 1 - mine, 1, axis)
            kept = lax.dynamic_slice_in_dim(block, mine, 1, axis)
            block = kept.astype(f32) + swap(sent.astype(bf16), mask).astype(f32)
        return block.reshape(rows // count, columns)

    cotangent_parts = gather_group(cotangent)
    weight_gate = fetch(expert_gate[0])
    weight_up = fetch(expert_up[0])
    weight_down = fetch(expert_down[0])
    table = jnp.sum(
        jnp.where(
            routes[:, :, None] == jnp.arange(experts, dtype=jnp.int32)[None, None, :],
            route_gates[:, :, None],
            0.0,
        ),
        axis=1,
    )
    tables = jnp.stack(gather_group(table.T))
    hosted = lax.axis_index("ep") ^ (bit_far * core)
    gate_column = lax.dynamic_index_in_dim(tables, hosted, 1, keepdims=False).reshape(-1)[:, None]

    query_heads = query_weight.shape[1] // HEAD_SIZE
    key_heads = key_matrix.shape[1] // HEAD_SIZE
    q_per_kv = query_heads // key_heads
    segment = segment_ids[0]
    padding = segment == jnp.max(segment)
    later = jnp.arange(length_total)[:, None] >= jnp.arange(length_total)[None, :]
    diagonal = jnp.arange(length_total)[:, None] == jnp.arange(length_total)[None, :]
    allowed = (
        later
        & (segment[:, None] == segment[None, :])
        & (jnp.logical_not(padding)[None, :] | diagonal)
    )
    position = jnp.arange(length_total, dtype=jnp.float32)
    inverse = BASE ** (-jnp.arange(HEAD_SIZE // 2, dtype=jnp.float32) * 2.0 / HEAD_SIZE)
    angle = position[:, None] * inverse[None, :]
    cosine_table = jnp.cos(angle)[:, None, :]
    sine_table = jnp.sin(angle)[:, None, :]
    tok_float = tokens.astype(jnp.float32)
    scale_first = lax.rsqrt(jnp.mean(tok_float * tok_float, axis=-1, keepdims=True) + EPS)
    normed_first = tok_float * scale_first
    h_first = (normed_first * attn_gain).astype(jnp.bfloat16)
    query_rows = jnp.dot(h_first, query_weight, preferred_element_type=jnp.float32).reshape(
        length_total, query_heads, HEAD_SIZE
    )
    key_rows = jnp.dot(h_first, key_matrix, preferred_element_type=jnp.float32).reshape(
        length_total, key_heads, HEAD_SIZE
    )
    value_low = jnp.dot(h_first, value_matrix, preferred_element_type=jnp.float32).astype(
        jnp.bfloat16
    )
    value_low = value_low.reshape(length_total, key_heads, HEAD_SIZE)
    query_rot = (
        apply_rotary(query_rows, cosine_table, sine_table)
        .astype(jnp.bfloat16)
        .reshape(length_total, key_heads, q_per_kv, HEAD_SIZE)
    )
    key_rot = apply_rotary(key_rows, cosine_table, sine_table).astype(jnp.bfloat16)
    score = scores_of(query_rot, key_rot, allowed)
    row_max = jnp.max(score, axis=-1, keepdims=True)
    expo = jnp.exp(score - row_max)
    row_sum = jnp.sum(expo, axis=-1, keepdims=True)
    log_total = row_max + jnp.log(row_sum)
    probs_low = (expo / row_sum).astype(jnp.bfloat16)
    attended = jnp.einsum(
        "kgts,skd->tkgd", probs_low, value_low, preferred_element_type=jnp.float32
    )
    attended = attended.reshape(length_total, query_heads * HEAD_SIZE).astype(jnp.bfloat16)
    mixed = tok_float + jnp.dot(attended, output_weight, preferred_element_type=jnp.float32)
    scale_second = lax.rsqrt(jnp.mean(mixed * mixed, axis=-1, keepdims=True) + EPS)
    normed_second = mixed * scale_second
    h_second = (normed_second * ffn_gain).astype(jnp.bfloat16)

    rows_in = jnp.concatenate(gather_group(h_second), axis=0)
    grad_in = jnp.concatenate(cotangent_parts, axis=0)
    gate_val = jnp.dot(rows_in, weight_gate, preferred_element_type=f32)
    up_val = jnp.dot(rows_in, weight_up, preferred_element_type=f32)
    act, act_back = jax.vjp(glu_value, gate_val, up_val)
    act_low = act.astype(bf16)
    result = jnp.dot(act_low, weight_down, preferred_element_type=f32).astype(bf16)
    weighted = (gate_column * result.astype(f32)).astype(bf16)
    slot_grads = (gate_column * grad_in.astype(f32)).astype(bf16)
    act_grad = jnp.einsum("td,fd->tf", slot_grads, weight_down, preferred_element_type=f32)
    gate_grad_val, up_grad_val = act_back(act_grad)
    gate_low = gate_grad_val.astype(bf16)
    up_low = up_grad_val.astype(bf16)
    rows_grad = jnp.einsum("tf,df->td", gate_low, weight_gate, preferred_element_type=f32)
    rows_grad = rows_grad + jnp.einsum("tf,df->td", up_low, weight_up, preferred_element_type=f32)
    rows_grad = rows_grad.astype(bf16)
    second_grad = reduce_group(
        [rows_grad[i * length_total : (i + 1) * length_total] for i in range(8)]
    )
    down_part = jnp.einsum("tf,td->fd", act_low, slot_grads, preferred_element_type=f32)
    gate_part = jnp.einsum("td,tf->df", rows_in, gate_low, preferred_element_type=f32)
    up_part = jnp.einsum("td,tf->df", rows_in, up_low, preferred_element_type=f32)
    expert_sums = (give(gate_part, 0)[None], give(up_part, 0)[None], give(down_part, 1)[None])
    combined = reduce_group([weighted[i * length_total : (i + 1) * length_total] for i in range(8)])
    layer_out = (mixed + combined).astype(bf16)
    grad_out = cotangent.astype(f32)
    ffn_gain_part = jnp.sum(second_grad * normed_second, axis=0)
    normed_grad = second_grad * ffn_gain
    mixed_grad = grad_out + scale_second * (
        normed_grad - normed_second * jnp.mean(normed_grad * normed_second, axis=-1, keepdims=True)
    )
    mixed_low = mixed_grad.astype(jnp.bfloat16)
    output_part = jnp.einsum("ti,td->di", attended, mixed_low, preferred_element_type=jnp.float32)
    output_grad = reduce_all(output_part).T
    attended_grad = jnp.einsum(
        "td,id->ti", mixed_low, output_weight, preferred_element_type=jnp.float32
    )
    attended_grad = attended_grad.astype(jnp.bfloat16).reshape(
        length_total, key_heads, q_per_kv, HEAD_SIZE
    )
    probs = jnp.exp(scores_of(query_rot, key_rot, allowed) - log_total)
    probs_again = probs.astype(jnp.bfloat16)
    value_part_grad = jnp.einsum(
        "kgts,tkgd->skd", probs_again, attended_grad, preferred_element_type=jnp.float32
    )
    prob_grad = jnp.einsum(
        "tkgd,skd->kgts", attended_grad, value_low, preferred_element_type=jnp.float32
    )
    inner = jnp.sum(probs * prob_grad, axis=-1, keepdims=True)
    score_grad = (probs * (prob_grad - inner)).astype(jnp.bfloat16)
    qrot_grad = jnp.einsum(
        "kgts,skd->tkgd", score_grad, key_rot, preferred_element_type=jnp.float32
    ) * HEAD_SIZE ** (-0.5)
    krot_grad = jnp.einsum(
        "kgts,tkgd->skd", score_grad, query_rot, preferred_element_type=jnp.float32
    ) * HEAD_SIZE ** (-0.5)
    query_grad_low = unrotate(
        qrot_grad.reshape(length_total, query_heads, HEAD_SIZE), cosine_table, sine_table
    )
    query_grad_low = query_grad_low.astype(jnp.bfloat16).reshape(
        length_total, query_heads * HEAD_SIZE
    )
    key_grad_low = (
        unrotate(krot_grad, cosine_table, sine_table)
        .astype(jnp.bfloat16)
        .reshape(length_total, key_heads * HEAD_SIZE)
    )
    value_grad_low = value_part_grad.astype(jnp.bfloat16).reshape(
        length_total, key_heads * HEAD_SIZE
    )
    projected = jnp.concatenate([query_grad_low, key_grad_low, value_grad_low], axis=1)
    projected_part = jnp.einsum("td,ti->di", h_first, projected, preferred_element_type=f32)
    first_grad = jnp.einsum(
        "ti,di->td", query_grad_low, query_weight, preferred_element_type=jnp.float32
    )
    first_grad = first_grad + jnp.einsum(
        "ti,di->td", key_grad_low, key_matrix, preferred_element_type=jnp.float32
    )
    first_grad = first_grad + jnp.einsum(
        "ti,di->td", value_grad_low, value_matrix, preferred_element_type=jnp.float32
    )
    attn_gain_part = jnp.sum(first_grad * normed_first, axis=0)
    normed_first_grad = first_grad * attn_gain
    tokens_grad = mixed_grad + scale_first * (
        normed_first_grad
        - normed_first * jnp.mean(normed_first_grad * normed_first, axis=-1, keepdims=True)
    )
    gains = jnp.stack([attn_gain_part, ffn_gain_part], axis=1)
    gains_high = gains.astype(bf16).astype(f32)
    gains = jnp.concatenate([gains_high, gains - gains_high], axis=1)
    gains = jnp.pad(gains, ((0, 0), (0, 124)))
    shared = reduce_all(jnp.concatenate([projected_part, gains], axis=1))
    split_q = query_weight.shape[1]
    split_k = split_q + key_matrix.shape[1]
    split_v = split_k + value_matrix.shape[1]
    gain_sums = shared[:, split_v : split_v + 2] + shared[:, split_v + 2 : split_v + 4]
    return (
        layer_out,
        tokens_grad,
        shared[:, :split_q],
        shared[:, split_q:split_k],
        shared[:, split_k:split_v],
        output_grad,
        gain_sums[:, 0],
        gain_sums[:, 1],
        expert_sums[0],
        expert_sums[1],
        expert_sums[2],
    )


def solution(mesh):
    in_specs = (
        P(("grp", "ep"), None),
        P(("grp", "ep"), None),
        P(("grp", "ep"), None),
        P(("grp", "ep"), None),
        P(),
        P(),
        P(),
        P(),
        P(),
        P(),
        P("ep", None, None),
        P("ep", None, None),
        P("ep", None, None),
        P(("grp", "ep"), None),
    )
    out_specs = (
        P(("grp", "ep"), None),
        P(("grp", "ep"), None),
        P(("grp", "ep"), None),
        P(("grp", "ep"), None),
        P(("grp", "ep"), None),
        P(None, ("grp", "ep")),
        P(("grp", "ep")),
        P(("grp", "ep")),
        P("ep", "grp", None),
        P("ep", "grp", None),
        P("ep", None, "grp"),
    )
    paired = mesh.shape["grp"] == 4 and mesh.shape["ep"] == 8
    local = local_dense if paired else local_routed
    return jax.shard_map(local, mesh=mesh, in_specs=in_specs, out_specs=out_specs, check_vma=False)
```

```python
import jax
import jax.numpy as jnp
from jax import lax
from jax.experimental import pallas as pl
from jax.experimental.pallas import tpu as pltpu
from jax.sharding import PartitionSpec as P

HEAD_SIZE = 128


EPS = 1e-06
BASE = 10000.0


def apply_rotary(value_rows, cosine_table, sine_table):
    half = value_rows.shape[-1] // 2
    first = value_rows[..., :half]
    second = value_rows[..., half:]
    return jnp.concatenate(
        [first * cosine_table - second * sine_table, second * cosine_table + first * sine_table],
        axis=-1,
    )


def unrotate(value_rows, cosine_table, sine_table):
    half = value_rows.shape[-1] // 2
    first = value_rows[..., :half]
    second = value_rows[..., half:]
    return jnp.concatenate(
        [first * cosine_table + second * sine_table, second * cosine_table - first * sine_table],
        axis=-1,
    )


def glu_value(gate_val, up_val):
    return jax.nn.gelu(gate_val, approximate=True) * up_val


def scores_of(query_rot, key_rot, allowed):
    score = jnp.einsum(
        "tkgd,skd->kgts", query_rot, key_rot, preferred_element_type=jnp.float32
    ) * HEAD_SIZE ** (-0.5)
    return jnp.where(allowed, score, -1e30)


def local_routed(
    tokens,
    segment_ids,
    routes,
    route_gates,
    attn_gain,
    ffn_gain,
    query_weight,
    key_matrix,
    value_matrix,
    output_weight,
    expert_gate,
    expert_up,
    expert_down,
    cotangent,
):
    length_total, width = tokens.shape
    choose = routes.shape[1]
    local_experts = expert_gate.shape[0]
    owners = lax.axis_size("ep")
    experts = owners * local_experts
    capacity = 3 * length_total * choose // (2 * experts)
    query_heads = query_weight.shape[1] // HEAD_SIZE
    key_heads = key_matrix.shape[1] // HEAD_SIZE
    q_per_kv = query_heads // key_heads
    segment = segment_ids[0]
    padding = segment == jnp.max(segment)
    later = jnp.arange(length_total)[:, None] >= jnp.arange(length_total)[None, :]
    diagonal = jnp.arange(length_total)[:, None] == jnp.arange(length_total)[None, :]
    allowed = (
        later
        & (segment[:, None] == segment[None, :])
        & (jnp.logical_not(padding)[None, :] | diagonal)
    )
    position = jnp.arange(length_total, dtype=jnp.float32)
    inverse = BASE ** (-jnp.arange(HEAD_SIZE // 2, dtype=jnp.float32) * 2.0 / HEAD_SIZE)
    angle = position[:, None] * inverse[None, :]
    cosine_table = jnp.cos(angle)[:, None, :]
    sine_table = jnp.sin(angle)[:, None, :]
    tok_float = tokens.astype(jnp.float32)
    scale_first = lax.rsqrt(jnp.mean(tok_float * tok_float, axis=-1, keepdims=True) + EPS)
    normed_first = tok_float * scale_first
    h_first = (normed_first * attn_gain).astype(jnp.bfloat16)
    query_rows = jnp.dot(h_first, query_weight, preferred_element_type=jnp.float32).reshape(
        length_total, query_heads, HEAD_SIZE
    )
    key_rows = jnp.dot(h_first, key_matrix, preferred_element_type=jnp.float32).reshape(
        length_total, key_heads, HEAD_SIZE
    )
    value_low = jnp.dot(h_first, value_matrix, preferred_element_type=jnp.float32).astype(
        jnp.bfloat16
    )
    value_low = value_low.reshape(length_total, key_heads, HEAD_SIZE)
    query_rot = (
        apply_rotary(query_rows, cosine_table, sine_table)
        .astype(jnp.bfloat16)
        .reshape(length_total, key_heads, q_per_kv, HEAD_SIZE)
    )
    key_rot = apply_rotary(key_rows, cosine_table, sine_table).astype(jnp.bfloat16)
    score = scores_of(query_rot, key_rot, allowed)
    row_max = jnp.max(score, axis=-1, keepdims=True)
    expo = jnp.exp(score - row_max)
    row_sum = jnp.sum(expo, axis=-1, keepdims=True)
    log_total = row_max + jnp.log(row_sum)
    probs_low = (expo / row_sum).astype(jnp.bfloat16)
    attended = jnp.einsum(
        "kgts,skd->tkgd", probs_low, value_low, preferred_element_type=jnp.float32
    )
    attended = attended.reshape(length_total, query_heads * HEAD_SIZE).astype(jnp.bfloat16)
    mixed = tok_float + jnp.dot(attended, output_weight, preferred_element_type=jnp.float32)
    scale_second = lax.rsqrt(jnp.mean(mixed * mixed, axis=-1, keepdims=True) + EPS)
    normed_second = mixed * scale_second
    h_second = (normed_second * ffn_gain).astype(jnp.bfloat16)
    flat_routes = routes.reshape(-1)
    assigns = flat_routes.shape[0]
    onehot = (flat_routes[:, None] == jnp.arange(experts, dtype=jnp.int32)[None, :]).astype(
        jnp.int32
    )
    position_in = jnp.sum(jnp.cumsum(onehot, axis=0) * onehot, axis=1) - 1
    slot_index = flat_routes * capacity + position_in
    source = (
        jnp.full((experts * capacity,), assigns, jnp.int32)
        .at[slot_index]
        .set(jnp.arange(assigns, dtype=jnp.int32))
    )
    token_of = source // choose
    h_ext = jnp.concatenate([h_second, jnp.zeros((1, width), jnp.bfloat16)], axis=0)
    send_rows = h_ext[token_of].reshape(owners, local_experts, capacity, width)
    row_entries = lax.all_to_all(send_rows, "ep", split_axis=0, concat_axis=0, tiled=True)
    gate_val = jnp.einsum(
        "secd,edf->secf", row_entries, expert_gate, preferred_element_type=jnp.float32
    )
    up_val = jnp.einsum(
        "secd,edf->secf", row_entries, expert_up, preferred_element_type=jnp.float32
    )
    act = glu_value(gate_val, up_val).astype(jnp.bfloat16)
    result = jnp.einsum("secf,efd->secd", act, expert_down, preferred_element_type=jnp.float32)
    outputs = (result.astype(jnp.bfloat16), row_entries, gate_val, up_val)
    returned = lax.all_to_all(outputs[0], "ep", split_axis=0, concat_axis=0, tiled=True).reshape(
        experts * capacity, width
    )
    picked = returned[slot_index].reshape(length_total, choose, width).astype(jnp.float32)
    layer_out = (mixed + jnp.sum(route_gates[:, :, None] * picked, axis=1)).astype(jnp.bfloat16)
    grad_out = cotangent.astype(jnp.float32)
    slot_grads = (
        (route_gates[:, :, None] * grad_out[:, None, :])
        .astype(jnp.bfloat16)
        .reshape(assigns, width)
    )
    slot_ext = jnp.concatenate([slot_grads, jnp.zeros((1, width), jnp.bfloat16)], axis=0)
    grad_send = slot_ext[source].reshape(owners, local_experts, capacity, width)
    grad_recv = lax.all_to_all(grad_send, "ep", split_axis=0, concat_axis=0, tiled=True)
    recv_rows = outputs[1]
    gate_val = outputs[2]
    up_val = outputs[3]
    act, act_back = jax.vjp(glu_value, gate_val, up_val)
    act_low = act.astype(jnp.bfloat16)
    down_part = jnp.einsum("secf,secd->efd", act_low, grad_recv, preferred_element_type=jnp.float32)
    act_grad = jnp.einsum(
        "secd,efd->secf", grad_recv, expert_down, preferred_element_type=jnp.float32
    )
    gate_grad_val, up_grad_val = act_back(act_grad)
    gate_low = gate_grad_val.astype(jnp.bfloat16)
    up_low = up_grad_val.astype(jnp.bfloat16)
    gate_part = jnp.einsum(
        "secd,secf->edf", recv_rows, gate_low, preferred_element_type=jnp.float32
    )
    up_part = jnp.einsum("secd,secf->edf", recv_rows, up_low, preferred_element_type=jnp.float32)
    rows_grad = jnp.einsum(
        "secf,edf->secd", gate_low, expert_gate, preferred_element_type=jnp.float32
    )
    rows_grad = rows_grad + jnp.einsum(
        "secf,edf->secd", up_low, expert_up, preferred_element_type=jnp.float32
    )
    rows_back = lax.all_to_all(
        rows_grad.astype(jnp.bfloat16), "ep", split_axis=0, concat_axis=0, tiled=True
    )
    rows_back = rows_back.reshape(experts * capacity, width)
    expert_sums = (
        lax.psum_scatter(
            gate_part.astype(jnp.bfloat16), "grp", scatter_dimension=1, tiled=True
        ).astype(jnp.float32),
        lax.psum_scatter(
            up_part.astype(jnp.bfloat16), "grp", scatter_dimension=1, tiled=True
        ).astype(jnp.float32),
        lax.psum_scatter(
            down_part.astype(jnp.bfloat16), "grp", scatter_dimension=2, tiled=True
        ).astype(jnp.float32),
    )
    second_grad = jnp.sum(
        rows_back[slot_index].reshape(length_total, choose, width).astype(jnp.float32), axis=1
    )
    ffn_gain_part = jnp.sum(second_grad * normed_second, axis=0)
    normed_grad = second_grad * ffn_gain
    mixed_grad = grad_out + scale_second * (
        normed_grad - normed_second * jnp.mean(normed_grad * normed_second, axis=-1, keepdims=True)
    )
    mixed_low = mixed_grad.astype(jnp.bfloat16)
    output_part = jnp.einsum("ti,td->id", attended, mixed_low, preferred_element_type=jnp.float32)
    attended_grad = jnp.einsum(
        "td,id->ti", mixed_low, output_weight, preferred_element_type=jnp.float32
    )
    attended_grad = attended_grad.astype(jnp.bfloat16).reshape(
        length_total, key_heads, q_per_kv, HEAD_SIZE
    )
    probs = jnp.exp(scores_of(query_rot, key_rot, allowed) - log_total)
    probs_again = probs.astype(jnp.bfloat16)
    value_part_grad = jnp.einsum(
        "kgts,tkgd->skd", probs_again, attended_grad, preferred_element_type=jnp.float32
    )
    prob_grad = jnp.einsum(
        "tkgd,skd->kgts", attended_grad, value_low, preferred_element_type=jnp.float32
    )
    inner = jnp.sum(probs * prob_grad, axis=-1, keepdims=True)
    score_grad = (probs * (prob_grad - inner)).astype(jnp.bfloat16)
    qrot_grad = jnp.einsum(
        "kgts,skd->tkgd", score_grad, key_rot, preferred_element_type=jnp.float32
    ) * HEAD_SIZE ** (-0.5)
    krot_grad = jnp.einsum(
        "kgts,tkgd->skd", score_grad, query_rot, preferred_element_type=jnp.float32
    ) * HEAD_SIZE ** (-0.5)
    query_grad_low = unrotate(
        qrot_grad.reshape(length_total, query_heads, HEAD_SIZE), cosine_table, sine_table
    )
    query_grad_low = query_grad_low.astype(jnp.bfloat16).reshape(
        length_total, query_heads * HEAD_SIZE
    )
    key_grad_low = (
        unrotate(krot_grad, cosine_table, sine_table)
        .astype(jnp.bfloat16)
        .reshape(length_total, key_heads * HEAD_SIZE)
    )
    value_grad_low = value_part_grad.astype(jnp.bfloat16).reshape(
        length_total, key_heads * HEAD_SIZE
    )
    query_part = jnp.einsum(
        "td,ti->di", h_first, query_grad_low, preferred_element_type=jnp.float32
    )
    key_part = jnp.einsum("td,ti->di", h_first, key_grad_low, preferred_element_type=jnp.float32)
    value_part = jnp.einsum(
        "td,ti->di", h_first, value_grad_low, preferred_element_type=jnp.float32
    )
    first_grad = jnp.einsum(
        "ti,di->td", query_grad_low, query_weight, preferred_element_type=jnp.float32
    )
    first_grad = first_grad + jnp.einsum(
        "ti,di->td", key_grad_low, key_matrix, preferred_element_type=jnp.float32
    )
    first_grad = first_grad + jnp.einsum(
        "ti,di->td", value_grad_low, value_matrix, preferred_element_type=jnp.float32
    )
    attn_gain_part = jnp.sum(first_grad * normed_first, axis=0)
    normed_first_grad = first_grad * attn_gain
    tokens_grad = mixed_grad + scale_first * (
        normed_first_grad
        - normed_first * jnp.mean(normed_first_grad * normed_first, axis=-1, keepdims=True)
    )
    shared = (
        lax.psum_scatter(query_part, ("grp", "ep"), scatter_dimension=0, tiled=True),
        lax.psum_scatter(key_part, ("grp", "ep"), scatter_dimension=0, tiled=True),
        lax.psum_scatter(value_part, ("grp", "ep"), scatter_dimension=0, tiled=True),
        lax.psum_scatter(output_part, ("grp", "ep"), scatter_dimension=1, tiled=True),
        lax.psum_scatter(attn_gain_part, ("grp", "ep"), scatter_dimension=0, tiled=True),
        lax.psum_scatter(ffn_gain_part, ("grp", "ep"), scatter_dimension=0, tiled=True),
    )
    return (
        layer_out,
        tokens_grad,
        shared[0],
        shared[1],
        shared[2],
        shared[3],
        shared[4],
        shared[5],
        expert_sums[0],
        expert_sums[1],
        expert_sums[2],
    )


SLOT_ORDER = (0, 4, 1, 5, 2, 6, 7, 3)


def moe_kernel(
    tab_ref, h_ref, dy_ref, wg_ref, wu_ref, wd_ref,
    grad_gate_ref, grad_up_ref, grad_down_ref, out_own_ref, out_sib_ref, d_own_ref, d_sib_ref,
    d_first_ref, d_second_ref,
    xb, dyb, tab, w_gate, w_up, w_down, acc_gate, acc_up, acc_down, act_s, gate_s, up_s, dz_s,
    sib, far_in, gather_send, gather_recv, tab_send, tab_recv, local_sem, part_send, part_recv,
    keep_sem, sum_send, sum_recv, store_sem,
):
    f32, bf16 = jnp.float32, jnp.bfloat16
    grp, ep = lax.axis_index("grp"), lax.axis_index("ep")
    core = lax.rem(grp, 2)
    low = lax.rem(ep, 4)
    y, z = lax.rem(low, 2), low // 2
    by_y = ep + 1 - 2 * y
    by_z = ep + 2 - 4 * z
    by_far = by_y + 2 - 4 * z
    first = by_y * (1 - core) + by_z * core
    second = by_z * (1 - core) + by_y * core
    other = grp + 1 - 2 * core
    hosted = lax.rem(ep + 4 * core, 8)
    rows = h_ref.shape[0]
    half = rows // 2

    def remote(src, dst, send, recv, device):
        return pltpu.make_async_remote_copy(
            src_ref=src, dst_ref=dst, send_sem=send, recv_sem=recv, device_id=device,
            device_id_type=pl.DeviceIdType.MESH,
        )

    members = (
        ((grp, first), 1), ((grp, second), 2), ((grp, by_far), 3), ((other, ep), 4),
        ((other, first), 5), ((other, second), 6), ((other, by_far), 7),
    )
    barrier = pltpu.get_barrier_semaphore()
    for device, _ in members:
        pl.semaphore_signal(barrier, inc=1, device_id=device, device_id_type=pl.DeviceIdType.MESH)
    pl.semaphore_wait(barrier, 7)

    def gather_copy(k, number):
        own, buf = ((h_ref, xb), (dy_ref, dyb))[k]
        src, dst, device = (
            (own, 1, (grp, first)), (own, 4, (other, ep)), (own, 2, (grp, second)),
            (buf.at[1], 5, (other, ep)), (buf.at[2], 6, (other, ep)),
            (buf.at[2], 3, (grp, first)), (buf.at[3], 7, (other, ep)),
        )[number]
        return remote(
            src, buf.at[dst], gather_send.at[k, number], gather_recv.at[k, number], device
        )

    arrival = {1: 0, 4: 1, 2: 2, 5: 3, 6: 4, 3: 5, 7: 6}

    def start(*numbers):
        for number in numbers:
            for k in (0, 1):
                gather_copy(k, number).start()

    def sent(*numbers):
        for number in numbers:
            for k in (0, 1):
                gather_copy(k, number).wait_send()

    def arrived(slot):
        for k in (0, 1):
            gather_copy(k, arrival[slot]).wait_recv()

    locals_in = [
        pltpu.make_async_copy(src, dst, local_sem.at[i])
        for i, (src, dst) in enumerate(
            ((h_ref, xb.at[0]), (dy_ref, dyb.at[0]), (wg_ref, w_gate), (wu_ref, w_up), (wd_ref, w_down))
        )
    ]
    for copy in locals_in:
        copy.start()
    table_copies = [
        remote(tab_ref, tab.at[slot], tab_send.at[slot], tab_recv.at[slot], device)
        for device, slot in members
    ]
    for copy in table_copies:
        copy.start()
    start(0, 1)
    tab[0] = tab_ref[...]
    acc_gate[...] = jnp.zeros_like(acc_gate)
    acc_up[...] = jnp.zeros_like(acc_up)
    acc_down[...] = jnp.zeros_like(acc_down)
    for copy in locals_in:
        copy.wait()
    for copy in table_copies:
        copy.wait_send()
        copy.wait_recv()

    def keep_copy(j, src):
        return pltpu.make_async_copy(src, out_own_ref.at[j], keep_sem.at[j])

    def part_copies(j, dest):
        grad_dst = d_sib_ref if j == 0 else sib.at[j - 1]
        return (
            remote(xb.at[dest], grad_dst, part_send.at[0, j], part_recv.at[0, j], (other, ep)),
            remote(
                dyb.at[dest], out_sib_ref.at[j], part_send.at[1, j], part_recv.at[1, j], (other, ep)
            ),
        )

    own_grad = pltpu.make_async_copy(xb.at[8], d_own_ref, keep_sem.at[4])
    send_first = remote(xb.at[4], d_first_ref, sum_send.at[0], sum_recv.at[0], (grp, first))
    send_far = remote(xb.at[7], far_in, sum_send.at[1], sum_recv.at[1], (grp, first))
    send_second = remote(xb.at[5], d_second_ref, sum_send.at[2], sum_recv.at[2], (grp, second))

    def dot_nt(a, b):
        return lax.dot_general(a, b, (((1,), (1,)), ((), ())), preferred_element_type=f32)

    def dot_tn(a, b):
        return lax.dot_general(a, b, (((0,), (0,)), ((), ())), preferred_element_type=f32)

    def gates(slot):
        block = jnp.transpose(tab[slot])
        lane = lax.broadcasted_iota(jnp.int32, block.shape, 1)
        return jnp.sum(jnp.where(lane == hosted, block, 0.0), axis=1, keepdims=True)

    c0 = 0.7978845608028654
    c1 = 0.044715

    def work_in(slot):
        column = gates(slot)
        for part in range(2):
            at = pl.ds(part * half, half)
            x = xb[slot, at, :]
            gate = column[part * half : (part + 1) * half]
            g = jnp.dot(x, w_gate[...], preferred_element_type=f32)
            u = jnp.dot(x, w_up[...], preferred_element_type=f32)
            dz = (gate * dyb[slot, at, :].astype(f32)).astype(bf16)
            dz_s[at, :] = dz
            da = dot_nt(dz, w_down[...])
            square = g * g
            t = jnp.tanh(c0 * (g + c1 * square * g))
            gelu = 0.5 * g * (1.0 + t)
            slope = 0.5 * (1.0 + t) + 0.5 * g * (1.0 - t * t) * (c0 * (1.0 + 3.0 * c1 * square))
            act_s[at, :] = (gelu * u).astype(bf16)
            gate_s[at, :] = (da * u * slope).astype(bf16)
            up_s[at, :] = (da * gelu).astype(bf16)
        for part in range(3):
            at = pl.ds(part * 512, 512)
            x = xb[slot, :, at]
            acc_gate[at, :] += dot_tn(x, gate_s[...])
            acc_up[at, :] += dot_tn(x, up_s[...])
            at = pl.ds(part * 256, 256)
            acc_down[at, :] += dot_tn(act_s[:, at], dz_s[...])

    def work_out(slot, dest):
        column = gates(slot)
        for part in range(2):
            at = pl.ds(part * half, half)
            gate = column[part * half : (part + 1) * half]
            dx = dot_nt(gate_s[at, :], w_gate[...]) + dot_nt(up_s[at, :], w_up[...])
            xb[dest, at, :] = dx.astype(bf16)
            result = jnp.dot(act_s[at, :], w_down[...], preferred_element_type=f32)
            dyb[dest, at, :] = (gate * result.astype(bf16).astype(f32)).astype(bf16)

    def slot_at(step):
        pair, odd = step // 2, lax.rem(step, 2)
        last = pair // 3
        return pair + 4 * (odd * (1 - last) + (1 - odd) * last)

    @pl.loop(0, 8)
    def _(step):
        def at_step(number):
            return pl.when(step == number)

        @at_step(1)
        def _():
            start(2)
            arrived(4)

        @at_step(2)
        def _():
            arrived(1)
            start(3)

        @at_step(3)
        def _():
            arrived(5)

        @at_step(4)
        def _():
            arrived(2)
            start(5, 4)

        @at_step(5)
        def _():
            arrived(6)

        @at_step(6)
        def _():
            arrived(3)
            start(6)
            arrived(7)

        slot = slot_at(step)
        first_step = (8 - step) // 8
        dest = (1 - first_step) * slot_at(step - 1 + first_step) + 8 * first_step
        work_in(slot)

        @at_step(3)
        def _():
            sent(3)

        @at_step(5)
        def _():
            sent(5, 4)

        work_out(slot, dest)

        for number, (slot_now, slot_before) in enumerate(zip(SLOT_ORDER, (8,) + SLOT_ORDER)):

            @at_step(number)
            def _(slot_now=slot_now, slot_before=slot_before):
                if slot_now < 4:
                    keep_copy(slot_now, dyb.at[slot_before]).start()
                else:
                    for copy in part_copies(slot_now - 4, slot_before):
                        copy.start()

        @at_step(0)
        def _():
            own_grad.start()

        @at_step(4)
        def _():
            part_copies(1, 1)[0].wait_recv()
            xb[4] = (xb[4].astype(f32) + sib[0].astype(f32)).astype(bf16)
            send_first.start()

    part_copies(3, 6)[0].wait_recv()
    xb[7] = (xb[7].astype(f32) + sib[2].astype(f32)).astype(bf16)
    send_far.start()
    w_gate[...] = acc_gate[...].astype(bf16)
    w_up[...] = acc_up[...].astype(bf16)
    w_down[...] = acc_down[...].astype(bf16)
    stores = [
        pltpu.make_async_copy(src, dst, store_sem.at[i])
        for i, (src, dst) in enumerate(
            ((w_gate, grad_gate_ref), (w_up, grad_up_ref), (w_down, grad_down_ref))
        )
    ]
    for copy in stores:
        copy.start()
    part_copies(2, 2)[0].wait_recv()
    send_far.wait_recv()
    xb[5] = (xb[5].astype(f32) + sib[1].astype(f32) + far_in[...].astype(f32)).astype(bf16)
    send_second.start()
    sent(0, 1, 2, 6)
    for j, slot_before in enumerate((0, 1, 2, 6)):
        for k, copy in enumerate(part_copies(j, slot_before)):
            copy.wait_send()
            if k == 1 or j == 0:
                copy.wait_recv()
    for j, slot_before in enumerate((8, 4, 5, 7)):
        keep_copy(j, dyb.at[slot_before]).wait()
    own_grad.wait()
    for copy in stores:
        copy.wait()
    send_first.wait()
    send_far.wait_send()
    send_second.wait()


def moe_call(table, rows_in, grad_in, weight_gate, weight_up, weight_down):
    f32, bf16 = jnp.float32, jnp.bfloat16
    rows, width = rows_in.shape
    hidden = weight_gate.shape[1]
    anywhere = pl.BlockSpec(memory_space=pl.ANY)
    chunk = jax.ShapeDtypeStruct((rows, width), bf16)
    four = jax.ShapeDtypeStruct((4, rows, width), bf16)
    wide = jax.ShapeDtypeStruct((width, hidden), bf16)
    tall = jax.ShapeDtypeStruct((hidden, width), bf16)
    dma = pltpu.SemaphoreType.DMA
    return pl.pallas_call(
        moe_kernel,
        out_shape=(wide, wide, tall, four, four, chunk, chunk, chunk, chunk),
        in_specs=[pl.BlockSpec(memory_space=pltpu.VMEM)] + [anywhere] * 5,
        out_specs=(anywhere,) * 9,
        scratch_shapes=[
            pltpu.VMEM((9, rows, width), bf16),
            pltpu.VMEM((9, rows, width), bf16),
            pltpu.VMEM((8,) + table.shape, f32),
            pltpu.VMEM((width, hidden), bf16),
            pltpu.VMEM((width, hidden), bf16),
            pltpu.VMEM((hidden, width), bf16),
            pltpu.VMEM((width, hidden), f32),
            pltpu.VMEM((width, hidden), f32),
            pltpu.VMEM((hidden, width), f32),
            pltpu.VMEM((rows, hidden), bf16),
            pltpu.VMEM((rows, hidden), bf16),
            pltpu.VMEM((rows, hidden), bf16),
            pltpu.VMEM((rows, width), bf16),
            pltpu.VMEM((3, rows, width), bf16),
            pltpu.VMEM((rows, width), bf16),
            dma((2, 7)),
            dma((2, 7)),
            dma((8,)),
            dma((8,)),
            dma((5,)),
            dma((2, 4)),
            dma((2, 4)),
            dma((5,)),
            dma((3,)),
            dma((3,)),
            dma((3,)),
        ],
        compiler_params=pltpu.CompilerParams(
            collective_id=0, has_side_effects=True, vmem_limit_bytes=63 * 2**20
        ),
        cost_estimate=pl.CostEstimate(
            flops=16 * 9 * rows * width * hidden, bytes_accessed=60 * 2**20, transcendentals=0
        ),
    )(table, rows_in, grad_in, weight_gate, weight_up, weight_down)


def local_dense(
    tokens,
    segment_ids,
    routes,
    route_gates,
    attn_gain,
    ffn_gain,
    query_weight,
    key_matrix,
    value_matrix,
    output_weight,
    expert_gate,
    expert_up,
    expert_down,
    cotangent,
):
    f32, bf16 = jnp.float32, jnp.bfloat16
    length_total, width = tokens.shape
    owners = lax.axis_size("ep")
    experts = owners
    bit_y, bit_z, bit_far, bit_core, bit_x = 1, 2, owners // 2, owners, 2 * owners
    names = ("grp", "ep")
    count = lax.axis_size("grp") * owners
    me = lax.axis_index("grp") * owners + lax.axis_index("ep")
    core = (me // bit_core) % 2
    side = (me // bit_x) % 2
    on_core1 = core == 1

    def swap(value, mask):
        return lax.ppermute(value, names, [(i, i ^ mask) for i in range(count)])

    def swap_mixed(value, mask0, mask1):
        return lax.ppermute(
            value, names, [(i, i ^ (mask1 if i & bit_core else mask0)) for i in range(count)]
        )

    def swap_core1(value, mask):
        return lax.ppermute(value, names, [(i, i ^ mask) for i in range(count) if i & bit_core])

    def reduce_outputs(own_parts, sibling_parts):
        own, to_first, to_second, far = [
            own_parts[i].astype(f32) + sibling_parts[i].astype(f32) for i in range(4)
        ]
        to_second = to_second + swap_mixed(far.astype(bf16), bit_y, bit_z).astype(f32)
        return own + swap_mixed(to_first.astype(bf16), bit_y, bit_z).astype(f32) + swap_mixed(
            to_second.astype(bf16), bit_z, bit_y
        ).astype(f32)

    def fetch(weight):
        rows = weight.shape[0] // 2
        half = lax.dynamic_slice_in_dim(weight, side * rows, rows, 0)
        here = swap_core1(half, bit_far)
        there = swap_core1(here, bit_x)
        low = jnp.where(side == 0, here, there)
        high = jnp.where(side == 0, there, here)
        return jnp.where(on_core1, jnp.concatenate([low, high], axis=0), weight)

    def give(grad, dim):
        size = grad.shape[dim] // 2
        sent = lax.dynamic_slice_in_dim(grad, (1 - side) * size, size, dim).astype(bf16)
        kept = lax.dynamic_slice_in_dim(grad, side * size, size, dim)
        half = kept.astype(f32) + swap(sent, bit_x).astype(f32)
        foreign = swap_core1(half.astype(bf16), bit_far).astype(f32)
        base = jnp.where(on_core1, foreign, half)
        size = size // 2
        sent = lax.dynamic_slice_in_dim(base, (1 - core) * size, size, dim).astype(bf16)
        kept = lax.dynamic_slice_in_dim(base, core * size, size, dim)
        return kept + swap(sent, bit_core).astype(f32)

    def reduce_all(value):
        order = [bit_core, bit_x, bit_y, bit_z, bit_far]
        bits = [bit_x, bit_core, bit_far, bit_z, bit_y]
        rows, columns = value.shape
        block = value.reshape((2,) * 5 + (rows // count, columns))
        for mask in order:
            axis = bits.index(mask)
            mine = (me // mask) % 2
            sent = lax.dynamic_slice_in_dim(block, 1 - mine, 1, axis)
            kept = lax.dynamic_slice_in_dim(block, mine, 1, axis)
            block = kept.astype(f32) + swap(sent.astype(bf16), mask).astype(f32)
        return block.reshape(rows // count, columns)

    weight_gate = fetch(expert_gate[0])
    weight_up = fetch(expert_up[0])
    weight_down = fetch(expert_down[0])
    table = jnp.sum(
        jnp.where(
            routes[:, :, None] == jnp.arange(experts, dtype=jnp.int32)[None, None, :],
            route_gates[:, :, None],
            0.0,
        ),
        axis=1,
    )
    query_heads = query_weight.shape[1] // HEAD_SIZE
    key_heads = key_matrix.shape[1] // HEAD_SIZE
    q_per_kv = query_heads // key_heads
    segment = segment_ids[0]
    padding = segment == jnp.max(segment)
    later = jnp.arange(length_total)[:, None] >= jnp.arange(length_total)[None, :]
    diagonal = jnp.arange(length_total)[:, None] == jnp.arange(length_total)[None, :]
    allowed = (
        later
        & (segment[:, None] == segment[None, :])
        & (jnp.logical_not(padding)[None, :] | diagonal)
    )
    position = jnp.arange(length_total, dtype=jnp.float32)
    inverse = BASE ** (-jnp.arange(HEAD_SIZE // 2, dtype=jnp.float32) * 2.0 / HEAD_SIZE)
    angle = position[:, None] * inverse[None, :]
    cosine_table = jnp.cos(angle)[:, None, :]
    sine_table = jnp.sin(angle)[:, None, :]
    tok_float = tokens.astype(jnp.float32)
    scale_first = lax.rsqrt(jnp.mean(tok_float * tok_float, axis=-1, keepdims=True) + EPS)
    normed_first = tok_float * scale_first
    h_first = (normed_first * attn_gain).astype(jnp.bfloat16)
    query_rows = jnp.dot(h_first, query_weight, preferred_element_type=jnp.float32).reshape(
        length_total, query_heads, HEAD_SIZE
    )
    key_rows = jnp.dot(h_first, key_matrix, preferred_element_type=jnp.float32).reshape(
        length_total, key_heads, HEAD_SIZE
    )
    value_low = jnp.dot(h_first, value_matrix, preferred_element_type=jnp.float32).astype(
        jnp.bfloat16
    )
    value_low = value_low.reshape(length_total, key_heads, HEAD_SIZE)
    query_rot = (
        apply_rotary(query_rows, cosine_table, sine_table)
        .astype(jnp.bfloat16)
        .reshape(length_total, key_heads, q_per_kv, HEAD_SIZE)
    )
    key_rot = apply_rotary(key_rows, cosine_table, sine_table).astype(jnp.bfloat16)
    score = scores_of(query_rot, key_rot, allowed)
    row_max = jnp.max(score, axis=-1, keepdims=True)
    expo = jnp.exp(score - row_max)
    row_sum = jnp.sum(expo, axis=-1, keepdims=True)
    log_total = row_max + jnp.log(row_sum)
    probs_low = (expo / row_sum).astype(jnp.bfloat16)
    attended = jnp.einsum(
        "kgts,skd->tkgd", probs_low, value_low, preferred_element_type=jnp.float32
    )
    attended = attended.reshape(length_total, query_heads * HEAD_SIZE).astype(jnp.bfloat16)
    mixed = tok_float + jnp.dot(attended, output_weight, preferred_element_type=jnp.float32)
    scale_second = lax.rsqrt(jnp.mean(mixed * mixed, axis=-1, keepdims=True) + EPS)
    normed_second = mixed * scale_second
    h_second = (normed_second * ffn_gain).astype(jnp.bfloat16)

    (
        gate_part,
        up_part,
        down_part,
        out_own,
        out_sib,
        *second_parts,
    ) = moe_call(table.T, h_second, cotangent, weight_gate, weight_up, weight_down)
    second_grad = sum(part.astype(f32) for part in second_parts)
    expert_sums = (give(gate_part, 0)[None], give(up_part, 0)[None], give(down_part, 1)[None])
    layer_out = (mixed + reduce_outputs(out_own, out_sib)).astype(bf16)
    grad_out = cotangent.astype(f32)
    ffn_gain_part = jnp.sum(second_grad * normed_second, axis=0)
    normed_grad = second_grad * ffn_gain
    mixed_grad = grad_out + scale_second * (
        normed_grad - normed_second * jnp.mean(normed_grad * normed_second, axis=-1, keepdims=True)
    )
    mixed_low = mixed_grad.astype(jnp.bfloat16)
    output_part = jnp.einsum("ti,td->di", attended, mixed_low, preferred_element_type=jnp.float32)
    output_grad = reduce_all(output_part).T
    attended_grad = jnp.einsum(
        "td,id->ti", mixed_low, output_weight, preferred_element_type=jnp.float32
    )
    attended_grad = attended_grad.astype(jnp.bfloat16).reshape(
        length_total, key_heads, q_per_kv, HEAD_SIZE
    )
    probs = jnp.exp(scores_of(query_rot, key_rot, allowed) - log_total)
    probs_again = probs.astype(jnp.bfloat16)
    value_part_grad = jnp.einsum(
        "kgts,tkgd->skd", probs_again, attended_grad, preferred_element_type=jnp.float32
    )
    prob_grad = jnp.einsum(
        "tkgd,skd->kgts", attended_grad, value_low, preferred_element_type=jnp.float32
    )
    inner = jnp.sum(probs * prob_grad, axis=-1, keepdims=True)
    score_grad = (probs * (prob_grad - inner)).astype(jnp.bfloat16)
    qrot_grad = jnp.einsum(
        "kgts,skd->tkgd", score_grad, key_rot, preferred_element_type=jnp.float32
    ) * HEAD_SIZE ** (-0.5)
    krot_grad = jnp.einsum(
        "kgts,tkgd->skd", score_grad, query_rot, preferred_element_type=jnp.float32
    ) * HEAD_SIZE ** (-0.5)
    query_grad_low = unrotate(
        qrot_grad.reshape(length_total, query_heads, HEAD_SIZE), cosine_table, sine_table
    )
    query_grad_low = query_grad_low.astype(jnp.bfloat16).reshape(
        length_total, query_heads * HEAD_SIZE
    )
    key_grad_low = (
        unrotate(krot_grad, cosine_table, sine_table)
        .astype(jnp.bfloat16)
        .reshape(length_total, key_heads * HEAD_SIZE)
    )
    value_grad_low = value_part_grad.astype(jnp.bfloat16).reshape(
        length_total, key_heads * HEAD_SIZE
    )
    projected = jnp.concatenate([query_grad_low, key_grad_low, value_grad_low], axis=1)
    projected_part = jnp.einsum("td,ti->di", h_first, projected, preferred_element_type=f32)
    first_grad = jnp.einsum(
        "ti,di->td", query_grad_low, query_weight, preferred_element_type=jnp.float32
    )
    first_grad = first_grad + jnp.einsum(
        "ti,di->td", key_grad_low, key_matrix, preferred_element_type=jnp.float32
    )
    first_grad = first_grad + jnp.einsum(
        "ti,di->td", value_grad_low, value_matrix, preferred_element_type=jnp.float32
    )
    attn_gain_part = jnp.sum(first_grad * normed_first, axis=0)
    normed_first_grad = first_grad * attn_gain
    tokens_grad = mixed_grad + scale_first * (
        normed_first_grad
        - normed_first * jnp.mean(normed_first_grad * normed_first, axis=-1, keepdims=True)
    )
    gains = jnp.stack([attn_gain_part, ffn_gain_part], axis=1)
    gains_high = gains.astype(bf16).astype(f32)
    gains = jnp.concatenate([gains_high, gains - gains_high], axis=1)
    gains = jnp.pad(gains, ((0, 0), (0, 124)))
    shared = reduce_all(jnp.concatenate([projected_part, gains], axis=1))
    split_q = query_weight.shape[1]
    split_k = split_q + key_matrix.shape[1]
    split_v = split_k + value_matrix.shape[1]
    gain_sums = shared[:, split_v : split_v + 2] + shared[:, split_v + 2 : split_v + 4]
    return (
        layer_out,
        tokens_grad,
        shared[:, :split_q],
        shared[:, split_q:split_k],
        shared[:, split_k:split_v],
        output_grad,
        gain_sums[:, 0],
        gain_sums[:, 1],
        expert_sums[0],
        expert_sums[1],
        expert_sums[2],
    )


def solution(mesh):
    in_specs = (
        P(("grp", "ep"), None),
        P(("grp", "ep"), None),
        P(("grp", "ep"), None),
        P(("grp", "ep"), None),
        P(),
        P(),
        P(),
        P(),
        P(),
        P(),
        P("ep", None, None),
        P("ep", None, None),
        P("ep", None, None),
        P(("grp", "ep"), None),
    )
    out_specs = (
        P(("grp", "ep"), None),
        P(("grp", "ep"), None),
        P(("grp", "ep"), None),
        P(("grp", "ep"), None),
        P(("grp", "ep"), None),
        P(None, ("grp", "ep")),
        P(("grp", "ep")),
        P(("grp", "ep")),
        P("ep", "grp", None),
        P("ep", "grp", None),
        P("ep", None, "grp"),
    )
    paired = mesh.shape["grp"] == 4 and mesh.shape["ep"] == 8
    local = local_dense if paired else local_routed
    return jax.shard_map(local, mesh=mesh, in_specs=in_specs, out_specs=out_specs, check_vma=False)
```

```python
import jax
import jax.numpy as jnp
from jax import lax
from jax.experimental import pallas as pl
from jax.experimental.pallas import tpu as pltpu
from jax.sharding import PartitionSpec as P

HEAD_SIZE = 128


EPS = 1e-06
BASE = 10000.0


def apply_rotary(value_rows, cosine_table, sine_table):
    half = value_rows.shape[-1] // 2
    first = value_rows[..., :half]
    second = value_rows[..., half:]
    return jnp.concatenate(
        [first * cosine_table - second * sine_table, second * cosine_table + first * sine_table],
        axis=-1,
    )


def unrotate(value_rows, cosine_table, sine_table):
    half = value_rows.shape[-1] // 2
    first = value_rows[..., :half]
    second = value_rows[..., half:]
    return jnp.concatenate(
        [first * cosine_table + second * sine_table, second * cosine_table - first * sine_table],
        axis=-1,
    )


def glu_value(gate_val, up_val):
    return jax.nn.gelu(gate_val, approximate=True) * up_val


def scores_of(query_rot, key_rot, allowed):
    score = jnp.einsum(
        "tkgd,skd->kgts", query_rot, key_rot, preferred_element_type=jnp.float32
    ) * HEAD_SIZE ** (-0.5)
    return jnp.where(allowed, score, -1e30)


def local_routed(
    tokens,
    segment_ids,
    routes,
    route_gates,
    attn_gain,
    ffn_gain,
    query_weight,
    key_matrix,
    value_matrix,
    output_weight,
    expert_gate,
    expert_up,
    expert_down,
    cotangent,
):
    length_total, width = tokens.shape
    choose = routes.shape[1]
    local_experts = expert_gate.shape[0]
    owners = lax.axis_size("ep")
    experts = owners * local_experts
    capacity = 3 * length_total * choose // (2 * experts)
    query_heads = query_weight.shape[1] // HEAD_SIZE
    key_heads = key_matrix.shape[1] // HEAD_SIZE
    q_per_kv = query_heads // key_heads
    segment = segment_ids[0]
    padding = segment == jnp.max(segment)
    later = jnp.arange(length_total)[:, None] >= jnp.arange(length_total)[None, :]
    diagonal = jnp.arange(length_total)[:, None] == jnp.arange(length_total)[None, :]
    allowed = (
        later
        & (segment[:, None] == segment[None, :])
        & (jnp.logical_not(padding)[None, :] | diagonal)
    )
    position = jnp.arange(length_total, dtype=jnp.float32)
    inverse = BASE ** (-jnp.arange(HEAD_SIZE // 2, dtype=jnp.float32) * 2.0 / HEAD_SIZE)
    angle = position[:, None] * inverse[None, :]
    cosine_table = jnp.cos(angle)[:, None, :]
    sine_table = jnp.sin(angle)[:, None, :]
    tok_float = tokens.astype(jnp.float32)
    scale_first = lax.rsqrt(jnp.mean(tok_float * tok_float, axis=-1, keepdims=True) + EPS)
    normed_first = tok_float * scale_first
    h_first = (normed_first * attn_gain).astype(jnp.bfloat16)
    query_rows = jnp.dot(h_first, query_weight, preferred_element_type=jnp.float32).reshape(
        length_total, query_heads, HEAD_SIZE
    )
    key_rows = jnp.dot(h_first, key_matrix, preferred_element_type=jnp.float32).reshape(
        length_total, key_heads, HEAD_SIZE
    )
    value_low = jnp.dot(h_first, value_matrix, preferred_element_type=jnp.float32).astype(
        jnp.bfloat16
    )
    value_low = value_low.reshape(length_total, key_heads, HEAD_SIZE)
    query_rot = (
        apply_rotary(query_rows, cosine_table, sine_table)
        .astype(jnp.bfloat16)
        .reshape(length_total, key_heads, q_per_kv, HEAD_SIZE)
    )
    key_rot = apply_rotary(key_rows, cosine_table, sine_table).astype(jnp.bfloat16)
    score = scores_of(query_rot, key_rot, allowed)
    row_max = jnp.max(score, axis=-1, keepdims=True)
    expo = jnp.exp(score - row_max)
    row_sum = jnp.sum(expo, axis=-1, keepdims=True)
    log_total = row_max + jnp.log(row_sum)
    probs_low = (expo / row_sum).astype(jnp.bfloat16)
    attended = jnp.einsum(
        "kgts,skd->tkgd", probs_low, value_low, preferred_element_type=jnp.float32
    )
    attended = attended.reshape(length_total, query_heads * HEAD_SIZE).astype(jnp.bfloat16)
    mixed = tok_float + jnp.dot(attended, output_weight, preferred_element_type=jnp.float32)
    scale_second = lax.rsqrt(jnp.mean(mixed * mixed, axis=-1, keepdims=True) + EPS)
    normed_second = mixed * scale_second
    h_second = (normed_second * ffn_gain).astype(jnp.bfloat16)
    flat_routes = routes.reshape(-1)
    assigns = flat_routes.shape[0]
    onehot = (flat_routes[:, None] == jnp.arange(experts, dtype=jnp.int32)[None, :]).astype(
        jnp.int32
    )
    position_in = jnp.sum(jnp.cumsum(onehot, axis=0) * onehot, axis=1) - 1
    slot_index = flat_routes * capacity + position_in
    source = (
        jnp.full((experts * capacity,), assigns, jnp.int32)
        .at[slot_index]
        .set(jnp.arange(assigns, dtype=jnp.int32))
    )
    token_of = source // choose
    h_ext = jnp.concatenate([h_second, jnp.zeros((1, width), jnp.bfloat16)], axis=0)
    send_rows = h_ext[token_of].reshape(owners, local_experts, capacity, width)
    row_entries = lax.all_to_all(send_rows, "ep", split_axis=0, concat_axis=0, tiled=True)
    gate_val = jnp.einsum(
        "secd,edf->secf", row_entries, expert_gate, preferred_element_type=jnp.float32
    )
    up_val = jnp.einsum(
        "secd,edf->secf", row_entries, expert_up, preferred_element_type=jnp.float32
    )
    act = glu_value(gate_val, up_val).astype(jnp.bfloat16)
    result = jnp.einsum("secf,efd->secd", act, expert_down, preferred_element_type=jnp.float32)
    outputs = (result.astype(jnp.bfloat16), row_entries, gate_val, up_val)
    returned = lax.all_to_all(outputs[0], "ep", split_axis=0, concat_axis=0, tiled=True).reshape(
        experts * capacity, width
    )
    picked = returned[slot_index].reshape(length_total, choose, width).astype(jnp.float32)
    layer_out = (mixed + jnp.sum(route_gates[:, :, None] * picked, axis=1)).astype(jnp.bfloat16)
    grad_out = cotangent.astype(jnp.float32)
    slot_grads = (
        (route_gates[:, :, None] * grad_out[:, None, :])
        .astype(jnp.bfloat16)
        .reshape(assigns, width)
    )
    slot_ext = jnp.concatenate([slot_grads, jnp.zeros((1, width), jnp.bfloat16)], axis=0)
    grad_send = slot_ext[source].reshape(owners, local_experts, capacity, width)
    grad_recv = lax.all_to_all(grad_send, "ep", split_axis=0, concat_axis=0, tiled=True)
    recv_rows = outputs[1]
    gate_val = outputs[2]
    up_val = outputs[3]
    act, act_back = jax.vjp(glu_value, gate_val, up_val)
    act_low = act.astype(jnp.bfloat16)
    down_part = jnp.einsum("secf,secd->efd", act_low, grad_recv, preferred_element_type=jnp.float32)
    act_grad = jnp.einsum(
        "secd,efd->secf", grad_recv, expert_down, preferred_element_type=jnp.float32
    )
    gate_grad_val, up_grad_val = act_back(act_grad)
    gate_low = gate_grad_val.astype(jnp.bfloat16)
    up_low = up_grad_val.astype(jnp.bfloat16)
    gate_part = jnp.einsum(
        "secd,secf->edf", recv_rows, gate_low, preferred_element_type=jnp.float32
    )
    up_part = jnp.einsum("secd,secf->edf", recv_rows, up_low, preferred_element_type=jnp.float32)
    rows_grad = jnp.einsum(
        "secf,edf->secd", gate_low, expert_gate, preferred_element_type=jnp.float32
    )
    rows_grad = rows_grad + jnp.einsum(
        "secf,edf->secd", up_low, expert_up, preferred_element_type=jnp.float32
    )
    rows_back = lax.all_to_all(
        rows_grad.astype(jnp.bfloat16), "ep", split_axis=0, concat_axis=0, tiled=True
    )
    rows_back = rows_back.reshape(experts * capacity, width)
    expert_sums = (
        lax.psum_scatter(
            gate_part.astype(jnp.bfloat16), "grp", scatter_dimension=1, tiled=True
        ).astype(jnp.float32),
        lax.psum_scatter(
            up_part.astype(jnp.bfloat16), "grp", scatter_dimension=1, tiled=True
        ).astype(jnp.float32),
        lax.psum_scatter(
            down_part.astype(jnp.bfloat16), "grp", scatter_dimension=2, tiled=True
        ).astype(jnp.float32),
    )
    second_grad = jnp.sum(
        rows_back[slot_index].reshape(length_total, choose, width).astype(jnp.float32), axis=1
    )
    ffn_gain_part = jnp.sum(second_grad * normed_second, axis=0)
    normed_grad = second_grad * ffn_gain
    mixed_grad = grad_out + scale_second * (
        normed_grad - normed_second * jnp.mean(normed_grad * normed_second, axis=-1, keepdims=True)
    )
    mixed_low = mixed_grad.astype(jnp.bfloat16)
    output_part = jnp.einsum("ti,td->id", attended, mixed_low, preferred_element_type=jnp.float32)
    attended_grad = jnp.einsum(
        "td,id->ti", mixed_low, output_weight, preferred_element_type=jnp.float32
    )
    attended_grad = attended_grad.astype(jnp.bfloat16).reshape(
        length_total, key_heads, q_per_kv, HEAD_SIZE
    )
    probs = jnp.exp(scores_of(query_rot, key_rot, allowed) - log_total)
    probs_again = probs.astype(jnp.bfloat16)
    value_part_grad = jnp.einsum(
        "kgts,tkgd->skd", probs_again, attended_grad, preferred_element_type=jnp.float32
    )
    prob_grad = jnp.einsum(
        "tkgd,skd->kgts", attended_grad, value_low, preferred_element_type=jnp.float32
    )
    inner = jnp.sum(probs * prob_grad, axis=-1, keepdims=True)
    score_grad = (probs * (prob_grad - inner)).astype(jnp.bfloat16)
    qrot_grad = jnp.einsum(
        "kgts,skd->tkgd", score_grad, key_rot, preferred_element_type=jnp.float32
    ) * HEAD_SIZE ** (-0.5)
    krot_grad = jnp.einsum(
        "kgts,tkgd->skd", score_grad, query_rot, preferred_element_type=jnp.float32
    ) * HEAD_SIZE ** (-0.5)
    query_grad_low = unrotate(
        qrot_grad.reshape(length_total, query_heads, HEAD_SIZE), cosine_table, sine_table
    )
    query_grad_low = query_grad_low.astype(jnp.bfloat16).reshape(
        length_total, query_heads * HEAD_SIZE
    )
    key_grad_low = (
        unrotate(krot_grad, cosine_table, sine_table)
        .astype(jnp.bfloat16)
        .reshape(length_total, key_heads * HEAD_SIZE)
    )
    value_grad_low = value_part_grad.astype(jnp.bfloat16).reshape(
        length_total, key_heads * HEAD_SIZE
    )
    query_part = jnp.einsum(
        "td,ti->di", h_first, query_grad_low, preferred_element_type=jnp.float32
    )
    key_part = jnp.einsum("td,ti->di", h_first, key_grad_low, preferred_element_type=jnp.float32)
    value_part = jnp.einsum(
        "td,ti->di", h_first, value_grad_low, preferred_element_type=jnp.float32
    )
    first_grad = jnp.einsum(
        "ti,di->td", query_grad_low, query_weight, preferred_element_type=jnp.float32
    )
    first_grad = first_grad + jnp.einsum(
        "ti,di->td", key_grad_low, key_matrix, preferred_element_type=jnp.float32
    )
    first_grad = first_grad + jnp.einsum(
        "ti,di->td", value_grad_low, value_matrix, preferred_element_type=jnp.float32
    )
    attn_gain_part = jnp.sum(first_grad * normed_first, axis=0)
    normed_first_grad = first_grad * attn_gain
    tokens_grad = mixed_grad + scale_first * (
        normed_first_grad
        - normed_first * jnp.mean(normed_first_grad * normed_first, axis=-1, keepdims=True)
    )
    shared = (
        lax.psum_scatter(query_part, ("grp", "ep"), scatter_dimension=0, tiled=True),
        lax.psum_scatter(key_part, ("grp", "ep"), scatter_dimension=0, tiled=True),
        lax.psum_scatter(value_part, ("grp", "ep"), scatter_dimension=0, tiled=True),
        lax.psum_scatter(output_part, ("grp", "ep"), scatter_dimension=1, tiled=True),
        lax.psum_scatter(attn_gain_part, ("grp", "ep"), scatter_dimension=0, tiled=True),
        lax.psum_scatter(ffn_gain_part, ("grp", "ep"), scatter_dimension=0, tiled=True),
    )
    return (
        layer_out,
        tokens_grad,
        shared[0],
        shared[1],
        shared[2],
        shared[3],
        shared[4],
        shared[5],
        expert_sums[0],
        expert_sums[1],
        expert_sums[2],
    )


SLOT_ORDER = (0, 4, 1, 5, 2, 6, 7, 3)


def moe_kernel(
    tab_ref, h_ref, dy_ref, wg_ref, wu_ref, wd_ref,
    grad_gate_ref, grad_up_ref, grad_down_ref, out_own_ref, out_sib_ref, d_own_ref, d_sib_ref,
    d_first_ref, d_second_ref,
    xb, dyb, tab, w_gate, w_up, w_down, acc_gate, acc_up, acc_down, act_s, gate_s, up_s, dz_s,
    sib, far_in, gather_send, gather_recv, tab_send, tab_recv, local_sem, part_send, part_recv,
    keep_sem, sum_send, sum_recv, store_sem,
):
    f32, bf16 = jnp.float32, jnp.bfloat16
    grp, ep = lax.axis_index("grp"), lax.axis_index("ep")
    core = lax.rem(grp, 2)
    low = lax.rem(ep, 4)
    y, z = lax.rem(low, 2), low // 2
    by_y = ep + 1 - 2 * y
    by_z = ep + 2 - 4 * z
    by_far = by_y + 2 - 4 * z
    first = by_y * (1 - core) + by_z * core
    second = by_z * (1 - core) + by_y * core
    other = grp + 1 - 2 * core
    hosted = lax.rem(ep + 4 * core, 8)
    rows = h_ref.shape[0]
    half = rows // 2

    def remote(src, dst, send, recv, device):
        return pltpu.make_async_remote_copy(
            src_ref=src, dst_ref=dst, send_sem=send, recv_sem=recv, device_id=device,
            device_id_type=pl.DeviceIdType.MESH,
        )

    members = (
        ((grp, first), 1), ((grp, second), 2), ((grp, by_far), 3), ((other, ep), 4),
        ((other, first), 5), ((other, second), 6), ((other, by_far), 7),
    )
    barrier = pltpu.get_barrier_semaphore()
    for device, _ in members:
        pl.semaphore_signal(barrier, inc=1, device_id=device, device_id_type=pl.DeviceIdType.MESH)
    pl.semaphore_wait(barrier, 7)

    def gather_copy(k, number):
        own, buf = ((h_ref, xb), (dy_ref, dyb))[k]
        src, dst, device = (
            (own, 1, (grp, first)), (own, 4, (other, ep)), (own, 2, (grp, second)),
            (buf.at[1], 5, (other, ep)), (buf.at[2], 6, (other, ep)),
            (buf.at[2], 3, (grp, first)), (buf.at[3], 7, (other, ep)),
        )[number]
        return remote(
            src, buf.at[dst], gather_send.at[k, number], gather_recv.at[k, number], device
        )

    arrival = {1: 0, 4: 1, 2: 2, 5: 3, 6: 4, 3: 5, 7: 6}

    def start(*numbers):
        for number in numbers:
            for k in (0, 1):
                gather_copy(k, number).start()

    def sent(*numbers):
        for number in numbers:
            for k in (0, 1):
                gather_copy(k, number).wait_send()

    def arrived(slot):
        for k in (0, 1):
            gather_copy(k, arrival[slot]).wait_recv()

    locals_in = [
        pltpu.make_async_copy(src, dst, local_sem.at[i])
        for i, (src, dst) in enumerate(
            ((h_ref, xb.at[0]), (dy_ref, dyb.at[0]), (wg_ref, w_gate), (wu_ref, w_up), (wd_ref, w_down))
        )
    ]
    for copy in locals_in:
        copy.start()
    table_copies = [
        remote(tab_ref, tab.at[slot], tab_send.at[slot], tab_recv.at[slot], device)
        for device, slot in members
    ]
    for copy in table_copies:
        copy.start()
    start(0, 1)
    tab[0] = tab_ref[...]
    acc_gate[...] = jnp.zeros_like(acc_gate)
    acc_up[...] = jnp.zeros_like(acc_up)
    acc_down[...] = jnp.zeros_like(acc_down)
    for copy in locals_in:
        copy.wait()
    for copy in table_copies:
        copy.wait_send()
        copy.wait_recv()

    def keep_copy(j, src):
        return pltpu.make_async_copy(src, out_own_ref.at[j], keep_sem.at[j])

    def part_copies(j, dest):
        grad_dst = d_sib_ref if j == 0 else sib.at[j - 1]
        return (
            remote(xb.at[dest], grad_dst, part_send.at[0, j], part_recv.at[0, j], (other, ep)),
            remote(
                dyb.at[dest], out_sib_ref.at[j], part_send.at[1, j], part_recv.at[1, j], (other, ep)
            ),
        )

    own_grad = pltpu.make_async_copy(xb.at[8], d_own_ref, keep_sem.at[4])
    send_first = remote(xb.at[4], d_first_ref, sum_send.at[0], sum_recv.at[0], (grp, first))
    send_far = remote(xb.at[7], far_in, sum_send.at[1], sum_recv.at[1], (grp, first))
    send_second = remote(xb.at[5], d_second_ref, sum_send.at[2], sum_recv.at[2], (grp, second))

    def dot_nt(a, b):
        return lax.dot_general(a, b, (((1,), (1,)), ((), ())), preferred_element_type=f32)

    def dot_tn(a, b):
        return lax.dot_general(a, b, (((0,), (0,)), ((), ())), preferred_element_type=f32)

    def gates(slot):
        block = jnp.transpose(tab[slot])
        lane = lax.broadcasted_iota(jnp.int32, block.shape, 1)
        return jnp.sum(jnp.where(lane == hosted, block, 0.0), axis=1, keepdims=True)

    c0 = 0.7978845608028654
    c1 = 0.044715

    def work_in(slot):
        column = gates(slot)
        for part in range(2):
            at = pl.ds(part * half, half)
            x = xb[slot, at, :]
            gate = column[part * half : (part + 1) * half]
            g = jnp.dot(x, w_gate[...], preferred_element_type=f32)
            u = jnp.dot(x, w_up[...], preferred_element_type=f32)
            dz = (gate * dyb[slot, at, :].astype(f32)).astype(bf16)
            dz_s[at, :] = dz
            da = dot_nt(dz, w_down[...])
            square = g * g
            t = jnp.tanh(c0 * (g + c1 * square * g))
            gelu = 0.5 * g * (1.0 + t)
            slope = 0.5 * (1.0 + t) + 0.5 * g * (1.0 - t * t) * (c0 * (1.0 + 3.0 * c1 * square))
            act_s[at, :] = (gelu * u).astype(bf16)
            gate_s[at, :] = (da * u * slope).astype(bf16)
            up_s[at, :] = (da * gelu).astype(bf16)
        for part in range(3):
            at = pl.ds(part * 512, 512)
            x = xb[slot, :, at]
            acc_gate[at, :] += dot_tn(x, gate_s[...])
            acc_up[at, :] += dot_tn(x, up_s[...])
            at = pl.ds(part * 256, 256)
            acc_down[at, :] += dot_tn(act_s[:, at], dz_s[...])

    def work_out(slot, dest):
        column = gates(slot)
        for part in range(2):
            at = pl.ds(part * half, half)
            gate = column[part * half : (part + 1) * half]
            dx = dot_nt(gate_s[at, :], w_gate[...]) + dot_nt(up_s[at, :], w_up[...])
            xb[dest, at, :] = dx.astype(bf16)
            result = jnp.dot(act_s[at, :], w_down[...], preferred_element_type=f32)
            dyb[dest, at, :] = (gate * result.astype(bf16).astype(f32)).astype(bf16)

    def slot_at(step):
        pair, odd = step // 2, lax.rem(step, 2)
        last = pair // 3
        return pair + 4 * (odd * (1 - last) + (1 - odd) * last)

    @pl.loop(0, 8)
    def _(step):
        def at_step(number):
            return pl.when(step == number)

        @at_step(1)
        def _():
            start(2)
            arrived(4)

        @at_step(2)
        def _():
            arrived(1)
            start(3)

        @at_step(3)
        def _():
            arrived(5)

        @at_step(4)
        def _():
            arrived(2)
            start(5, 4)

        @at_step(5)
        def _():
            arrived(6)

        @at_step(6)
        def _():
            arrived(3)
            start(6)
            arrived(7)

        slot = slot_at(step)
        first_step = (8 - step) // 8
        dest = (1 - first_step) * slot_at(step - 1 + first_step) + 8 * first_step
        work_in(slot)

        @at_step(3)
        def _():
            sent(3)

        @at_step(5)
        def _():
            sent(5, 4)

        work_out(slot, dest)

        for number, (slot_now, slot_before) in enumerate(zip(SLOT_ORDER, (8,) + SLOT_ORDER)):

            @at_step(number)
            def _(slot_now=slot_now, slot_before=slot_before):
                if slot_now < 4:
                    keep_copy(slot_now, dyb.at[slot_before]).start()
                else:
                    for copy in part_copies(slot_now - 4, slot_before):
                        copy.start()

        @at_step(0)
        def _():
            own_grad.start()

        @at_step(4)
        def _():
            part_copies(1, 1)[0].wait_recv()
            xb[4] = (xb[4].astype(f32) + sib[0].astype(f32)).astype(bf16)
            send_first.start()

    part_copies(3, 6)[0].wait_recv()
    xb[7] = (xb[7].astype(f32) + sib[2].astype(f32)).astype(bf16)
    send_far.start()
    w_gate[...] = acc_gate[...].astype(bf16)
    w_up[...] = acc_up[...].astype(bf16)
    w_down[...] = acc_down[...].astype(bf16)
    stores = [
        pltpu.make_async_copy(src, dst, store_sem.at[i])
        for i, (src, dst) in enumerate(
            ((w_gate, grad_gate_ref), (w_up, grad_up_ref), (w_down, grad_down_ref))
        )
    ]
    for copy in stores:
        copy.start()
    part_copies(2, 2)[0].wait_recv()
    send_far.wait_recv()
    xb[5] = (xb[5].astype(f32) + sib[1].astype(f32) + far_in[...].astype(f32)).astype(bf16)
    send_second.start()
    sent(0, 1, 2, 6)
    for j, slot_before in enumerate((0, 1, 2, 6)):
        for k, copy in enumerate(part_copies(j, slot_before)):
            copy.wait_send()
            if k == 1 or j == 0:
                copy.wait_recv()
    for j, slot_before in enumerate((8, 4, 5, 7)):
        keep_copy(j, dyb.at[slot_before]).wait()
    own_grad.wait()
    for copy in stores:
        copy.wait()
    send_first.wait()
    send_far.wait_send()
    send_second.wait()


def moe_call(table, rows_in, grad_in, weight_gate, weight_up, weight_down):
    f32, bf16 = jnp.float32, jnp.bfloat16
    rows, width = rows_in.shape
    hidden = weight_gate.shape[1]
    anywhere = pl.BlockSpec(memory_space=pl.ANY)
    chunk = jax.ShapeDtypeStruct((rows, width), bf16)
    four = jax.ShapeDtypeStruct((4, rows, width), bf16)
    wide = jax.ShapeDtypeStruct((width, hidden), bf16)
    tall = jax.ShapeDtypeStruct((hidden, width), bf16)
    dma = pltpu.SemaphoreType.DMA
    return pl.pallas_call(
        moe_kernel,
        out_shape=(wide, wide, tall, four, four, chunk, chunk, chunk, chunk),
        in_specs=[pl.BlockSpec(memory_space=pltpu.VMEM)] + [anywhere] * 5,
        out_specs=(anywhere,) * 9,
        scratch_shapes=[
            pltpu.VMEM((9, rows, width), bf16),
            pltpu.VMEM((9, rows, width), bf16),
            pltpu.VMEM((8,) + table.shape, f32),
            pltpu.VMEM((width, hidden), bf16),
            pltpu.VMEM((width, hidden), bf16),
            pltpu.VMEM((hidden, width), bf16),
            pltpu.VMEM((width, hidden), f32),
            pltpu.VMEM((width, hidden), f32),
            pltpu.VMEM((hidden, width), f32),
            pltpu.VMEM((rows, hidden), bf16),
            pltpu.VMEM((rows, hidden), bf16),
            pltpu.VMEM((rows, hidden), bf16),
            pltpu.VMEM((rows, width), bf16),
            pltpu.VMEM((3, rows, width), bf16),
            pltpu.VMEM((rows, width), bf16),
            dma((2, 7)),
            dma((2, 7)),
            dma((8,)),
            dma((8,)),
            dma((5,)),
            dma((2, 4)),
            dma((2, 4)),
            dma((5,)),
            dma((3,)),
            dma((3,)),
            dma((3,)),
        ],
        compiler_params=pltpu.CompilerParams(
            collective_id=0, has_side_effects=True, vmem_limit_bytes=63 * 2**20
        ),
        cost_estimate=pl.CostEstimate(
            flops=16 * 9 * rows * width * hidden, bytes_accessed=60 * 2**20, transcendentals=0
        ),
    )(table, rows_in, grad_in, weight_gate, weight_up, weight_down)


def backward_kernel(
    attn_gain_ref, ffn_gain_ref, cos_ref, sin_ref, seg_row_ref, seg_col_ref, lse_ref, key_ref,
    value_ref, second0_ref, second1_ref, second2_ref, second3_ref, mixed_ref, cot_ref, att_ref,
    query_ref, tok_ref, wo_ref, wq_ref, wk_ref, wv_ref, gg_ref, gu_ref, gd_ref, own_ref, sibling_ref,
    query_out, kv_out, out_out, layer_ref, tokens_ref, gate_out, up_out, down_out, ra_ref, rb_ref, rf_ref,
    pool, w_big, w_key, w_value, grad, proj, bias, key_acc, value_acc, gain_acc,
    out_buf, out_land, query_buf, kv_buf, kv_land,
    ex_land, ef_land, ec_land, ec_down_land, kept, stage, stage_down, load_sem, out_send, out_recv, ex_send, ex_recv, ef_send, ef_recv, ec_send, ec_recv,
    halve_send, halve_recv, free_sem, store_sem,
):
    f32, bf16 = jnp.float32, jnp.bfloat16
    grp, ep = lax.axis_index("grp"), lax.axis_index("ep")
    core = lax.rem(grp, 2)
    x = grp // 2
    y = lax.rem(ep, 2)
    z_low = lax.rem(ep // 2, 2)
    z_high = ep // 4
    by_y = (grp, ep + 1 - 2 * y)
    by_z = (grp, ep + 2 - 4 * z_low)
    by_far = (grp, ep + 4 - 8 * z_high)
    by_core = (grp + 1 - 2 * core, ep)
    by_x = (grp + 2 - 4 * x, ep)
    first = (grp, by_y[1] * (1 - core) + by_z[1] * core)
    second = (grp, by_z[1] * (1 - core) + by_y[1] * core)
    rows, width = grad.shape
    head = cos_ref.shape[1]
    heads = width // head
    key_width = key_ref.shape[1]
    per_key = heads * head // key_width
    block = width // 32

    def remote(src, dst, send, recv, device):
        return pltpu.make_async_remote_copy(
            src_ref=src, dst_ref=dst, send_sem=send, recv_sem=recv, device_id=device,
            device_id_type=pl.DeviceIdType.MESH,
        )

    partners = (by_core, by_y, by_z, by_x, by_far)
    barrier = pltpu.get_barrier_semaphore()
    for device in partners:
        pl.semaphore_signal(barrier, inc=1, device_id=device, device_id_type=pl.DeviceIdType.MESH)
    pl.semaphore_wait(barrier, 5)

    wide_half = width // 2
    quarter = width // 4
    ex_dst = tuple(ex_land.at[m] for m in range(3))
    ef_dst = tuple(ef_land.at[m] for m in range(3))
    ec_dst = (ec_land.at[0], ec_land.at[1], ec_down_land)

    def part(ref, m, index, size):
        at = pl.ds(pl.multiple_of(index * size, size), size)
        return ref.at[:, at] if m == 2 else ref.at[at, :]

    grads = (gg_ref, gu_ref, gd_ref)

    def ex_copy(m):
        return remote(
            part(grads[m], m, 1 - x, wide_half), ex_dst[m], ex_send.at[m], ex_recv.at[m], by_x
        )

    def ef_copy(m):
        return remote(ex_dst[m], ef_dst[m], ef_send.at[m], ef_recv.at[m], by_far)

    def ec_copy(m, base):
        return remote(
            part(base[m], m, 1 - core, quarter), ec_dst[m], ec_send.at[m], ec_recv.at[m], by_core
        )

    def kept_copy(m):
        return pltpu.make_async_copy(part(grads[m], m, x, wide_half), kept, load_sem.at[20 + m])

    def load(number, src, dst):
        return pltpu.make_async_copy(src, dst, load_sem.at[number])

    for m in range(3):
        ex_copy(m).start()
    loads = (
        (own_ref.at[3], pool.at[6]),
        (sibling_ref.at[3], pool.at[9]),
        (own_ref.at[1], pool.at[5]),
        (sibling_ref.at[1], pool.at[8]),
        (second0_ref, pool.at[1]),
        (second1_ref, pool.at[2]),
        (second2_ref, pool.at[3]),
        (second3_ref, pool.at[4]),
        (mixed_ref, grad),
        (cot_ref, pool.at[0]),
        (wo_ref, w_big),
        (own_ref.at[2], pool.at[7]),
    )
    for number, (src, dst) in enumerate(loads):
        load(number, src, dst).start()

    def wait_load(number):
        load(number, *loads[number]).wait()

    def add_into(dst, *others):
        @pl.loop(0, rows // 128)
        def _(step):
            at = pl.ds(pl.multiple_of(step * 128, 128), 128)
            total = dst[at, :].astype(f32)
            for other in others:
                total = total + other[at, :].astype(f32)
            dst[at, :] = total.astype(bf16)

    far_copy = lambda: remote(pool.at[6], rf_ref, out_send.at[0], out_recv.at[0], first)
    first_copy = lambda: remote(pool.at[5], ra_ref, out_send.at[1], out_recv.at[1], first)
    second_copy = lambda: remote(pool.at[7], rb_ref, out_send.at[2], out_recv.at[2], second)
    wait_load(0)
    wait_load(1)
    add_into(pool.at[6], pool.at[9])
    far_copy().start()
    wait_load(2)
    wait_load(3)
    add_into(pool.at[5], pool.at[8])
    first_copy().start()
    sib2 = lambda: load(12, sibling_ref.at[2], pool.at[8])
    sib2().start()
    kept_copy(0).start()

    for number in range(4, 10):
        wait_load(number)
    gain_acc[...] = jnp.zeros_like(gain_acc)

    @pl.loop(0, rows // 128)
    def _(step):
        at = pl.ds(pl.multiple_of(step * 128, 128), 128)
        value = grad[at, :]
        scale = lax.rsqrt(jnp.mean(value * value, axis=-1, keepdims=True) + EPS)
        normed = value * scale
        down = (
            pool[1, at, :].astype(f32)
            + pool[2, at, :].astype(f32)
            + pool[3, at, :].astype(f32)
            + pool[4, at, :].astype(f32)
        )
        product = down * normed
        gain_acc[1:2, :] += jnp.sum(product, axis=0, keepdims=True)
        mean = jnp.mean(product * ffn_gain_ref[...], axis=-1, keepdims=True)
        result = pool[0, at, :].astype(f32) + scale * (down * ffn_gain_ref[...] - normed * mean)
        grad[at, :] = result
        pool[3, at, :] = result.astype(bf16)

    att_load = lambda: load(13, att_ref, pool.at[1])
    query_load = lambda: load(14, query_ref, pool.at[2])
    tok_load = lambda: load(15, tok_ref, pool.at[0])
    key_weight_load = lambda: load(16, wk_ref, w_key)
    value_weight_load = lambda: load(17, wv_ref, w_value)
    for copy in (att_load, query_load, tok_load, key_weight_load, value_weight_load):
        copy().start()

    position = lax.broadcasted_iota(jnp.int32, (rows, rows), 0)
    other_position = lax.broadcasted_iota(jnp.int32, (rows, rows), 1)
    padding = seg_row_ref[...] == jnp.max(seg_row_ref[...])
    allowed = (
        (other_position <= position)
        & (seg_col_ref[...] == seg_row_ref[...])
        & (jnp.logical_not(padding) | (other_position == position))
    )
    bias[...] = jnp.where(allowed, 0.0, -1e30)

    def dot_nt(a, b):
        return lax.dot_general(a, b, (((1,), (1,)), ((), ())), preferred_element_type=f32)

    def dot_tn(a, b):
        return lax.dot_general(a, b, (((0,), (0,)), ((), ())), preferred_element_type=f32)

    levels = ((core, by_core), (y, by_y), (x, by_x), (z_low, by_z), (z_high, by_far))
    offsets = (0, 16, 24, 28, 30)
    starts = [0]
    for level, (bit, _) in enumerate(levels):
        starts.append(starts[-1] + bit * (16 >> level))

    def halve_copy(job, buf, land, level):
        bit, device = levels[level]
        size = 16 >> level
        return remote(
            buf.at[pl.ds(starts[level] + (1 - bit) * size, size)],
            land.at[pl.ds(offsets[level], size)],
            halve_send.at[job, level],
            halve_recv.at[job, level],
            device,
        )

    def absorb(job, buf, land, level, result=None):
        halve_copy(job, buf, land, level).wait_recv()
        size = 16 >> level
        if result is None:

            @pl.loop(0, size)
            def _(i):
                at = starts[level + 1] + i
                buf[at] = (buf[at].astype(f32) + land[offsets[level] + i].astype(f32)).astype(bf16)

        else:
            result[...] = buf[starts[5]].astype(f32) + land[offsets[4]].astype(f32)
        if job == 0:
            pl.semaphore_signal(
                free_sem.at[level], inc=1, device_id=levels[level][1],
                device_id_type=pl.DeviceIdType.MESH,
            )
        if level < 4:
            launch(job, level + 1)

    jobs = ((out_buf, out_land), (query_buf, out_land), (kv_buf, kv_land))

    def launch(job, level):
        if job == 1:
            pl.semaphore_wait(free_sem.at[level], 1)
        halve_copy(job, *jobs[job], level).start()

    def begin(job):
        launch(job, 0)

    def advance(job, level):
        absorb(job, *jobs[job], level, (out_out, query_out, kv_out)[job] if level == 4 else None)

    def place(buf, tile, value, columns):
        for b in range(8):
            high, low, odd = b >> 2, (b >> 1) & 1, b & 1
            to = ((((tile & 1) * 2 + odd) * 2 + (tile >> 1)) * 2 + low) * 2 + high
            buf[to, :, columns] = value[b * block : (b + 1) * block].astype(bf16)

    att_load().wait()
    for tile in range(4):
        at = slice(tile * 8 * block, (tile + 1) * 8 * block)
        place(out_buf, tile, dot_tn(pool[3, :, at], pool[1]), slice(None))
    begin(0)
    wait_load(10)
    for half in range(2):
        at = slice(half * rows // 2, (half + 1) * rows // 2)
        pool[4, at, :] = dot_nt(pool[3, at, :], w_big[...]).astype(bf16)
    query_weight_load = lambda: load(18, wq_ref, w_big)
    query_weight_load().start()

    tok_load().wait()

    def first_norm(at):
        value = pool[0, at, :].astype(f32)
        scale = lax.rsqrt(jnp.mean(value * value, axis=-1, keepdims=True) + EPS)
        return scale, value * scale

    @pl.loop(0, rows // 128)
    def _(step):
        at = pl.ds(pl.multiple_of(step * 128, 128), 128)
        pool[1, at, :] = (first_norm(at)[1] * attn_gain_ref[...]).astype(bf16)

    def send_second():
        wait_load(11)
        sib2().wait()
        far_copy().wait_recv()
        far_load = load(19, rf_ref, pool.at[9])
        far_load.start()
        far_load.wait()
        add_into(pool.at[7], pool.at[8], pool.at[9])
        second_copy().start()

    def expert_second(m):
        kept_copy(m).wait()
        ex_copy(m).wait_recv()
        dst = ex_dst[m]
        at_rows = dst.shape[0]

        @pl.loop(0, at_rows // 128)
        def _(step):
            at = pl.ds(pl.multiple_of(step * 128, 128), 128)
            dst[at, :] = (dst[at, :].astype(f32) + kept[at, :].astype(f32)).astype(bf16)

        if m < 2:
            kept_copy(m + 1).start()

        @pl.when(core == 1)
        def _():
            ef_copy(m).start()

        @pl.when(core == 0)
        def _():
            ec_copy(m, ex_dst).start()

    results = (gate_out, up_out, down_out)

    def store_copy(m):
        return pltpu.make_async_copy(stage_down if m == 2 else stage, results[m], store_sem.at[m])

    def expert_third(m):
        @pl.when(core == 1)
        def _():
            ef_copy(m).wait_recv()
            ec_copy(m, ef_dst).start()

    def expert_last(m):
        if m == 1:
            store_copy(0).wait()
        ec_copy(m, ex_dst).wait_recv()
        at = pl.ds(pl.multiple_of(core * quarter, quarter), quarter)

        def finish(base):
            if m == 2:
                stage_down[...] = base[:, at].astype(f32) + ec_dst[m][...].astype(f32)
            else:
                stage[...] = base[at, :].astype(f32) + ec_dst[m][...].astype(f32)

        @pl.when(core == 0)
        def _():
            finish(ex_dst[m])

        @pl.when(core == 1)
        def _():
            finish(ef_dst[m])

        store_copy(m).start()

    def turn_back(value, at):
        swapped = pltpu.roll(value, head // 2, 1)
        return value * cos_ref[at, :] - swapped * sin_ref[at, :]

    scale = head ** (-0.5)
    query_load().wait()
    key_acc[...] = jnp.zeros_like(key_acc)
    value_acc[...] = jnp.zeros_like(value_acc)

    def between(number):
        if number == 1:
            advance(0, 0)
        elif number == 3:
            send_second()
        elif number == 4:
            expert_second(0)
        elif number == 6:
            advance(0, 1)
        elif number == 9:
            advance(0, 2)

    for number in range(heads):
        columns = slice(number * head, (number + 1) * head)
        kv = number // per_key
        kv_columns = slice(kv * head, (kv + 1) * head)
        for half in range(2):
            at = slice(half * rows // 2, (half + 1) * rows // 2)
            seen = slice(0, (half + 1) * rows // 2)
            q = pool[2, at, columns]
            da = pool[4, at, columns]
            k = key_ref[seen, kv_columns]
            score = dot_nt(q, k) * scale + bias[at, seen]
            probs = jnp.exp(score - lse_ref[at, number : number + 1])
            dprob = dot_nt(da, value_ref[seen, kv_columns])
            inner = jnp.sum(probs * dprob, axis=-1, keepdims=True)
            dscore = (probs * (dprob - inner)).astype(bf16)
            value_acc[seen, kv_columns] += dot_tn(probs.astype(bf16), da)
            key_acc[seen, kv_columns] += dot_tn(dscore, q)
            dq = jnp.dot(dscore, k, preferred_element_type=f32) * scale
            proj[at, columns] = turn_back(dq, at).astype(bf16)
        between(number)

    for kv in range(key_width // head):
        columns = slice(kv * head, (kv + 1) * head)
        to = slice(width + kv * head, width + (kv + 1) * head)
        proj[:, to] = turn_back(key_acc[:, columns] * scale, slice(None)).astype(bf16)
        to = slice(width + key_width + kv * head, width + key_width + (kv + 1) * head)
        proj[:, to] = value_acc[:, columns].astype(bf16)

    for tile in range(4):
        at = slice(tile * 8 * block, (tile + 1) * 8 * block)
        place(query_buf, tile, dot_tn(pool[1, :, at], proj[:, :width]), slice(None))
    begin(1)
    for tile in range(4):
        at = slice(tile * 8 * block, (tile + 1) * 8 * block)
        place(kv_buf, tile, dot_tn(pool[1, :, at], proj[:, width:]), slice(0, 2 * key_width))
    expert_second(1)
    query_weight_load().wait()
    key_weight_load().wait()
    value_weight_load().wait()
    for quarter_step in range(4):
        at = slice(quarter_step * rows // 4, (quarter_step + 1) * rows // 4)
        down = dot_nt(proj[at, :width], w_big[...])
        down = down + dot_nt(proj[at, width : width + key_width], w_key[...])
        down = down + dot_nt(proj[at, width + key_width :], w_value[...])
        factor, normed = first_norm(at)
        product = down * normed
        gain_acc[0:1, :] += jnp.sum(product, axis=0, keepdims=True)
        mean = jnp.mean(product * attn_gain_ref[...], axis=-1, keepdims=True)
        grad[at, :] = grad[at, :] + factor * (down * attn_gain_ref[...] - normed * mean)
        if quarter_step == 1:
            advance(1, 0)
    tokens_store = lambda: pltpu.make_async_copy(grad, tokens_ref, store_sem.at[3])
    tokens_store().start()

    gains = gain_acc[...]
    high = gains.astype(bf16).astype(f32)
    row = lax.broadcasted_iota(jnp.int32, gains.shape, 0)
    lower = pltpu.roll(gains - high, 2, 0)
    both = jnp.transpose(jnp.where(row < 2, high, lower))
    both = jnp.concatenate([both, jnp.zeros((width, head - 8), f32)], axis=1)
    for tile in range(4):
        at = slice(tile * 8 * block, (tile + 1) * 8 * block)
        place(kv_buf, tile, both[at], slice(2 * key_width, 2 * key_width + head))
    begin(2)

    expert_third(0)
    expert_last(0)
    advance(1, 1)
    advance(2, 0)
    advance(0, 3)
    advance(2, 1)
    expert_second(2)
    advance(1, 2)
    expert_third(1)
    expert_last(1)
    advance(2, 2)
    advance(0, 4)
    advance(1, 3)
    advance(2, 3)

    tokens_store().wait()
    first_copy().wait_recv()
    second_copy().wait_recv()
    last_loads = (
        (own_ref.at[0], pool.at[3]),
        (sibling_ref.at[0], pool.at[4]),
        (ra_ref, pool.at[8]),
        (rb_ref, pool.at[9]),
        (mixed_ref, grad),
    )
    for number, (src, dst) in enumerate(last_loads):
        load(number, src, dst).start()
    for number, (src, dst) in enumerate(last_loads):
        load(number, src, dst).wait()

    @pl.loop(0, rows // 128)
    def _(step):
        at = pl.ds(pl.multiple_of(step * 128, 128), 128)
        total = grad[at, :]
        for i in (3, 4, 8, 9):
            total = total + pool[i, at, :].astype(f32)
        pool[3, at, :] = total.astype(bf16)

    layer_store = pltpu.make_async_copy(pool.at[3], layer_ref, store_sem.at[4])
    layer_store.start()
    advance(1, 4)
    advance(2, 4)
    expert_third(2)
    expert_last(2)

    for copy in (far_copy, first_copy, second_copy):
        copy().wait_send()
    for m in range(3):
        ex_copy(m).wait_send()
        ec_copy(m, ex_dst).wait_send()

        @pl.when(core == 1)
        def _(m=m):
            ef_copy(m).wait_send()

        if m > 0:
            store_copy(m).wait()
    for job in range(3):
        for level in range(5):
            halve_copy(job, *jobs[job], level).wait_send()
    layer_store.wait()


def backward_call(vmem_args, any_args):
    f32, bf16 = jnp.float32, jnp.bfloat16
    rows, head = vmem_args[2].shape
    key_width = vmem_args[7].shape[1]
    width = vmem_args[0].shape[1]
    hidden = any_args[13].shape[1]
    block = width // 32
    extra = 2 * key_width + head
    anywhere = pl.BlockSpec(memory_space=pl.ANY)
    inside = pl.BlockSpec(memory_space=pltpu.VMEM)
    shape = jax.ShapeDtypeStruct
    dma = pltpu.SemaphoreType.DMA
    vmem = pltpu.VMEM
    return pl.pallas_call(
        backward_kernel,
        out_shape=(
            shape((block, width), f32),
            shape((block, extra), f32),
            shape((block, width), f32),
            shape((rows, width), bf16),
            shape((rows, width), f32),
            shape((width // 4, hidden), f32),
            shape((width // 4, hidden), f32),
            shape((hidden, width // 4), f32),
            shape((rows, width), bf16),
            shape((rows, width), bf16),
            shape((rows, width), bf16),
        ),
        in_specs=[inside] * len(vmem_args) + [anywhere] * len(any_args),
        out_specs=(inside,) * 3 + (anywhere,) * 8,
        scratch_shapes=[
            vmem((10, rows, width), bf16),
            vmem((width, width), bf16),
            vmem((width, key_width), bf16),
            vmem((width, key_width), bf16),
            vmem((rows, width), f32),
            vmem((rows, width + 2 * key_width), bf16),
            vmem((rows, rows), f32),
            vmem((rows, key_width), f32),
            vmem((rows, key_width), f32),
            vmem((8, width), f32),
            vmem((32, block, width), bf16),
            vmem((31, block, width), bf16),
            vmem((32, block, width), bf16),
            vmem((32, block, extra), bf16),
            vmem((31, block, extra), bf16),
            vmem((3, width // 2, hidden), bf16),
            vmem((3, width // 2, hidden), bf16),
            vmem((2, width // 4, hidden), bf16),
            vmem((hidden, width // 4), bf16),
            vmem((width // 2, hidden), bf16),
            vmem((width // 4, hidden), f32),
            vmem((hidden, width // 4), f32),
            dma((23,)),
            dma((3,)),
            dma((3,)),
            dma((3,)),
            dma((3,)),
            dma((3,)),
            dma((3,)),
            dma((3,)),
            dma((3,)),
            dma((3, 5)),
            dma((3, 5)),
            pltpu.SemaphoreType.REGULAR((5,)),
            dma((5,)),
        ],
        compiler_params=pltpu.CompilerParams(
            collective_id=1, has_side_effects=True, vmem_limit_bytes=64 * 2**20
        ),
        cost_estimate=pl.CostEstimate(
            flops=30 * rows * width * width, bytes_accessed=60 * 2**20, transcendentals=0
        ),
    )(*vmem_args, *any_args)


def local_dense(
    tokens,
    segment_ids,
    routes,
    route_gates,
    attn_gain,
    ffn_gain,
    query_weight,
    key_matrix,
    value_matrix,
    output_weight,
    expert_gate,
    expert_up,
    expert_down,
    cotangent,
):
    f32, bf16 = jnp.float32, jnp.bfloat16
    length_total, width = tokens.shape
    owners = lax.axis_size("ep")
    experts = owners
    bit_y, bit_z, bit_far, bit_core, bit_x = 1, 2, owners // 2, owners, 2 * owners
    names = ("grp", "ep")
    count = lax.axis_size("grp") * owners
    me = lax.axis_index("grp") * owners + lax.axis_index("ep")
    core = (me // bit_core) % 2
    side = (me // bit_x) % 2
    on_core1 = core == 1

    def swap_core1(value, mask):
        return lax.ppermute(value, names, [(i, i ^ mask) for i in range(count) if i & bit_core])

    def fetch(weight):
        rows = weight.shape[0] // 2
        half = lax.dynamic_slice_in_dim(weight, side * rows, rows, 0)
        here = swap_core1(half, bit_far)
        there = swap_core1(here, bit_x)
        low = jnp.where(side == 0, here, there)
        high = jnp.where(side == 0, there, here)
        return jnp.where(on_core1, jnp.concatenate([low, high], axis=0), weight)

    weight_gate = fetch(expert_gate[0])
    weight_up = fetch(expert_up[0])
    weight_down = fetch(expert_down[0])
    table = jnp.sum(
        jnp.where(
            routes[:, :, None] == jnp.arange(experts, dtype=jnp.int32)[None, None, :],
            route_gates[:, :, None],
            0.0,
        ),
        axis=1,
    )
    query_heads = query_weight.shape[1] // HEAD_SIZE
    key_heads = key_matrix.shape[1] // HEAD_SIZE
    q_per_kv = query_heads // key_heads
    segment = segment_ids[0]
    padding = segment == jnp.max(segment)
    later = jnp.arange(length_total)[:, None] >= jnp.arange(length_total)[None, :]
    diagonal = jnp.arange(length_total)[:, None] == jnp.arange(length_total)[None, :]
    allowed = (
        later
        & (segment[:, None] == segment[None, :])
        & (jnp.logical_not(padding)[None, :] | diagonal)
    )
    position = jnp.arange(length_total, dtype=jnp.float32)
    inverse = BASE ** (-jnp.arange(HEAD_SIZE // 2, dtype=jnp.float32) * 2.0 / HEAD_SIZE)
    angle = position[:, None] * inverse[None, :]
    cosine_table = jnp.cos(angle)[:, None, :]
    sine_table = jnp.sin(angle)[:, None, :]
    tok_float = tokens.astype(jnp.float32)
    scale_first = lax.rsqrt(jnp.mean(tok_float * tok_float, axis=-1, keepdims=True) + EPS)
    normed_first = tok_float * scale_first
    h_first = (normed_first * attn_gain).astype(jnp.bfloat16)
    query_rows = jnp.dot(h_first, query_weight, preferred_element_type=jnp.float32).reshape(
        length_total, query_heads, HEAD_SIZE
    )
    key_rows = jnp.dot(h_first, key_matrix, preferred_element_type=jnp.float32).reshape(
        length_total, key_heads, HEAD_SIZE
    )
    value_low = jnp.dot(h_first, value_matrix, preferred_element_type=jnp.float32).astype(
        jnp.bfloat16
    )
    value_low = value_low.reshape(length_total, key_heads, HEAD_SIZE)
    query_rot = (
        apply_rotary(query_rows, cosine_table, sine_table)
        .astype(jnp.bfloat16)
        .reshape(length_total, key_heads, q_per_kv, HEAD_SIZE)
    )
    key_rot = apply_rotary(key_rows, cosine_table, sine_table).astype(jnp.bfloat16)
    score = scores_of(query_rot, key_rot, allowed)
    row_max = jnp.max(score, axis=-1, keepdims=True)
    expo = jnp.exp(score - row_max)
    row_sum = jnp.sum(expo, axis=-1, keepdims=True)
    log_total = row_max + jnp.log(row_sum)
    probs_low = (expo / row_sum).astype(jnp.bfloat16)
    attended = jnp.einsum(
        "kgts,skd->tkgd", probs_low, value_low, preferred_element_type=jnp.float32
    )
    attended = attended.reshape(length_total, query_heads * HEAD_SIZE).astype(jnp.bfloat16)
    mixed = tok_float + jnp.dot(attended, output_weight, preferred_element_type=jnp.float32)
    scale_second = lax.rsqrt(jnp.mean(mixed * mixed, axis=-1, keepdims=True) + EPS)
    normed_second = mixed * scale_second
    h_second = (normed_second * ffn_gain).astype(jnp.bfloat16)

    (
        gate_part,
        up_part,
        down_part,
        out_own,
        out_sib,
        *second_parts,
    ) = moe_call(table.T, h_second, cotangent, weight_gate, weight_up, weight_down)
    log_total = log_total.reshape(query_heads, length_total).T
    log_total = jnp.pad(log_total, ((0, 0), (0, HEAD_SIZE - query_heads)))
    cosine = cosine_table[:, 0, :]
    sine = sine_table[:, 0, :]
    (
        query_grad,
        extra_grad,
        output_grad,
        layer_out,
        tokens_grad,
        gate_grad,
        up_grad,
        down_grad,
        _,
        _,
        _,
    ) = backward_call(
        (
            attn_gain[None, :],
            ffn_gain[None, :],
            jnp.concatenate([cosine, cosine], axis=1),
            jnp.concatenate([-sine, sine], axis=1),
            segment_ids,
            segment_ids.T,
            log_total,
            key_rot.reshape(length_total, -1),
            value_low.reshape(length_total, -1),
        ),
        (
            *second_parts,
            mixed,
            cotangent,
            attended,
            query_rot.reshape(length_total, -1),
            tokens,
            output_weight,
            query_weight,
            key_matrix,
            value_matrix,
            gate_part,
            up_part,
            down_part,
            out_own,
            out_sib,
        ),
    )
    split_k = key_matrix.shape[1]
    split_v = split_k + value_matrix.shape[1]
    gain_sums = extra_grad[:, split_v : split_v + 2] + extra_grad[:, split_v + 2 : split_v + 4]
    return (
        layer_out,
        tokens_grad,
        query_grad,
        extra_grad[:, :split_k],
        extra_grad[:, split_k:split_v],
        output_grad.T,
        gain_sums[:, 0],
        gain_sums[:, 1],
        gate_grad[None],
        up_grad[None],
        down_grad[None],
    )


def solution(mesh):
    in_specs = (
        P(("grp", "ep"), None),
        P(("grp", "ep"), None),
        P(("grp", "ep"), None),
        P(("grp", "ep"), None),
        P(),
        P(),
        P(),
        P(),
        P(),
        P(),
        P("ep", None, None),
        P("ep", None, None),
        P("ep", None, None),
        P(("grp", "ep"), None),
    )
    out_specs = (
        P(("grp", "ep"), None),
        P(("grp", "ep"), None),
        P(("grp", "ep"), None),
        P(("grp", "ep"), None),
        P(("grp", "ep"), None),
        P(None, ("grp", "ep")),
        P(("grp", "ep")),
        P(("grp", "ep")),
        P("ep", "grp", None),
        P("ep", "grp", None),
        P("ep", None, "grp"),
    )
    paired = mesh.shape["grp"] == 4 and mesh.shape["ep"] == 8
    local = local_dense if paired else local_routed
    return jax.shard_map(local, mesh=mesh, in_specs=in_specs, out_specs=out_specs, check_vma=False)
```

```python
import jax
import jax.numpy as jnp
from jax import lax
from jax.experimental import pallas as pl
from jax.experimental.pallas import tpu as pltpu
from jax.sharding import PartitionSpec as P

HEAD_SIZE = 128


EPS = 1e-06
BASE = 10000.0


def apply_rotary(value_rows, cosine_table, sine_table):
    half = value_rows.shape[-1] // 2
    first = value_rows[..., :half]
    second = value_rows[..., half:]
    return jnp.concatenate(
        [first * cosine_table - second * sine_table, second * cosine_table + first * sine_table],
        axis=-1,
    )


def unrotate(value_rows, cosine_table, sine_table):
    half = value_rows.shape[-1] // 2
    first = value_rows[..., :half]
    second = value_rows[..., half:]
    return jnp.concatenate(
        [first * cosine_table + second * sine_table, second * cosine_table - first * sine_table],
        axis=-1,
    )


def glu_value(gate_val, up_val):
    return jax.nn.gelu(gate_val, approximate=True) * up_val


def scores_of(query_rot, key_rot, allowed):
    score = jnp.einsum(
        "tkgd,skd->kgts", query_rot, key_rot, preferred_element_type=jnp.float32
    ) * HEAD_SIZE ** (-0.5)
    return jnp.where(allowed, score, -1e30)


def local_routed(
    tokens,
    segment_ids,
    routes,
    route_gates,
    attn_gain,
    ffn_gain,
    query_weight,
    key_matrix,
    value_matrix,
    output_weight,
    expert_gate,
    expert_up,
    expert_down,
    cotangent,
):
    length_total, width = tokens.shape
    choose = routes.shape[1]
    local_experts = expert_gate.shape[0]
    owners = lax.axis_size("ep")
    experts = owners * local_experts
    capacity = 3 * length_total * choose // (2 * experts)
    query_heads = query_weight.shape[1] // HEAD_SIZE
    key_heads = key_matrix.shape[1] // HEAD_SIZE
    q_per_kv = query_heads // key_heads
    segment = segment_ids[0]
    padding = segment == jnp.max(segment)
    later = jnp.arange(length_total)[:, None] >= jnp.arange(length_total)[None, :]
    diagonal = jnp.arange(length_total)[:, None] == jnp.arange(length_total)[None, :]
    allowed = (
        later
        & (segment[:, None] == segment[None, :])
        & (jnp.logical_not(padding)[None, :] | diagonal)
    )
    position = jnp.arange(length_total, dtype=jnp.float32)
    inverse = BASE ** (-jnp.arange(HEAD_SIZE // 2, dtype=jnp.float32) * 2.0 / HEAD_SIZE)
    angle = position[:, None] * inverse[None, :]
    cosine_table = jnp.cos(angle)[:, None, :]
    sine_table = jnp.sin(angle)[:, None, :]
    tok_float = tokens.astype(jnp.float32)
    scale_first = lax.rsqrt(jnp.mean(tok_float * tok_float, axis=-1, keepdims=True) + EPS)
    normed_first = tok_float * scale_first
    h_first = (normed_first * attn_gain).astype(jnp.bfloat16)
    query_rows = jnp.dot(h_first, query_weight, preferred_element_type=jnp.float32).reshape(
        length_total, query_heads, HEAD_SIZE
    )
    key_rows = jnp.dot(h_first, key_matrix, preferred_element_type=jnp.float32).reshape(
        length_total, key_heads, HEAD_SIZE
    )
    value_low = jnp.dot(h_first, value_matrix, preferred_element_type=jnp.float32).astype(
        jnp.bfloat16
    )
    value_low = value_low.reshape(length_total, key_heads, HEAD_SIZE)
    query_rot = (
        apply_rotary(query_rows, cosine_table, sine_table)
        .astype(jnp.bfloat16)
        .reshape(length_total, key_heads, q_per_kv, HEAD_SIZE)
    )
    key_rot = apply_rotary(key_rows, cosine_table, sine_table).astype(jnp.bfloat16)
    score = scores_of(query_rot, key_rot, allowed)
    row_max = jnp.max(score, axis=-1, keepdims=True)
    expo = jnp.exp(score - row_max)
    row_sum = jnp.sum(expo, axis=-1, keepdims=True)
    log_total = row_max + jnp.log(row_sum)
    probs_low = (expo / row_sum).astype(jnp.bfloat16)
    attended = jnp.einsum(
        "kgts,skd->tkgd", probs_low, value_low, preferred_element_type=jnp.float32
    )
    attended = attended.reshape(length_total, query_heads * HEAD_SIZE).astype(jnp.bfloat16)
    mixed = tok_float + jnp.dot(attended, output_weight, preferred_element_type=jnp.float32)
    scale_second = lax.rsqrt(jnp.mean(mixed * mixed, axis=-1, keepdims=True) + EPS)
    normed_second = mixed * scale_second
    h_second = (normed_second * ffn_gain).astype(jnp.bfloat16)
    flat_routes = routes.reshape(-1)
    assigns = flat_routes.shape[0]
    onehot = (flat_routes[:, None] == jnp.arange(experts, dtype=jnp.int32)[None, :]).astype(
        jnp.int32
    )
    position_in = jnp.sum(jnp.cumsum(onehot, axis=0) * onehot, axis=1) - 1
    slot_index = flat_routes * capacity + position_in
    source = (
        jnp.full((experts * capacity,), assigns, jnp.int32)
        .at[slot_index]
        .set(jnp.arange(assigns, dtype=jnp.int32))
    )
    token_of = source // choose
    h_ext = jnp.concatenate([h_second, jnp.zeros((1, width), jnp.bfloat16)], axis=0)
    send_rows = h_ext[token_of].reshape(owners, local_experts, capacity, width)
    row_entries = lax.all_to_all(send_rows, "ep", split_axis=0, concat_axis=0, tiled=True)
    gate_val = jnp.einsum(
        "secd,edf->secf", row_entries, expert_gate, preferred_element_type=jnp.float32
    )
    up_val = jnp.einsum(
        "secd,edf->secf", row_entries, expert_up, preferred_element_type=jnp.float32
    )
    act = glu_value(gate_val, up_val).astype(jnp.bfloat16)
    result = jnp.einsum("secf,efd->secd", act, expert_down, preferred_element_type=jnp.float32)
    outputs = (result.astype(jnp.bfloat16), row_entries, gate_val, up_val)
    returned = lax.all_to_all(outputs[0], "ep", split_axis=0, concat_axis=0, tiled=True).reshape(
        experts * capacity, width
    )
    picked = returned[slot_index].reshape(length_total, choose, width).astype(jnp.float32)
    layer_out = (mixed + jnp.sum(route_gates[:, :, None] * picked, axis=1)).astype(jnp.bfloat16)
    grad_out = cotangent.astype(jnp.float32)
    slot_grads = (
        (route_gates[:, :, None] * grad_out[:, None, :])
        .astype(jnp.bfloat16)
        .reshape(assigns, width)
    )
    slot_ext = jnp.concatenate([slot_grads, jnp.zeros((1, width), jnp.bfloat16)], axis=0)
    grad_send = slot_ext[source].reshape(owners, local_experts, capacity, width)
    grad_recv = lax.all_to_all(grad_send, "ep", split_axis=0, concat_axis=0, tiled=True)
    recv_rows = outputs[1]
    gate_val = outputs[2]
    up_val = outputs[3]
    act, act_back = jax.vjp(glu_value, gate_val, up_val)
    act_low = act.astype(jnp.bfloat16)
    down_part = jnp.einsum("secf,secd->efd", act_low, grad_recv, preferred_element_type=jnp.float32)
    act_grad = jnp.einsum(
        "secd,efd->secf", grad_recv, expert_down, preferred_element_type=jnp.float32
    )
    gate_grad_val, up_grad_val = act_back(act_grad)
    gate_low = gate_grad_val.astype(jnp.bfloat16)
    up_low = up_grad_val.astype(jnp.bfloat16)
    gate_part = jnp.einsum(
        "secd,secf->edf", recv_rows, gate_low, preferred_element_type=jnp.float32
    )
    up_part = jnp.einsum("secd,secf->edf", recv_rows, up_low, preferred_element_type=jnp.float32)
    rows_grad = jnp.einsum(
        "secf,edf->secd", gate_low, expert_gate, preferred_element_type=jnp.float32
    )
    rows_grad = rows_grad + jnp.einsum(
        "secf,edf->secd", up_low, expert_up, preferred_element_type=jnp.float32
    )
    rows_back = lax.all_to_all(
        rows_grad.astype(jnp.bfloat16), "ep", split_axis=0, concat_axis=0, tiled=True
    )
    rows_back = rows_back.reshape(experts * capacity, width)
    expert_sums = (
        lax.psum_scatter(
            gate_part.astype(jnp.bfloat16), "grp", scatter_dimension=1, tiled=True
        ).astype(jnp.float32),
        lax.psum_scatter(
            up_part.astype(jnp.bfloat16), "grp", scatter_dimension=1, tiled=True
        ).astype(jnp.float32),
        lax.psum_scatter(
            down_part.astype(jnp.bfloat16), "grp", scatter_dimension=2, tiled=True
        ).astype(jnp.float32),
    )
    second_grad = jnp.sum(
        rows_back[slot_index].reshape(length_total, choose, width).astype(jnp.float32), axis=1
    )
    ffn_gain_part = jnp.sum(second_grad * normed_second, axis=0)
    normed_grad = second_grad * ffn_gain
    mixed_grad = grad_out + scale_second * (
        normed_grad - normed_second * jnp.mean(normed_grad * normed_second, axis=-1, keepdims=True)
    )
    mixed_low = mixed_grad.astype(jnp.bfloat16)
    output_part = jnp.einsum("ti,td->id", attended, mixed_low, preferred_element_type=jnp.float32)
    attended_grad = jnp.einsum(
        "td,id->ti", mixed_low, output_weight, preferred_element_type=jnp.float32
    )
    attended_grad = attended_grad.astype(jnp.bfloat16).reshape(
        length_total, key_heads, q_per_kv, HEAD_SIZE
    )
    probs = jnp.exp(scores_of(query_rot, key_rot, allowed) - log_total)
    probs_again = probs.astype(jnp.bfloat16)
    value_part_grad = jnp.einsum(
        "kgts,tkgd->skd", probs_again, attended_grad, preferred_element_type=jnp.float32
    )
    prob_grad = jnp.einsum(
        "tkgd,skd->kgts", attended_grad, value_low, preferred_element_type=jnp.float32
    )
    inner = jnp.sum(probs * prob_grad, axis=-1, keepdims=True)
    score_grad = (probs * (prob_grad - inner)).astype(jnp.bfloat16)
    qrot_grad = jnp.einsum(
        "kgts,skd->tkgd", score_grad, key_rot, preferred_element_type=jnp.float32
    ) * HEAD_SIZE ** (-0.5)
    krot_grad = jnp.einsum(
        "kgts,tkgd->skd", score_grad, query_rot, preferred_element_type=jnp.float32
    ) * HEAD_SIZE ** (-0.5)
    query_grad_low = unrotate(
        qrot_grad.reshape(length_total, query_heads, HEAD_SIZE), cosine_table, sine_table
    )
    query_grad_low = query_grad_low.astype(jnp.bfloat16).reshape(
        length_total, query_heads * HEAD_SIZE
    )
    key_grad_low = (
        unrotate(krot_grad, cosine_table, sine_table)
        .astype(jnp.bfloat16)
        .reshape(length_total, key_heads * HEAD_SIZE)
    )
    value_grad_low = value_part_grad.astype(jnp.bfloat16).reshape(
        length_total, key_heads * HEAD_SIZE
    )
    query_part = jnp.einsum(
        "td,ti->di", h_first, query_grad_low, preferred_element_type=jnp.float32
    )
    key_part = jnp.einsum("td,ti->di", h_first, key_grad_low, preferred_element_type=jnp.float32)
    value_part = jnp.einsum(
        "td,ti->di", h_first, value_grad_low, preferred_element_type=jnp.float32
    )
    first_grad = jnp.einsum(
        "ti,di->td", query_grad_low, query_weight, preferred_element_type=jnp.float32
    )
    first_grad = first_grad + jnp.einsum(
        "ti,di->td", key_grad_low, key_matrix, preferred_element_type=jnp.float32
    )
    first_grad = first_grad + jnp.einsum(
        "ti,di->td", value_grad_low, value_matrix, preferred_element_type=jnp.float32
    )
    attn_gain_part = jnp.sum(first_grad * normed_first, axis=0)
    normed_first_grad = first_grad * attn_gain
    tokens_grad = mixed_grad + scale_first * (
        normed_first_grad
        - normed_first * jnp.mean(normed_first_grad * normed_first, axis=-1, keepdims=True)
    )
    shared = (
        lax.psum_scatter(query_part, ("grp", "ep"), scatter_dimension=0, tiled=True),
        lax.psum_scatter(key_part, ("grp", "ep"), scatter_dimension=0, tiled=True),
        lax.psum_scatter(value_part, ("grp", "ep"), scatter_dimension=0, tiled=True),
        lax.psum_scatter(output_part, ("grp", "ep"), scatter_dimension=1, tiled=True),
        lax.psum_scatter(attn_gain_part, ("grp", "ep"), scatter_dimension=0, tiled=True),
        lax.psum_scatter(ffn_gain_part, ("grp", "ep"), scatter_dimension=0, tiled=True),
    )
    return (
        layer_out,
        tokens_grad,
        shared[0],
        shared[1],
        shared[2],
        shared[3],
        shared[4],
        shared[5],
        expert_sums[0],
        expert_sums[1],
        expert_sums[2],
    )


def forward_kernel(
    attn_gain_ref, ffn_gain_ref, cos_ref, sin_ref, seg_row_ref, seg_col_ref, tab_ref, tok_ref,
    wq_ref, wk_ref, wv_ref, wo_ref, dy_ref, gate_ref, up_ref, down_ref,
    query_ref, key_ref, value_ref, lse_ref, att_ref, mixed_ref, grad_gu_ref, grad_down_ref,
    out_own_ref, out_sib_ref, d_own_ref, d_sib_ref, d_first_ref, d_second_ref, part_d_ref,
    part_o_ref,
    xb, dyb, tab, w_gu, w_down, sib, far_in, gather_send, gather_recv, tab_send, tab_recv,
    fetch_send, fetch_recv, pass_send, pass_recv, local_sem, part_send, part_recv, keep_sem,
    sum_send, sum_recv, store_sem, stage_sem,
):
    f32, bf16 = jnp.float32, jnp.bfloat16
    grp, ep = lax.axis_index("grp"), lax.axis_index("ep")
    core = lax.rem(grp, 2)
    side = grp // 2
    low = lax.rem(ep, 4)
    y, z = lax.rem(low, 2), low // 2
    by_y = ep + 1 - 2 * y
    by_z = ep + 2 - 4 * z
    by_both = by_y + 2 - 4 * z
    by_far = ep + 4 - 8 * (ep // 4)
    first = by_y * (1 - core) + by_z * core
    second = by_z * (1 - core) + by_y * core
    other = grp + 1 - 2 * core
    across = (grp + 2 - 4 * side, ep)
    away = (grp, by_far)
    rows, width = tok_ref.shape
    half = rows // 2
    hidden = gate_ref.shape[1]
    mine = hidden // 2
    head = cos_ref.shape[1]
    heads = width // head
    key_width = wk_ref.shape[1]
    per_key = heads * head // key_width

    def remote(src, dst, send, recv, device):
        return pltpu.make_async_remote_copy(
            src_ref=src, dst_ref=dst, send_sem=send, recv_sem=recv, device_id=device,
            device_id_type=pl.DeviceIdType.MESH,
        )

    members = (
        ((grp, first), 1), ((grp, second), 2), ((grp, by_both), 3), ((other, ep), 4),
        ((other, first), 5), ((other, second), 6), ((other, by_both), 7),
    )
    barrier = pltpu.get_barrier_semaphore()
    for device in [device for device, _ in members] + [across, away]:
        pl.semaphore_signal(barrier, inc=1, device_id=device, device_id_type=pl.DeviceIdType.MESH)
    pl.semaphore_wait(barrier, 9)

    units = pl.ds(pl.multiple_of(core * mine, mine), mine)
    own_weights = (
        (gate_ref.at[:, units], w_gu.at[0, :, pl.ds(0, mine)]),
        (up_ref.at[:, units], w_gu.at[0, :, pl.ds(mine, mine)]),
        (down_ref.at[units, :], w_down.at[0]),
    )
    wide_at = pl.ds(pl.multiple_of(side * (width // 2), width // 2), width // 2)
    deep_at = pl.ds(pl.multiple_of(side * (mine // 2), mine // 2), mine // 2)
    deep_from = pl.ds(pl.multiple_of(core * mine + side * (mine // 2), mine // 2), mine // 2)
    pieces = (
        (gate_ref.at[wide_at, units], w_gu.at[1, wide_at, pl.ds(0, mine)]),
        (up_ref.at[wide_at, units], w_gu.at[1, wide_at, pl.ds(mine, mine)]),
        (down_ref.at[deep_from, :], w_down.at[1, deep_at, :]),
    )

    def fetch_copy(m):
        return remote(*pieces[m], fetch_send.at[m], fetch_recv.at[m], away)

    def pass_copy(m):
        return remote(pieces[m][1], pieces[m][1], pass_send.at[m], pass_recv.at[m], across)

    def load(number, src, dst):
        return pltpu.make_async_copy(src, dst, local_sem.at[number])

    def gather_copy(k, number):
        own, buf = ((xb.at[0], xb), (dy_ref, dyb))[k]
        src, dst, device = (
            (own, 1, (grp, first)), (own, 4, (other, ep)), (own, 2, (grp, second)),
            (buf.at[1], 5, (other, ep)), (buf.at[2], 6, (other, ep)),
            (buf.at[2], 3, (grp, first)), (buf.at[3], 7, (other, ep)),
        )[number]
        return remote(
            src, buf.at[dst], gather_send.at[k, number], gather_recv.at[k, number], device
        )

    arrival = {1: 0, 4: 1, 2: 2, 5: 3, 6: 4, 3: 5, 7: 6}

    def start(k, *numbers):
        for number in numbers:
            gather_copy(k, number).start()

    def arrived(k, slot):
        gather_copy(k, arrival[slot]).wait_recv()

    def table_copy(slot):
        device = members[slot - 1][0]
        return remote(tab_ref, tab.at[slot], tab_send.at[slot], tab_recv.at[slot], device)

    fetch_copy(0).start()
    fetch_copy(1).start()
    start(1, 0, 1, 2)
    for slot in range(1, 8):
        table_copy(slot).start()
    own_dy = lambda: load(0, dy_ref, dyb.at[0])
    tab[0] = tab_ref[...]

    def dot_nt(a, b):
        return lax.dot_general(a, b, (((1,), (1,)), ((), ())), preferred_element_type=f32)

    def dot_tn(a, b):
        return lax.dot_general(a, b, (((0,), (0,)), ((), ())), preferred_element_type=f32)

    def attention(w_big, w_key, w_value, tok, act, query, key, value, bias, mixed, lse):
        tok_load = load(4, tok_ref, tok)
        query_load = load(5, wq_ref, w_big)
        key_load = load(6, wk_ref, w_key)
        value_load = load(7, wv_ref, w_value)
        for copy in (tok_load, query_load, key_load, value_load):
            copy.start()
        own_dy().start()
        for m, (src, dst) in enumerate(own_weights):
            load(1 + m, src, dst).start()
        position = lax.broadcasted_iota(jnp.int32, (rows, rows), 0)
        other_position = lax.broadcasted_iota(jnp.int32, (rows, rows), 1)
        padding = seg_row_ref[...] == jnp.max(seg_row_ref[...])
        allowed = (
            (other_position <= position)
            & (seg_col_ref[...] == seg_row_ref[...])
            & (jnp.logical_not(padding) | (other_position == position))
        )
        bias[...] = jnp.where(allowed, 0.0, -1e30)
        lse[...] = jnp.zeros_like(lse)
        tok_load.wait()

        @pl.loop(0, rows // 128)
        def _(step):
            at = pl.ds(pl.multiple_of(step * 128, 128), 128)
            entry = tok[at, :].astype(f32)
            factor = lax.rsqrt(jnp.mean(entry * entry, axis=-1, keepdims=True) + EPS)
            act[at, :] = (entry * factor * attn_gain_ref[...]).astype(bf16)

        def turn(entry, at):
            swapped = pltpu.roll(entry, head // 2, 1)
            return entry * cos_ref[at, :] + swapped * sin_ref[at, :]

        key_load.wait()
        value_load.wait()
        key_rows = jnp.dot(act[...], w_key[...], preferred_element_type=f32)
        for kv in range(key_width // head):
            columns = slice(kv * head, (kv + 1) * head)
            key[:, columns] = turn(key_rows[:, columns], slice(None)).astype(bf16)
        value[...] = jnp.dot(act[...], w_value[...], preferred_element_type=f32).astype(bf16)
        query_load.wait()
        for tile in range(width // 256):
            columns = slice(tile * 256, (tile + 1) * 256)
            entry = jnp.dot(act[...], w_big[:, columns], preferred_element_type=f32)
            for part in range(256 // head):
                columns = slice(part * head, (part + 1) * head)
                to = slice(tile * 256 + part * head, tile * 256 + (part + 1) * head)
                query[:, to] = turn(entry[:, columns], slice(None)).astype(bf16)
        out_load = load(8, wo_ref, w_big)
        out_load.start()
        stores = [
            pltpu.make_async_copy(src, dst, store_sem.at[i])
            for i, (src, dst) in enumerate(((query, query_ref), (key, key_ref), (value, value_ref)))
        ]
        for copy in stores:
            copy.start()
        scale = head ** (-0.5)
        lane = lax.broadcasted_iota(jnp.int32, (half, head), 1)
        for number in range(heads):
            columns = slice(number * head, (number + 1) * head)
            kv = number // per_key
            kv_columns = slice(kv * head, (kv + 1) * head)
            for part in range(2):
                at = slice(part * half, (part + 1) * half)
                seen = slice(0, (part + 1) * half)
                score = dot_nt(query[at, columns], key[seen, kv_columns]) * scale + bias[at, seen]
                top = jnp.max(score, axis=-1, keepdims=True)
                expo = jnp.exp(score - top)
                total = jnp.sum(expo, axis=-1, keepdims=True)
                lse[at, :] = jnp.where(lane == number, top + jnp.log(total), lse[at, :])
                probs = (expo / total).astype(bf16)
                mixed_value = jnp.dot(probs, value[seen, kv_columns], preferred_element_type=f32)
                act[at, columns] = mixed_value.astype(bf16)
        out_load.wait()
        arrived(1, 1)
        start(1, 3)
        att_store = pltpu.make_async_copy(act, att_ref, store_sem.at[3])
        att_store.start()
        lse_store = pltpu.make_async_copy(lse, lse_ref, store_sem.at[4])
        lse_store.start()
        for part in range(4):
            at = slice(part * rows // 4, (part + 1) * rows // 4)
            total = tok[at, :].astype(f32) + jnp.dot(
                act[at, :], w_big[...], preferred_element_type=f32
            )
            mixed[at, :] = total
            factor = lax.rsqrt(jnp.mean(total * total, axis=-1, keepdims=True) + EPS)
            xb[0, at, :] = (total * factor * ffn_gain_ref[...]).astype(bf16)
        start(0, 0, 1)
        mixed_store = pltpu.make_async_copy(mixed, mixed_ref, store_sem.at[5])
        mixed_store.start()
        for copy in stores + [att_store, lse_store, mixed_store]:
            copy.wait()

    vmem = pltpu.VMEM
    pl.run_scoped(
        attention,
        vmem((width, width), bf16),
        vmem((width, key_width), bf16),
        vmem((width, key_width), bf16),
        vmem((rows, width), bf16),
        vmem((rows, width), bf16),
        vmem((rows, width), bf16),
        vmem((rows, key_width), bf16),
        vmem((rows, key_width), bf16),
        vmem((rows, rows), f32),
        vmem((rows, width), f32),
        vmem((rows, head), f32),
    )

    def experts(acc_gu, acc_down, act_s, gu_s, dz_s, stage):
        fetch_copy(2).start()
        own_dy().wait()
        for m, (src, dst) in enumerate(own_weights):
            load(1 + m, src, dst).wait()
        for slot in range(1, 8):
            table_copy(slot).wait_send()
            table_copy(slot).wait_recv()
        acc_gu[...] = jnp.zeros_like(acc_gu)
        acc_down[...] = jnp.zeros_like(acc_down)

        def gates(slot, hosted):
            block = jnp.transpose(tab[slot])
            lane = lax.broadcasted_iota(jnp.int32, block.shape, 1)
            return jnp.sum(jnp.where(lane == hosted, block, 0.0), axis=1, keepdims=True)

        c0 = 0.7978845608028654
        c1 = 0.044715

        def work(which, slot, hosted, deliver):
            column = gates(slot, hosted)
            for part in range(2):
                at = pl.ds(part * half, half)
                gate = column[part * half : (part + 1) * half]
                gu = jnp.dot(xb[slot, at, :], w_gu[which], preferred_element_type=f32)
                dz = (gate * dyb[slot, at, :].astype(f32)).astype(bf16)
                dz_s[at, :] = dz
                da = dot_nt(dz, w_down[which])
                g, u = gu[:, :mine], gu[:, mine:]
                square = g * g
                t = jnp.tanh(c0 * (g + c1 * square * g))
                gelu = 0.5 * g * (1.0 + t)
                slope = 0.5 * (1.0 + t) + 0.5 * g * (1.0 - t * t) * (c0 * (1.0 + 3.0 * c1 * square))
                act_s[at, :] = (gelu * u).astype(bf16)
                gu_s[at, :mine] = (da * u * slope).astype(bf16)
                gu_s[at, mine:] = (da * gelu).astype(bf16)
            for part in range(3):
                at = pl.ds(part * (width // 3), width // 3)
                acc_gu[at, :] += dot_tn(xb[slot, :, at], gu_s[...])
                acc_down[:, at] += dot_tn(act_s[...], dz_s[:, at])
            for part in range(2):
                at = pl.ds(part * half, half)
                gate = column[part * half : (part + 1) * half]
                dx = dot_nt(gu_s[at, :], w_gu[which])
                result = gate * jnp.dot(act_s[at, :], w_down[which], preferred_element_type=f32)
                deliver(at, dx, result)

        def slot_up(step):
            return step // 2 + 4 * lax.rem(step, 2)

        def stage_out(k, step):
            buf = lax.rem(step, 2)
            dst = (part_d_ref, part_o_ref)[k].at[slot_up(step)]
            return pltpu.make_async_copy(stage.at[k, buf], dst, stage_sem.at[k, buf])

        @pl.loop(0, 8)
        def _(step):
            def at_step(number):
                return pl.when(step == number)

            @at_step(1)
            def _():
                arrived(0, 4)
                arrived(1, 4)
                arrived(1, 2)
                start(1, 4, 5)

            @at_step(2)
            def _():
                arrived(0, 1)
                start(0, 3, 2)

            @at_step(3)
            def _():
                arrived(0, 5)
                arrived(1, 5)

            @at_step(4)
            def _():
                arrived(0, 2)
                start(0, 4, 5)
                fetch_copy(0).wait_recv()
                pass_copy(0).start()
                fetch_copy(1).wait_recv()
                pass_copy(1).start()

            @at_step(5)
            def _():
                arrived(0, 6)
                arrived(1, 6)
                arrived(1, 3)
                start(1, 6)

            @at_step(6)
            def _():
                arrived(0, 3)
                start(0, 6)
                fetch_copy(2).wait_recv()
                pass_copy(2).start()

            @at_step(7)
            def _():
                arrived(0, 7)
                arrived(1, 7)

            @pl.when(step >= 2)
            def _():
                stage_out(0, step - 2).wait()
                stage_out(1, step - 2).wait()

            buf = lax.rem(step, 2)

            def deliver(at, dx, result):
                stage[0, buf, at, :] = dx.astype(bf16)
                stage[1, buf, at, :] = result.astype(bf16)

            work(0, slot_up(step), ep, deliver)
            stage_out(0, step).start()
            stage_out(1, step).start()

        for k in range(2):
            for step in (6, 7):
                stage_out(k, step).wait()
        for k in range(2):
            for number in range(7):
                gather_copy(k, number).wait_send()

        def grad_copies(which):
            return (
                pltpu.make_async_copy(w_gu.at[which], grad_gu_ref.at[which], store_sem.at[6 + 2 * which]),
                pltpu.make_async_copy(
                    w_down.at[which], grad_down_ref.at[which], store_sem.at[7 + 2 * which]
                ),
            )

        def slot_down(step):
            pair = step // 2
            return 3 - 2 * lax.rem(pair, 2) - pair // 2 + 4 * (1 - lax.rem(step, 2))

        def stage_in(k, step):
            buf = lax.rem(step, 2)
            src = (part_d_ref, part_o_ref)[k].at[slot_down(step)]
            return pltpu.make_async_copy(src, stage.at[k, buf], stage_sem.at[k, buf])

        stage_in(0, 0).start()
        stage_in(1, 0).start()
        w_gu[0] = acc_gu[...].astype(bf16)
        w_down[0] = acc_down[...].astype(bf16)
        for copy in grad_copies(0):
            copy.start()
        acc_gu[...] = jnp.zeros_like(acc_gu)
        acc_down[...] = jnp.zeros_like(acc_down)
        for m in range(3):
            pass_copy(m).wait()
            fetch_copy(m).wait_send()

        def keep_copy(j):
            return pltpu.make_async_copy(dyb.at[j], out_own_ref.at[j], keep_sem.at[j])

        def grad_part(j):
            dst = d_sib_ref if j == 0 else sib.at[j - 1]
            return remote(xb.at[4 + j], dst, part_send.at[0, j], part_recv.at[0, j], (other, ep))

        def out_part(j):
            return remote(
                dyb.at[4 + j], out_sib_ref.at[j], part_send.at[1, j], part_recv.at[1, j], (other, ep)
            )

        own_grad = lambda: pltpu.make_async_copy(xb.at[0], d_own_ref, keep_sem.at[4])
        send_far = lambda: remote(xb.at[3], far_in, sum_send.at[0], sum_recv.at[0], (grp, first))
        send_first = lambda: remote(
            xb.at[1], d_first_ref, sum_send.at[1], sum_recv.at[1], (grp, first)
        )
        send_second = lambda: remote(
            xb.at[2], d_second_ref, sum_send.at[2], sum_recv.at[2], (grp, second)
        )

        def add_into(dst, *others):
            @pl.loop(0, rows // 128)
            def _(i):
                at = pl.ds(pl.multiple_of(i * 128, 128), 128)
                total = dst[at, :].astype(f32)
                for part in others:
                    total = total + part[at, :].astype(f32)
                dst[at, :] = total.astype(bf16)

        @pl.loop(0, 8)
        def _(step):
            def at_step(number):
                return pl.when(step == number)

            stage_in(0, step).wait()
            stage_in(1, step).wait()

            @pl.when(step < 7)
            def _():
                stage_in(0, step + 1).start()
                stage_in(1, step + 1).start()

            buf = lax.rem(step, 2)
            slot = slot_down(step)

            def deliver(at, dx, result):
                xb[slot, at, :] = (dx + stage[0, buf, at, :].astype(f32)).astype(bf16)
                dyb[slot, at, :] = (result + stage[1, buf, at, :].astype(f32)).astype(bf16)

            work(1, slot, ep + 4 - 8 * (ep // 4), deliver)
            for number, j in enumerate((3, 1, 2, 0)):

                @at_step(2 * number)
                def _(j=j):
                    grad_part(j).start()
                    out_part(j).start()

                @at_step(2 * number + 1)
                def _(j=j):
                    keep_copy(j).start()

            @at_step(1)
            def _():
                grad_part(3).wait_recv()
                add_into(xb.at[3], sib.at[2])
                send_far().start()

            @at_step(3)
            def _():
                grad_part(1).wait_recv()
                add_into(xb.at[1], sib.at[0])
                send_first().start()

            @at_step(5)
            def _():
                grad_part(2).wait_recv()
                send_far().wait_recv()
                add_into(xb.at[2], sib.at[1], far_in)
                send_second().start()

        own_grad().start()
        w_gu[1] = acc_gu[...].astype(bf16)
        w_down[1] = acc_down[...].astype(bf16)
        for copy in grad_copies(1):
            copy.start()
        for j in range(4):
            grad_part(j).wait_send()
            out_part(j).wait()
            keep_copy(j).wait()
        grad_part(0).wait_recv()
        own_grad().wait()
        send_far().wait_send()
        send_first().wait()
        send_second().wait()
        for which in range(2):
            for copy in grad_copies(which):
                copy.wait()

    pl.run_scoped(
        experts,
        vmem((width, hidden), f32),
        vmem((mine, width), f32),
        vmem((rows, mine), bf16),
        vmem((rows, hidden), bf16),
        vmem((rows, width), bf16),
        vmem((2, 2, rows, width), bf16),
    )


def forward_call(vmem_args, any_args):
    f32, bf16 = jnp.float32, jnp.bfloat16
    rows, width = any_args[0].shape
    head = vmem_args[2].shape[1]
    key_width = any_args[2].shape[1]
    hidden = any_args[6].shape[1]
    anywhere = pl.BlockSpec(memory_space=pl.ANY)
    inside = pl.BlockSpec(memory_space=pltpu.VMEM)
    shape = jax.ShapeDtypeStruct
    dma = pltpu.SemaphoreType.DMA
    vmem = pltpu.VMEM
    chunk = shape((rows, width), bf16)
    four = shape((4, rows, width), bf16)
    eight = shape((8, rows, width), bf16)
    return pl.pallas_call(
        forward_kernel,
        out_shape=(
            chunk,
            shape((rows, key_width), bf16),
            shape((rows, key_width), bf16),
            shape((rows, head), f32),
            chunk,
            shape((rows, width), f32),
            shape((2, width, hidden), bf16),
            shape((2, hidden // 2, width), bf16),
            four,
            four,
            chunk,
            chunk,
            chunk,
            chunk,
            eight,
            eight,
        ),
        in_specs=[inside] * len(vmem_args) + [anywhere] * len(any_args),
        out_specs=(anywhere,) * 16,
        scratch_shapes=[
            vmem((8, rows, width), bf16),
            vmem((8, rows, width), bf16),
            vmem((8,) + vmem_args[6].shape, f32),
            vmem((2, width, hidden), bf16),
            vmem((2, hidden // 2, width), bf16),
            vmem((3, rows, width), bf16),
            vmem((rows, width), bf16),
            dma((2, 7)),
            dma((2, 7)),
            dma((8,)),
            dma((8,)),
            dma((3,)),
            dma((3,)),
            dma((3,)),
            dma((3,)),
            dma((9,)),
            dma((2, 4)),
            dma((2, 4)),
            dma((5,)),
            dma((3,)),
            dma((3,)),
            dma((10,)),
            dma((2, 2)),
        ],
        compiler_params=pltpu.CompilerParams(
            collective_id=0, has_side_effects=True, vmem_limit_bytes=64 * 2**20
        ),
        cost_estimate=pl.CostEstimate(
            flops=160 * rows * width * hidden, bytes_accessed=60 * 2**20, transcendentals=0
        ),
    )(*vmem_args, *any_args)


def backward_kernel(
    attn_gain_ref, ffn_gain_ref, cos_ref, sin_ref, seg_row_ref, seg_col_ref, lse_ref, key_ref,
    value_ref, second0_ref, second1_ref, second2_ref, second3_ref, mixed_ref, cot_ref, att_ref,
    query_ref, tok_ref, wo_ref, wq_ref, wk_ref, wv_ref, ggu_ref, gd_ref, own_ref, sibling_ref,
    query_out, kv_out, out_out, layer_ref, tokens_ref, gate_out, up_out, down_out, ra_ref, rb_ref, rf_ref,
    pool, w_big, w_key, w_value, grad, proj, bias, key_acc, value_acc, gain_acc,
    out_buf, out_land, query_buf, kv_buf, kv_land,
    ex_gu, ex_down, ef_gu, ef_down, ec_gu, ec_down, kept_gu, kept_down, stage, stage_down, load_sem, out_send, out_recv, ex_send, ex_recv, ef_send, ef_recv, ec_send, ec_recv,
    halve_send, halve_recv, free_sem, store_sem,
):
    f32, bf16 = jnp.float32, jnp.bfloat16
    grp, ep = lax.axis_index("grp"), lax.axis_index("ep")
    core = lax.rem(grp, 2)
    x = grp // 2
    y = lax.rem(ep, 2)
    z_low = lax.rem(ep // 2, 2)
    z_high = ep // 4
    by_y = (grp, ep + 1 - 2 * y)
    by_z = (grp, ep + 2 - 4 * z_low)
    by_far = (grp, ep + 4 - 8 * z_high)
    by_core = (grp + 1 - 2 * core, ep)
    by_x = (grp + 2 - 4 * x, ep)
    first = (grp, by_y[1] * (1 - core) + by_z[1] * core)
    second = (grp, by_z[1] * (1 - core) + by_y[1] * core)
    rows, width = grad.shape
    head = cos_ref.shape[1]
    heads = width // head
    key_width = key_ref.shape[1]
    per_key = heads * head // key_width
    block = width // 32

    def remote(src, dst, send, recv, device):
        return pltpu.make_async_remote_copy(
            src_ref=src, dst_ref=dst, send_sem=send, recv_sem=recv, device_id=device,
            device_id_type=pl.DeviceIdType.MESH,
        )

    partners = (by_core, by_y, by_z, by_x, by_far)
    barrier = pltpu.get_barrier_semaphore()
    for device in partners:
        pl.semaphore_signal(barrier, inc=1, device_id=device, device_id_type=pl.DeviceIdType.MESH)
    pl.semaphore_wait(barrier, 5)

    wide_half = width // 2
    quarter = width // 4
    mine = gd_ref.shape[1]
    ex_dst = (ex_gu, ex_down)

    def part(ref, m, index, size):
        at = pl.ds(pl.multiple_of(index * size, size), size)
        return ref.at[:, at] if m == 1 else ref.at[at, :]

    def ex_copy(which, m):
        src = part((ggu_ref, gd_ref)[m].at[which], m, 1 - x, wide_half)
        return remote(src, ex_dst[m].at[which], ex_send.at[which, m], ex_recv.at[which, m], by_x)

    def ef_copy(m):
        return remote(ex_dst[m].at[1], (ef_gu, ef_down)[m], ef_send.at[m], ef_recv.at[m], by_far)

    def ec_copy(m):
        src = part(ex_dst[m].at[0], m, 1 - core, quarter)
        return remote(src, (ec_gu, ec_down)[m], ec_send.at[m], ec_recv.at[m], by_core)

    def kept_copy(which, m):
        src = part((ggu_ref, gd_ref)[m].at[which], m, x, wide_half)
        return pltpu.make_async_copy(src, (kept_gu, kept_down)[m], load_sem.at[20 + m])

    def load(number, src, dst):
        return pltpu.make_async_copy(src, dst, load_sem.at[number])

    for which in (1, 0):
        for m in range(2):
            ex_copy(which, m).start()
    loads = (
        (own_ref.at[3], pool.at[6]),
        (sibling_ref.at[3], pool.at[9]),
        (own_ref.at[1], pool.at[5]),
        (sibling_ref.at[1], pool.at[8]),
        (second0_ref, pool.at[1]),
        (second1_ref, pool.at[2]),
        (second2_ref, pool.at[3]),
        (second3_ref, pool.at[4]),
        (mixed_ref, grad),
        (cot_ref, pool.at[0]),
        (wo_ref, w_big),
        (own_ref.at[2], pool.at[7]),
    )
    for number, (src, dst) in enumerate(loads):
        load(number, src, dst).start()

    def wait_load(number):
        load(number, *loads[number]).wait()

    def add_into(dst, *others):
        @pl.loop(0, rows // 128)
        def _(step):
            at = pl.ds(pl.multiple_of(step * 128, 128), 128)
            total = dst[at, :].astype(f32)
            for other in others:
                total = total + other[at, :].astype(f32)
            dst[at, :] = total.astype(bf16)

    far_copy = lambda: remote(pool.at[6], rf_ref, out_send.at[0], out_recv.at[0], first)
    first_copy = lambda: remote(pool.at[5], ra_ref, out_send.at[1], out_recv.at[1], first)
    second_copy = lambda: remote(pool.at[7], rb_ref, out_send.at[2], out_recv.at[2], second)
    wait_load(0)
    wait_load(1)
    add_into(pool.at[6], pool.at[9])
    far_copy().start()
    wait_load(2)
    wait_load(3)
    add_into(pool.at[5], pool.at[8])
    first_copy().start()
    sib2 = lambda: load(12, sibling_ref.at[2], pool.at[8])
    sib2().start()
    for m in range(2):
        kept_copy(1, m).start()

    for number in range(4, 10):
        wait_load(number)
    gain_acc[...] = jnp.zeros_like(gain_acc)

    @pl.loop(0, rows // 128)
    def _(step):
        at = pl.ds(pl.multiple_of(step * 128, 128), 128)
        value = grad[at, :]
        scale = lax.rsqrt(jnp.mean(value * value, axis=-1, keepdims=True) + EPS)
        normed = value * scale
        down = (
            pool[1, at, :].astype(f32)
            + pool[2, at, :].astype(f32)
            + pool[3, at, :].astype(f32)
            + pool[4, at, :].astype(f32)
        )
        product = down * normed
        gain_acc[1:2, :] += jnp.sum(product, axis=0, keepdims=True)
        mean = jnp.mean(product * ffn_gain_ref[...], axis=-1, keepdims=True)
        result = pool[0, at, :].astype(f32) + scale * (down * ffn_gain_ref[...] - normed * mean)
        grad[at, :] = result
        pool[3, at, :] = result.astype(bf16)

    att_load = lambda: load(13, att_ref, pool.at[1])
    query_load = lambda: load(14, query_ref, pool.at[2])
    tok_load = lambda: load(15, tok_ref, pool.at[0])
    key_weight_load = lambda: load(16, wk_ref, w_key)
    value_weight_load = lambda: load(17, wv_ref, w_value)
    for copy in (att_load, query_load, tok_load, key_weight_load, value_weight_load):
        copy().start()

    position = lax.broadcasted_iota(jnp.int32, (rows, rows), 0)
    other_position = lax.broadcasted_iota(jnp.int32, (rows, rows), 1)
    padding = seg_row_ref[...] == jnp.max(seg_row_ref[...])
    allowed = (
        (other_position <= position)
        & (seg_col_ref[...] == seg_row_ref[...])
        & (jnp.logical_not(padding) | (other_position == position))
    )
    bias[...] = jnp.where(allowed, 0.0, -1e30)

    def dot_nt(a, b):
        return lax.dot_general(a, b, (((1,), (1,)), ((), ())), preferred_element_type=f32)

    def dot_tn(a, b):
        return lax.dot_general(a, b, (((0,), (0,)), ((), ())), preferred_element_type=f32)

    levels = ((core, by_core), (y, by_y), (x, by_x), (z_low, by_z), (z_high, by_far))
    offsets = (0, 16, 24, 28, 30)
    starts = [0]
    for level, (bit, _) in enumerate(levels):
        starts.append(starts[-1] + bit * (16 >> level))

    def halve_copy(job, buf, land, level):
        bit, device = levels[level]
        size = 16 >> level
        return remote(
            buf.at[pl.ds(starts[level] + (1 - bit) * size, size)],
            land.at[pl.ds(offsets[level], size)],
            halve_send.at[job, level],
            halve_recv.at[job, level],
            device,
        )

    def absorb(job, buf, land, level, result=None):
        halve_copy(job, buf, land, level).wait_recv()
        size = 16 >> level
        if result is None:

            @pl.loop(0, size)
            def _(i):
                at = starts[level + 1] + i
                buf[at] = (buf[at].astype(f32) + land[offsets[level] + i].astype(f32)).astype(bf16)

        else:
            result[...] = buf[starts[5]].astype(f32) + land[offsets[4]].astype(f32)
        if job == 0:
            pl.semaphore_signal(
                free_sem.at[level], inc=1, device_id=levels[level][1],
                device_id_type=pl.DeviceIdType.MESH,
            )
        if level < 4:
            launch(job, level + 1)

    jobs = ((out_buf, out_land), (query_buf, out_land), (kv_buf, kv_land))

    def launch(job, level):
        if job == 1:
            pl.semaphore_wait(free_sem.at[level], 1)
        halve_copy(job, *jobs[job], level).start()

    def begin(job):
        launch(job, 0)

    def advance(job, level):
        absorb(job, *jobs[job], level, (out_out, query_out, kv_out)[job] if level == 4 else None)

    def place(buf, tile, value, columns):
        for b in range(8):
            high, low, odd = b >> 2, (b >> 1) & 1, b & 1
            to = ((((tile & 1) * 2 + odd) * 2 + (tile >> 1)) * 2 + low) * 2 + high
            buf[to, :, columns] = value[b * block : (b + 1) * block].astype(bf16)

    att_load().wait()
    for tile in range(4):
        at = slice(tile * 8 * block, (tile + 1) * 8 * block)
        place(out_buf, tile, dot_tn(pool[3, :, at], pool[1]), slice(None))
    begin(0)
    wait_load(10)
    for half in range(2):
        at = slice(half * rows // 2, (half + 1) * rows // 2)
        pool[4, at, :] = dot_nt(pool[3, at, :], w_big[...]).astype(bf16)
    query_weight_load = lambda: load(18, wq_ref, w_big)
    query_weight_load().start()

    tok_load().wait()

    def first_norm(at):
        value = pool[0, at, :].astype(f32)
        scale = lax.rsqrt(jnp.mean(value * value, axis=-1, keepdims=True) + EPS)
        return scale, value * scale

    @pl.loop(0, rows // 128)
    def _(step):
        at = pl.ds(pl.multiple_of(step * 128, 128), 128)
        pool[1, at, :] = (first_norm(at)[1] * attn_gain_ref[...]).astype(bf16)

    def send_second():
        wait_load(11)
        sib2().wait()
        far_copy().wait_recv()
        far_load = load(19, rf_ref, pool.at[9])
        far_load.start()
        far_load.wait()
        add_into(pool.at[7], pool.at[8], pool.at[9])
        second_copy().start()

    def merge(dst, other):
        @pl.loop(0, dst.shape[0] // 128)
        def _(step):
            at = pl.ds(pl.multiple_of(step * 128, 128), 128)
            dst[at, :] = (dst[at, :].astype(f32) + other[at, :].astype(f32)).astype(bf16)

    def expert_second(which):
        for m in range(2):
            kept_copy(which, m).wait()
            ex_copy(which, m).wait_recv()
            merge(ex_dst[m].at[which], (kept_gu, kept_down)[m])
            if which == 1:
                ef_copy(m).start()
                kept_copy(0, m).start()

    def expert_third():
        for m in range(2):
            ef_copy(m).wait_recv()
            merge(ex_dst[m].at[0], (ef_gu, ef_down)[m])
            ec_copy(m).start()

    def final_copies():
        here = pl.ds(pl.multiple_of(core * mine, mine), mine)
        there = pl.ds(pl.multiple_of((1 - core) * mine, mine), mine)
        low, high = pl.ds(0, mine), pl.ds(mine, mine)
        pairs = (
            (stage.at[0, :, low], gate_out.at[:, here]),
            (stage.at[0, :, high], up_out.at[:, here]),
            (stage.at[1, :, low], gate_out.at[:, there]),
            (stage.at[1, :, high], up_out.at[:, there]),
            (stage_down.at[0], down_out.at[here, :]),
            (stage_down.at[1], down_out.at[there, :]),
        )
        return [
            pltpu.make_async_copy(src, dst, store_sem.at[4 + i]) for i, (src, dst) in enumerate(pairs)
        ]

    def expert_last():
        at = pl.ds(pl.multiple_of(core * quarter, quarter), quarter)
        stage[0] = ex_gu[0, at, :].astype(f32)
        stage_down[0] = ex_down[0, :, at].astype(f32)
        for m in range(2):
            ec_copy(m).wait_recv()
        stage[1] = ec_gu[...].astype(f32)
        stage_down[1] = ec_down[...].astype(f32)
        for copy in final_copies():
            copy.start()

    def turn_back(value, at):
        swapped = pltpu.roll(value, head // 2, 1)
        return value * cos_ref[at, :] - swapped * sin_ref[at, :]

    scale = head ** (-0.5)
    query_load().wait()
    key_acc[...] = jnp.zeros_like(key_acc)
    value_acc[...] = jnp.zeros_like(value_acc)

    def between(number):
        if number == 1:
            advance(0, 0)
        elif number == 3:
            send_second()
        elif number == 4:
            expert_second(1)
        elif number == 6:
            advance(0, 1)
        elif number == 9:
            advance(0, 2)

    for number in range(heads):
        columns = slice(number * head, (number + 1) * head)
        kv = number // per_key
        kv_columns = slice(kv * head, (kv + 1) * head)
        for half in range(2):
            at = slice(half * rows // 2, (half + 1) * rows // 2)
            seen = slice(0, (half + 1) * rows // 2)
            q = pool[2, at, columns]
            da = pool[4, at, columns]
            k = key_ref[seen, kv_columns]
            score = dot_nt(q, k) * scale + bias[at, seen]
            probs = jnp.exp(score - lse_ref[at, number : number + 1])
            dprob = dot_nt(da, value_ref[seen, kv_columns])
            inner = jnp.sum(probs * dprob, axis=-1, keepdims=True)
            dscore = (probs * (dprob - inner)).astype(bf16)
            value_acc[seen, kv_columns] += dot_tn(probs.astype(bf16), da)
            key_acc[seen, kv_columns] += dot_tn(dscore, q)
            dq = jnp.dot(dscore, k, preferred_element_type=f32) * scale
            proj[at, columns] = turn_back(dq, at).astype(bf16)
        between(number)

    for kv in range(key_width // head):
        columns = slice(kv * head, (kv + 1) * head)
        to = slice(width + kv * head, width + (kv + 1) * head)
        proj[:, to] = turn_back(key_acc[:, columns] * scale, slice(None)).astype(bf16)
        to = slice(width + key_width + kv * head, width + key_width + (kv + 1) * head)
        proj[:, to] = value_acc[:, columns].astype(bf16)

    for tile in range(4):
        at = slice(tile * 8 * block, (tile + 1) * 8 * block)
        place(query_buf, tile, dot_tn(pool[1, :, at], proj[:, :width]), slice(None))
    begin(1)
    for tile in range(4):
        at = slice(tile * 8 * block, (tile + 1) * 8 * block)
        place(kv_buf, tile, dot_tn(pool[1, :, at], proj[:, width:]), slice(0, 2 * key_width))
    query_weight_load().wait()
    key_weight_load().wait()
    value_weight_load().wait()
    for quarter_step in range(4):
        at = slice(quarter_step * rows // 4, (quarter_step + 1) * rows // 4)
        down = dot_nt(proj[at, :width], w_big[...])
        down = down + dot_nt(proj[at, width : width + key_width], w_key[...])
        down = down + dot_nt(proj[at, width + key_width :], w_value[...])
        factor, normed = first_norm(at)
        product = down * normed
        gain_acc[0:1, :] += jnp.sum(product, axis=0, keepdims=True)
        mean = jnp.mean(product * attn_gain_ref[...], axis=-1, keepdims=True)
        grad[at, :] = grad[at, :] + factor * (down * attn_gain_ref[...] - normed * mean)
        if quarter_step == 1:
            advance(1, 0)
    tokens_store = lambda: pltpu.make_async_copy(grad, tokens_ref, store_sem.at[0])
    tokens_store().start()

    gains = gain_acc[...]
    high = gains.astype(bf16).astype(f32)
    row = lax.broadcasted_iota(jnp.int32, gains.shape, 0)
    lower = pltpu.roll(gains - high, 2, 0)
    both = jnp.transpose(jnp.where(row < 2, high, lower))
    both = jnp.concatenate([both, jnp.zeros((width, head - 8), f32)], axis=1)
    for tile in range(4):
        at = slice(tile * 8 * block, (tile + 1) * 8 * block)
        place(kv_buf, tile, both[at], slice(2 * key_width, 2 * key_width + head))
    begin(2)

    advance(1, 1)
    advance(2, 0)
    advance(0, 3)
    expert_second(0)
    expert_third()
    advance(2, 1)
    advance(1, 2)
    advance(2, 2)
    advance(0, 4)
    advance(1, 3)
    advance(2, 3)
    expert_last()

    tokens_store().wait()
    first_copy().wait_recv()
    second_copy().wait_recv()
    last_loads = (
        (own_ref.at[0], pool.at[3]),
        (sibling_ref.at[0], pool.at[4]),
        (ra_ref, pool.at[8]),
        (rb_ref, pool.at[9]),
        (mixed_ref, grad),
    )
    for number, (src, dst) in enumerate(last_loads):
        load(number, src, dst).start()
    for number, (src, dst) in enumerate(last_loads):
        load(number, src, dst).wait()

    @pl.loop(0, rows // 128)
    def _(step):
        at = pl.ds(pl.multiple_of(step * 128, 128), 128)
        total = grad[at, :]
        for i in (3, 4, 8, 9):
            total = total + pool[i, at, :].astype(f32)
        pool[3, at, :] = total.astype(bf16)

    layer_store = pltpu.make_async_copy(pool.at[3], layer_ref, store_sem.at[1])
    layer_store.start()
    advance(1, 4)
    advance(2, 4)

    for copy in (far_copy, first_copy, second_copy):
        copy().wait_send()
    for m in range(2):
        for which in range(2):
            ex_copy(which, m).wait_send()
        ef_copy(m).wait_send()
        ec_copy(m).wait_send()
    for copy in final_copies():
        copy.wait()
    for job in range(3):
        for level in range(5):
            halve_copy(job, *jobs[job], level).wait_send()
    layer_store.wait()


def backward_call(vmem_args, any_args):
    f32, bf16 = jnp.float32, jnp.bfloat16
    rows, head = vmem_args[2].shape
    key_width = vmem_args[7].shape[1]
    width = vmem_args[0].shape[1]
    hidden = any_args[13].shape[2]
    block = width // 32
    extra = 2 * key_width + head
    anywhere = pl.BlockSpec(memory_space=pl.ANY)
    inside = pl.BlockSpec(memory_space=pltpu.VMEM)
    shape = jax.ShapeDtypeStruct
    dma = pltpu.SemaphoreType.DMA
    vmem = pltpu.VMEM
    return pl.pallas_call(
        backward_kernel,
        out_shape=(
            shape((block, width), f32),
            shape((block, extra), f32),
            shape((block, width), f32),
            shape((rows, width), bf16),
            shape((rows, width), f32),
            shape((width // 4, hidden), f32),
            shape((width // 4, hidden), f32),
            shape((hidden, width // 4), f32),
            shape((rows, width), bf16),
            shape((rows, width), bf16),
            shape((rows, width), bf16),
        ),
        in_specs=[inside] * len(vmem_args) + [anywhere] * len(any_args),
        out_specs=(inside,) * 3 + (anywhere,) * 8,
        scratch_shapes=[
            vmem((10, rows, width), bf16),
            vmem((width, width), bf16),
            vmem((width, key_width), bf16),
            vmem((width, key_width), bf16),
            vmem((rows, width), f32),
            vmem((rows, width + 2 * key_width), bf16),
            vmem((rows, rows), f32),
            vmem((rows, key_width), f32),
            vmem((rows, key_width), f32),
            vmem((8, width), f32),
            vmem((32, block, width), bf16),
            vmem((31, block, width), bf16),
            vmem((32, block, width), bf16),
            vmem((32, block, extra), bf16),
            vmem((31, block, extra), bf16),
            vmem((2, width // 2, hidden), bf16),
            vmem((2, hidden // 2, width // 2), bf16),
            vmem((width // 2, hidden), bf16),
            vmem((hidden // 2, width // 2), bf16),
            vmem((width // 4, hidden), bf16),
            vmem((hidden // 2, width // 4), bf16),
            vmem((width // 2, hidden), bf16),
            vmem((hidden // 2, width // 2), bf16),
            vmem((2, width // 4, hidden), f32),
            vmem((2, hidden // 2, width // 4), f32),
            dma((23,)),
            dma((3,)),
            dma((3,)),
            dma((2, 2)),
            dma((2, 2)),
            dma((2,)),
            dma((2,)),
            dma((2,)),
            dma((2,)),
            dma((3, 5)),
            dma((3, 5)),
            pltpu.SemaphoreType.REGULAR((5,)),
            dma((10,)),
        ],
        compiler_params=pltpu.CompilerParams(
            collective_id=1, has_side_effects=True, vmem_limit_bytes=64 * 2**20
        ),
        cost_estimate=pl.CostEstimate(
            flops=30 * rows * width * width, bytes_accessed=60 * 2**20, transcendentals=0
        ),
    )(*vmem_args, *any_args)


def local_dense(
    tokens,
    segment_ids,
    routes,
    route_gates,
    attn_gain,
    ffn_gain,
    query_weight,
    key_matrix,
    value_matrix,
    output_weight,
    expert_gate,
    expert_up,
    expert_down,
    cotangent,
):
    experts = lax.axis_size("ep")
    table = jnp.sum(
        jnp.where(
            routes.T[None, :, :] == jnp.arange(experts, dtype=jnp.int32)[:, None, None],
            route_gates.T[None, :, :],
            0.0,
        ),
        axis=1,
    )
    position = jnp.arange(tokens.shape[0], dtype=jnp.float32)
    inverse = BASE ** (-jnp.arange(HEAD_SIZE // 2, dtype=jnp.float32) * 2.0 / HEAD_SIZE)
    angle = position[:, None] * inverse[None, :]
    cosine = jnp.cos(angle)
    sine = jnp.sin(angle)
    small = (
        attn_gain[None, :],
        ffn_gain[None, :],
        jnp.concatenate([cosine, cosine], axis=1),
        jnp.concatenate([-sine, sine], axis=1),
        segment_ids,
        segment_ids.T,
    )
    (
        query_rot,
        key_rot,
        value_low,
        log_total,
        attended,
        mixed,
        grad_gu,
        grad_down,
        out_own,
        out_sib,
        *second_parts,
        _,
        _,
    ) = forward_call(
        small + (table,),
        (
            tokens,
            query_weight,
            key_matrix,
            value_matrix,
            output_weight,
            cotangent,
            expert_gate[0],
            expert_up[0],
            expert_down[0],
        ),
    )
    (
        query_grad,
        extra_grad,
        output_grad,
        layer_out,
        tokens_grad,
        gate_grad,
        up_grad,
        down_grad,
        *_,
    ) = backward_call(
        small + (log_total, key_rot, value_low),
        (
            *second_parts,
            mixed,
            cotangent,
            attended,
            query_rot,
            tokens,
            output_weight,
            query_weight,
            key_matrix,
            value_matrix,
            grad_gu,
            grad_down,
            out_own,
            out_sib,
        ),
    )
    split_k = key_matrix.shape[1]
    split_v = split_k + value_matrix.shape[1]
    gain_sums = extra_grad[:, split_v : split_v + 2] + extra_grad[:, split_v + 2 : split_v + 4]
    return (
        layer_out,
        tokens_grad,
        query_grad,
        extra_grad[:, :split_k],
        extra_grad[:, split_k:split_v],
        output_grad.T,
        gain_sums[:, 0],
        gain_sums[:, 1],
        gate_grad[None],
        up_grad[None],
        down_grad[None],
    )


def solution(mesh):
    in_specs = (
        P(("grp", "ep"), None),
        P(("grp", "ep"), None),
        P(("grp", "ep"), None),
        P(("grp", "ep"), None),
        P(),
        P(),
        P(),
        P(),
        P(),
        P(),
        P("ep", None, None),
        P("ep", None, None),
        P("ep", None, None),
        P(("grp", "ep"), None),
    )
    out_specs = (
        P(("grp", "ep"), None),
        P(("grp", "ep"), None),
        P(("grp", "ep"), None),
        P(("grp", "ep"), None),
        P(("grp", "ep"), None),
        P(None, ("grp", "ep")),
        P(("grp", "ep")),
        P(("grp", "ep")),
        P("ep", "grp", None),
        P("ep", "grp", None),
        P("ep", None, "grp"),
    )
    paired = mesh.shape["grp"] == 4 and mesh.shape["ep"] == 8
    local = local_dense if paired else local_routed
    return jax.shard_map(local, mesh=mesh, in_specs=in_specs, out_specs=out_specs, check_vma=False)
```

```python
import jax
import jax.numpy as jnp
from jax import lax
from jax.experimental import pallas as pl
from jax.experimental.pallas import tpu as pltpu
from jax.sharding import PartitionSpec as P

HEAD_SIZE = 128


EPS = 1e-06
BASE = 10000.0


def apply_rotary(value_rows, cosine_table, sine_table):
    half = value_rows.shape[-1] // 2
    first = value_rows[..., :half]
    second = value_rows[..., half:]
    return jnp.concatenate(
        [first * cosine_table - second * sine_table, second * cosine_table + first * sine_table],
        axis=-1,
    )


def unrotate(value_rows, cosine_table, sine_table):
    half = value_rows.shape[-1] // 2
    first = value_rows[..., :half]
    second = value_rows[..., half:]
    return jnp.concatenate(
        [first * cosine_table + second * sine_table, second * cosine_table - first * sine_table],
        axis=-1,
    )


def glu_value(gate_val, up_val):
    return jax.nn.gelu(gate_val, approximate=True) * up_val


def scores_of(query_rot, key_rot, allowed):
    score = jnp.einsum(
        "tkgd,skd->kgts", query_rot, key_rot, preferred_element_type=jnp.float32
    ) * HEAD_SIZE ** (-0.5)
    return jnp.where(allowed, score, -1e30)


def local_routed(
    tokens,
    segment_ids,
    routes,
    route_gates,
    attn_gain,
    ffn_gain,
    query_weight,
    key_matrix,
    value_matrix,
    output_weight,
    expert_gate,
    expert_up,
    expert_down,
    cotangent,
):
    length_total, width = tokens.shape
    choose = routes.shape[1]
    local_experts = expert_gate.shape[0]
    owners = lax.axis_size("ep")
    experts = owners * local_experts
    capacity = 3 * length_total * choose // (2 * experts)
    query_heads = query_weight.shape[1] // HEAD_SIZE
    key_heads = key_matrix.shape[1] // HEAD_SIZE
    q_per_kv = query_heads // key_heads
    segment = segment_ids[0]
    padding = segment == jnp.max(segment)
    later = jnp.arange(length_total)[:, None] >= jnp.arange(length_total)[None, :]
    diagonal = jnp.arange(length_total)[:, None] == jnp.arange(length_total)[None, :]
    allowed = (
        later
        & (segment[:, None] == segment[None, :])
        & (jnp.logical_not(padding)[None, :] | diagonal)
    )
    position = jnp.arange(length_total, dtype=jnp.float32)
    inverse = BASE ** (-jnp.arange(HEAD_SIZE // 2, dtype=jnp.float32) * 2.0 / HEAD_SIZE)
    angle = position[:, None] * inverse[None, :]
    cosine_table = jnp.cos(angle)[:, None, :]
    sine_table = jnp.sin(angle)[:, None, :]
    tok_float = tokens.astype(jnp.float32)
    scale_first = lax.rsqrt(jnp.mean(tok_float * tok_float, axis=-1, keepdims=True) + EPS)
    normed_first = tok_float * scale_first
    h_first = (normed_first * attn_gain).astype(jnp.bfloat16)
    query_rows = jnp.dot(h_first, query_weight, preferred_element_type=jnp.float32).reshape(
        length_total, query_heads, HEAD_SIZE
    )
    key_rows = jnp.dot(h_first, key_matrix, preferred_element_type=jnp.float32).reshape(
        length_total, key_heads, HEAD_SIZE
    )
    value_low = jnp.dot(h_first, value_matrix, preferred_element_type=jnp.float32).astype(
        jnp.bfloat16
    )
    value_low = value_low.reshape(length_total, key_heads, HEAD_SIZE)
    query_rot = (
        apply_rotary(query_rows, cosine_table, sine_table)
        .astype(jnp.bfloat16)
        .reshape(length_total, key_heads, q_per_kv, HEAD_SIZE)
    )
    key_rot = apply_rotary(key_rows, cosine_table, sine_table).astype(jnp.bfloat16)
    score = scores_of(query_rot, key_rot, allowed)
    row_max = jnp.max(score, axis=-1, keepdims=True)
    expo = jnp.exp(score - row_max)
    row_sum = jnp.sum(expo, axis=-1, keepdims=True)
    log_total = row_max + jnp.log(row_sum)
    probs_low = (expo / row_sum).astype(jnp.bfloat16)
    attended = jnp.einsum(
        "kgts,skd->tkgd", probs_low, value_low, preferred_element_type=jnp.float32
    )
    attended = attended.reshape(length_total, query_heads * HEAD_SIZE).astype(jnp.bfloat16)
    mixed = tok_float + jnp.dot(attended, output_weight, preferred_element_type=jnp.float32)
    scale_second = lax.rsqrt(jnp.mean(mixed * mixed, axis=-1, keepdims=True) + EPS)
    normed_second = mixed * scale_second
    h_second = (normed_second * ffn_gain).astype(jnp.bfloat16)
    flat_routes = routes.reshape(-1)
    assigns = flat_routes.shape[0]
    onehot = (flat_routes[:, None] == jnp.arange(experts, dtype=jnp.int32)[None, :]).astype(
        jnp.int32
    )
    position_in = jnp.sum(jnp.cumsum(onehot, axis=0) * onehot, axis=1) - 1
    slot_index = flat_routes * capacity + position_in
    source = (
        jnp.full((experts * capacity,), assigns, jnp.int32)
        .at[slot_index]
        .set(jnp.arange(assigns, dtype=jnp.int32))
    )
    token_of = source // choose
    h_ext = jnp.concatenate([h_second, jnp.zeros((1, width), jnp.bfloat16)], axis=0)
    send_rows = h_ext[token_of].reshape(owners, local_experts, capacity, width)
    row_entries = lax.all_to_all(send_rows, "ep", split_axis=0, concat_axis=0, tiled=True)
    gate_val = jnp.einsum(
        "secd,edf->secf", row_entries, expert_gate, preferred_element_type=jnp.float32
    )
    up_val = jnp.einsum(
        "secd,edf->secf", row_entries, expert_up, preferred_element_type=jnp.float32
    )
    act = glu_value(gate_val, up_val).astype(jnp.bfloat16)
    result = jnp.einsum("secf,efd->secd", act, expert_down, preferred_element_type=jnp.float32)
    outputs = (result.astype(jnp.bfloat16), row_entries, gate_val, up_val)
    returned = lax.all_to_all(outputs[0], "ep", split_axis=0, concat_axis=0, tiled=True).reshape(
        experts * capacity, width
    )
    picked = returned[slot_index].reshape(length_total, choose, width).astype(jnp.float32)
    layer_out = (mixed + jnp.sum(route_gates[:, :, None] * picked, axis=1)).astype(jnp.bfloat16)
    grad_out = cotangent.astype(jnp.float32)
    slot_grads = (
        (route_gates[:, :, None] * grad_out[:, None, :])
        .astype(jnp.bfloat16)
        .reshape(assigns, width)
    )
    slot_ext = jnp.concatenate([slot_grads, jnp.zeros((1, width), jnp.bfloat16)], axis=0)
    grad_send = slot_ext[source].reshape(owners, local_experts, capacity, width)
    grad_recv = lax.all_to_all(grad_send, "ep", split_axis=0, concat_axis=0, tiled=True)
    recv_rows = outputs[1]
    gate_val = outputs[2]
    up_val = outputs[3]
    act, act_back = jax.vjp(glu_value, gate_val, up_val)
    act_low = act.astype(jnp.bfloat16)
    down_part = jnp.einsum("secf,secd->efd", act_low, grad_recv, preferred_element_type=jnp.float32)
    act_grad = jnp.einsum(
        "secd,efd->secf", grad_recv, expert_down, preferred_element_type=jnp.float32
    )
    gate_grad_val, up_grad_val = act_back(act_grad)
    gate_low = gate_grad_val.astype(jnp.bfloat16)
    up_low = up_grad_val.astype(jnp.bfloat16)
    gate_part = jnp.einsum(
        "secd,secf->edf", recv_rows, gate_low, preferred_element_type=jnp.float32
    )
    up_part = jnp.einsum("secd,secf->edf", recv_rows, up_low, preferred_element_type=jnp.float32)
    rows_grad = jnp.einsum(
        "secf,edf->secd", gate_low, expert_gate, preferred_element_type=jnp.float32
    )
    rows_grad = rows_grad + jnp.einsum(
        "secf,edf->secd", up_low, expert_up, preferred_element_type=jnp.float32
    )
    rows_back = lax.all_to_all(
        rows_grad.astype(jnp.bfloat16), "ep", split_axis=0, concat_axis=0, tiled=True
    )
    rows_back = rows_back.reshape(experts * capacity, width)
    expert_sums = (
        lax.psum_scatter(
            gate_part.astype(jnp.bfloat16), "grp", scatter_dimension=1, tiled=True
        ).astype(jnp.float32),
        lax.psum_scatter(
            up_part.astype(jnp.bfloat16), "grp", scatter_dimension=1, tiled=True
        ).astype(jnp.float32),
        lax.psum_scatter(
            down_part.astype(jnp.bfloat16), "grp", scatter_dimension=2, tiled=True
        ).astype(jnp.float32),
    )
    second_grad = jnp.sum(
        rows_back[slot_index].reshape(length_total, choose, width).astype(jnp.float32), axis=1
    )
    ffn_gain_part = jnp.sum(second_grad * normed_second, axis=0)
    normed_grad = second_grad * ffn_gain
    mixed_grad = grad_out + scale_second * (
        normed_grad - normed_second * jnp.mean(normed_grad * normed_second, axis=-1, keepdims=True)
    )
    mixed_low = mixed_grad.astype(jnp.bfloat16)
    output_part = jnp.einsum("ti,td->id", attended, mixed_low, preferred_element_type=jnp.float32)
    attended_grad = jnp.einsum(
        "td,id->ti", mixed_low, output_weight, preferred_element_type=jnp.float32
    )
    attended_grad = attended_grad.astype(jnp.bfloat16).reshape(
        length_total, key_heads, q_per_kv, HEAD_SIZE
    )
    probs = jnp.exp(scores_of(query_rot, key_rot, allowed) - log_total)
    probs_again = probs.astype(jnp.bfloat16)
    value_part_grad = jnp.einsum(
        "kgts,tkgd->skd", probs_again, attended_grad, preferred_element_type=jnp.float32
    )
    prob_grad = jnp.einsum(
        "tkgd,skd->kgts", attended_grad, value_low, preferred_element_type=jnp.float32
    )
    inner = jnp.sum(probs * prob_grad, axis=-1, keepdims=True)
    score_grad = (probs * (prob_grad - inner)).astype(jnp.bfloat16)
    qrot_grad = jnp.einsum(
        "kgts,skd->tkgd", score_grad, key_rot, preferred_element_type=jnp.float32
    ) * HEAD_SIZE ** (-0.5)
    krot_grad = jnp.einsum(
        "kgts,tkgd->skd", score_grad, query_rot, preferred_element_type=jnp.float32
    ) * HEAD_SIZE ** (-0.5)
    query_grad_low = unrotate(
        qrot_grad.reshape(length_total, query_heads, HEAD_SIZE), cosine_table, sine_table
    )
    query_grad_low = query_grad_low.astype(jnp.bfloat16).reshape(
        length_total, query_heads * HEAD_SIZE
    )
    key_grad_low = (
        unrotate(krot_grad, cosine_table, sine_table)
        .astype(jnp.bfloat16)
        .reshape(length_total, key_heads * HEAD_SIZE)
    )
    value_grad_low = value_part_grad.astype(jnp.bfloat16).reshape(
        length_total, key_heads * HEAD_SIZE
    )
    query_part = jnp.einsum(
        "td,ti->di", h_first, query_grad_low, preferred_element_type=jnp.float32
    )
    key_part = jnp.einsum("td,ti->di", h_first, key_grad_low, preferred_element_type=jnp.float32)
    value_part = jnp.einsum(
        "td,ti->di", h_first, value_grad_low, preferred_element_type=jnp.float32
    )
    first_grad = jnp.einsum(
        "ti,di->td", query_grad_low, query_weight, preferred_element_type=jnp.float32
    )
    first_grad = first_grad + jnp.einsum(
        "ti,di->td", key_grad_low, key_matrix, preferred_element_type=jnp.float32
    )
    first_grad = first_grad + jnp.einsum(
        "ti,di->td", value_grad_low, value_matrix, preferred_element_type=jnp.float32
    )
    attn_gain_part = jnp.sum(first_grad * normed_first, axis=0)
    normed_first_grad = first_grad * attn_gain
    tokens_grad = mixed_grad + scale_first * (
        normed_first_grad
        - normed_first * jnp.mean(normed_first_grad * normed_first, axis=-1, keepdims=True)
    )
    shared = (
        lax.psum_scatter(query_part, ("grp", "ep"), scatter_dimension=0, tiled=True),
        lax.psum_scatter(key_part, ("grp", "ep"), scatter_dimension=0, tiled=True),
        lax.psum_scatter(value_part, ("grp", "ep"), scatter_dimension=0, tiled=True),
        lax.psum_scatter(output_part, ("grp", "ep"), scatter_dimension=1, tiled=True),
        lax.psum_scatter(attn_gain_part, ("grp", "ep"), scatter_dimension=0, tiled=True),
        lax.psum_scatter(ffn_gain_part, ("grp", "ep"), scatter_dimension=0, tiled=True),
    )
    return (
        layer_out,
        tokens_grad,
        shared[0],
        shared[1],
        shared[2],
        shared[3],
        shared[4],
        shared[5],
        expert_sums[0],
        expert_sums[1],
        expert_sums[2],
    )


def forward_kernel(
    attn_gain_ref, ffn_gain_ref, cos_ref, sin_ref, seg_row_ref, seg_col_ref, tab_ref, tok_ref,
    wq_ref, wk_ref, wv_ref, wo_ref, dy_ref, gate_ref, up_ref, down_ref,
    query_ref, key_ref, value_ref, lse_ref, att_ref, mixed_ref, grad_gu_ref, grad_down_ref,
    out_own_ref, out_sib_ref, d_own_ref, d_sib_ref, d_first_ref, d_second_ref, part_d_ref,
    part_o_ref, ex_gu_ref, ex_down_ref,
    xb, dyb, tab, w_gu, w_down, sib, far_in, gather_send, gather_recv, tab_send, tab_recv,
    fetch_send, fetch_recv, pass_send, pass_recv, local_sem, part_send, part_recv, keep_sem,
    sum_send, sum_recv, ex_send, ex_recv, store_sem, stage_sem,
):
    f32, bf16 = jnp.float32, jnp.bfloat16
    grp, ep = lax.axis_index("grp"), lax.axis_index("ep")
    core = lax.rem(grp, 2)
    side = grp // 2
    low = lax.rem(ep, 4)
    y, z = lax.rem(low, 2), low // 2
    by_y = ep + 1 - 2 * y
    by_z = ep + 2 - 4 * z
    by_both = by_y + 2 - 4 * z
    by_far = ep + 4 - 8 * (ep // 4)
    first = by_y * (1 - core) + by_z * core
    second = by_z * (1 - core) + by_y * core
    other = grp + 1 - 2 * core
    across = (grp + 2 - 4 * side, ep)
    away = (grp, by_far)
    rows, width = tok_ref.shape
    half = rows // 2
    hidden = gate_ref.shape[1]
    mine = hidden // 2
    head = cos_ref.shape[1]
    heads = width // head
    key_width = wk_ref.shape[1]
    per_key = heads * head // key_width

    def remote(src, dst, send, recv, device):
        return pltpu.make_async_remote_copy(
            src_ref=src, dst_ref=dst, send_sem=send, recv_sem=recv, device_id=device,
            device_id_type=pl.DeviceIdType.MESH,
        )

    members = (
        ((grp, first), 1), ((grp, second), 2), ((grp, by_both), 3), ((other, ep), 4),
        ((other, first), 5), ((other, second), 6), ((other, by_both), 7),
    )
    barrier = pltpu.get_barrier_semaphore()
    for device in [device for device, _ in members] + [across, away]:
        pl.semaphore_signal(barrier, inc=1, device_id=device, device_id_type=pl.DeviceIdType.MESH)
    pl.semaphore_wait(barrier, 9)

    units = pl.ds(pl.multiple_of(core * mine, mine), mine)
    own_weights = (
        (gate_ref.at[:, units], w_gu.at[0, :, pl.ds(0, mine)]),
        (up_ref.at[:, units], w_gu.at[0, :, pl.ds(mine, mine)]),
        (down_ref.at[units, :], w_down.at[0]),
    )
    wide_at = pl.ds(pl.multiple_of(side * (width // 2), width // 2), width // 2)
    deep_at = pl.ds(pl.multiple_of(side * (mine // 2), mine // 2), mine // 2)
    deep_from = pl.ds(pl.multiple_of(core * mine + side * (mine // 2), mine // 2), mine // 2)
    pieces = (
        (gate_ref.at[wide_at, units], w_gu.at[1, wide_at, pl.ds(0, mine)]),
        (up_ref.at[wide_at, units], w_gu.at[1, wide_at, pl.ds(mine, mine)]),
        (down_ref.at[deep_from, :], w_down.at[1, deep_at, :]),
    )

    def fetch_copy(m):
        return remote(*pieces[m], fetch_send.at[m], fetch_recv.at[m], away)

    def pass_copy(m):
        return remote(pieces[m][1], pieces[m][1], pass_send.at[m], pass_recv.at[m], across)

    def load(number, src, dst):
        return pltpu.make_async_copy(src, dst, local_sem.at[number])

    def gather_copy(k, number):
        own, buf = ((xb.at[0], xb), (dy_ref, dyb))[k]
        src, dst, device = (
            (own, 1, (grp, first)), (own, 4, (other, ep)), (own, 2, (grp, second)),
            (buf.at[1], 5, (other, ep)), (buf.at[2], 6, (other, ep)),
            (buf.at[2], 3, (grp, first)), (buf.at[3], 7, (other, ep)),
        )[number]
        if k == 1 and number == 5:
            src, device = buf.at[2 - core], (grp, by_y)
        return remote(
            src, buf.at[dst], gather_send.at[k, number], gather_recv.at[k, number], device
        )

    arrival = {1: 0, 4: 1, 2: 2, 5: 3, 6: 4, 3: 5, 7: 6}

    def start(k, *numbers):
        for number in numbers:
            gather_copy(k, number).start()

    def arrived(k, slot):
        gather_copy(k, arrival[slot]).wait_recv()

    def table_copy(slot):
        device = members[slot - 1][0]
        return remote(tab_ref, tab.at[slot], tab_send.at[slot], tab_recv.at[slot], device)

    fetch_copy(0).start()
    start(1, 0, 1, 2)
    for slot in range(1, 8):
        table_copy(slot).start()
    own_dy = lambda: load(0, dy_ref, dyb.at[0])
    tab[0] = tab_ref[...]

    def dot_nt(a, b):
        return lax.dot_general(a, b, (((1,), (1,)), ((), ())), preferred_element_type=f32)

    def dot_tn(a, b):
        return lax.dot_general(a, b, (((0,), (0,)), ((), ())), preferred_element_type=f32)

    def attention(w_big, w_key, w_value, tok, act, query, key, value, bias, mixed, lse):
        tok_load = load(4, tok_ref, tok)
        query_load = load(5, wq_ref, w_big)
        key_load = load(6, wk_ref, w_key)
        value_load = load(7, wv_ref, w_value)
        for copy in (tok_load, query_load, key_load, value_load):
            copy.start()
        own_dy().start()
        for m, (src, dst) in enumerate(own_weights):
            load(1 + m, src, dst).start()
        position = lax.broadcasted_iota(jnp.int32, (rows, rows), 0)
        other_position = lax.broadcasted_iota(jnp.int32, (rows, rows), 1)
        padding = seg_row_ref[...] == jnp.max(seg_row_ref[...])
        allowed = (
            (other_position <= position)
            & (seg_col_ref[...] == seg_row_ref[...])
            & (jnp.logical_not(padding) | (other_position == position))
        )
        bias[...] = jnp.where(allowed, 0.0, -1e30)
        lse[...] = jnp.zeros_like(lse)
        tok_load.wait()

        @pl.loop(0, rows // 128)
        def _(step):
            at = pl.ds(pl.multiple_of(step * 128, 128), 128)
            entry = tok[at, :].astype(f32)
            factor = lax.rsqrt(jnp.mean(entry * entry, axis=-1, keepdims=True) + EPS)
            act[at, :] = (entry * factor * attn_gain_ref[...]).astype(bf16)

        def turn(entry, at):
            swapped = pltpu.roll(entry, head // 2, 1)
            return entry * cos_ref[at, :] + swapped * sin_ref[at, :]

        key_load.wait()
        value_load.wait()
        key_rows = jnp.dot(act[...], w_key[...], preferred_element_type=f32)
        for kv in range(key_width // head):
            columns = slice(kv * head, (kv + 1) * head)
            key[:, columns] = turn(key_rows[:, columns], slice(None)).astype(bf16)
        value[...] = jnp.dot(act[...], w_value[...], preferred_element_type=f32).astype(bf16)
        query_load.wait()
        for tile in range(width // 256):
            columns = slice(tile * 256, (tile + 1) * 256)
            entry = jnp.dot(act[...], w_big[:, columns], preferred_element_type=f32)
            for part in range(256 // head):
                columns = slice(part * head, (part + 1) * head)
                to = slice(tile * 256 + part * head, tile * 256 + (part + 1) * head)
                query[:, to] = turn(entry[:, columns], slice(None)).astype(bf16)
        out_load = load(8, wo_ref, w_big)
        out_load.start()
        stores = [
            pltpu.make_async_copy(src, dst, store_sem.at[i])
            for i, (src, dst) in enumerate(((query, query_ref), (key, key_ref), (value, value_ref)))
        ]
        for copy in stores:
            copy.start()
        scale = head ** (-0.5)
        lane = lax.broadcasted_iota(jnp.int32, (half, head), 1)
        for number in range(heads):
            columns = slice(number * head, (number + 1) * head)
            kv = number // per_key
            kv_columns = slice(kv * head, (kv + 1) * head)
            for part in range(2):
                at = slice(part * half, (part + 1) * half)
                seen = slice(0, (part + 1) * half)
                score = dot_nt(query[at, columns], key[seen, kv_columns]) * scale + bias[at, seen]
                top = jnp.max(score, axis=-1, keepdims=True)
                expo = jnp.exp(score - top)
                total = jnp.sum(expo, axis=-1, keepdims=True)
                lse[at, :] = jnp.where(lane == number, top + jnp.log(total), lse[at, :])
                probs = (expo / total).astype(bf16)
                mixed_value = jnp.dot(probs, value[seen, kv_columns], preferred_element_type=f32)
                act[at, columns] = mixed_value.astype(bf16)
        fetch_copy(1).start()
        out_load.wait()
        att_store = pltpu.make_async_copy(act, att_ref, store_sem.at[3])
        att_store.start()
        lse_store = pltpu.make_async_copy(lse, lse_ref, store_sem.at[4])
        lse_store.start()
        for part in range(4):
            at = slice(part * rows // 4, (part + 1) * rows // 4)
            total = tok[at, :].astype(f32) + jnp.dot(
                act[at, :], w_big[...], preferred_element_type=f32
            )
            mixed[at, :] = total
            factor = lax.rsqrt(jnp.mean(total * total, axis=-1, keepdims=True) + EPS)
            xb[0, at, :] = (total * factor * ffn_gain_ref[...]).astype(bf16)
        start(0, 0, 1, 2)
        mixed_store = pltpu.make_async_copy(mixed, mixed_ref, store_sem.at[5])
        mixed_store.start()
        for copy in stores + [att_store, lse_store, mixed_store]:
            copy.wait()

    vmem = pltpu.VMEM
    pl.run_scoped(
        attention,
        vmem((width, width), bf16),
        vmem((width, key_width), bf16),
        vmem((width, key_width), bf16),
        vmem((rows, width), bf16),
        vmem((rows, width), bf16),
        vmem((rows, width), bf16),
        vmem((rows, key_width), bf16),
        vmem((rows, key_width), bf16),
        vmem((rows, rows), f32),
        vmem((rows, width), f32),
        vmem((rows, head), f32),
    )

    def experts(acc_gu, acc_down, act_s, gu_s, dz_s, stage):
        own_dy().wait()
        for m, (src, dst) in enumerate(own_weights):
            load(1 + m, src, dst).wait()
        for slot in range(1, 8):
            table_copy(slot).wait_send()
            table_copy(slot).wait_recv()
        acc_gu[...] = jnp.zeros_like(acc_gu)
        acc_down[...] = jnp.zeros_like(acc_down)

        def gates(slot, hosted):
            block = jnp.transpose(tab[slot])
            lane = lax.broadcasted_iota(jnp.int32, block.shape, 1)
            return jnp.sum(jnp.where(lane == hosted, block, 0.0), axis=1, keepdims=True)

        c0 = 0.7978845608028654
        c1 = 0.044715

        def work(which, slot, hosted, deliver):
            column = gates(slot, hosted)
            for part in range(2):
                at = pl.ds(part * half, half)
                gate = column[part * half : (part + 1) * half]
                gu = jnp.dot(xb[slot, at, :], w_gu[which], preferred_element_type=f32)
                dz = (gate * dyb[slot, at, :].astype(f32)).astype(bf16)
                dz_s[at, :] = dz
                da = dot_nt(dz, w_down[which])
                g, u = gu[:, :mine], gu[:, mine:]
                square = g * g
                t = jnp.tanh(c0 * (g + c1 * square * g))
                gelu = 0.5 * g * (1.0 + t)
                slope = 0.5 * (1.0 + t) + 0.5 * g * (1.0 - t * t) * (c0 * (1.0 + 3.0 * c1 * square))
                act_s[at, :] = (gelu * u).astype(bf16)
                gu_s[at, :mine] = (da * u * slope).astype(bf16)
                gu_s[at, mine:] = (da * gelu).astype(bf16)
            for part in range(3):
                at = pl.ds(part * (width // 3), width // 3)
                acc_gu[which, at, :] += dot_tn(xb[slot, :, at], gu_s[...])
                acc_down[which, :, at] += dot_tn(act_s[...], dz_s[:, at])
            for part in range(2):
                at = pl.ds(part * half, half)
                gate = column[part * half : (part + 1) * half]
                dx = dot_nt(gu_s[at, :], w_gu[which])
                result = gate * jnp.dot(act_s[at, :], w_down[which], preferred_element_type=f32)
                deliver(at, dx, result)

        def slot_up(step):
            pair, odd = step // 2, lax.rem(step, 2)
            middle = (lax.rem(pair, 2) * (1 - pair // 3) + pair // 2 * (1 - pair // 3))
            turned = core * (1 - odd) + (1 - core) * odd
            swapped = middle * (3 - 2 * pair) * turned
            return pair + swapped + 4 * odd

        def stage_out(k, step):
            buf = lax.rem(step, 2)
            dst = (part_d_ref, part_o_ref)[k].at[slot_up(step)]
            return pltpu.make_async_copy(stage.at[k, buf], dst, stage_sem.at[k, buf])

        @pl.loop(0, 8)
        def _(step):
            def at_step(number):
                return pl.when(step == number)

            @at_step(1)
            def _():
                arrived(0, 4)
                arrived(1, 4)

            @at_step(2)
            def _():
                arrived(1, 1)
                start(1, 3)
                arrived(1, 2)
                start(1, 5, 4)
                fetch_copy(0).wait_recv()
                pass_copy(0).start()
                fetch_copy(2).start()
                @pl.when(core == 0)
                def _():
                    arrived(0, 1)
                    start(0, 3)

                @pl.when(core == 1)
                def _():
                    arrived(0, 2)
                    start(0, 5, 4)


            @at_step(3)
            def _():
                @pl.when(core == 0)
                def _():
                    arrived(0, 6)
                    arrived(1, 6)

                @pl.when(core == 1)
                def _():
                    arrived(0, 5)
                    arrived(1, 5)


            @at_step(4)
            def _():
                @pl.when(core == 0)
                def _():
                    arrived(0, 2)
                    start(0, 5, 4)

                @pl.when(core == 1)
                def _():
                    arrived(0, 1)
                    start(0, 3)

                fetch_copy(1).wait_recv()
                pass_copy(1).start()

            @at_step(5)
            def _():
                @pl.when(core == 0)
                def _():
                    arrived(0, 5)
                    arrived(1, 5)

                @pl.when(core == 1)
                def _():
                    arrived(0, 6)
                    arrived(1, 6)

                arrived(1, 3)
                start(1, 6)

            @at_step(6)
            def _():
                arrived(0, 3)
                start(0, 6)
                fetch_copy(2).wait_recv()
                pass_copy(2).start()

            @at_step(7)
            def _():
                arrived(0, 7)
                arrived(1, 7)

            @pl.when(step >= 2)
            def _():
                stage_out(0, step - 2).wait()
                stage_out(1, step - 2).wait()

            buf = lax.rem(step, 2)

            def deliver(at, dx, result):
                stage[0, buf, at, :] = dx.astype(bf16)
                stage[1, buf, at, :] = result.astype(bf16)

            work(0, slot_up(step), ep, deliver)
            stage_out(0, step).start()
            stage_out(1, step).start()

        for k in range(2):
            for step in (6, 7):
                stage_out(k, step).wait()
        for k in range(2):
            for number in range(7):
                gather_copy(k, number).wait_send()

        def grad_copies(which):
            return (
                pltpu.make_async_copy(w_gu.at[which], grad_gu_ref.at[which], store_sem.at[6 + 2 * which]),
                pltpu.make_async_copy(
                    w_down.at[which], grad_down_ref.at[which], store_sem.at[7 + 2 * which]
                ),
            )

        def slot_down(step):
            pair = step // 2
            return 3 - 2 * lax.rem(pair, 2) - pair // 2 + 4 * (1 - lax.rem(step, 2))

        def stage_in(k, step):
            buf = lax.rem(step, 2)
            src = (part_d_ref, part_o_ref)[k].at[slot_down(step)]
            return pltpu.make_async_copy(src, stage.at[k, buf], stage_sem.at[k, buf])

        stage_in(0, 0).start()
        stage_in(1, 0).start()
        def flush(which):
            w_gu[which] = acc_gu[which].astype(bf16)
            w_down[which] = acc_down[which].astype(bf16)
            for copy in grad_copies(which):
                copy.start()

        def exchange(m):
            at = pl.ds(pl.multiple_of((1 - side) * (width // 2), width // 2), width // 2)
            src = w_down.at[0, :, at] if m else w_gu.at[0, at, :]
            return remote(src, (ex_gu_ref, ex_down_ref)[m], ex_send.at[m], ex_recv.at[m], across)

        for m in range(3):
            pass_copy(m).wait()
            fetch_copy(m).wait_send()

        def keep_copy(j):
            return pltpu.make_async_copy(dyb.at[j], out_own_ref.at[j], keep_sem.at[j])

        def grad_part(j):
            dst = d_sib_ref if j == 0 else sib.at[j - 1]
            return remote(xb.at[4 + j], dst, part_send.at[0, j], part_recv.at[0, j], (other, ep))

        def out_part(j):
            return remote(
                dyb.at[4 + j], out_sib_ref.at[j], part_send.at[1, j], part_recv.at[1, j], (other, ep)
            )

        own_grad = lambda: pltpu.make_async_copy(xb.at[0], d_own_ref, keep_sem.at[4])
        send_far = lambda: remote(xb.at[3], far_in, sum_send.at[0], sum_recv.at[0], (grp, first))
        send_first = lambda: remote(
            xb.at[1], d_first_ref, sum_send.at[1], sum_recv.at[1], (grp, first)
        )
        send_second = lambda: remote(
            xb.at[2], d_second_ref, sum_send.at[2], sum_recv.at[2], (grp, second)
        )

        def add_into(dst, *others):
            @pl.loop(0, rows // 128)
            def _(i):
                at = pl.ds(pl.multiple_of(i * 128, 128), 128)
                total = dst[at, :].astype(f32)
                for part in others:
                    total = total + part[at, :].astype(f32)
                dst[at, :] = total.astype(bf16)

        @pl.loop(0, 8)
        def _(step):
            def at_step(number):
                return pl.when(step == number)

            stage_in(0, step).wait()
            stage_in(1, step).wait()

            @pl.when(step < 7)
            def _():
                stage_in(0, step + 1).start()
                stage_in(1, step + 1).start()

            buf = lax.rem(step, 2)
            slot = slot_down(step)

            def deliver(at, dx, result):
                xb[slot, at, :] = (dx + stage[0, buf, at, :].astype(f32)).astype(bf16)
                dyb[slot, at, :] = (result + stage[1, buf, at, :].astype(f32)).astype(bf16)

            work(1, slot, ep + 4 - 8 * (ep // 4), deliver)
            for number, j in enumerate((3, 1, 2, 0)):

                @at_step(2 * number)
                def _(j=j):
                    grad_part(j).start()
                    out_part(j).start()

                @at_step(2 * number + 1)
                def _(j=j):
                    keep_copy(j).start()

            @at_step(1)
            def _():
                grad_part(3).wait_recv()
                add_into(xb.at[3], sib.at[2])
                send_far().start()
                flush(0)
                for m in range(2):
                    exchange(m).start()

            @at_step(3)
            def _():
                grad_part(1).wait_recv()
                add_into(xb.at[1], sib.at[0])
                send_first().start()

            @at_step(5)
            def _():
                grad_part(2).wait_recv()
                send_far().wait_recv()
                add_into(xb.at[2], sib.at[1], far_in)
                send_second().start()

        own_grad().start()
        flush(1)
        for j in range(4):
            grad_part(j).wait_send()
            out_part(j).wait()
            keep_copy(j).wait()
        grad_part(0).wait_recv()
        own_grad().wait()
        send_far().wait_send()
        send_first().wait()
        send_second().wait()
        for which in range(2):
            for copy in grad_copies(which):
                copy.wait()
            exchange(which).wait()

    pl.run_scoped(
        experts,
        vmem((2, width, hidden), f32),
        vmem((2, mine, width), f32),
        vmem((rows, mine), bf16),
        vmem((rows, hidden), bf16),
        vmem((rows, width), bf16),
        vmem((2, 2, rows, width), bf16),
    )


def forward_call(vmem_args, any_args):
    f32, bf16 = jnp.float32, jnp.bfloat16
    rows, width = any_args[0].shape
    head = vmem_args[2].shape[1]
    key_width = any_args[2].shape[1]
    hidden = any_args[6].shape[1]
    anywhere = pl.BlockSpec(memory_space=pl.ANY)
    inside = pl.BlockSpec(memory_space=pltpu.VMEM)
    shape = jax.ShapeDtypeStruct
    dma = pltpu.SemaphoreType.DMA
    vmem = pltpu.VMEM
    chunk = shape((rows, width), bf16)
    four = shape((4, rows, width), bf16)
    eight = shape((8, rows, width), bf16)
    return pl.pallas_call(
        forward_kernel,
        out_shape=(
            chunk,
            shape((rows, key_width), bf16),
            shape((rows, key_width), bf16),
            shape((rows, head), f32),
            chunk,
            shape((rows, width), f32),
            shape((2, width, hidden), bf16),
            shape((2, hidden // 2, width), bf16),
            four,
            four,
            chunk,
            chunk,
            chunk,
            chunk,
            eight,
            eight,
            shape((width // 2, hidden), bf16),
            shape((hidden // 2, width // 2), bf16),
        ),
        in_specs=[inside] * len(vmem_args) + [anywhere] * len(any_args),
        out_specs=(anywhere,) * 18,
        scratch_shapes=[
            vmem((8, rows, width), bf16),
            vmem((8, rows, width), bf16),
            vmem((8,) + vmem_args[6].shape, f32),
            vmem((2, width, hidden), bf16),
            vmem((2, hidden // 2, width), bf16),
            vmem((3, rows, width), bf16),
            vmem((rows, width), bf16),
            dma((2, 7)),
            dma((2, 7)),
            dma((8,)),
            dma((8,)),
            dma((3,)),
            dma((3,)),
            dma((3,)),
            dma((3,)),
            dma((9,)),
            dma((2, 4)),
            dma((2, 4)),
            dma((5,)),
            dma((3,)),
            dma((3,)),
            dma((2,)),
            dma((2,)),
            dma((10,)),
            dma((2, 2)),
        ],
        compiler_params=pltpu.CompilerParams(
            collective_id=0, has_side_effects=True, vmem_limit_bytes=64 * 2**20
        ),
        cost_estimate=pl.CostEstimate(
            flops=160 * rows * width * hidden, bytes_accessed=60 * 2**20, transcendentals=0
        ),
    )(*vmem_args, *any_args)


def backward_kernel(
    attn_gain_ref, ffn_gain_ref, cos_ref, sin_ref, seg_row_ref, seg_col_ref, lse_ref, key_ref,
    value_ref, second0_ref, second1_ref, second2_ref, second3_ref, mixed_ref, cot_ref, att_ref,
    query_ref, tok_ref, wo_ref, wq_ref, wk_ref, wv_ref, ggu_ref, gd_ref, own_ref, sibling_ref,
    first_gu_ref, first_down_ref,
    query_out, kv_out, out_out, layer_ref, tokens_ref, gate_out, up_out, down_out, ra_ref, rb_ref, rf_ref,
    pool, w_big, w_key, w_value, grad, proj, bias, key_acc, value_acc, gain_acc,
    out_buf, out_land, query_buf, query_land, kv_buf, kv_land,
    ex_gu, ex_down, ef_gu, ef_down, ec_gu, ec_down, kept_gu, kept_down, stage, stage_down, load_sem, out_send, out_recv, ex_send, ex_recv, ef_send, ef_recv, ec_send, ec_recv,
    halve_send, halve_recv, free_sem, store_sem,
):
    f32, bf16 = jnp.float32, jnp.bfloat16
    grp, ep = lax.axis_index("grp"), lax.axis_index("ep")
    core = lax.rem(grp, 2)
    x = grp // 2
    y = lax.rem(ep, 2)
    z_low = lax.rem(ep // 2, 2)
    z_high = ep // 4
    by_y = (grp, ep + 1 - 2 * y)
    by_z = (grp, ep + 2 - 4 * z_low)
    by_far = (grp, ep + 4 - 8 * z_high)
    by_core = (grp + 1 - 2 * core, ep)
    by_x = (grp + 2 - 4 * x, ep)
    first = (grp, by_y[1] * (1 - core) + by_z[1] * core)
    second = (grp, by_z[1] * (1 - core) + by_y[1] * core)
    rows, width = grad.shape
    head = cos_ref.shape[1]
    heads = width // head
    key_width = key_ref.shape[1]
    per_key = heads * head // key_width
    block = width // 32

    def remote(src, dst, send, recv, device):
        return pltpu.make_async_remote_copy(
            src_ref=src, dst_ref=dst, send_sem=send, recv_sem=recv, device_id=device,
            device_id_type=pl.DeviceIdType.MESH,
        )

    partners = (by_core, by_y, by_z, by_x, by_far)
    barrier = pltpu.get_barrier_semaphore()
    for device in partners:
        pl.semaphore_signal(barrier, inc=1, device_id=device, device_id_type=pl.DeviceIdType.MESH)
    pl.semaphore_wait(barrier, 5)

    wide_half = width // 2
    quarter = width // 4
    mine = gd_ref.shape[1]
    ex_dst = (ex_gu, ex_down)

    def part(ref, m, index, size):
        at = pl.ds(pl.multiple_of(index * size, size), size)
        return ref.at[:, at] if m == 1 else ref.at[at, :]

    def piece(i):
        at = pl.ds(i * quarter, quarter)
        if i == 2:
            return part(gd_ref.at[1], 1, 1 - x, wide_half), ex_down.at[1], ef_down
        start = pl.multiple_of((1 - x) * wide_half + i * quarter, quarter)
        return ggu_ref.at[1, pl.ds(start, quarter), :], ex_gu.at[1, at, :], ef_gu.at[at, :]

    def ex_copy(i):
        src, dst, _ = piece(i)
        return remote(src, dst, ex_send.at[i], ex_recv.at[i], by_x)

    def ef_copy(i):
        _, src, dst = piece(i)
        return remote(src, dst, ef_send.at[i], ef_recv.at[i], by_far)

    def ec_copy(m):
        src = part(ex_dst[m].at[0], m, 1 - core, quarter)
        return remote(src, (ec_gu, ec_down)[m], ec_send.at[m], ec_recv.at[m], by_core)

    def kept_copy(which, m):
        src = part((ggu_ref, gd_ref)[m].at[which], m, x, wide_half)
        return pltpu.make_async_copy(src, (kept_gu, kept_down)[m], load_sem.at[22 + m])

    def load(number, src, dst):
        return pltpu.make_async_copy(src, dst, load_sem.at[number])

    ex_copy(0).start()
    loads = (
        (own_ref.at[3], pool.at[6]),
        (sibling_ref.at[3], pool.at[9]),
        (own_ref.at[1], pool.at[5]),
        (sibling_ref.at[1], pool.at[8]),
        (second0_ref, pool.at[1]),
        (second1_ref, pool.at[2]),
        (second2_ref, pool.at[3]),
        (second3_ref, pool.at[4]),
        (mixed_ref, grad),
        (cot_ref, pool.at[0]),
        (wo_ref, w_big),
        (own_ref.at[2], pool.at[7]),
    )
    for number, (src, dst) in enumerate(loads):
        load(number, src, dst).start()

    def wait_load(number):
        load(number, *loads[number]).wait()

    def add_into(dst, *others):
        @pl.loop(0, rows // 128)
        def _(step):
            at = pl.ds(pl.multiple_of(step * 128, 128), 128)
            total = dst[at, :].astype(f32)
            for other in others:
                total = total + other[at, :].astype(f32)
            dst[at, :] = total.astype(bf16)

    def merge(dst, other):
        @pl.loop(0, dst.shape[0] // 128)
        def _(step):
            at = pl.ds(pl.multiple_of(step * 128, 128), 128)
            dst[at, :] = (dst[at, :].astype(f32) + other[at, :].astype(f32)).astype(bf16)

    def expert_piece(i):
        if i != 1:
            kept_copy(1, i // 2).wait()
        ex_copy(i).wait_recv()
        merge(piece(i)[1], kept_down if i == 2 else kept_gu.at[pl.ds(i * quarter, quarter), :])
        ef_copy(i).start()
        if i > 0:
            kept_copy(0, i - 1).start()

    def expert_own():
        for m in range(2):
            kept_copy(0, m).wait()
            arrived_copies[m].wait()
            merge(ex_dst[m].at[0], (kept_gu, kept_down)[m])

    def expert_third():
        for i in range(3):
            ef_copy(i).wait_recv()
        for m in range(2):
            merge(ex_dst[m].at[0], (ef_gu, ef_down)[m])
            ec_copy(m).start()
        at = pl.ds(pl.multiple_of(core * quarter, quarter), quarter)
        stage[...] = ex_gu[0, at, :].astype(f32)
        stage_down[...] = ex_down[0, :, at].astype(f32)
        for copy in final_copies(0):
            copy.start()

    far_copy = lambda: remote(pool.at[6], rf_ref, out_send.at[0], out_recv.at[0], first)
    first_copy = lambda: remote(pool.at[5], ra_ref, out_send.at[1], out_recv.at[1], first)
    second_copy = lambda: remote(pool.at[7], rb_ref, out_send.at[2], out_recv.at[2], second)
    wait_load(0)
    wait_load(1)
    add_into(pool.at[6], pool.at[9])
    far_copy().start()
    wait_load(2)
    wait_load(3)
    add_into(pool.at[5], pool.at[8])
    first_copy().start()
    sib2 = lambda: load(12, sibling_ref.at[2], pool.at[8])
    sib2().start()
    arrived_copies = [
        load(20 + m, (first_gu_ref, first_down_ref)[m], ex_dst[m].at[0]) for m in range(2)
    ]
    for m in range(2):
        arrived_copies[m].start()
        kept_copy(1, m).start()

    for number in range(4, 10):
        wait_load(number)
    gain_acc[...] = jnp.zeros_like(gain_acc)

    @pl.loop(0, rows // 128)
    def _(step):
        at = pl.ds(pl.multiple_of(step * 128, 128), 128)
        value = grad[at, :]
        scale = lax.rsqrt(jnp.mean(value * value, axis=-1, keepdims=True) + EPS)
        normed = value * scale
        down = (
            pool[1, at, :].astype(f32)
            + pool[2, at, :].astype(f32)
            + pool[3, at, :].astype(f32)
            + pool[4, at, :].astype(f32)
        )
        product = down * normed
        gain_acc[1:2, :] += jnp.sum(product, axis=0, keepdims=True)
        mean = jnp.mean(product * ffn_gain_ref[...], axis=-1, keepdims=True)
        result = pool[0, at, :].astype(f32) + scale * (down * ffn_gain_ref[...] - normed * mean)
        grad[at, :] = result
        pool[3, at, :] = result.astype(bf16)

    att_load = lambda: load(13, att_ref, pool.at[1])
    query_load = lambda: load(14, query_ref, pool.at[2])
    tok_load = lambda: load(15, tok_ref, pool.at[0])
    key_weight_load = lambda: load(16, wk_ref, w_key)
    value_weight_load = lambda: load(17, wv_ref, w_value)
    for copy in (att_load, query_load, tok_load, key_weight_load, value_weight_load):
        copy().start()

    position = lax.broadcasted_iota(jnp.int32, (rows, rows), 0)
    other_position = lax.broadcasted_iota(jnp.int32, (rows, rows), 1)
    padding = seg_row_ref[...] == jnp.max(seg_row_ref[...])
    allowed = (
        (other_position <= position)
        & (seg_col_ref[...] == seg_row_ref[...])
        & (jnp.logical_not(padding) | (other_position == position))
    )
    bias[...] = jnp.where(allowed, 0.0, -1e30)

    def dot_nt(a, b):
        return lax.dot_general(a, b, (((1,), (1,)), ((), ())), preferred_element_type=f32)

    def dot_tn(a, b):
        return lax.dot_general(a, b, (((0,), (0,)), ((), ())), preferred_element_type=f32)

    far_levels = ((z_low, by_z), (z_high, by_far))
    orders = (
        ((core, by_core), (y, by_y), (x, by_x)) + far_levels,
        ((core, by_core), (x, by_x), (y, by_y)) + far_levels,
    )
    offsets = (0, 16, 24, 28, 30)
    places = []
    for levels in orders:
        starts = [0]
        for level, (bit, _) in enumerate(levels):
            starts.append(starts[-1] + bit * (16 >> level))
        places.append(starts)

    def landing(job, land, level):
        size = 16 >> level
        if job == 1 and level > 0:
            return query_land.at[pl.ds(offsets[level] - 16, size)]
        return land.at[pl.ds(offsets[level], size)]

    def halve_copy(job, buf, land, level):
        bit, device = orders[min(job, 1)][level]
        starts = places[min(job, 1)]
        size = 16 >> level
        return remote(
            buf.at[pl.ds(starts[level] + (1 - bit) * size, size)],
            landing(job, land, level),
            halve_send.at[job, level],
            halve_recv.at[job, level],
            device,
        )

    def absorb(job, buf, land, level, result=None):
        halve_copy(job, buf, land, level).wait_recv()
        starts = places[min(job, 1)]
        size = 16 >> level
        arrivals = landing(job, land, level)
        if result is None:

            @pl.loop(0, size)
            def _(i):
                at = starts[level + 1] + i
                buf[at] = (buf[at].astype(f32) + arrivals[i].astype(f32)).astype(bf16)

        else:
            result[...] = buf[starts[5]].astype(f32) + arrivals[0].astype(f32)
        if job == 0 and level == 0:
            pl.semaphore_signal(
                free_sem, inc=1, device_id=by_core,
                device_id_type=pl.DeviceIdType.MESH,
            )
        if level < 4:
            launch(job, level + 1)

    jobs = ((out_buf, out_land), (query_buf, out_land), (kv_buf, kv_land))

    def launch(job, level):
        if job == 1 and level == 0:
            pl.semaphore_wait(free_sem, 1)
        halve_copy(job, *jobs[job], level).start()

    def begin(job):
        launch(job, 0)

    def advance(job, level):
        absorb(job, *jobs[job], level, (out_out, query_out, kv_out)[job] if level == 4 else None)

    def place(buf, tile, value, columns):
        for b in range(8):
            high, low, odd = b >> 2, (b >> 1) & 1, b & 1
            middle = odd * 2 + (tile >> 1) if buf is out_buf else (tile >> 1) * 2 + odd
            to = (((tile & 1) * 4 + middle) * 2 + low) * 2 + high
            buf[to, :, columns] = value[b * block : (b + 1) * block].astype(bf16)

    ex_copy(1).start()
    att_load().wait()
    for tile in range(4):
        at = slice(tile * 8 * block, (tile + 1) * 8 * block)
        place(out_buf, tile, dot_tn(pool[3, :, at], pool[1]), slice(None))
    begin(0)
    wait_load(10)
    for half in range(2):
        at = slice(half * rows // 2, (half + 1) * rows // 2)
        pool[4, at, :] = dot_nt(pool[3, at, :], w_big[...]).astype(bf16)
    query_weight_load = lambda: load(18, wq_ref, w_big)
    query_weight_load().start()
    ex_copy(2).start()
    expert_piece(0)

    tok_load().wait()

    def first_norm(at):
        value = pool[0, at, :].astype(f32)
        scale = lax.rsqrt(jnp.mean(value * value, axis=-1, keepdims=True) + EPS)
        return scale, value * scale

    @pl.loop(0, rows // 128)
    def _(step):
        at = pl.ds(pl.multiple_of(step * 128, 128), 128)
        pool[1, at, :] = (first_norm(at)[1] * attn_gain_ref[...]).astype(bf16)

    def send_second():
        wait_load(11)
        sib2().wait()
        far_copy().wait_recv()
        far_load = load(19, rf_ref, pool.at[9])
        far_load.start()
        far_load.wait()
        add_into(pool.at[7], pool.at[8], pool.at[9])
        second_copy().start()

    def final_copies(which):
        own = core * (1 - which) + (1 - core) * which
        units = pl.ds(pl.multiple_of(own * mine, mine), mine)
        pairs = (
            (stage.at[:, pl.ds(0, mine)], gate_out.at[:, units]),
            (stage.at[:, pl.ds(mine, mine)], up_out.at[:, units]),
            (stage_down, down_out.at[units, :]),
        )
        return [
            pltpu.make_async_copy(src, dst, store_sem.at[4 + 3 * which + i])
            for i, (src, dst) in enumerate(pairs)
        ]

    def expert_last():
        for copy in final_copies(0):
            copy.wait()
        for m in range(2):
            ec_copy(m).wait_recv()
        stage[...] = ec_gu[...].astype(f32)
        stage_down[...] = ec_down[...].astype(f32)
        for copy in final_copies(1):
            copy.start()

    def turn_back(value, at):
        swapped = pltpu.roll(value, head // 2, 1)
        return value * cos_ref[at, :] - swapped * sin_ref[at, :]

    scale = head ** (-0.5)
    query_load().wait()
    key_acc[...] = jnp.zeros_like(key_acc)
    value_acc[...] = jnp.zeros_like(value_acc)

    def between(number):
        if number == 1:
            advance(0, 0)
        elif number == 3:
            expert_piece(1)
        elif number == 7:
            send_second()
        elif number == 11:
            expert_piece(2)

    for number in range(heads):
        columns = slice(number * head, (number + 1) * head)
        kv = number // per_key
        kv_columns = slice(kv * head, (kv + 1) * head)
        for half in range(2):
            at = slice(half * rows // 2, (half + 1) * rows // 2)
            seen = slice(0, (half + 1) * rows // 2)
            q = pool[2, at, columns]
            da = pool[4, at, columns]
            k = key_ref[seen, kv_columns]
            score = dot_nt(q, k) * scale + bias[at, seen]
            probs = jnp.exp(score - lse_ref[at, number : number + 1])
            dprob = dot_nt(da, value_ref[seen, kv_columns])
            inner = jnp.sum(probs * dprob, axis=-1, keepdims=True)
            dscore = (probs * (dprob - inner)).astype(bf16)
            value_acc[seen, kv_columns] += dot_tn(probs.astype(bf16), da)
            key_acc[seen, kv_columns] += dot_tn(dscore, q)
            dq = jnp.dot(dscore, k, preferred_element_type=f32) * scale
            proj[at, columns] = turn_back(dq, at).astype(bf16)
        between(number)

    for kv in range(key_width // head):
        columns = slice(kv * head, (kv + 1) * head)
        to = slice(width + kv * head, width + (kv + 1) * head)
        proj[:, to] = turn_back(key_acc[:, columns] * scale, slice(None)).astype(bf16)
        to = slice(width + key_width + kv * head, width + key_width + (kv + 1) * head)
        proj[:, to] = value_acc[:, columns].astype(bf16)

    for tile in range(4):
        at = slice(tile * 8 * block, (tile + 1) * 8 * block)
        place(query_buf, tile, dot_tn(pool[1, :, at], proj[:, :width]), slice(None))
    begin(1)
    for tile in range(4):
        at = slice(tile * 8 * block, (tile + 1) * 8 * block)
        place(kv_buf, tile, dot_tn(pool[1, :, at], proj[:, width:]), slice(0, 2 * key_width))
    query_weight_load().wait()
    key_weight_load().wait()
    value_weight_load().wait()
    for quarter_step in range(4):
        at = slice(quarter_step * rows // 4, (quarter_step + 1) * rows // 4)
        down = dot_nt(proj[at, :width], w_big[...])
        down = down + dot_nt(proj[at, width : width + key_width], w_key[...])
        down = down + dot_nt(proj[at, width + key_width :], w_value[...])
        factor, normed = first_norm(at)
        product = down * normed
        gain_acc[0:1, :] += jnp.sum(product, axis=0, keepdims=True)
        mean = jnp.mean(product * attn_gain_ref[...], axis=-1, keepdims=True)
        grad[at, :] = grad[at, :] + factor * (down * attn_gain_ref[...] - normed * mean)
        if quarter_step == 0:
            advance(1, 0)
        elif quarter_step == 1:
            expert_own()
    tokens_store = lambda: pltpu.make_async_copy(grad, tokens_ref, store_sem.at[0])
    tokens_store().start()

    gains = gain_acc[...]
    high = gains.astype(bf16).astype(f32)
    row = lax.broadcasted_iota(jnp.int32, gains.shape, 0)
    lower = pltpu.roll(gains - high, 2, 0)
    both = jnp.transpose(jnp.where(row < 2, high, lower))
    both = jnp.concatenate([both, jnp.zeros((width, head - 8), f32)], axis=1)
    for tile in range(4):
        at = slice(tile * 8 * block, (tile + 1) * 8 * block)
        place(kv_buf, tile, both[at], slice(2 * key_width, 2 * key_width + head))
    begin(2)

    advance(2, 0)
    advance(0, 1)
    advance(1, 1)
    advance(2, 1)
    advance(0, 2)
    advance(1, 2)
    advance(2, 2)
    expert_third()
    advance(0, 3)
    advance(1, 3)
    advance(2, 3)

    tokens_store().wait()
    first_copy().wait_recv()
    second_copy().wait_recv()
    last_loads = (
        (own_ref.at[0], pool.at[3]),
        (sibling_ref.at[0], pool.at[4]),
        (ra_ref, pool.at[8]),
        (rb_ref, pool.at[9]),
        (mixed_ref, grad),
    )
    for number, (src, dst) in enumerate(last_loads):
        load(number, src, dst).start()
    for number, (src, dst) in enumerate(last_loads):
        load(number, src, dst).wait()

    @pl.loop(0, rows // 128)
    def _(step):
        at = pl.ds(pl.multiple_of(step * 128, 128), 128)
        total = grad[at, :]
        for i in (3, 4, 8, 9):
            total = total + pool[i, at, :].astype(f32)
        pool[3, at, :] = total.astype(bf16)

    layer_store = pltpu.make_async_copy(pool.at[3], layer_ref, store_sem.at[1])
    layer_store.start()
    expert_last()
    advance(0, 4)
    advance(1, 4)
    advance(2, 4)

    for copy in (far_copy, first_copy, second_copy):
        copy().wait_send()
    for m in range(2):
        ec_copy(m).wait_send()
    for i in range(3):
        ex_copy(i).wait_send()
        ef_copy(i).wait_send()
    for copy in final_copies(1):
        copy.wait()
    for job in range(3):
        for level in range(5):
            halve_copy(job, *jobs[job], level).wait_send()
    layer_store.wait()


def backward_call(vmem_args, any_args):
    f32, bf16 = jnp.float32, jnp.bfloat16
    rows, head = vmem_args[2].shape
    key_width = vmem_args[7].shape[1]
    width = vmem_args[0].shape[1]
    hidden = any_args[13].shape[2]
    block = width // 32
    extra = 2 * key_width + head
    anywhere = pl.BlockSpec(memory_space=pl.ANY)
    inside = pl.BlockSpec(memory_space=pltpu.VMEM)
    shape = jax.ShapeDtypeStruct
    dma = pltpu.SemaphoreType.DMA
    vmem = pltpu.VMEM
    return pl.pallas_call(
        backward_kernel,
        out_shape=(
            shape((block, width), f32),
            shape((block, extra), f32),
            shape((block, width), f32),
            shape((rows, width), bf16),
            shape((rows, width), f32),
            shape((width // 4, hidden), f32),
            shape((width // 4, hidden), f32),
            shape((hidden, width // 4), f32),
            shape((rows, width), bf16),
            shape((rows, width), bf16),
            shape((rows, width), bf16),
        ),
        in_specs=[inside] * len(vmem_args) + [anywhere] * len(any_args),
        out_specs=(inside,) * 3 + (anywhere,) * 8,
        scratch_shapes=[
            vmem((10, rows, width), bf16),
            vmem((width, width), bf16),
            vmem((width, key_width), bf16),
            vmem((width, key_width), bf16),
            vmem((rows, width), f32),
            vmem((rows, width + 2 * key_width), bf16),
            vmem((rows, rows), f32),
            vmem((rows, key_width), f32),
            vmem((rows, key_width), f32),
            vmem((8, width), f32),
            vmem((32, block, width), bf16),
            vmem((31, block, width), bf16),
            vmem((32, block, width), bf16),
            vmem((15, block, width), bf16),
            vmem((32, block, extra), bf16),
            vmem((31, block, extra), bf16),
            vmem((2, width // 2, hidden), bf16),
            vmem((2, hidden // 2, width // 2), bf16),
            vmem((width // 2, hidden), bf16),
            vmem((hidden // 2, width // 2), bf16),
            vmem((width // 4, hidden), bf16),
            vmem((hidden // 2, width // 4), bf16),
            vmem((width // 2, hidden), bf16),
            vmem((hidden // 2, width // 2), bf16),
            vmem((width // 4, hidden), f32),
            vmem((hidden // 2, width // 4), f32),
            dma((24,)),
            dma((3,)),
            dma((3,)),
            dma((3,)),
            dma((3,)),
            dma((3,)),
            dma((3,)),
            dma((2,)),
            dma((2,)),
            dma((3, 5)),
            dma((3, 5)),
            pltpu.SemaphoreType.REGULAR,
            dma((10,)),
        ],
        compiler_params=pltpu.CompilerParams(
            collective_id=1, has_side_effects=True, vmem_limit_bytes=64 * 2**20
        ),
        cost_estimate=pl.CostEstimate(
            flops=30 * rows * width * width, bytes_accessed=60 * 2**20, transcendentals=0
        ),
    )(*vmem_args, *any_args)


def local_dense(
    tokens,
    segment_ids,
    routes,
    route_gates,
    attn_gain,
    ffn_gain,
    query_weight,
    key_matrix,
    value_matrix,
    output_weight,
    expert_gate,
    expert_up,
    expert_down,
    cotangent,
):
    experts = lax.axis_size("ep")
    table = jnp.sum(
        jnp.where(
            routes.T[None, :, :] == jnp.arange(experts, dtype=jnp.int32)[:, None, None],
            route_gates.T[None, :, :],
            0.0,
        ),
        axis=1,
    )
    position = jnp.arange(tokens.shape[0], dtype=jnp.float32)
    inverse = BASE ** (-jnp.arange(HEAD_SIZE // 2, dtype=jnp.float32) * 2.0 / HEAD_SIZE)
    angle = position[:, None] * inverse[None, :]
    cosine = jnp.cos(angle)
    sine = jnp.sin(angle)
    small = (
        attn_gain[None, :],
        ffn_gain[None, :],
        jnp.concatenate([cosine, cosine], axis=1),
        jnp.concatenate([-sine, sine], axis=1),
        segment_ids,
        segment_ids.T,
    )
    (
        query_rot,
        key_rot,
        value_low,
        log_total,
        attended,
        mixed,
        grad_gu,
        grad_down,
        out_own,
        out_sib,
        own_grad,
        sibling_grad,
        first_grad,
        second_grad,
        _,
        _,
        met_gu,
        met_down,
    ) = forward_call(
        small + (table,),
        (
            tokens,
            query_weight,
            key_matrix,
            value_matrix,
            output_weight,
            cotangent,
            expert_gate[0],
            expert_up[0],
            expert_down[0],
        ),
    )
    (
        query_grad,
        extra_grad,
        output_grad,
        layer_out,
        tokens_grad,
        gate_grad,
        up_grad,
        down_grad,
        *_,
    ) = backward_call(
        small + (log_total, key_rot, value_low),
        (
            own_grad,
            sibling_grad,
            first_grad,
            second_grad,
            mixed,
            cotangent,
            attended,
            query_rot,
            tokens,
            output_weight,
            query_weight,
            key_matrix,
            value_matrix,
            grad_gu,
            grad_down,
            out_own,
            out_sib,
            met_gu,
            met_down,
        ),
    )
    split_k = key_matrix.shape[1]
    split_v = split_k + value_matrix.shape[1]
    gain_sums = extra_grad[:, split_v : split_v + 2] + extra_grad[:, split_v + 2 : split_v + 4]
    return (
        layer_out,
        tokens_grad,
        query_grad,
        extra_grad[:, :split_k],
        extra_grad[:, split_k:split_v],
        output_grad.T,
        gain_sums[:, 0],
        gain_sums[:, 1],
        gate_grad[None],
        up_grad[None],
        down_grad[None],
    )


def solution(mesh):
    in_specs = (
        P(("grp", "ep"), None),
        P(("grp", "ep"), None),
        P(("grp", "ep"), None),
        P(("grp", "ep"), None),
        P(),
        P(),
        P(),
        P(),
        P(),
        P(),
        P("ep", None, None),
        P("ep", None, None),
        P("ep", None, None),
        P(("grp", "ep"), None),
    )
    out_specs = (
        P(("grp", "ep"), None),
        P(("grp", "ep"), None),
        P(("grp", "ep"), None),
        P(("grp", "ep"), None),
        P(("grp", "ep"), None),
        P(None, ("grp", "ep")),
        P(("grp", "ep")),
        P(("grp", "ep")),
        P("ep", "grp", None),
        P("ep", "grp", None),
        P("ep", None, "grp"),
    )
    paired = mesh.shape["grp"] == 4 and mesh.shape["ep"] == 8
    local = local_dense if paired else local_routed
    return jax.shard_map(local, mesh=mesh, in_specs=in_specs, out_specs=out_specs, check_vma=False)
```

```python
import jax
import jax.numpy as jnp
import numpy as np
from jax import lax
from jax.experimental import pallas as pl
from jax.experimental.pallas import tpu as pltpu
from jax.sharding import PartitionSpec as P

HEAD_SIZE = 128


EPS = 1e-06
BASE = 10000.0


def apply_rotary(value_rows, cosine_table, sine_table):
    half = value_rows.shape[-1] // 2
    first = value_rows[..., :half]
    second = value_rows[..., half:]
    return jnp.concatenate(
        [first * cosine_table - second * sine_table, second * cosine_table + first * sine_table],
        axis=-1,
    )


def unrotate(value_rows, cosine_table, sine_table):
    half = value_rows.shape[-1] // 2
    first = value_rows[..., :half]
    second = value_rows[..., half:]
    return jnp.concatenate(
        [first * cosine_table + second * sine_table, second * cosine_table - first * sine_table],
        axis=-1,
    )


def glu_value(gate_val, up_val):
    return jax.nn.gelu(gate_val, approximate=True) * up_val


def scores_of(query_rot, key_rot, allowed):
    score = jnp.einsum(
        "tkgd,skd->kgts", query_rot, key_rot, preferred_element_type=jnp.float32
    ) * HEAD_SIZE ** (-0.5)
    return jnp.where(allowed, score, -1e30)


def local_routed(
    tokens,
    segment_ids,
    routes,
    route_gates,
    attn_gain,
    ffn_gain,
    query_weight,
    key_matrix,
    value_matrix,
    output_weight,
    expert_gate,
    expert_up,
    expert_down,
    cotangent,
):
    length_total, width = tokens.shape
    choose = routes.shape[1]
    local_experts = expert_gate.shape[0]
    owners = lax.axis_size("ep")
    experts = owners * local_experts
    capacity = 3 * length_total * choose // (2 * experts)
    query_heads = query_weight.shape[1] // HEAD_SIZE
    key_heads = key_matrix.shape[1] // HEAD_SIZE
    q_per_kv = query_heads // key_heads
    segment = segment_ids[0]
    padding = segment == jnp.max(segment)
    later = jnp.arange(length_total)[:, None] >= jnp.arange(length_total)[None, :]
    diagonal = jnp.arange(length_total)[:, None] == jnp.arange(length_total)[None, :]
    allowed = (
        later
        & (segment[:, None] == segment[None, :])
        & (jnp.logical_not(padding)[None, :] | diagonal)
    )
    position = jnp.arange(length_total, dtype=jnp.float32)
    inverse = BASE ** (-jnp.arange(HEAD_SIZE // 2, dtype=jnp.float32) * 2.0 / HEAD_SIZE)
    angle = position[:, None] * inverse[None, :]
    cosine_table = jnp.cos(angle)[:, None, :]
    sine_table = jnp.sin(angle)[:, None, :]
    tok_float = tokens.astype(jnp.float32)
    scale_first = lax.rsqrt(jnp.mean(tok_float * tok_float, axis=-1, keepdims=True) + EPS)
    normed_first = tok_float * scale_first
    h_first = (normed_first * attn_gain).astype(jnp.bfloat16)
    query_rows = jnp.dot(h_first, query_weight, preferred_element_type=jnp.float32).reshape(
        length_total, query_heads, HEAD_SIZE
    )
    key_rows = jnp.dot(h_first, key_matrix, preferred_element_type=jnp.float32).reshape(
        length_total, key_heads, HEAD_SIZE
    )
    value_low = jnp.dot(h_first, value_matrix, preferred_element_type=jnp.float32).astype(
        jnp.bfloat16
    )
    value_low = value_low.reshape(length_total, key_heads, HEAD_SIZE)
    query_rot = (
        apply_rotary(query_rows, cosine_table, sine_table)
        .astype(jnp.bfloat16)
        .reshape(length_total, key_heads, q_per_kv, HEAD_SIZE)
    )
    key_rot = apply_rotary(key_rows, cosine_table, sine_table).astype(jnp.bfloat16)
    score = scores_of(query_rot, key_rot, allowed)
    row_max = jnp.max(score, axis=-1, keepdims=True)
    expo = jnp.exp(score - row_max)
    row_sum = jnp.sum(expo, axis=-1, keepdims=True)
    log_total = row_max + jnp.log(row_sum)
    probs_low = (expo / row_sum).astype(jnp.bfloat16)
    attended = jnp.einsum(
        "kgts,skd->tkgd", probs_low, value_low, preferred_element_type=jnp.float32
    )
    attended = attended.reshape(length_total, query_heads * HEAD_SIZE).astype(jnp.bfloat16)
    mixed = tok_float + jnp.dot(attended, output_weight, preferred_element_type=jnp.float32)
    scale_second = lax.rsqrt(jnp.mean(mixed * mixed, axis=-1, keepdims=True) + EPS)
    normed_second = mixed * scale_second
    h_second = (normed_second * ffn_gain).astype(jnp.bfloat16)
    flat_routes = routes.reshape(-1)
    assigns = flat_routes.shape[0]
    onehot = (flat_routes[:, None] == jnp.arange(experts, dtype=jnp.int32)[None, :]).astype(
        jnp.int32
    )
    position_in = jnp.sum(jnp.cumsum(onehot, axis=0) * onehot, axis=1) - 1
    slot_index = flat_routes * capacity + position_in
    source = (
        jnp.full((experts * capacity,), assigns, jnp.int32)
        .at[slot_index]
        .set(jnp.arange(assigns, dtype=jnp.int32))
    )
    token_of = source // choose
    h_ext = jnp.concatenate([h_second, jnp.zeros((1, width), jnp.bfloat16)], axis=0)
    send_rows = h_ext[token_of].reshape(owners, local_experts, capacity, width)
    row_entries = lax.all_to_all(send_rows, "ep", split_axis=0, concat_axis=0, tiled=True)
    gate_val = jnp.einsum(
        "secd,edf->secf", row_entries, expert_gate, preferred_element_type=jnp.float32
    )
    up_val = jnp.einsum(
        "secd,edf->secf", row_entries, expert_up, preferred_element_type=jnp.float32
    )
    act = glu_value(gate_val, up_val).astype(jnp.bfloat16)
    result = jnp.einsum("secf,efd->secd", act, expert_down, preferred_element_type=jnp.float32)
    outputs = (result.astype(jnp.bfloat16), row_entries, gate_val, up_val)
    returned = lax.all_to_all(outputs[0], "ep", split_axis=0, concat_axis=0, tiled=True).reshape(
        experts * capacity, width
    )
    picked = returned[slot_index].reshape(length_total, choose, width).astype(jnp.float32)
    layer_out = (mixed + jnp.sum(route_gates[:, :, None] * picked, axis=1)).astype(jnp.bfloat16)
    grad_out = cotangent.astype(jnp.float32)
    slot_grads = (
        (route_gates[:, :, None] * grad_out[:, None, :])
        .astype(jnp.bfloat16)
        .reshape(assigns, width)
    )
    slot_ext = jnp.concatenate([slot_grads, jnp.zeros((1, width), jnp.bfloat16)], axis=0)
    grad_send = slot_ext[source].reshape(owners, local_experts, capacity, width)
    grad_recv = lax.all_to_all(grad_send, "ep", split_axis=0, concat_axis=0, tiled=True)
    recv_rows = outputs[1]
    gate_val = outputs[2]
    up_val = outputs[3]
    act, act_back = jax.vjp(glu_value, gate_val, up_val)
    act_low = act.astype(jnp.bfloat16)
    down_part = jnp.einsum("secf,secd->efd", act_low, grad_recv, preferred_element_type=jnp.float32)
    act_grad = jnp.einsum(
        "secd,efd->secf", grad_recv, expert_down, preferred_element_type=jnp.float32
    )
    gate_grad_val, up_grad_val = act_back(act_grad)
    gate_low = gate_grad_val.astype(jnp.bfloat16)
    up_low = up_grad_val.astype(jnp.bfloat16)
    gate_part = jnp.einsum(
        "secd,secf->edf", recv_rows, gate_low, preferred_element_type=jnp.float32
    )
    up_part = jnp.einsum("secd,secf->edf", recv_rows, up_low, preferred_element_type=jnp.float32)
    rows_grad = jnp.einsum(
        "secf,edf->secd", gate_low, expert_gate, preferred_element_type=jnp.float32
    )
    rows_grad = rows_grad + jnp.einsum(
        "secf,edf->secd", up_low, expert_up, preferred_element_type=jnp.float32
    )
    rows_back = lax.all_to_all(
        rows_grad.astype(jnp.bfloat16), "ep", split_axis=0, concat_axis=0, tiled=True
    )
    rows_back = rows_back.reshape(experts * capacity, width)
    expert_sums = (
        lax.psum_scatter(
            gate_part.astype(jnp.bfloat16), "grp", scatter_dimension=1, tiled=True
        ).astype(jnp.float32),
        lax.psum_scatter(
            up_part.astype(jnp.bfloat16), "grp", scatter_dimension=1, tiled=True
        ).astype(jnp.float32),
        lax.psum_scatter(
            down_part.astype(jnp.bfloat16), "grp", scatter_dimension=2, tiled=True
        ).astype(jnp.float32),
    )
    second_grad = jnp.sum(
        rows_back[slot_index].reshape(length_total, choose, width).astype(jnp.float32), axis=1
    )
    ffn_gain_part = jnp.sum(second_grad * normed_second, axis=0)
    normed_grad = second_grad * ffn_gain
    mixed_grad = grad_out + scale_second * (
        normed_grad - normed_second * jnp.mean(normed_grad * normed_second, axis=-1, keepdims=True)
    )
    mixed_low = mixed_grad.astype(jnp.bfloat16)
    output_part = jnp.einsum("ti,td->id", attended, mixed_low, preferred_element_type=jnp.float32)
    attended_grad = jnp.einsum(
        "td,id->ti", mixed_low, output_weight, preferred_element_type=jnp.float32
    )
    attended_grad = attended_grad.astype(jnp.bfloat16).reshape(
        length_total, key_heads, q_per_kv, HEAD_SIZE
    )
    probs = jnp.exp(scores_of(query_rot, key_rot, allowed) - log_total)
    probs_again = probs.astype(jnp.bfloat16)
    value_part_grad = jnp.einsum(
        "kgts,tkgd->skd", probs_again, attended_grad, preferred_element_type=jnp.float32
    )
    prob_grad = jnp.einsum(
        "tkgd,skd->kgts", attended_grad, value_low, preferred_element_type=jnp.float32
    )
    inner = jnp.sum(probs * prob_grad, axis=-1, keepdims=True)
    score_grad = (probs * (prob_grad - inner)).astype(jnp.bfloat16)
    qrot_grad = jnp.einsum(
        "kgts,skd->tkgd", score_grad, key_rot, preferred_element_type=jnp.float32
    ) * HEAD_SIZE ** (-0.5)
    krot_grad = jnp.einsum(
        "kgts,tkgd->skd", score_grad, query_rot, preferred_element_type=jnp.float32
    ) * HEAD_SIZE ** (-0.5)
    query_grad_low = unrotate(
        qrot_grad.reshape(length_total, query_heads, HEAD_SIZE), cosine_table, sine_table
    )
    query_grad_low = query_grad_low.astype(jnp.bfloat16).reshape(
        length_total, query_heads * HEAD_SIZE
    )
    key_grad_low = (
        unrotate(krot_grad, cosine_table, sine_table)
        .astype(jnp.bfloat16)
        .reshape(length_total, key_heads * HEAD_SIZE)
    )
    value_grad_low = value_part_grad.astype(jnp.bfloat16).reshape(
        length_total, key_heads * HEAD_SIZE
    )
    query_part = jnp.einsum(
        "td,ti->di", h_first, query_grad_low, preferred_element_type=jnp.float32
    )
    key_part = jnp.einsum("td,ti->di", h_first, key_grad_low, preferred_element_type=jnp.float32)
    value_part = jnp.einsum(
        "td,ti->di", h_first, value_grad_low, preferred_element_type=jnp.float32
    )
    first_grad = jnp.einsum(
        "ti,di->td", query_grad_low, query_weight, preferred_element_type=jnp.float32
    )
    first_grad = first_grad + jnp.einsum(
        "ti,di->td", key_grad_low, key_matrix, preferred_element_type=jnp.float32
    )
    first_grad = first_grad + jnp.einsum(
        "ti,di->td", value_grad_low, value_matrix, preferred_element_type=jnp.float32
    )
    attn_gain_part = jnp.sum(first_grad * normed_first, axis=0)
    normed_first_grad = first_grad * attn_gain
    tokens_grad = mixed_grad + scale_first * (
        normed_first_grad
        - normed_first * jnp.mean(normed_first_grad * normed_first, axis=-1, keepdims=True)
    )
    shared = (
        lax.psum_scatter(query_part, ("grp", "ep"), scatter_dimension=0, tiled=True),
        lax.psum_scatter(key_part, ("grp", "ep"), scatter_dimension=0, tiled=True),
        lax.psum_scatter(value_part, ("grp", "ep"), scatter_dimension=0, tiled=True),
        lax.psum_scatter(output_part, ("grp", "ep"), scatter_dimension=1, tiled=True),
        lax.psum_scatter(attn_gain_part, ("grp", "ep"), scatter_dimension=0, tiled=True),
        lax.psum_scatter(ffn_gain_part, ("grp", "ep"), scatter_dimension=0, tiled=True),
    )
    return (
        layer_out,
        tokens_grad,
        shared[0],
        shared[1],
        shared[2],
        shared[3],
        shared[4],
        shared[5],
        expert_sums[0],
        expert_sums[1],
        expert_sums[2],
    )


def forward_kernel(
    attn_gain_ref, ffn_gain_ref, cos_ref, sin_ref, seg_row_ref, tab_ref, tok_ref,
    wq_ref, wk_ref, wv_ref, wo_ref, dy_ref, gate_ref, up_ref, down_ref,
    query_ref, key_ref, value_ref, lse_ref, att_ref, mixed_ref, grad_gu_ref, grad_down_ref,
    out_own_ref, out_sib_ref, d_own_ref, d_sib_ref, d_first_ref, d_second_ref, part_d_ref,
    part_o_ref, ex_gu_ref, ex_down_ref,
    xb, dyb, tab, w_gu, w_down, sib, far_in, gather_send, gather_recv, tab_send, tab_recv,
    fetch_send, fetch_recv, pass_send, pass_recv, local_sem, part_send, part_recv, keep_sem,
    sum_send, sum_recv, ex_send, ex_recv, store_sem, stage_sem,
):
    f32, bf16 = jnp.float32, jnp.bfloat16
    grp, ep = lax.axis_index("grp"), lax.axis_index("ep")
    core = lax.rem(grp, 2)
    side = grp // 2
    low = lax.rem(ep, 4)
    y, z = lax.rem(low, 2), low // 2
    by_y = ep + 1 - 2 * y
    by_z = ep + 2 - 4 * z
    by_both = by_y + 2 - 4 * z
    by_far = ep + 4 - 8 * (ep // 4)
    first = by_y * (1 - core) + by_z * core
    second = by_z * (1 - core) + by_y * core
    other = grp + 1 - 2 * core
    across = (grp + 2 - 4 * side, ep)
    away = (grp, by_far)
    rows, width = tok_ref.shape
    half = rows // 2
    hidden = gate_ref.shape[1]
    mine = hidden // 2
    head = cos_ref.shape[1]
    heads = width // head
    key_width = wk_ref.shape[1]
    per_key = heads * head // key_width

    def remote(src, dst, send, recv, device):
        return pltpu.make_async_remote_copy(
            src_ref=src, dst_ref=dst, send_sem=send, recv_sem=recv, device_id=device,
            device_id_type=pl.DeviceIdType.MESH,
        )

    members = (
        ((grp, first), 1), ((grp, second), 2), ((grp, by_both), 3), ((other, ep), 4),
        ((other, first), 5), ((other, second), 6), ((other, by_both), 7),
    )
    barrier = pltpu.get_barrier_semaphore()
    for device in [device for device, _ in members] + [across, away]:
        pl.semaphore_signal(barrier, inc=1, device_id=device, device_id_type=pl.DeviceIdType.MESH)
    pl.semaphore_wait(barrier, 9)

    units = pl.ds(pl.multiple_of(core * mine, mine), mine)
    own_weights = (
        (gate_ref.at[:, units], w_gu.at[0, :, pl.ds(0, mine)]),
        (up_ref.at[:, units], w_gu.at[0, :, pl.ds(mine, mine)]),
        (down_ref.at[units, :], w_down.at[0]),
    )
    wide_at = pl.ds(pl.multiple_of(side * (width // 2), width // 2), width // 2)
    deep_at = pl.ds(pl.multiple_of(side * (mine // 2), mine // 2), mine // 2)
    deep_from = pl.ds(pl.multiple_of(core * mine + side * (mine // 2), mine // 2), mine // 2)
    pieces = (
        (gate_ref.at[wide_at, units], w_gu.at[1, wide_at, pl.ds(0, mine)]),
        (up_ref.at[wide_at, units], w_gu.at[1, wide_at, pl.ds(mine, mine)]),
        (down_ref.at[deep_from, :], w_down.at[1, deep_at, :]),
    )

    def fetch_copy(m):
        return remote(*pieces[m], fetch_send.at[m], fetch_recv.at[m], away)

    def pass_copy(m):
        return remote(pieces[m][1], pieces[m][1], pass_send.at[m], pass_recv.at[m], across)

    def load(number, src, dst):
        return pltpu.make_async_copy(src, dst, local_sem.at[number])

    def gather_copy(k, number):
        own, buf = ((xb.at[0], xb), (dy_ref, dyb))[k]
        src, dst, device = (
            (own, 1, (grp, first)), (own, 4, (other, ep)), (own, 2, (grp, second)),
            (buf.at[1], 5, (other, ep)), (buf.at[2], 6, (other, ep)),
            (buf.at[2], 3, (grp, first)), (buf.at[3], 7, (other, ep)),
        )[number]
        if k == 1 and number == 5:
            src, device = buf.at[2 - core], (grp, by_y)
        return remote(
            src, buf.at[dst], gather_send.at[k, number], gather_recv.at[k, number], device
        )

    arrival = {1: 0, 4: 1, 2: 2, 5: 3, 6: 4, 3: 5, 7: 6}

    def start(k, *numbers):
        for number in numbers:
            gather_copy(k, number).start()

    def arrived(k, slot):
        gather_copy(k, arrival[slot]).wait_recv()

    def table_copy(slot):
        device = members[slot - 1][0]
        return remote(tab_ref, tab.at[slot], tab_send.at[slot], tab_recv.at[slot], device)

    fetch_copy(0).start()
    start(1, 0, 1, 2)
    for slot in range(1, 8):
        table_copy(slot).start()
    own_dy = lambda: load(0, dy_ref, dyb.at[0])
    tab[0] = tab_ref[...]

    def dot_nt(a, b):
        return lax.dot_general(a, b, (((1,), (1,)), ((), ())), preferred_element_type=f32)

    def dot_tn(a, b):
        return lax.dot_general(a, b, (((0,), (0,)), ((), ())), preferred_element_type=f32)

    def attention(w_big, w_key, w_value, tok, act, query, key, value, bias, mixed, lse):
        tok_load = load(4, tok_ref, tok)
        query_load = load(5, wq_ref, w_big)
        key_load = load(6, wk_ref, w_key)
        value_load = load(7, wv_ref, w_value)
        for copy in (tok_load, query_load, key_load, value_load):
            copy.start()
        own_dy().start()
        for m, (src, dst) in enumerate(own_weights):
            load(1 + m, src, dst).start()
        segment = jnp.broadcast_to(seg_row_ref[...].astype(f32), (8, rows))
        segment_column = jnp.transpose(segment)[:, :1].astype(jnp.int32)
        position = lax.broadcasted_iota(jnp.int32, (rows, rows), 0)
        other_position = lax.broadcasted_iota(jnp.int32, (rows, rows), 1)
        padding = seg_row_ref[...] == jnp.max(seg_row_ref[...])
        allowed = (
            (other_position <= position)
            & (segment_column == seg_row_ref[...])
            & (jnp.logical_not(padding) | (other_position == position))
        )
        bias[...] = jnp.where(allowed, 0.0, -1e30)
        lse[...] = jnp.zeros_like(lse)
        tok_load.wait()

        @pl.loop(0, rows // 128)
        def _(step):
            at = pl.ds(pl.multiple_of(step * 128, 128), 128)
            entry = tok[at, :].astype(f32)
            factor = lax.rsqrt(jnp.mean(entry * entry, axis=-1, keepdims=True) + EPS)
            act[at, :] = (entry * factor * attn_gain_ref[...][None, :]).astype(bf16)

        def turn(entry, at):
            swapped = pltpu.roll(entry, head // 2, 1)
            return entry * cos_ref[at, :] + swapped * sin_ref[at, :]

        key_load.wait()
        value_load.wait()
        key_rows = jnp.dot(act[...], w_key[...], preferred_element_type=f32)
        for kv in range(key_width // head):
            columns = slice(kv * head, (kv + 1) * head)
            key[:, columns] = turn(key_rows[:, columns], slice(None)).astype(bf16)
        value[...] = jnp.dot(act[...], w_value[...], preferred_element_type=f32).astype(bf16)
        query_load.wait()
        for tile in range(width // 256):
            columns = slice(tile * 256, (tile + 1) * 256)
            entry = jnp.dot(act[...], w_big[:, columns], preferred_element_type=f32)
            for part in range(256 // head):
                columns = slice(part * head, (part + 1) * head)
                to = slice(tile * 256 + part * head, tile * 256 + (part + 1) * head)
                query[:, to] = turn(entry[:, columns], slice(None)).astype(bf16)
        out_load = load(8, wo_ref, w_big)
        out_load.start()
        stores = [
            pltpu.make_async_copy(src, dst, store_sem.at[i])
            for i, (src, dst) in enumerate(((query, query_ref), (key, key_ref), (value, value_ref)))
        ]
        for copy in stores:
            copy.start()
        scale = head ** (-0.5)
        lane = lax.broadcasted_iota(jnp.int32, (half, head), 1)
        for number in range(heads):
            columns = slice(number * head, (number + 1) * head)
            kv = number // per_key
            kv_columns = slice(kv * head, (kv + 1) * head)
            for part in range(2):
                at = slice(part * half, (part + 1) * half)
                seen = slice(0, (part + 1) * half)
                score = dot_nt(query[at, columns], key[seen, kv_columns]) * scale + bias[at, seen]
                top = jnp.max(score, axis=-1, keepdims=True)
                expo = jnp.exp(score - top)
                total = jnp.sum(expo, axis=-1, keepdims=True)
                lse[at, :] = jnp.where(lane == number, top + jnp.log(total), lse[at, :])
                probs = (expo / total).astype(bf16)
                mixed_value = jnp.dot(probs, value[seen, kv_columns], preferred_element_type=f32)
                act[at, columns] = mixed_value.astype(bf16)
        fetch_copy(1).start()
        out_load.wait()
        att_store = pltpu.make_async_copy(act, att_ref, store_sem.at[3])
        att_store.start()
        lse_store = pltpu.make_async_copy(lse, lse_ref, store_sem.at[4])
        lse_store.start()
        for part in range(4):
            at = slice(part * rows // 4, (part + 1) * rows // 4)
            total = tok[at, :].astype(f32) + jnp.dot(
                act[at, :], w_big[...], preferred_element_type=f32
            )
            mixed[at, :] = total
            factor = lax.rsqrt(jnp.mean(total * total, axis=-1, keepdims=True) + EPS)
            xb[0, at, :] = (total * factor * ffn_gain_ref[...][None, :]).astype(bf16)
        start(0, 0, 1, 2)
        mixed_store = pltpu.make_async_copy(mixed, mixed_ref, store_sem.at[5])
        mixed_store.start()
        for copy in stores + [att_store, lse_store, mixed_store]:
            copy.wait()

    vmem = pltpu.VMEM
    pl.run_scoped(
        attention,
        vmem((width, width), bf16),
        vmem((width, key_width), bf16),
        vmem((width, key_width), bf16),
        vmem((rows, width), bf16),
        vmem((rows, width), bf16),
        vmem((rows, width), bf16),
        vmem((rows, key_width), bf16),
        vmem((rows, key_width), bf16),
        vmem((rows, rows), f32),
        vmem((rows, width), f32),
        vmem((rows, head), f32),
    )

    def experts(acc_gu, acc_down, act_s, gu_s, dz_s, stage):
        own_dy().wait()
        for m, (src, dst) in enumerate(own_weights):
            load(1 + m, src, dst).wait()
        for slot in range(1, 8):
            table_copy(slot).wait_send()
            table_copy(slot).wait_recv()
        acc_gu[...] = jnp.zeros_like(acc_gu)
        acc_down[...] = jnp.zeros_like(acc_down)

        def gates(slot, hosted):
            block = jnp.transpose(tab[slot])
            lane = lax.broadcasted_iota(jnp.int32, block.shape, 1)
            return jnp.sum(jnp.where(lane == hosted, block, 0.0), axis=1, keepdims=True)

        c0 = 0.7978845608028654
        c1 = 0.044715

        def work(which, slot, hosted, deliver):
            column = gates(slot, hosted)
            for part in range(2):
                at = pl.ds(part * half, half)
                gate = column[part * half : (part + 1) * half]
                gu = jnp.dot(xb[slot, at, :], w_gu[which], preferred_element_type=f32)
                dz = (gate * dyb[slot, at, :].astype(f32)).astype(bf16)
                dz_s[at, :] = dz
                da = dot_nt(dz, w_down[which])
                g, u = gu[:, :mine], gu[:, mine:]
                square = g * g
                t = jnp.tanh(c0 * (g + c1 * square * g))
                gelu = 0.5 * g * (1.0 + t)
                slope = 0.5 * (1.0 + t) + 0.5 * g * (1.0 - t * t) * (c0 * (1.0 + 3.0 * c1 * square))
                act_s[at, :] = (gelu * u).astype(bf16)
                gu_s[at, :mine] = (da * u * slope).astype(bf16)
                gu_s[at, mine:] = (da * gelu).astype(bf16)
            for part in range(3):
                at = pl.ds(part * (width // 3), width // 3)
                acc_gu[which, at, :] += dot_tn(xb[slot, :, at], gu_s[...])
                acc_down[which, :, at] += dot_tn(act_s[...], dz_s[:, at])
            for part in range(2):
                at = pl.ds(part * half, half)
                gate = column[part * half : (part + 1) * half]
                dx = dot_nt(gu_s[at, :], w_gu[which])
                result = gate * jnp.dot(act_s[at, :], w_down[which], preferred_element_type=f32)
                deliver(at, dx, result)

        def slot_up(step):
            pair, odd = step // 2, lax.rem(step, 2)
            middle = (lax.rem(pair, 2) * (1 - pair // 3) + pair // 2 * (1 - pair // 3))
            turned = core * (1 - odd) + (1 - core) * odd
            swapped = middle * (3 - 2 * pair) * turned
            return pair + swapped + 4 * odd

        def stage_out(k, step):
            buf = lax.rem(step, 2)
            dst = (part_d_ref, part_o_ref)[k].at[slot_up(step)]
            return pltpu.make_async_copy(stage.at[k, buf], dst, stage_sem.at[k, buf])

        @pl.loop(0, 8)
        def _(step):
            def at_step(number):
                return pl.when(step == number)

            @at_step(1)
            def _():
                fetch_copy(2).start()
                arrived(0, 4)
                arrived(1, 4)

            @at_step(2)
            def _():
                arrived(1, 1)
                start(1, 3)
                arrived(1, 2)
                start(1, 5, 4)
                fetch_copy(0).wait_recv()
                pass_copy(0).start()
                @pl.when(core == 0)
                def _():
                    arrived(0, 1)
                    start(0, 3)

                @pl.when(core == 1)
                def _():
                    arrived(0, 2)
                    start(0, 5, 4)


            @at_step(3)
            def _():
                @pl.when(core == 0)
                def _():
                    arrived(0, 6)
                    arrived(1, 6)

                @pl.when(core == 1)
                def _():
                    arrived(0, 5)
                    arrived(1, 5)


            @at_step(4)
            def _():
                @pl.when(core == 0)
                def _():
                    arrived(0, 2)
                    start(0, 5, 4)

                @pl.when(core == 1)
                def _():
                    arrived(0, 1)
                    start(0, 3)

                for m in (1, 2):
                    fetch_copy(m).wait_recv()
                    pass_copy(m).start()

            @at_step(5)
            def _():
                @pl.when(core == 0)
                def _():
                    arrived(0, 5)
                    arrived(1, 5)

                @pl.when(core == 1)
                def _():
                    arrived(0, 6)
                    arrived(1, 6)

                arrived(1, 3)
                start(1, 6)

            @at_step(6)
            def _():
                arrived(0, 3)
                start(0, 6)

            @at_step(7)
            def _():
                arrived(0, 7)
                arrived(1, 7)

            @pl.when(step >= 2)
            def _():
                stage_out(0, step - 2).wait()
                stage_out(1, step - 2).wait()

            buf = lax.rem(step, 2)

            def deliver(at, dx, result):
                stage[0, buf, at, :] = dx.astype(bf16)
                stage[1, buf, at, :] = result.astype(bf16)

            work(0, slot_up(step), ep, deliver)
            stage_out(0, step).start()
            stage_out(1, step).start()

        for k in range(2):
            for step in (6, 7):
                stage_out(k, step).wait()
        for k in range(2):
            for number in range(7):
                gather_copy(k, number).wait_send()

        def grad_copies(which):
            return (
                pltpu.make_async_copy(w_gu.at[which], grad_gu_ref.at[which], store_sem.at[6 + 2 * which]),
                pltpu.make_async_copy(
                    w_down.at[which], grad_down_ref.at[which], store_sem.at[7 + 2 * which]
                ),
            )

        def slot_down(step):
            pair = step // 2
            return 3 - 2 * lax.rem(pair, 2) - pair // 2 + 4 * (1 - lax.rem(step, 2))

        def stage_in(k, step):
            buf = lax.rem(step, 2)
            src = (part_d_ref, part_o_ref)[k].at[slot_down(step)]
            return pltpu.make_async_copy(src, stage.at[k, buf], stage_sem.at[k, buf])

        stage_in(0, 0).start()
        stage_in(1, 0).start()
        def flush(which):
            w_gu[which] = acc_gu[which].astype(bf16)
            w_down[which] = acc_down[which].astype(bf16)
            for copy in grad_copies(which):
                copy.start()

        def exchange(m):
            at = pl.ds(pl.multiple_of((1 - side) * (width // 2), width // 2), width // 2)
            src = w_down.at[0, :, at] if m else w_gu.at[0, at, :]
            return remote(src, (ex_gu_ref, ex_down_ref)[m], ex_send.at[m], ex_recv.at[m], across)

        for m in range(3):
            pass_copy(m).wait()
            fetch_copy(m).wait_send()

        def keep_copy(j):
            return pltpu.make_async_copy(dyb.at[j], out_own_ref.at[j], keep_sem.at[j])

        def grad_part(j):
            dst = d_sib_ref if j == 0 else sib.at[j - 1]
            return remote(xb.at[4 + j], dst, part_send.at[0, j], part_recv.at[0, j], (other, ep))

        def out_part(j):
            return remote(
                dyb.at[4 + j], out_sib_ref.at[j], part_send.at[1, j], part_recv.at[1, j], (other, ep)
            )

        own_grad = lambda: pltpu.make_async_copy(xb.at[0], d_own_ref, keep_sem.at[4])
        send_far = lambda: remote(xb.at[3], far_in, sum_send.at[0], sum_recv.at[0], (grp, first))
        send_first = lambda: remote(
            xb.at[1], d_first_ref, sum_send.at[1], sum_recv.at[1], (grp, first)
        )
        send_second = lambda: remote(
            xb.at[2], d_second_ref, sum_send.at[2], sum_recv.at[2], (grp, second)
        )

        def add_into(dst, *others):
            @pl.loop(0, rows // 128)
            def _(i):
                at = pl.ds(pl.multiple_of(i * 128, 128), 128)
                total = dst[at, :].astype(f32)
                for part in others:
                    total = total + part[at, :].astype(f32)
                dst[at, :] = total.astype(bf16)

        @pl.loop(0, 8)
        def _(step):
            def at_step(number):
                return pl.when(step == number)

            stage_in(0, step).wait()
            stage_in(1, step).wait()

            @pl.when(step < 7)
            def _():
                stage_in(0, step + 1).start()
                stage_in(1, step + 1).start()

            buf = lax.rem(step, 2)
            slot = slot_down(step)

            def deliver(at, dx, result):
                xb[slot, at, :] = (dx + stage[0, buf, at, :].astype(f32)).astype(bf16)
                dyb[slot, at, :] = (result + stage[1, buf, at, :].astype(f32)).astype(bf16)

            work(1, slot, ep + 4 - 8 * (ep // 4), deliver)
            for number, j in enumerate((3, 1, 2, 0)):

                @at_step(2 * number)
                def _(j=j):
                    grad_part(j).start()
                    out_part(j).start()

                @at_step(2 * number + 1)
                def _(j=j):
                    keep_copy(j).start()

            @at_step(1)
            def _():
                grad_part(3).wait_recv()
                add_into(xb.at[3], sib.at[2])
                send_far().start()
                flush(0)
                for m in range(2):
                    exchange(m).start()

            @at_step(3)
            def _():
                grad_part(1).wait_recv()
                add_into(xb.at[1], sib.at[0])
                send_first().start()

            @at_step(5)
            def _():
                grad_part(2).wait_recv()
                send_far().wait_recv()
                add_into(xb.at[2], sib.at[1], far_in)
                send_second().start()

        own_grad().start()
        flush(1)
        for j in range(4):
            grad_part(j).wait_send()
            out_part(j).wait()
            keep_copy(j).wait()
        grad_part(0).wait_recv()
        own_grad().wait()
        send_far().wait_send()
        send_first().wait()
        send_second().wait()
        for which in range(2):
            for copy in grad_copies(which):
                copy.wait()
            exchange(which).wait()

    pl.run_scoped(
        experts,
        vmem((2, width, hidden), f32),
        vmem((2, mine, width), f32),
        vmem((rows, mine), bf16),
        vmem((rows, hidden), bf16),
        vmem((rows, width), bf16),
        vmem((2, 2, rows, width), bf16),
    )


def forward_call(vmem_args, any_args):
    f32, bf16 = jnp.float32, jnp.bfloat16
    rows, width = any_args[0].shape
    head = vmem_args[2].shape[1]
    key_width = any_args[2].shape[1]
    hidden = any_args[6].shape[1]
    anywhere = pl.BlockSpec(memory_space=pl.ANY)
    inside = pl.BlockSpec(memory_space=pltpu.VMEM)
    shape = jax.ShapeDtypeStruct
    dma = pltpu.SemaphoreType.DMA
    vmem = pltpu.VMEM
    chunk = shape((rows, width), bf16)
    four = shape((4, rows, width), bf16)
    eight = shape((8, rows, width), bf16)
    return pl.pallas_call(
        forward_kernel,
        out_shape=(
            chunk,
            shape((rows, key_width), bf16),
            shape((rows, key_width), bf16),
            shape((rows, head), f32),
            chunk,
            shape((rows, width), f32),
            shape((2, width, hidden), bf16),
            shape((2, hidden // 2, width), bf16),
            four,
            four,
            chunk,
            chunk,
            chunk,
            chunk,
            eight,
            eight,
            shape((width // 2, hidden), bf16),
            shape((hidden // 2, width // 2), bf16),
        ),
        in_specs=[inside] * len(vmem_args) + [anywhere] * len(any_args),
        out_specs=(anywhere,) * 18,
        scratch_shapes=[
            vmem((8, rows, width), bf16),
            vmem((8, rows, width), bf16),
            vmem((8,) + vmem_args[5].shape, f32),
            vmem((2, width, hidden), bf16),
            vmem((2, hidden // 2, width), bf16),
            vmem((3, rows, width), bf16),
            vmem((rows, width), bf16),
            dma((2, 7)),
            dma((2, 7)),
            dma((8,)),
            dma((8,)),
            dma((3,)),
            dma((3,)),
            dma((3,)),
            dma((3,)),
            dma((9,)),
            dma((2, 4)),
            dma((2, 4)),
            dma((5,)),
            dma((3,)),
            dma((3,)),
            dma((2,)),
            dma((2,)),
            dma((10,)),
            dma((2, 2)),
        ],
        compiler_params=pltpu.CompilerParams(
            collective_id=0, has_side_effects=True, vmem_limit_bytes=64 * 2**20
        ),
        cost_estimate=pl.CostEstimate(
            flops=160 * rows * width * hidden, bytes_accessed=60 * 2**20, transcendentals=0
        ),
    )(*vmem_args, *any_args)


def backward_kernel(
    attn_gain_ref, ffn_gain_ref, cos_ref, sin_ref, seg_row_ref, lse_ref, key_ref,
    value_ref, second0_ref, second1_ref, second2_ref, second3_ref, mixed_ref, cot_ref, att_ref,
    query_ref, tok_ref, wo_ref, wq_ref, wk_ref, wv_ref, ggu_ref, gd_ref, own_ref, sibling_ref,
    first_gu_ref, first_down_ref,
    query_out, kv_out, out_out, layer_ref, tokens_ref, gate_out, up_out, down_out, ra_ref, rb_ref, rf_ref,
    pool, w_big, w_key, w_value, grad, proj, bias, key_acc, value_acc, gain_acc,
    out_buf, out_land, query_buf, later_buf, query_land, kv_buf, kv_land,
    ex_gu, ex_down, ef_gu, ef_down, ec_gu, ec_down, kept_gu, kept_down, stage, stage_down, load_sem, out_send, out_recv, ex_send, ex_recv, ef_send, ef_recv, ec_send, ec_recv,
    halve_send, halve_recv, free_sem, store_sem,
):
    f32, bf16 = jnp.float32, jnp.bfloat16
    grp, ep = lax.axis_index("grp"), lax.axis_index("ep")
    core = lax.rem(grp, 2)
    x = grp // 2
    y = lax.rem(ep, 2)
    z_low = lax.rem(ep // 2, 2)
    z_high = ep // 4
    by_y = (grp, ep + 1 - 2 * y)
    by_z = (grp, ep + 2 - 4 * z_low)
    by_far = (grp, ep + 4 - 8 * z_high)
    by_core = (grp + 1 - 2 * core, ep)
    by_x = (grp + 2 - 4 * x, ep)
    first = (grp, by_y[1] * (1 - core) + by_z[1] * core)
    second = (grp, by_z[1] * (1 - core) + by_y[1] * core)
    rows, width = grad.shape
    head = cos_ref.shape[1]
    heads = width // head
    key_width = key_ref.shape[1]
    per_key = heads * head // key_width
    block = width // 32

    def remote(src, dst, send, recv, device):
        return pltpu.make_async_remote_copy(
            src_ref=src, dst_ref=dst, send_sem=send, recv_sem=recv, device_id=device,
            device_id_type=pl.DeviceIdType.MESH,
        )

    partners = (by_core, by_y, by_z, by_x, by_far)
    barrier = pltpu.get_barrier_semaphore()
    for device in partners:
        pl.semaphore_signal(barrier, inc=1, device_id=device, device_id_type=pl.DeviceIdType.MESH)
    pl.semaphore_wait(barrier, 5)

    wide_half = width // 2
    quarter = width // 4
    mine = gd_ref.shape[1]
    ex_dst = (ex_gu, ex_down)

    def part(ref, m, index, size):
        at = pl.ds(pl.multiple_of(index * size, size), size)
        return ref.at[:, at] if m == 1 else ref.at[at, :]

    def piece(i):
        at = pl.ds(i * quarter, quarter)
        if i == 2:
            return part(gd_ref.at[1], 1, 1 - x, wide_half), ex_down.at[1], ef_down
        start = pl.multiple_of((1 - x) * wide_half + i * quarter, quarter)
        return ggu_ref.at[1, pl.ds(start, quarter), :], ex_gu.at[1, at, :], ef_gu.at[at, :]

    def ex_copy(i):
        src, dst, _ = piece(i)
        return remote(src, dst, ex_send.at[i], ex_recv.at[i], by_x)

    def ef_copy(i):
        _, src, dst = piece(i)
        return remote(src, dst, ef_send.at[i], ef_recv.at[i], by_far)

    def ec_copy(m):
        src = part(ex_dst[m].at[0], m, 1 - core, quarter)
        return remote(src, (ec_gu, ec_down)[m], ec_send.at[m], ec_recv.at[m], by_core)

    def kept_copy(which, m):
        src = part((ggu_ref, gd_ref)[m].at[which], m, x, wide_half)
        return pltpu.make_async_copy(src, (kept_gu, kept_down)[m], load_sem.at[22 + m])

    def load(number, src, dst):
        return pltpu.make_async_copy(src, dst, load_sem.at[number])

    ex_copy(0).start()
    loads = (
        (own_ref.at[3], pool.at[6]),
        (sibling_ref.at[3], pool.at[9]),
        (own_ref.at[1], pool.at[5]),
        (sibling_ref.at[1], pool.at[8]),
        (second0_ref, pool.at[1]),
        (second1_ref, pool.at[2]),
        (second2_ref, pool.at[3]),
        (second3_ref, pool.at[4]),
        (mixed_ref, grad),
        (cot_ref, pool.at[0]),
        (wo_ref, w_big),
        (own_ref.at[2], pool.at[7]),
    )
    for number, (src, dst) in enumerate(loads):
        load(number, src, dst).start()

    def wait_load(number):
        load(number, *loads[number]).wait()

    def add_into(dst, *others):
        @pl.loop(0, rows // 128)
        def _(step):
            at = pl.ds(pl.multiple_of(step * 128, 128), 128)
            total = dst[at, :].astype(f32)
            for other in others:
                total = total + other[at, :].astype(f32)
            dst[at, :] = total.astype(bf16)

    def merge(dst, other):
        @pl.loop(0, dst.shape[0] // 128)
        def _(step):
            at = pl.ds(pl.multiple_of(step * 128, 128), 128)
            dst[at, :] = (dst[at, :].astype(f32) + other[at, :].astype(f32)).astype(bf16)

    def expert_piece(i):
        if i != 1:
            kept_copy(1, i // 2).wait()
        ex_copy(i).wait_recv()
        merge(piece(i)[1], kept_down if i == 2 else kept_gu.at[pl.ds(i * quarter, quarter), :])
        ef_copy(i).start()
        if i > 0:
            kept_copy(0, i - 1).start()

    def expert_own():
        for m in range(2):
            kept_copy(0, m).wait()
            arrived_copies[m].wait()
            merge(ex_dst[m].at[0], (kept_gu, kept_down)[m])

    def expert_third():
        for i in range(3):
            ef_copy(i).wait_recv()
        for m in range(2):
            merge(ex_dst[m].at[0], (ef_gu, ef_down)[m])
            ec_copy(m).start()
        at = pl.ds(pl.multiple_of(core * quarter, quarter), quarter)
        stage[...] = ex_gu[0, at, :].astype(f32)
        stage_down[...] = ex_down[0, :, at].astype(f32)
        for copy in final_copies(0):
            copy.start()

    far_copy = lambda: remote(pool.at[6], rf_ref, out_send.at[0], out_recv.at[0], first)
    first_copy = lambda: remote(pool.at[5], ra_ref, out_send.at[1], out_recv.at[1], first)
    second_copy = lambda: remote(pool.at[7], rb_ref, out_send.at[2], out_recv.at[2], second)
    wait_load(0)
    wait_load(1)
    add_into(pool.at[6], pool.at[9])
    far_copy().start()
    wait_load(2)
    wait_load(3)
    add_into(pool.at[5], pool.at[8])
    first_copy().start()
    sib2 = lambda: load(12, sibling_ref.at[2], pool.at[8])
    sib2().start()
    arrived_copies = [
        load(20 + m, (first_gu_ref, first_down_ref)[m], ex_dst[m].at[0]) for m in range(2)
    ]
    for m in range(2):
        arrived_copies[m].start()
        kept_copy(1, m).start()

    for number in range(4, 10):
        wait_load(number)
    gain_acc[...] = jnp.zeros_like(gain_acc)

    @pl.loop(0, rows // 128)
    def _(step):
        at = pl.ds(pl.multiple_of(step * 128, 128), 128)
        value = grad[at, :]
        scale = lax.rsqrt(jnp.mean(value * value, axis=-1, keepdims=True) + EPS)
        normed = value * scale
        down = (
            pool[1, at, :].astype(f32)
            + pool[2, at, :].astype(f32)
            + pool[3, at, :].astype(f32)
            + pool[4, at, :].astype(f32)
        )
        product = down * normed
        gain_acc[1:2, :] += jnp.sum(product, axis=0, keepdims=True)
        mean = jnp.mean(product * ffn_gain_ref[...][None, :], axis=-1, keepdims=True)
        result = pool[0, at, :].astype(f32) + scale * (down * ffn_gain_ref[...][None, :] - normed * mean)
        grad[at, :] = result
        pool[3, at, :] = result.astype(bf16)

    att_load = lambda: load(13, att_ref, pool.at[1])
    query_load = lambda: load(14, query_ref, pool.at[2])
    tok_load = lambda: load(15, tok_ref, pool.at[0])
    key_weight_load = lambda: load(16, wk_ref, w_key)
    value_weight_load = lambda: load(17, wv_ref, w_value)
    for copy in (att_load, query_load, tok_load, key_weight_load, value_weight_load):
        copy().start()

    segment = jnp.broadcast_to(seg_row_ref[...].astype(f32), (8, rows))
    segment_column = jnp.transpose(segment)[:, :1].astype(jnp.int32)
    position = lax.broadcasted_iota(jnp.int32, (rows, rows), 0)
    other_position = lax.broadcasted_iota(jnp.int32, (rows, rows), 1)
    padding = seg_row_ref[...] == jnp.max(seg_row_ref[...])
    allowed = (
        (other_position <= position)
        & (segment_column == seg_row_ref[...])
        & (jnp.logical_not(padding) | (other_position == position))
    )
    bias[...] = jnp.where(allowed, 0.0, -1e30)

    def dot_nt(a, b):
        return lax.dot_general(a, b, (((1,), (1,)), ((), ())), preferred_element_type=f32)

    def dot_tn(a, b):
        return lax.dot_general(a, b, (((0,), (0,)), ((), ())), preferred_element_type=f32)

    far_levels = ((z_low, by_z), (z_high, by_far))
    orders = (
        ((core, by_core), (y, by_y), (x, by_x)) + far_levels,
        ((core, by_core), (x, by_x), (y, by_y)) + far_levels,
    )
    offsets = (0, 16, 24, 28, 30)
    places = []
    for levels in orders:
        starts = [0]
        for level, (bit, _) in enumerate(levels):
            starts.append(starts[-1] + bit * (16 >> level))
        places.append(starts)

    def landing(job, land, level):
        size = 16 >> level
        if job in (1, 2):
            columns = pl.ds((job - 1) * (width // 2), width // 2)
            if level > 0:
                return query_land.at[pl.ds(offsets[level] - 16, size), :, columns]
            return out_land.at[pl.ds(0, size), :, columns]
        return land.at[pl.ds(offsets[level], size)]

    def halve_copy(job, buf, land, level):
        bit, device = orders[min(job, 1)][level]
        starts = places[min(job, 1)]
        size = 16 >> level
        return remote(
            buf.at[pl.ds(starts[level] + (1 - bit) * size, size)],
            landing(job, land, level),
            halve_send.at[job, level],
            halve_recv.at[job, level],
            device,
        )

    def absorb(job, buf, land, level, result=None):
        halve_copy(job, buf, land, level).wait_recv()
        starts = places[min(job, 1)]
        size = 16 >> level
        arrivals = landing(job, land, level)
        if result is None:

            @pl.loop(0, size)
            def _(i):
                at = starts[level + 1] + i
                buf[at] = (buf[at].astype(f32) + arrivals[i].astype(f32)).astype(bf16)

        else:
            result[...] = buf[starts[5]].astype(f32) + arrivals[0].astype(f32)
        if job == 0 and level == 0:
            for later in range(2):
                pl.semaphore_signal(
                    free_sem.at[later], inc=1, device_id=by_core,
                    device_id_type=pl.DeviceIdType.MESH,
                )
        if level < 4:
            launch(job, level + 1)

    jobs = (
        (out_buf, out_land), (query_buf, out_land), (later_buf, out_land), (kv_buf, kv_land)
    )

    def launch(job, level):
        if job in (1, 2) and level == 0:
            pl.semaphore_wait(free_sem.at[job - 1], 1)
        halve_copy(job, *jobs[job], level).start()

    def begin(job):
        launch(job, 0)

    def advance(job, level):
        results = (
            out_out,
            query_out.at[:, pl.ds(0, width // 2)],
            query_out.at[:, pl.ds(width // 2, width // 2)],
            kv_out,
        )
        absorb(job, *jobs[job], level, results[job] if level == 4 else None)

    def place(buf, tile, value, columns):
        for b in range(8):
            high, low, odd = b >> 2, (b >> 1) & 1, b & 1
            middle = odd * 2 + (tile >> 1) if buf is out_buf else (tile >> 1) * 2 + odd
            to = (((tile & 1) * 4 + middle) * 2 + low) * 2 + high
            buf[to, :, columns] = value[b * block : (b + 1) * block].astype(bf16)

    ex_copy(1).start()
    att_load().wait()
    for tile in range(4):
        at = slice(tile * 8 * block, (tile + 1) * 8 * block)
        place(out_buf, tile, dot_tn(pool[3, :, at], pool[1]), slice(None))
    begin(0)
    wait_load(10)
    for half in range(2):
        at = slice(half * rows // 2, (half + 1) * rows // 2)
        pool[4, at, :] = dot_nt(pool[3, at, :], w_big[...]).astype(bf16)
    query_weight_load = lambda: load(18, wq_ref, w_big)
    query_weight_load().start()
    ex_copy(2).start()
    expert_piece(0)

    tok_load().wait()

    def first_norm(at):
        value = pool[0, at, :].astype(f32)
        scale = lax.rsqrt(jnp.mean(value * value, axis=-1, keepdims=True) + EPS)
        return scale, value * scale

    @pl.loop(0, rows // 128)
    def _(step):
        at = pl.ds(pl.multiple_of(step * 128, 128), 128)
        pool[1, at, :] = (first_norm(at)[1] * attn_gain_ref[...][None, :]).astype(bf16)

    def send_second():
        wait_load(11)
        sib2().wait()
        far_copy().wait_recv()
        far_load = load(19, rf_ref, pool.at[9])
        far_load.start()
        far_load.wait()
        add_into(pool.at[7], pool.at[8], pool.at[9])
        second_copy().start()

    def final_copies(which):
        own = core * (1 - which) + (1 - core) * which
        units = pl.ds(pl.multiple_of(own * mine, mine), mine)
        pairs = (
            (stage.at[:, pl.ds(0, mine)], gate_out.at[:, units]),
            (stage.at[:, pl.ds(mine, mine)], up_out.at[:, units]),
            (stage_down, down_out.at[units, :]),
        )
        return [
            pltpu.make_async_copy(src, dst, store_sem.at[4 + 3 * which + i])
            for i, (src, dst) in enumerate(pairs)
        ]

    def expert_last():
        for copy in final_copies(0):
            copy.wait()
        for m in range(2):
            ec_copy(m).wait_recv()
        stage[...] = ec_gu[...].astype(f32)
        stage_down[...] = ec_down[...].astype(f32)
        for copy in final_copies(1):
            copy.start()

    def turn_back(value, at):
        swapped = pltpu.roll(value, head // 2, 1)
        return value * cos_ref[at, :] - swapped * sin_ref[at, :]

    scale = head ** (-0.5)
    query_load().wait()
    key_acc[...] = jnp.zeros_like(key_acc)
    value_acc[...] = jnp.zeros_like(value_acc)

    def place_query(part, buf):
        columns = slice(part * width // 2, (part + 1) * width // 2)
        for tile in range(4):
            at = slice(tile * 8 * block, (tile + 1) * 8 * block)
            place(buf, tile, dot_tn(pool[1, :, at], proj[:, columns]), slice(None))
        begin(1 + part)

    def between(number):
        if number == 1:
            advance(0, 0)
        elif number == 3:
            expert_piece(1)
        elif number == 5:
            place_query(0, query_buf)
        elif number == 7:
            send_second()
        elif number == 8:
            advance(1, 0)
        elif number == 10:
            expert_piece(2)

    for number in range(heads):
        columns = slice(number * head, (number + 1) * head)
        kv = number // per_key
        kv_columns = slice(kv * head, (kv + 1) * head)
        for half in range(2):
            at = slice(half * rows // 2, (half + 1) * rows // 2)
            seen = slice(0, (half + 1) * rows // 2)
            q = pool[2, at, columns]
            da = pool[4, at, columns]
            k = key_ref[seen, kv_columns]
            score = dot_nt(q, k) * scale + bias[at, seen]
            probs = jnp.exp(score - lse_ref[at, number : number + 1])
            dprob = dot_nt(da, value_ref[seen, kv_columns])
            inner = jnp.sum(probs * dprob, axis=-1, keepdims=True)
            dscore = (probs * (dprob - inner)).astype(bf16)
            value_acc[seen, kv_columns] += dot_tn(probs.astype(bf16), da)
            key_acc[seen, kv_columns] += dot_tn(dscore, q)
            dq = jnp.dot(dscore, k, preferred_element_type=f32) * scale
            proj[at, columns] = turn_back(dq, at).astype(bf16)
        between(number)

    for kv in range(key_width // head):
        columns = slice(kv * head, (kv + 1) * head)
        to = slice(width + kv * head, width + (kv + 1) * head)
        proj[:, to] = turn_back(key_acc[:, columns] * scale, slice(None)).astype(bf16)
        to = slice(width + key_width + kv * head, width + key_width + (kv + 1) * head)
        proj[:, to] = value_acc[:, columns].astype(bf16)

    place_query(1, later_buf)
    for tile in range(4):
        at = slice(tile * 8 * block, (tile + 1) * 8 * block)
        place(kv_buf, tile, dot_tn(pool[1, :, at], proj[:, width:]), slice(0, 2 * key_width))
    query_weight_load().wait()
    key_weight_load().wait()
    value_weight_load().wait()
    for quarter_step in range(4):
        at = slice(quarter_step * rows // 4, (quarter_step + 1) * rows // 4)
        down = dot_nt(proj[at, :width], w_big[...])
        down = down + dot_nt(proj[at, width : width + key_width], w_key[...])
        down = down + dot_nt(proj[at, width + key_width :], w_value[...])
        factor, normed = first_norm(at)
        product = down * normed
        gain_acc[0:1, :] += jnp.sum(product, axis=0, keepdims=True)
        mean = jnp.mean(product * attn_gain_ref[...][None, :], axis=-1, keepdims=True)
        grad[at, :] = grad[at, :] + factor * (down * attn_gain_ref[...][None, :] - normed * mean)
        if quarter_step == 0:
            advance(2, 0)
        elif quarter_step == 1:
            advance(1, 1)
        elif quarter_step == 2:
            expert_own()
    tokens_store = lambda: pltpu.make_async_copy(grad, tokens_ref, store_sem.at[0])
    tokens_store().start()

    gains = gain_acc[...]
    high = gains.astype(bf16).astype(f32)
    row = lax.broadcasted_iota(jnp.int32, gains.shape, 0)
    lower = pltpu.roll(gains - high, 2, 0)
    both = jnp.transpose(jnp.where(row < 2, high, lower))
    both = jnp.concatenate([both, jnp.zeros((width, head - 8), f32)], axis=1)
    for tile in range(4):
        at = slice(tile * 8 * block, (tile + 1) * 8 * block)
        place(kv_buf, tile, both[at], slice(2 * key_width, 2 * key_width + head))
    begin(3)

    advance(3, 0)
    advance(0, 1)
    advance(2, 1)
    advance(1, 2)
    advance(3, 1)
    advance(0, 2)
    advance(2, 2)
    advance(1, 3)
    advance(3, 2)
    advance(0, 3)
    advance(2, 3)
    expert_third()
    advance(3, 3)

    tokens_store().wait()
    first_copy().wait_recv()
    second_copy().wait_recv()
    last_loads = (
        (own_ref.at[0], pool.at[3]),
        (sibling_ref.at[0], pool.at[4]),
        (ra_ref, pool.at[8]),
        (rb_ref, pool.at[9]),
        (mixed_ref, grad),
    )
    for number, (src, dst) in enumerate(last_loads):
        load(number, src, dst).start()
    for number, (src, dst) in enumerate(last_loads):
        load(number, src, dst).wait()

    @pl.loop(0, rows // 128)
    def _(step):
        at = pl.ds(pl.multiple_of(step * 128, 128), 128)
        total = grad[at, :]
        for i in (3, 4, 8, 9):
            total = total + pool[i, at, :].astype(f32)
        pool[3, at, :] = total.astype(bf16)

    layer_store = pltpu.make_async_copy(pool.at[3], layer_ref, store_sem.at[1])
    layer_store.start()
    expert_last()
    for job in (1, 0, 2, 3):
        advance(job, 4)

    for copy in (far_copy, first_copy, second_copy):
        copy().wait_send()
    for m in range(2):
        ec_copy(m).wait_send()
    for i in range(3):
        ex_copy(i).wait_send()
        ef_copy(i).wait_send()
    for copy in final_copies(1):
        copy.wait()
    for job in range(4):
        for level in range(5):
            halve_copy(job, *jobs[job], level).wait_send()
    layer_store.wait()


def backward_call(vmem_args, any_args):
    f32, bf16 = jnp.float32, jnp.bfloat16
    rows, head = vmem_args[2].shape
    key_width = vmem_args[6].shape[1]
    width = vmem_args[0].shape[0]
    hidden = any_args[13].shape[2]
    block = width // 32
    extra = 2 * key_width + head
    anywhere = pl.BlockSpec(memory_space=pl.ANY)
    inside = pl.BlockSpec(memory_space=pltpu.VMEM)
    shape = jax.ShapeDtypeStruct
    dma = pltpu.SemaphoreType.DMA
    vmem = pltpu.VMEM
    return pl.pallas_call(
        backward_kernel,
        out_shape=(
            shape((block, width), f32),
            shape((block, extra), f32),
            shape((block, width), f32),
            shape((rows, width), bf16),
            shape((rows, width), f32),
            shape((width // 4, hidden), f32),
            shape((width // 4, hidden), f32),
            shape((hidden, width // 4), f32),
            shape((rows, width), bf16),
            shape((rows, width), bf16),
            shape((rows, width), bf16),
        ),
        in_specs=[inside] * len(vmem_args) + [anywhere] * len(any_args),
        out_specs=(inside,) * 3 + (anywhere,) * 8,
        scratch_shapes=[
            vmem((10, rows, width), bf16),
            vmem((width, width), bf16),
            vmem((width, key_width), bf16),
            vmem((width, key_width), bf16),
            vmem((rows, width), f32),
            vmem((rows, width + 2 * key_width), bf16),
            vmem((rows, rows), f32),
            vmem((rows, key_width), f32),
            vmem((rows, key_width), f32),
            vmem((8, width), f32),
            vmem((32, block, width), bf16),
            vmem((31, block, width), bf16),
            vmem((32, block, width // 2), bf16),
            vmem((32, block, width // 2), bf16),
            vmem((15, block, width), bf16),
            vmem((32, block, extra), bf16),
            vmem((31, block, extra), bf16),
            vmem((2, width // 2, hidden), bf16),
            vmem((2, hidden // 2, width // 2), bf16),
            vmem((width // 2, hidden), bf16),
            vmem((hidden // 2, width // 2), bf16),
            vmem((width // 4, hidden), bf16),
            vmem((hidden // 2, width // 4), bf16),
            vmem((width // 2, hidden), bf16),
            vmem((hidden // 2, width // 2), bf16),
            vmem((width // 4, hidden), f32),
            vmem((hidden // 2, width // 4), f32),
            dma((24,)),
            dma((3,)),
            dma((3,)),
            dma((3,)),
            dma((3,)),
            dma((3,)),
            dma((3,)),
            dma((2,)),
            dma((2,)),
            dma((4, 5)),
            dma((4, 5)),
            pltpu.SemaphoreType.REGULAR((2,)),
            dma((10,)),
        ],
        compiler_params=pltpu.CompilerParams(
            collective_id=1, has_side_effects=True, vmem_limit_bytes=64 * 2**20
        ),
        cost_estimate=pl.CostEstimate(
            flops=30 * rows * width * width, bytes_accessed=60 * 2**20, transcendentals=0
        ),
    )(*vmem_args, *any_args)


def local_dense(
    tokens,
    segment_ids,
    routes,
    route_gates,
    attn_gain,
    ffn_gain,
    query_weight,
    key_matrix,
    value_matrix,
    output_weight,
    expert_gate,
    expert_up,
    expert_down,
    cotangent,
):
    experts = lax.axis_size("ep")
    table = jnp.sum(
        jnp.where(
            routes.T[None, :, :] == jnp.arange(experts, dtype=jnp.int32)[:, None, None],
            route_gates.T[None, :, :],
            0.0,
        ),
        axis=1,
    )
    power = -np.arange(HEAD_SIZE // 2, dtype=np.float32) * np.float32(2.0 / HEAD_SIZE)
    inverse = np.float32(BASE) ** power
    angle = np.arange(tokens.shape[0], dtype=np.float32)[:, None] * inverse[None, :]
    cosine = np.cos(angle)
    sine = np.sin(angle)
    small = (
        attn_gain,
        ffn_gain,
        jnp.asarray(np.concatenate([cosine, cosine], axis=1), jnp.float32),
        jnp.asarray(np.concatenate([-sine, sine], axis=1), jnp.float32),
        segment_ids,
    )
    (
        query_rot,
        key_rot,
        value_low,
        log_total,
        attended,
        mixed,
        grad_gu,
        grad_down,
        out_own,
        out_sib,
        own_grad,
        sibling_grad,
        first_grad,
        second_grad,
        _,
        _,
        met_gu,
        met_down,
    ) = forward_call(
        small + (table,),
        (
            tokens,
            query_weight,
            key_matrix,
            value_matrix,
            output_weight,
            cotangent,
            expert_gate[0],
            expert_up[0],
            expert_down[0],
        ),
    )
    (
        query_grad,
        extra_grad,
        output_grad,
        layer_out,
        tokens_grad,
        gate_grad,
        up_grad,
        down_grad,
        *_,
    ) = backward_call(
        small + (log_total, key_rot, value_low),
        (
            own_grad,
            sibling_grad,
            first_grad,
            second_grad,
            mixed,
            cotangent,
            attended,
            query_rot,
            tokens,
            output_weight,
            query_weight,
            key_matrix,
            value_matrix,
            grad_gu,
            grad_down,
            out_own,
            out_sib,
            met_gu,
            met_down,
        ),
    )
    split_k = key_matrix.shape[1]
    split_v = split_k + value_matrix.shape[1]
    gain_sums = extra_grad[:, split_v : split_v + 2] + extra_grad[:, split_v + 2 : split_v + 4]
    return (
        layer_out,
        tokens_grad,
        query_grad,
        extra_grad[:, :split_k],
        extra_grad[:, split_k:split_v],
        output_grad.T,
        gain_sums[:, 0],
        gain_sums[:, 1],
        gate_grad[None],
        up_grad[None],
        down_grad[None],
    )


def solution(mesh):
    in_specs = (
        P(("grp", "ep"), None),
        P(("grp", "ep"), None),
        P(("grp", "ep"), None),
        P(("grp", "ep"), None),
        P(),
        P(),
        P(),
        P(),
        P(),
        P(),
        P("ep", None, None),
        P("ep", None, None),
        P("ep", None, None),
        P(("grp", "ep"), None),
    )
    out_specs = (
        P(("grp", "ep"), None),
        P(("grp", "ep"), None),
        P(("grp", "ep"), None),
        P(("grp", "ep"), None),
        P(("grp", "ep"), None),
        P(None, ("grp", "ep")),
        P(("grp", "ep")),
        P(("grp", "ep")),
        P("ep", "grp", None),
        P("ep", "grp", None),
        P("ep", None, "grp"),
    )
    paired = mesh.shape["grp"] == 4 and mesh.shape["ep"] == 8
    local = local_dense if paired else local_routed
    return jax.shard_map(local, mesh=mesh, in_specs=in_specs, out_specs=out_specs, check_vma=False)
```

```python
import jax
import jax.numpy as jnp
import numpy as np
from jax import lax
from jax.experimental import pallas as pl
from jax.experimental.pallas import tpu as pltpu
from jax.sharding import PartitionSpec as P

HEAD_SIZE = 128


EPS = 1e-06
BASE = 10000.0


def apply_rotary(value_rows, cosine_table, sine_table):
    half = value_rows.shape[-1] // 2
    first = value_rows[..., :half]
    second = value_rows[..., half:]
    return jnp.concatenate(
        [first * cosine_table - second * sine_table, second * cosine_table + first * sine_table],
        axis=-1,
    )


def unrotate(value_rows, cosine_table, sine_table):
    half = value_rows.shape[-1] // 2
    first = value_rows[..., :half]
    second = value_rows[..., half:]
    return jnp.concatenate(
        [first * cosine_table + second * sine_table, second * cosine_table - first * sine_table],
        axis=-1,
    )


def glu_value(gate_val, up_val):
    return jax.nn.gelu(gate_val, approximate=True) * up_val


def scores_of(query_rot, key_rot, allowed):
    score = jnp.einsum(
        "tkgd,skd->kgts", query_rot, key_rot, preferred_element_type=jnp.float32
    ) * HEAD_SIZE ** (-0.5)
    return jnp.where(allowed, score, -1e30)


def local_routed(
    tokens,
    segment_ids,
    routes,
    route_gates,
    attn_gain,
    ffn_gain,
    query_weight,
    key_matrix,
    value_matrix,
    output_weight,
    expert_gate,
    expert_up,
    expert_down,
    cotangent,
):
    length_total, width = tokens.shape
    choose = routes.shape[1]
    local_experts = expert_gate.shape[0]
    owners = lax.axis_size("ep")
    experts = owners * local_experts
    capacity = 3 * length_total * choose // (2 * experts)
    query_heads = query_weight.shape[1] // HEAD_SIZE
    key_heads = key_matrix.shape[1] // HEAD_SIZE
    q_per_kv = query_heads // key_heads
    segment = segment_ids[0]
    padding = segment == jnp.max(segment)
    later = jnp.arange(length_total)[:, None] >= jnp.arange(length_total)[None, :]
    diagonal = jnp.arange(length_total)[:, None] == jnp.arange(length_total)[None, :]
    allowed = (
        later
        & (segment[:, None] == segment[None, :])
        & (jnp.logical_not(padding)[None, :] | diagonal)
    )
    position = jnp.arange(length_total, dtype=jnp.float32)
    inverse = BASE ** (-jnp.arange(HEAD_SIZE // 2, dtype=jnp.float32) * 2.0 / HEAD_SIZE)
    angle = position[:, None] * inverse[None, :]
    cosine_table = jnp.cos(angle)[:, None, :]
    sine_table = jnp.sin(angle)[:, None, :]
    tok_float = tokens.astype(jnp.float32)
    scale_first = lax.rsqrt(jnp.mean(tok_float * tok_float, axis=-1, keepdims=True) + EPS)
    normed_first = tok_float * scale_first
    h_first = (normed_first * attn_gain).astype(jnp.bfloat16)
    query_rows = jnp.dot(h_first, query_weight, preferred_element_type=jnp.float32).reshape(
        length_total, query_heads, HEAD_SIZE
    )
    key_rows = jnp.dot(h_first, key_matrix, preferred_element_type=jnp.float32).reshape(
        length_total, key_heads, HEAD_SIZE
    )
    value_low = jnp.dot(h_first, value_matrix, preferred_element_type=jnp.float32).astype(
        jnp.bfloat16
    )
    value_low = value_low.reshape(length_total, key_heads, HEAD_SIZE)
    query_rot = (
        apply_rotary(query_rows, cosine_table, sine_table)
        .astype(jnp.bfloat16)
        .reshape(length_total, key_heads, q_per_kv, HEAD_SIZE)
    )
    key_rot = apply_rotary(key_rows, cosine_table, sine_table).astype(jnp.bfloat16)
    score = scores_of(query_rot, key_rot, allowed)
    row_max = jnp.max(score, axis=-1, keepdims=True)
    expo = jnp.exp(score - row_max)
    row_sum = jnp.sum(expo, axis=-1, keepdims=True)
    log_total = row_max + jnp.log(row_sum)
    probs_low = (expo / row_sum).astype(jnp.bfloat16)
    attended = jnp.einsum(
        "kgts,skd->tkgd", probs_low, value_low, preferred_element_type=jnp.float32
    )
    attended = attended.reshape(length_total, query_heads * HEAD_SIZE).astype(jnp.bfloat16)
    mixed = tok_float + jnp.dot(attended, output_weight, preferred_element_type=jnp.float32)
    scale_second = lax.rsqrt(jnp.mean(mixed * mixed, axis=-1, keepdims=True) + EPS)
    normed_second = mixed * scale_second
    h_second = (normed_second * ffn_gain).astype(jnp.bfloat16)
    flat_routes = routes.reshape(-1)
    assigns = flat_routes.shape[0]
    onehot = (flat_routes[:, None] == jnp.arange(experts, dtype=jnp.int32)[None, :]).astype(
        jnp.int32
    )
    position_in = jnp.sum(jnp.cumsum(onehot, axis=0) * onehot, axis=1) - 1
    slot_index = flat_routes * capacity + position_in
    source = (
        jnp.full((experts * capacity,), assigns, jnp.int32)
        .at[slot_index]
        .set(jnp.arange(assigns, dtype=jnp.int32))
    )
    token_of = source // choose
    h_ext = jnp.concatenate([h_second, jnp.zeros((1, width), jnp.bfloat16)], axis=0)
    send_rows = h_ext[token_of].reshape(owners, local_experts, capacity, width)
    row_entries = lax.all_to_all(send_rows, "ep", split_axis=0, concat_axis=0, tiled=True)
    gate_val = jnp.einsum(
        "secd,edf->secf", row_entries, expert_gate, preferred_element_type=jnp.float32
    )
    up_val = jnp.einsum(
        "secd,edf->secf", row_entries, expert_up, preferred_element_type=jnp.float32
    )
    act = glu_value(gate_val, up_val).astype(jnp.bfloat16)
    result = jnp.einsum("secf,efd->secd", act, expert_down, preferred_element_type=jnp.float32)
    outputs = (result.astype(jnp.bfloat16), row_entries, gate_val, up_val)
    returned = lax.all_to_all(outputs[0], "ep", split_axis=0, concat_axis=0, tiled=True).reshape(
        experts * capacity, width
    )
    picked = returned[slot_index].reshape(length_total, choose, width).astype(jnp.float32)
    layer_out = (mixed + jnp.sum(route_gates[:, :, None] * picked, axis=1)).astype(jnp.bfloat16)
    grad_out = cotangent.astype(jnp.float32)
    slot_grads = (
        (route_gates[:, :, None] * grad_out[:, None, :])
        .astype(jnp.bfloat16)
        .reshape(assigns, width)
    )
    slot_ext = jnp.concatenate([slot_grads, jnp.zeros((1, width), jnp.bfloat16)], axis=0)
    grad_send = slot_ext[source].reshape(owners, local_experts, capacity, width)
    grad_recv = lax.all_to_all(grad_send, "ep", split_axis=0, concat_axis=0, tiled=True)
    recv_rows = outputs[1]
    gate_val = outputs[2]
    up_val = outputs[3]
    act, act_back = jax.vjp(glu_value, gate_val, up_val)
    act_low = act.astype(jnp.bfloat16)
    down_part = jnp.einsum("secf,secd->efd", act_low, grad_recv, preferred_element_type=jnp.float32)
    act_grad = jnp.einsum(
        "secd,efd->secf", grad_recv, expert_down, preferred_element_type=jnp.float32
    )
    gate_grad_val, up_grad_val = act_back(act_grad)
    gate_low = gate_grad_val.astype(jnp.bfloat16)
    up_low = up_grad_val.astype(jnp.bfloat16)
    gate_part = jnp.einsum(
        "secd,secf->edf", recv_rows, gate_low, preferred_element_type=jnp.float32
    )
    up_part = jnp.einsum("secd,secf->edf", recv_rows, up_low, preferred_element_type=jnp.float32)
    rows_grad = jnp.einsum(
        "secf,edf->secd", gate_low, expert_gate, preferred_element_type=jnp.float32
    )
    rows_grad = rows_grad + jnp.einsum(
        "secf,edf->secd", up_low, expert_up, preferred_element_type=jnp.float32
    )
    rows_back = lax.all_to_all(
        rows_grad.astype(jnp.bfloat16), "ep", split_axis=0, concat_axis=0, tiled=True
    )
    rows_back = rows_back.reshape(experts * capacity, width)
    expert_sums = (
        lax.psum_scatter(
            gate_part.astype(jnp.bfloat16), "grp", scatter_dimension=1, tiled=True
        ).astype(jnp.float32),
        lax.psum_scatter(
            up_part.astype(jnp.bfloat16), "grp", scatter_dimension=1, tiled=True
        ).astype(jnp.float32),
        lax.psum_scatter(
            down_part.astype(jnp.bfloat16), "grp", scatter_dimension=2, tiled=True
        ).astype(jnp.float32),
    )
    second_grad = jnp.sum(
        rows_back[slot_index].reshape(length_total, choose, width).astype(jnp.float32), axis=1
    )
    ffn_gain_part = jnp.sum(second_grad * normed_second, axis=0)
    normed_grad = second_grad * ffn_gain
    mixed_grad = grad_out + scale_second * (
        normed_grad - normed_second * jnp.mean(normed_grad * normed_second, axis=-1, keepdims=True)
    )
    mixed_low = mixed_grad.astype(jnp.bfloat16)
    output_part = jnp.einsum("ti,td->id", attended, mixed_low, preferred_element_type=jnp.float32)
    attended_grad = jnp.einsum(
        "td,id->ti", mixed_low, output_weight, preferred_element_type=jnp.float32
    )
    attended_grad = attended_grad.astype(jnp.bfloat16).reshape(
        length_total, key_heads, q_per_kv, HEAD_SIZE
    )
    probs = jnp.exp(scores_of(query_rot, key_rot, allowed) - log_total)
    probs_again = probs.astype(jnp.bfloat16)
    value_part_grad = jnp.einsum(
        "kgts,tkgd->skd", probs_again, attended_grad, preferred_element_type=jnp.float32
    )
    prob_grad = jnp.einsum(
        "tkgd,skd->kgts", attended_grad, value_low, preferred_element_type=jnp.float32
    )
    inner = jnp.sum(probs * prob_grad, axis=-1, keepdims=True)
    score_grad = (probs * (prob_grad - inner)).astype(jnp.bfloat16)
    qrot_grad = jnp.einsum(
        "kgts,skd->tkgd", score_grad, key_rot, preferred_element_type=jnp.float32
    ) * HEAD_SIZE ** (-0.5)
    krot_grad = jnp.einsum(
        "kgts,tkgd->skd", score_grad, query_rot, preferred_element_type=jnp.float32
    ) * HEAD_SIZE ** (-0.5)
    query_grad_low = unrotate(
        qrot_grad.reshape(length_total, query_heads, HEAD_SIZE), cosine_table, sine_table
    )
    query_grad_low = query_grad_low.astype(jnp.bfloat16).reshape(
        length_total, query_heads * HEAD_SIZE
    )
    key_grad_low = (
        unrotate(krot_grad, cosine_table, sine_table)
        .astype(jnp.bfloat16)
        .reshape(length_total, key_heads * HEAD_SIZE)
    )
    value_grad_low = value_part_grad.astype(jnp.bfloat16).reshape(
        length_total, key_heads * HEAD_SIZE
    )
    query_part = jnp.einsum(
        "td,ti->di", h_first, query_grad_low, preferred_element_type=jnp.float32
    )
    key_part = jnp.einsum("td,ti->di", h_first, key_grad_low, preferred_element_type=jnp.float32)
    value_part = jnp.einsum(
        "td,ti->di", h_first, value_grad_low, preferred_element_type=jnp.float32
    )
    first_grad = jnp.einsum(
        "ti,di->td", query_grad_low, query_weight, preferred_element_type=jnp.float32
    )
    first_grad = first_grad + jnp.einsum(
        "ti,di->td", key_grad_low, key_matrix, preferred_element_type=jnp.float32
    )
    first_grad = first_grad + jnp.einsum(
        "ti,di->td", value_grad_low, value_matrix, preferred_element_type=jnp.float32
    )
    attn_gain_part = jnp.sum(first_grad * normed_first, axis=0)
    normed_first_grad = first_grad * attn_gain
    tokens_grad = mixed_grad + scale_first * (
        normed_first_grad
        - normed_first * jnp.mean(normed_first_grad * normed_first, axis=-1, keepdims=True)
    )
    shared = (
        lax.psum_scatter(query_part, ("grp", "ep"), scatter_dimension=0, tiled=True),
        lax.psum_scatter(key_part, ("grp", "ep"), scatter_dimension=0, tiled=True),
        lax.psum_scatter(value_part, ("grp", "ep"), scatter_dimension=0, tiled=True),
        lax.psum_scatter(output_part, ("grp", "ep"), scatter_dimension=1, tiled=True),
        lax.psum_scatter(attn_gain_part, ("grp", "ep"), scatter_dimension=0, tiled=True),
        lax.psum_scatter(ffn_gain_part, ("grp", "ep"), scatter_dimension=0, tiled=True),
    )
    return (
        layer_out,
        tokens_grad,
        shared[0],
        shared[1],
        shared[2],
        shared[3],
        shared[4],
        shared[5],
        expert_sums[0],
        expert_sums[1],
        expert_sums[2],
    )


def forward_kernel(
    attn_gain_ref, ffn_gain_ref, cos_ref, sin_ref, seg_row_ref, tab_ref, tok_ref,
    wq_ref, wk_ref, wv_ref, wo_ref, dy_ref, gate_ref, up_ref, down_ref,
    query_ref, key_ref, value_ref, lse_ref, att_ref, mixed_ref, grad_gu_ref, grad_down_ref,
    out_own_ref, out_sib_ref, d_own_ref, d_sib_ref, d_first_ref, d_second_ref, part_d_ref,
    part_o_ref, ex_gu_ref, ex_down_ref,
    xb, dyb, tab, w_gu, w_down, sib, far_in, gather_send, gather_recv, tab_send, tab_recv,
    fetch_send, fetch_recv, pass_send, pass_recv, local_sem, part_send, part_recv, keep_sem,
    sum_send, sum_recv, ex_send, ex_recv, store_sem, stage_sem,
):
    f32, bf16 = jnp.float32, jnp.bfloat16
    grp, ep = lax.axis_index("grp"), lax.axis_index("ep")
    core = lax.rem(grp, 2)
    side = grp // 2
    low = lax.rem(ep, 4)
    y, z = lax.rem(low, 2), low // 2
    by_y = ep + 1 - 2 * y
    by_z = ep + 2 - 4 * z
    by_both = by_y + 2 - 4 * z
    by_far = ep + 4 - 8 * (ep // 4)
    first = by_y * (1 - core) + by_z * core
    second = by_z * (1 - core) + by_y * core
    other = grp + 1 - 2 * core
    across = (grp + 2 - 4 * side, ep)
    away = (grp, by_far)
    rows, width = tok_ref.shape
    half = rows // 2
    hidden = gate_ref.shape[1]
    mine = hidden // 2
    head = cos_ref.shape[1]
    heads = width // head
    key_width = wk_ref.shape[1]
    per_key = heads * head // key_width

    def remote(src, dst, send, recv, device):
        return pltpu.make_async_remote_copy(
            src_ref=src, dst_ref=dst, send_sem=send, recv_sem=recv, device_id=device,
            device_id_type=pl.DeviceIdType.MESH,
        )

    members = (
        ((grp, first), 1), ((grp, second), 2), ((grp, by_both), 3), ((other, ep), 4),
        ((other, first), 5), ((other, second), 6), ((other, by_both), 7),
    )
    barrier = pltpu.get_barrier_semaphore()
    for device in [device for device, _ in members] + [across, away]:
        pl.semaphore_signal(barrier, inc=1, device_id=device, device_id_type=pl.DeviceIdType.MESH)
    pl.semaphore_wait(barrier, 9)

    units = pl.ds(pl.multiple_of(core * mine, mine), mine)
    own_weights = (
        (gate_ref.at[:, units], w_gu.at[0, :, pl.ds(0, mine)]),
        (up_ref.at[:, units], w_gu.at[0, :, pl.ds(mine, mine)]),
        (down_ref.at[units, :], w_down.at[0]),
    )
    wide_at = pl.ds(pl.multiple_of(side * (width // 2), width // 2), width // 2)
    deep_at = pl.ds(pl.multiple_of(side * (mine // 2), mine // 2), mine // 2)
    deep_from = pl.ds(pl.multiple_of(core * mine + side * (mine // 2), mine // 2), mine // 2)
    pieces = (
        (gate_ref.at[wide_at, units], w_gu.at[1, wide_at, pl.ds(0, mine)]),
        (up_ref.at[wide_at, units], w_gu.at[1, wide_at, pl.ds(mine, mine)]),
        (down_ref.at[deep_from, :], w_down.at[1, deep_at, :]),
    )

    def fetch_copy(m):
        return remote(*pieces[m], fetch_send.at[m], fetch_recv.at[m], away)

    def pass_copy(m):
        return remote(pieces[m][1], pieces[m][1], pass_send.at[m], pass_recv.at[m], across)

    def load(number, src, dst):
        return pltpu.make_async_copy(src, dst, local_sem.at[number])

    def gather_copy(k, number):
        own, buf = ((xb.at[0], xb), (dy_ref, dyb))[k]
        src, dst, device = (
            (own, 1, (grp, first)), (own, 4, (other, ep)), (own, 2, (grp, second)),
            (buf.at[1], 5, (other, ep)), (buf.at[2], 6, (other, ep)),
            (buf.at[2], 3, (grp, first)), (buf.at[3], 7, (other, ep)),
        )[number]
        if k == 1 and number == 5:
            src, device = buf.at[2 - core], (grp, by_y)
        return remote(
            src, buf.at[dst], gather_send.at[k, number], gather_recv.at[k, number], device
        )

    arrival = {1: 0, 4: 1, 2: 2, 5: 3, 6: 4, 3: 5, 7: 6}

    def start(k, *numbers):
        for number in numbers:
            gather_copy(k, number).start()

    def arrived(k, slot):
        gather_copy(k, arrival[slot]).wait_recv()

    def table_copy(slot):
        device = members[slot - 1][0]
        return remote(tab_ref, tab.at[slot], tab_send.at[slot], tab_recv.at[slot], device)

    fetch_copy(0).start()
    start(1, 0, 1, 2)
    for slot in range(1, 8):
        table_copy(slot).start()
    own_dy = lambda: load(0, dy_ref, dyb.at[0])
    tab[0] = tab_ref[...]

    def dot_nt(a, b):
        return lax.dot_general(a, b, (((1,), (1,)), ((), ())), preferred_element_type=f32)

    def dot_tn(a, b):
        return lax.dot_general(a, b, (((0,), (0,)), ((), ())), preferred_element_type=f32)

    def attention(w_big, w_key, w_value, tok, act, query, key, value, bias, mixed, lse):
        tok_load = load(4, tok_ref, tok)
        query_load = load(5, wq_ref, w_big)
        key_load = load(6, wk_ref, w_key)
        value_load = load(7, wv_ref, w_value)
        for copy in (tok_load, query_load, key_load, value_load):
            copy.start()
        own_dy().start()
        for m, (src, dst) in enumerate(own_weights):
            load(1 + m, src, dst).start()
        segment = jnp.broadcast_to(seg_row_ref[...].astype(f32), (8, rows))
        segment_column = jnp.transpose(segment)[:, :1].astype(jnp.int32)
        position = lax.broadcasted_iota(jnp.int32, (rows, rows), 0)
        other_position = lax.broadcasted_iota(jnp.int32, (rows, rows), 1)
        padding = seg_row_ref[...] == jnp.max(seg_row_ref[...])
        allowed = (
            (other_position <= position)
            & (segment_column == seg_row_ref[...])
            & (jnp.logical_not(padding) | (other_position == position))
        )
        bias[...] = jnp.where(allowed, 0.0, -1e30)
        lse[...] = jnp.zeros_like(lse)
        tok_load.wait()

        @pl.loop(0, rows // 128)
        def _(step):
            at = pl.ds(pl.multiple_of(step * 128, 128), 128)
            entry = tok[at, :].astype(f32)
            factor = lax.rsqrt(jnp.mean(entry * entry, axis=-1, keepdims=True) + EPS)
            act[at, :] = (entry * factor * attn_gain_ref[...][None, :]).astype(bf16)

        def turn(entry, at):
            swapped = pltpu.roll(entry, head // 2, 1)
            return entry * cos_ref[at, :] + swapped * sin_ref[at, :]

        key_load.wait()
        value_load.wait()
        key_rows = jnp.dot(act[...], w_key[...], preferred_element_type=f32)
        for kv in range(key_width // head):
            columns = slice(kv * head, (kv + 1) * head)
            key[:, columns] = turn(key_rows[:, columns], slice(None)).astype(bf16)
        value[...] = jnp.dot(act[...], w_value[...], preferred_element_type=f32).astype(bf16)
        query_load.wait()
        for tile in range(width // 256):
            columns = slice(tile * 256, (tile + 1) * 256)
            entry = jnp.dot(act[...], w_big[:, columns], preferred_element_type=f32)
            for part in range(256 // head):
                columns = slice(part * head, (part + 1) * head)
                to = slice(tile * 256 + part * head, tile * 256 + (part + 1) * head)
                query[:, to] = turn(entry[:, columns], slice(None)).astype(bf16)
        out_load = load(8, wo_ref, w_big)
        out_load.start()
        stores = [
            pltpu.make_async_copy(src, dst, store_sem.at[i])
            for i, (src, dst) in enumerate(((query, query_ref), (key, key_ref), (value, value_ref)))
        ]
        for copy in stores:
            copy.start()
        scale = head ** (-0.5)
        lane = lax.broadcasted_iota(jnp.int32, (half, head), 1)
        for number in range(heads):
            columns = slice(number * head, (number + 1) * head)
            kv = number // per_key
            kv_columns = slice(kv * head, (kv + 1) * head)
            for part in range(2):
                at = slice(part * half, (part + 1) * half)
                seen = slice(0, (part + 1) * half)
                score = dot_nt(query[at, columns], key[seen, kv_columns]) * scale + bias[at, seen]
                top = jnp.max(score, axis=-1, keepdims=True)
                expo = jnp.exp(score - top)
                total = jnp.sum(expo, axis=-1, keepdims=True)
                lse[at, :] = jnp.where(lane == number, top + jnp.log(total), lse[at, :])
                probs = (expo / total).astype(bf16)
                mixed_value = jnp.dot(probs, value[seen, kv_columns], preferred_element_type=f32)
                act[at, columns] = mixed_value.astype(bf16)
        fetch_copy(1).start()
        out_load.wait()
        att_store = pltpu.make_async_copy(act, att_ref, store_sem.at[3])
        att_store.start()
        lse_store = pltpu.make_async_copy(lse, lse_ref, store_sem.at[4])
        lse_store.start()
        for part in range(4):
            at = slice(part * rows // 4, (part + 1) * rows // 4)
            total = tok[at, :].astype(f32) + jnp.dot(
                act[at, :], w_big[...], preferred_element_type=f32
            )
            mixed[at, :] = total
            factor = lax.rsqrt(jnp.mean(total * total, axis=-1, keepdims=True) + EPS)
            xb[0, at, :] = (total * factor * ffn_gain_ref[...][None, :]).astype(bf16)
        start(0, 0, 1, 2)
        mixed_store = pltpu.make_async_copy(mixed, mixed_ref, store_sem.at[5])
        mixed_store.start()
        for copy in stores + [att_store, lse_store, mixed_store]:
            copy.wait()

    vmem = pltpu.VMEM
    pl.run_scoped(
        attention,
        vmem((width, width), bf16),
        vmem((width, key_width), bf16),
        vmem((width, key_width), bf16),
        vmem((rows, width), bf16),
        vmem((rows, width), bf16),
        vmem((rows, width), bf16),
        vmem((rows, key_width), bf16),
        vmem((rows, key_width), bf16),
        vmem((rows, rows), f32),
        vmem((rows, width), f32),
        vmem((rows, head), f32),
    )

    def experts(acc_gu, acc_down, act_s, gu_s, dz_s, stage):
        own_dy().wait()
        for m, (src, dst) in enumerate(own_weights):
            load(1 + m, src, dst).wait()
        for slot in range(1, 8):
            table_copy(slot).wait_send()
            table_copy(slot).wait_recv()
        acc_gu[...] = jnp.zeros_like(acc_gu)
        acc_down[...] = jnp.zeros_like(acc_down)

        def gates(slot, hosted):
            block = jnp.transpose(tab[slot])
            lane = lax.broadcasted_iota(jnp.int32, block.shape, 1)
            return jnp.sum(jnp.where(lane == hosted, block, 0.0), axis=1, keepdims=True)

        c0 = 0.7978845608028654
        c1 = 0.044715

        def work(which, slot, hosted, deliver):
            column = gates(slot, hosted)
            for part in range(2):
                at = pl.ds(part * half, half)
                gate = column[part * half : (part + 1) * half]
                gu = jnp.dot(xb[slot, at, :], w_gu[which], preferred_element_type=f32)
                dz = (gate * dyb[slot, at, :].astype(f32)).astype(bf16)
                dz_s[at, :] = dz
                da = dot_nt(dz, w_down[which])
                g, u = gu[:, :mine], gu[:, mine:]
                square = g * g
                t = jnp.tanh(c0 * (g + c1 * square * g))
                gelu = 0.5 * g * (1.0 + t)
                slope = 0.5 * (1.0 + t) + 0.5 * g * (1.0 - t * t) * (c0 * (1.0 + 3.0 * c1 * square))
                act_s[at, :] = (gelu * u).astype(bf16)
                gu_s[at, :mine] = (da * u * slope).astype(bf16)
                gu_s[at, mine:] = (da * gelu).astype(bf16)
            for part in range(3):
                at = pl.ds(part * (width // 3), width // 3)
                acc_gu[which, at, :] += dot_tn(xb[slot, :, at], gu_s[...])
                acc_down[which, :, at] += dot_tn(act_s[...], dz_s[:, at])
            for part in range(2):
                at = pl.ds(part * half, half)
                gate = column[part * half : (part + 1) * half]
                dx = dot_nt(gu_s[at, :], w_gu[which])
                result = gate * jnp.dot(act_s[at, :], w_down[which], preferred_element_type=f32)
                deliver(at, dx, result)

        def slot_up(step):
            pair, odd = step // 2, lax.rem(step, 2)
            middle = (lax.rem(pair, 2) * (1 - pair // 3) + pair // 2 * (1 - pair // 3))
            turned = core * (1 - odd) + (1 - core) * odd
            swapped = middle * (3 - 2 * pair) * turned
            return pair + swapped + 4 * odd

        def stage_out(k, step):
            buf = lax.rem(step, 2)
            dst = (part_d_ref, part_o_ref)[k].at[slot_up(step)]
            return pltpu.make_async_copy(stage.at[k, buf], dst, stage_sem.at[k, buf])

        @pl.loop(0, 8)
        def _(step):
            def at_step(number):
                return pl.when(step == number)

            @at_step(1)
            def _():
                fetch_copy(2).start()
                arrived(0, 4)
                arrived(1, 4)

            @at_step(2)
            def _():
                arrived(1, 1)
                start(1, 3)
                arrived(1, 2)
                start(1, 5, 4)
                fetch_copy(0).wait_recv()
                pass_copy(0).start()
                @pl.when(core == 0)
                def _():
                    arrived(0, 1)
                    start(0, 3)

                @pl.when(core == 1)
                def _():
                    arrived(0, 2)
                    start(0, 5, 4)


            @at_step(3)
            def _():
                @pl.when(core == 0)
                def _():
                    arrived(0, 6)
                    arrived(1, 6)

                @pl.when(core == 1)
                def _():
                    arrived(0, 5)
                    arrived(1, 5)


            @at_step(4)
            def _():
                @pl.when(core == 0)
                def _():
                    arrived(0, 2)
                    start(0, 5, 4)

                @pl.when(core == 1)
                def _():
                    arrived(0, 1)
                    start(0, 3)

                for m in (1, 2):
                    fetch_copy(m).wait_recv()
                    pass_copy(m).start()

            @at_step(5)
            def _():
                @pl.when(core == 0)
                def _():
                    arrived(0, 5)
                    arrived(1, 5)

                @pl.when(core == 1)
                def _():
                    arrived(0, 6)
                    arrived(1, 6)

                arrived(1, 3)
                start(1, 6)

            @at_step(6)
            def _():
                arrived(0, 3)
                start(0, 6)

            @at_step(7)
            def _():
                arrived(0, 7)
                arrived(1, 7)

            @pl.when(step >= 2)
            def _():
                stage_out(0, step - 2).wait()
                stage_out(1, step - 2).wait()

            buf = lax.rem(step, 2)

            def deliver(at, dx, result):
                stage[0, buf, at, :] = dx.astype(bf16)
                stage[1, buf, at, :] = result.astype(bf16)

            work(0, slot_up(step), ep, deliver)
            stage_out(0, step).start()
            stage_out(1, step).start()

        for k in range(2):
            for step in (6, 7):
                stage_out(k, step).wait()
        for k in range(2):
            for number in range(7):
                gather_copy(k, number).wait_send()

        def grad_copies(which):
            return (
                pltpu.make_async_copy(w_gu.at[which], grad_gu_ref.at[which], store_sem.at[6 + 2 * which]),
                pltpu.make_async_copy(
                    w_down.at[which], grad_down_ref.at[which], store_sem.at[7 + 2 * which]
                ),
            )

        def slot_down(step):
            pair = step // 2
            return 3 - 2 * lax.rem(pair, 2) - pair // 2 + 4 * (1 - lax.rem(step, 2))

        def stage_in(k, step):
            buf = lax.rem(step, 2)
            src = (part_d_ref, part_o_ref)[k].at[slot_down(step)]
            return pltpu.make_async_copy(src, stage.at[k, buf], stage_sem.at[k, buf])

        stage_in(0, 0).start()
        stage_in(1, 0).start()
        def flush(which):
            w_gu[which] = acc_gu[which].astype(bf16)
            w_down[which] = acc_down[which].astype(bf16)
            for copy in grad_copies(which):
                copy.start()

        def exchange(m):
            at = pl.ds(pl.multiple_of((1 - side) * (width // 2), width // 2), width // 2)
            src = w_down.at[0, :, at] if m else w_gu.at[0, at, :]
            return remote(src, (ex_gu_ref, ex_down_ref)[m], ex_send.at[m], ex_recv.at[m], across)

        for m in range(3):
            pass_copy(m).wait()
            fetch_copy(m).wait_send()

        def keep_copy(j):
            return pltpu.make_async_copy(dyb.at[j], out_own_ref.at[j], keep_sem.at[j])

        def grad_part(j):
            dst = d_sib_ref if j == 0 else sib.at[j - 1]
            return remote(xb.at[4 + j], dst, part_send.at[0, j], part_recv.at[0, j], (other, ep))

        def out_part(j):
            return remote(
                dyb.at[4 + j], out_sib_ref.at[j], part_send.at[1, j], part_recv.at[1, j], (other, ep)
            )

        own_grad = lambda: pltpu.make_async_copy(xb.at[0], d_own_ref, keep_sem.at[4])
        send_far = lambda: remote(xb.at[3], far_in, sum_send.at[0], sum_recv.at[0], (grp, first))
        send_first = lambda: remote(
            xb.at[1], d_first_ref, sum_send.at[1], sum_recv.at[1], (grp, first)
        )
        send_second = lambda: remote(
            xb.at[2], d_second_ref, sum_send.at[2], sum_recv.at[2], (grp, second)
        )

        def add_into(dst, *others):
            @pl.loop(0, rows // 128)
            def _(i):
                at = pl.ds(pl.multiple_of(i * 128, 128), 128)
                total = dst[at, :].astype(f32)
                for part in others:
                    total = total + part[at, :].astype(f32)
                dst[at, :] = total.astype(bf16)

        @pl.loop(0, 8)
        def _(step):
            def at_step(number):
                return pl.when(step == number)

            stage_in(0, step).wait()
            stage_in(1, step).wait()

            @pl.when(step < 7)
            def _():
                stage_in(0, step + 1).start()
                stage_in(1, step + 1).start()

            buf = lax.rem(step, 2)
            slot = slot_down(step)

            def deliver(at, dx, result):
                xb[slot, at, :] = (dx + stage[0, buf, at, :].astype(f32)).astype(bf16)
                dyb[slot, at, :] = (result + stage[1, buf, at, :].astype(f32)).astype(bf16)

            work(1, slot, ep + 4 - 8 * (ep // 4), deliver)
            for number, j in enumerate((3, 1, 2, 0)):

                @at_step(2 * number)
                def _(j=j):
                    grad_part(j).start()
                    out_part(j).start()

                @at_step(2 * number + 1)
                def _(j=j):
                    keep_copy(j).start()

            @at_step(1)
            def _():
                grad_part(3).wait_recv()
                add_into(xb.at[3], sib.at[2])
                send_far().start()
                flush(0)
                for m in range(2):
                    exchange(m).start()

            @at_step(3)
            def _():
                grad_part(1).wait_recv()
                add_into(xb.at[1], sib.at[0])
                send_first().start()

            @at_step(5)
            def _():
                grad_part(2).wait_recv()
                send_far().wait_recv()
                add_into(xb.at[2], sib.at[1], far_in)
                send_second().start()

        own_grad().start()
        flush(1)
        for j in range(4):
            grad_part(j).wait_send()
            out_part(j).wait()
            keep_copy(j).wait()
        grad_part(0).wait_recv()
        own_grad().wait()
        send_far().wait_send()
        send_first().wait()
        send_second().wait()
        for which in range(2):
            for copy in grad_copies(which):
                copy.wait()
            exchange(which).wait()

    pl.run_scoped(
        experts,
        vmem((2, width, hidden), f32),
        vmem((2, mine, width), f32),
        vmem((rows, mine), bf16),
        vmem((rows, hidden), bf16),
        vmem((rows, width), bf16),
        vmem((2, 2, rows, width), bf16),
    )


def forward_call(vmem_args, any_args):
    f32, bf16 = jnp.float32, jnp.bfloat16
    rows, width = any_args[0].shape
    head = vmem_args[2].shape[1]
    key_width = any_args[2].shape[1]
    hidden = any_args[6].shape[1]
    anywhere = pl.BlockSpec(memory_space=pl.ANY)
    inside = pl.BlockSpec(memory_space=pltpu.VMEM)
    shape = jax.ShapeDtypeStruct
    dma = pltpu.SemaphoreType.DMA
    vmem = pltpu.VMEM
    chunk = shape((rows, width), bf16)
    four = shape((4, rows, width), bf16)
    eight = shape((8, rows, width), bf16)
    return pl.pallas_call(
        forward_kernel,
        out_shape=(
            chunk,
            shape((rows, key_width), bf16),
            shape((rows, key_width), bf16),
            shape((rows, head), f32),
            chunk,
            shape((rows, width), f32),
            shape((2, width, hidden), bf16),
            shape((2, hidden // 2, width), bf16),
            four,
            four,
            chunk,
            chunk,
            chunk,
            chunk,
            eight,
            eight,
            shape((width // 2, hidden), bf16),
            shape((hidden // 2, width // 2), bf16),
        ),
        in_specs=[inside] * len(vmem_args) + [anywhere] * len(any_args),
        out_specs=(anywhere,) * 18,
        scratch_shapes=[
            vmem((8, rows, width), bf16),
            vmem((8, rows, width), bf16),
            vmem((8,) + vmem_args[5].shape, f32),
            vmem((2, width, hidden), bf16),
            vmem((2, hidden // 2, width), bf16),
            vmem((3, rows, width), bf16),
            vmem((rows, width), bf16),
            dma((2, 7)),
            dma((2, 7)),
            dma((8,)),
            dma((8,)),
            dma((3,)),
            dma((3,)),
            dma((3,)),
            dma((3,)),
            dma((9,)),
            dma((2, 4)),
            dma((2, 4)),
            dma((5,)),
            dma((3,)),
            dma((3,)),
            dma((2,)),
            dma((2,)),
            dma((10,)),
            dma((2, 2)),
        ],
        compiler_params=pltpu.CompilerParams(
            collective_id=0, has_side_effects=True, vmem_limit_bytes=64 * 2**20
        ),
        cost_estimate=pl.CostEstimate(
            flops=160 * rows * width * hidden, bytes_accessed=60 * 2**20, transcendentals=0
        ),
    )(*vmem_args, *any_args)


def backward_kernel(
    attn_gain_ref, ffn_gain_ref, cos_ref, sin_ref, seg_row_ref, lse_ref, key_ref,
    value_ref, second0_ref, second1_ref, second2_ref, second3_ref, mixed_ref, cot_ref, att_ref,
    query_ref, tok_ref, wo_ref, wq_ref, wk_ref, wv_ref, ggu_ref, gd_ref, own_ref, sibling_ref,
    first_gu_ref, first_down_ref,
    query_out, kv_out, out_out, tokens_ref, gate_out, up_out, down_out, ra_ref, rb_ref, rf_ref,
    pool, w_big, w_key, w_value, grad, proj, bias, key_acc, value_acc, gain_acc,
    out_buf, out_land, query_buf, later_buf, query_land, kv_buf, kv_land,
    ex_gu, ex_down, ef_gu, ef_down, ec_gu, ec_down, kept_gu, kept_down, stage, stage_down, load_sem, out_send, out_recv, ex_send, ex_recv, ef_send, ef_recv, ec_send, ec_recv,
    halve_send, halve_recv, free_sem, store_sem,
):
    f32, bf16 = jnp.float32, jnp.bfloat16
    grp, ep = lax.axis_index("grp"), lax.axis_index("ep")
    core = lax.rem(grp, 2)
    x = grp // 2
    y = lax.rem(ep, 2)
    z_low = lax.rem(ep // 2, 2)
    z_high = ep // 4
    by_y = (grp, ep + 1 - 2 * y)
    by_z = (grp, ep + 2 - 4 * z_low)
    by_far = (grp, ep + 4 - 8 * z_high)
    by_core = (grp + 1 - 2 * core, ep)
    by_x = (grp + 2 - 4 * x, ep)
    first = (grp, by_y[1] * (1 - core) + by_z[1] * core)
    second = (grp, by_z[1] * (1 - core) + by_y[1] * core)
    rows, width = grad.shape
    head = cos_ref.shape[1]
    heads = width // head
    key_width = key_ref.shape[1]
    per_key = heads * head // key_width
    block = width // 32

    def remote(src, dst, send, recv, device):
        return pltpu.make_async_remote_copy(
            src_ref=src, dst_ref=dst, send_sem=send, recv_sem=recv, device_id=device,
            device_id_type=pl.DeviceIdType.MESH,
        )

    partners = (by_core, by_y, by_z, by_x, by_far)
    barrier = pltpu.get_barrier_semaphore()
    for device in partners:
        pl.semaphore_signal(barrier, inc=1, device_id=device, device_id_type=pl.DeviceIdType.MESH)
    pl.semaphore_wait(barrier, 5)

    wide_half = width // 2
    quarter = width // 4
    mine = gd_ref.shape[1]
    ex_dst = (ex_gu, ex_down)

    def part(ref, m, index, size):
        at = pl.ds(pl.multiple_of(index * size, size), size)
        return ref.at[:, at] if m == 1 else ref.at[at, :]

    def piece(i):
        at = pl.ds(i * quarter, quarter)
        if i == 2:
            return part(gd_ref.at[1], 1, 1 - x, wide_half), ex_down.at[1], ef_down
        start = pl.multiple_of((1 - x) * wide_half + i * quarter, quarter)
        return ggu_ref.at[1, pl.ds(start, quarter), :], ex_gu.at[1, at, :], ef_gu.at[at, :]

    def ex_copy(i):
        src, dst, _ = piece(i)
        return remote(src, dst, ex_send.at[i], ex_recv.at[i], by_x)

    def ef_copy(i):
        _, src, dst = piece(i)
        return remote(src, dst, ef_send.at[i], ef_recv.at[i], by_far)

    def ec_copy(m):
        src = part(ex_dst[m].at[0], m, 1 - core, quarter)
        return remote(src, (ec_gu, ec_down)[m], ec_send.at[m], ec_recv.at[m], by_core)

    def kept_copy(which, m):
        src = part((ggu_ref, gd_ref)[m].at[which], m, x, wide_half)
        return pltpu.make_async_copy(src, (kept_gu, kept_down)[m], load_sem.at[22 + m])

    def load(number, src, dst):
        return pltpu.make_async_copy(src, dst, load_sem.at[number])

    ex_copy(0).start()
    loads = (
        (own_ref.at[3], pool.at[6]),
        (sibling_ref.at[3], pool.at[9]),
        (own_ref.at[1], pool.at[5]),
        (sibling_ref.at[1], pool.at[8]),
        (second0_ref, pool.at[1]),
        (second1_ref, pool.at[2]),
        (second2_ref, pool.at[3]),
        (second3_ref, pool.at[4]),
        (mixed_ref, grad),
        (cot_ref, pool.at[0]),
        (wo_ref, w_big),
        (own_ref.at[2], pool.at[7]),
    )
    for number, (src, dst) in enumerate(loads):
        load(number, src, dst).start()

    def wait_load(number):
        load(number, *loads[number]).wait()

    def add_into(dst, *others):
        @pl.loop(0, rows // 128)
        def _(step):
            at = pl.ds(pl.multiple_of(step * 128, 128), 128)
            total = dst[at, :].astype(f32)
            for other in others:
                total = total + other[at, :].astype(f32)
            dst[at, :] = total.astype(bf16)

    def merge(dst, other):
        @pl.loop(0, dst.shape[0] // 128)
        def _(step):
            at = pl.ds(pl.multiple_of(step * 128, 128), 128)
            dst[at, :] = (dst[at, :].astype(f32) + other[at, :].astype(f32)).astype(bf16)

    def expert_piece(i):
        if i != 1:
            kept_copy(1, i // 2).wait()
        ex_copy(i).wait_recv()
        merge(piece(i)[1], kept_down if i == 2 else kept_gu.at[pl.ds(i * quarter, quarter), :])
        ef_copy(i).start()
        if i > 0:
            kept_copy(0, i - 1).start()

    def expert_own():
        for m in range(2):
            kept_copy(0, m).wait()
            arrived_copies[m].wait()
            merge(ex_dst[m].at[0], (kept_gu, kept_down)[m])

    def expert_third():
        for i in range(3):
            ef_copy(i).wait_recv()
        for m in range(2):
            merge(ex_dst[m].at[0], (ef_gu, ef_down)[m])
            ec_copy(m).start()
        at = pl.ds(pl.multiple_of(core * quarter, quarter), quarter)
        stage[...] = ex_gu[0, at, :].astype(f32)
        stage_down[...] = ex_down[0, :, at].astype(f32)
        for copy in final_copies(0):
            copy.start()

    far_copy = lambda: remote(pool.at[6], rf_ref, out_send.at[0], out_recv.at[0], first)
    first_copy = lambda: remote(pool.at[5], ra_ref, out_send.at[1], out_recv.at[1], first)
    second_copy = lambda: remote(pool.at[7], rb_ref, out_send.at[2], out_recv.at[2], second)
    wait_load(0)
    wait_load(1)
    add_into(pool.at[6], pool.at[9])
    far_copy().start()
    wait_load(2)
    wait_load(3)
    add_into(pool.at[5], pool.at[8])
    first_copy().start()
    sib2 = lambda: load(12, sibling_ref.at[2], pool.at[8])
    sib2().start()
    arrived_copies = [
        load(20 + m, (first_gu_ref, first_down_ref)[m], ex_dst[m].at[0]) for m in range(2)
    ]
    for m in range(2):
        arrived_copies[m].start()
        kept_copy(1, m).start()

    for number in range(4, 10):
        wait_load(number)
    gain_acc[...] = jnp.zeros_like(gain_acc)

    @pl.loop(0, rows // 128)
    def _(step):
        at = pl.ds(pl.multiple_of(step * 128, 128), 128)
        value = grad[at, :]
        scale = lax.rsqrt(jnp.mean(value * value, axis=-1, keepdims=True) + EPS)
        normed = value * scale
        down = (
            pool[1, at, :].astype(f32)
            + pool[2, at, :].astype(f32)
            + pool[3, at, :].astype(f32)
            + pool[4, at, :].astype(f32)
        )
        product = down * normed
        gain_acc[1:2, :] += jnp.sum(product, axis=0, keepdims=True)
        mean = jnp.mean(product * ffn_gain_ref[...][None, :], axis=-1, keepdims=True)
        result = pool[0, at, :].astype(f32) + scale * (down * ffn_gain_ref[...][None, :] - normed * mean)
        grad[at, :] = result
        pool[3, at, :] = result.astype(bf16)

    att_load = lambda: load(13, att_ref, pool.at[1])
    query_load = lambda: load(14, query_ref, pool.at[2])
    tok_load = lambda: load(15, tok_ref, pool.at[0])
    key_weight_load = lambda: load(16, wk_ref, w_key)
    value_weight_load = lambda: load(17, wv_ref, w_value)
    for copy in (att_load, query_load, tok_load, key_weight_load, value_weight_load):
        copy().start()

    segment = jnp.broadcast_to(seg_row_ref[...].astype(f32), (8, rows))
    segment_column = jnp.transpose(segment)[:, :1].astype(jnp.int32)
    position = lax.broadcasted_iota(jnp.int32, (rows, rows), 0)
    other_position = lax.broadcasted_iota(jnp.int32, (rows, rows), 1)
    padding = seg_row_ref[...] == jnp.max(seg_row_ref[...])
    allowed = (
        (other_position <= position)
        & (segment_column == seg_row_ref[...])
        & (jnp.logical_not(padding) | (other_position == position))
    )
    bias[...] = jnp.where(allowed, 0.0, -1e30)

    def dot_nt(a, b):
        return lax.dot_general(a, b, (((1,), (1,)), ((), ())), preferred_element_type=f32)

    def dot_tn(a, b):
        return lax.dot_general(a, b, (((0,), (0,)), ((), ())), preferred_element_type=f32)

    far_levels = ((z_low, by_z), (z_high, by_far))
    orders = (
        ((core, by_core), (y, by_y), (x, by_x)) + far_levels,
        ((core, by_core), (x, by_x), (y, by_y)) + far_levels,
    )
    offsets = (0, 16, 24, 28, 30)
    places = []
    for levels in orders:
        starts = [0]
        for level, (bit, _) in enumerate(levels):
            starts.append(starts[-1] + bit * (16 >> level))
        places.append(starts)

    def landing(job, land, level):
        size = 16 >> level
        if job in (1, 2):
            columns = pl.ds((job - 1) * (width // 2), width // 2)
            if level > 0:
                return query_land.at[pl.ds(offsets[level] - 16, size), :, columns]
            return out_land.at[pl.ds(0, size), :, columns]
        return land.at[pl.ds(offsets[level], size)]

    def halve_copy(job, buf, land, level):
        bit, device = orders[min(job, 1)][level]
        starts = places[min(job, 1)]
        size = 16 >> level
        return remote(
            buf.at[pl.ds(starts[level] + (1 - bit) * size, size)],
            landing(job, land, level),
            halve_send.at[job, level],
            halve_recv.at[job, level],
            device,
        )

    def absorb(job, buf, land, level, result=None):
        halve_copy(job, buf, land, level).wait_recv()
        starts = places[min(job, 1)]
        size = 16 >> level
        arrivals = landing(job, land, level)
        if result is None:

            @pl.loop(0, size)
            def _(i):
                at = starts[level + 1] + i
                buf[at] = (buf[at].astype(f32) + arrivals[i].astype(f32)).astype(bf16)

        else:
            result[...] = buf[starts[5]].astype(f32) + arrivals[0].astype(f32)
        if job == 0 and level == 0:
            for later in range(2):
                pl.semaphore_signal(
                    free_sem.at[later], inc=1, device_id=by_core,
                    device_id_type=pl.DeviceIdType.MESH,
                )
        if level < 4:
            launch(job, level + 1)

    jobs = (
        (out_buf, out_land), (query_buf, out_land), (later_buf, out_land), (kv_buf, kv_land)
    )

    def launch(job, level):
        if job in (1, 2) and level == 0:
            pl.semaphore_wait(free_sem.at[job - 1], 1)
        halve_copy(job, *jobs[job], level).start()

    def begin(job):
        launch(job, 0)

    def advance(job, level):
        results = (
            out_out,
            query_out.at[:, pl.ds(0, width // 2)],
            query_out.at[:, pl.ds(width // 2, width // 2)],
            kv_out,
        )
        absorb(job, *jobs[job], level, results[job] if level == 4 else None)

    def place(buf, tile, value, columns):
        for b in range(8):
            high, low, odd = b >> 2, (b >> 1) & 1, b & 1
            middle = odd * 2 + (tile >> 1) if buf is out_buf else (tile >> 1) * 2 + odd
            to = (((tile & 1) * 4 + middle) * 2 + low) * 2 + high
            buf[to, :, columns] = value[b * block : (b + 1) * block].astype(bf16)

    ex_copy(1).start()
    att_load().wait()
    for tile in range(4):
        at = slice(tile * 8 * block, (tile + 1) * 8 * block)
        place(out_buf, tile, dot_tn(pool[3, :, at], pool[1]), slice(None))
    begin(0)
    wait_load(10)
    for half in range(2):
        at = slice(half * rows // 2, (half + 1) * rows // 2)
        pool[4, at, :] = dot_nt(pool[3, at, :], w_big[...]).astype(bf16)
    query_weight_load = lambda: load(18, wq_ref, w_big)
    query_weight_load().start()
    ex_copy(2).start()
    expert_piece(0)

    tok_load().wait()

    def first_norm(at):
        value = pool[0, at, :].astype(f32)
        scale = lax.rsqrt(jnp.mean(value * value, axis=-1, keepdims=True) + EPS)
        return scale, value * scale

    @pl.loop(0, rows // 128)
    def _(step):
        at = pl.ds(pl.multiple_of(step * 128, 128), 128)
        pool[1, at, :] = (first_norm(at)[1] * attn_gain_ref[...][None, :]).astype(bf16)

    def send_second():
        wait_load(11)
        sib2().wait()
        far_copy().wait_recv()
        far_load = load(19, rf_ref, pool.at[9])
        far_load.start()
        far_load.wait()
        add_into(pool.at[7], pool.at[8], pool.at[9])
        second_copy().start()

    def final_copies(which):
        own = core * (1 - which) + (1 - core) * which
        units = pl.ds(pl.multiple_of(own * mine, mine), mine)
        pairs = (
            (stage.at[:, pl.ds(0, mine)], gate_out.at[:, units]),
            (stage.at[:, pl.ds(mine, mine)], up_out.at[:, units]),
            (stage_down, down_out.at[units, :]),
        )
        return [
            pltpu.make_async_copy(src, dst, store_sem.at[4 + 3 * which + i])
            for i, (src, dst) in enumerate(pairs)
        ]

    def expert_last():
        for copy in final_copies(0):
            copy.wait()
        for m in range(2):
            ec_copy(m).wait_recv()
        stage[...] = ec_gu[...].astype(f32)
        stage_down[...] = ec_down[...].astype(f32)
        for copy in final_copies(1):
            copy.start()

    def turn_back(value, at):
        swapped = pltpu.roll(value, head // 2, 1)
        return value * cos_ref[at, :] - swapped * sin_ref[at, :]

    scale = head ** (-0.5)
    query_load().wait()
    key_acc[...] = jnp.zeros_like(key_acc)
    value_acc[...] = jnp.zeros_like(value_acc)

    def place_query(part, buf):
        columns = slice(part * width // 2, (part + 1) * width // 2)
        for tile in range(4):
            at = slice(tile * 8 * block, (tile + 1) * 8 * block)
            place(buf, tile, dot_tn(pool[1, :, at], proj[:, columns]), slice(None))
        begin(1 + part)

    def between(number):
        if number == 1:
            advance(0, 0)
        elif number == 3:
            expert_piece(1)
        elif number == 5:
            place_query(0, query_buf)
        elif number == 7:
            send_second()
        elif number == 8:
            advance(1, 0)
        elif number == 10:
            expert_piece(2)

    for number in range(heads):
        columns = slice(number * head, (number + 1) * head)
        kv = number // per_key
        kv_columns = slice(kv * head, (kv + 1) * head)
        for half in range(2):
            at = slice(half * rows // 2, (half + 1) * rows // 2)
            seen = slice(0, (half + 1) * rows // 2)
            q = pool[2, at, columns]
            da = pool[4, at, columns]
            k = key_ref[seen, kv_columns]
            score = dot_nt(q, k) * scale + bias[at, seen]
            probs = jnp.exp(score - lse_ref[at, number : number + 1])
            dprob = dot_nt(da, value_ref[seen, kv_columns])
            inner = jnp.sum(probs * dprob, axis=-1, keepdims=True)
            dscore = (probs * (dprob - inner)).astype(bf16)
            value_acc[seen, kv_columns] += dot_tn(probs.astype(bf16), da)
            key_acc[seen, kv_columns] += dot_tn(dscore, q)
            dq = jnp.dot(dscore, k, preferred_element_type=f32) * scale
            proj[at, columns] = turn_back(dq, at).astype(bf16)
        between(number)

    for kv in range(key_width // head):
        columns = slice(kv * head, (kv + 1) * head)
        to = slice(width + kv * head, width + (kv + 1) * head)
        proj[:, to] = turn_back(key_acc[:, columns] * scale, slice(None)).astype(bf16)
        to = slice(width + key_width + kv * head, width + key_width + (kv + 1) * head)
        proj[:, to] = value_acc[:, columns].astype(bf16)

    place_query(1, later_buf)
    for tile in range(4):
        at = slice(tile * 8 * block, (tile + 1) * 8 * block)
        place(kv_buf, tile, dot_tn(pool[1, :, at], proj[:, width:]), slice(0, 2 * key_width))
    query_weight_load().wait()
    key_weight_load().wait()
    value_weight_load().wait()
    for quarter_step in range(4):
        at = slice(quarter_step * rows // 4, (quarter_step + 1) * rows // 4)
        down = dot_nt(proj[at, :width], w_big[...])
        down = down + dot_nt(proj[at, width : width + key_width], w_key[...])
        down = down + dot_nt(proj[at, width + key_width :], w_value[...])
        factor, normed = first_norm(at)
        product = down * normed
        gain_acc[0:1, :] += jnp.sum(product, axis=0, keepdims=True)
        mean = jnp.mean(product * attn_gain_ref[...][None, :], axis=-1, keepdims=True)
        grad[at, :] = grad[at, :] + factor * (down * attn_gain_ref[...][None, :] - normed * mean)
        if quarter_step == 0:
            advance(2, 0)
        elif quarter_step == 1:
            advance(1, 1)
        elif quarter_step == 2:
            expert_own()
    tokens_store = lambda: pltpu.make_async_copy(grad, tokens_ref, store_sem.at[0])
    tokens_store().start()

    gains = gain_acc[...]
    high = gains.astype(bf16).astype(f32)
    row = lax.broadcasted_iota(jnp.int32, gains.shape, 0)
    lower = pltpu.roll(gains - high, 2, 0)
    both = jnp.transpose(jnp.where(row < 2, high, lower))
    both = jnp.concatenate([both, jnp.zeros((width, head - 8), f32)], axis=1)
    for tile in range(4):
        at = slice(tile * 8 * block, (tile + 1) * 8 * block)
        place(kv_buf, tile, both[at], slice(2 * key_width, 2 * key_width + head))
    begin(3)

    advance(3, 0)
    advance(0, 1)
    advance(2, 1)
    advance(1, 2)
    advance(3, 1)
    advance(0, 2)
    advance(2, 2)
    advance(1, 3)
    advance(3, 2)
    advance(0, 3)
    advance(2, 3)
    expert_third()
    advance(3, 3)

    first_copy().wait_recv()
    second_copy().wait_recv()
    expert_last()
    for job in (1, 0, 2, 3):
        advance(job, 4)

    for copy in (far_copy, first_copy, second_copy):
        copy().wait_send()
    for m in range(2):
        ec_copy(m).wait_send()
    for i in range(3):
        ex_copy(i).wait_send()
        ef_copy(i).wait_send()
    for copy in final_copies(1):
        copy.wait()
    for job in range(4):
        for level in range(5):
            halve_copy(job, *jobs[job], level).wait_send()
    tokens_store().wait()


def backward_call(vmem_args, any_args):
    f32, bf16 = jnp.float32, jnp.bfloat16
    rows, head = vmem_args[2].shape
    key_width = vmem_args[6].shape[1]
    width = vmem_args[0].shape[0]
    hidden = any_args[13].shape[2]
    block = width // 32
    extra = 2 * key_width + head
    anywhere = pl.BlockSpec(memory_space=pl.ANY)
    inside = pl.BlockSpec(memory_space=pltpu.VMEM)
    shape = jax.ShapeDtypeStruct
    dma = pltpu.SemaphoreType.DMA
    vmem = pltpu.VMEM
    return pl.pallas_call(
        backward_kernel,
        out_shape=(
            shape((block, width), f32),
            shape((block, extra), f32),
            shape((block, width), f32),
            shape((rows, width), f32),
            shape((width // 4, hidden), f32),
            shape((width // 4, hidden), f32),
            shape((hidden, width // 4), f32),
            shape((rows, width), bf16),
            shape((rows, width), bf16),
            shape((rows, width), bf16),
        ),
        in_specs=[inside] * len(vmem_args) + [anywhere] * len(any_args),
        out_specs=(inside,) * 3 + (anywhere,) * 7,
        scratch_shapes=[
            vmem((10, rows, width), bf16),
            vmem((width, width), bf16),
            vmem((width, key_width), bf16),
            vmem((width, key_width), bf16),
            vmem((rows, width), f32),
            vmem((rows, width + 2 * key_width), bf16),
            vmem((rows, rows), f32),
            vmem((rows, key_width), f32),
            vmem((rows, key_width), f32),
            vmem((8, width), f32),
            vmem((32, block, width), bf16),
            vmem((31, block, width), bf16),
            vmem((32, block, width // 2), bf16),
            vmem((32, block, width // 2), bf16),
            vmem((15, block, width), bf16),
            vmem((32, block, extra), bf16),
            vmem((31, block, extra), bf16),
            vmem((2, width // 2, hidden), bf16),
            vmem((2, hidden // 2, width // 2), bf16),
            vmem((width // 2, hidden), bf16),
            vmem((hidden // 2, width // 2), bf16),
            vmem((width // 4, hidden), bf16),
            vmem((hidden // 2, width // 4), bf16),
            vmem((width // 2, hidden), bf16),
            vmem((hidden // 2, width // 2), bf16),
            vmem((width // 4, hidden), f32),
            vmem((hidden // 2, width // 4), f32),
            dma((24,)),
            dma((3,)),
            dma((3,)),
            dma((3,)),
            dma((3,)),
            dma((3,)),
            dma((3,)),
            dma((2,)),
            dma((2,)),
            dma((4, 5)),
            dma((4, 5)),
            pltpu.SemaphoreType.REGULAR((2,)),
            dma((10,)),
        ],
        compiler_params=pltpu.CompilerParams(
            collective_id=1, has_side_effects=True, vmem_limit_bytes=64 * 2**20
        ),
        cost_estimate=pl.CostEstimate(
            flops=30 * rows * width * width, bytes_accessed=60 * 2**20, transcendentals=0
        ),
    )(*vmem_args, *any_args)


def local_dense(
    tokens,
    segment_ids,
    routes,
    route_gates,
    attn_gain,
    ffn_gain,
    query_weight,
    key_matrix,
    value_matrix,
    output_weight,
    expert_gate,
    expert_up,
    expert_down,
    cotangent,
):
    experts = lax.axis_size("ep")
    table = jnp.sum(
        jnp.where(
            routes.T[None, :, :] == jnp.arange(experts, dtype=jnp.int32)[:, None, None],
            route_gates.T[None, :, :],
            0.0,
        ),
        axis=1,
    )
    power = -np.arange(HEAD_SIZE // 2, dtype=np.float32) * np.float32(2.0 / HEAD_SIZE)
    inverse = np.float32(BASE) ** power
    angle = np.arange(tokens.shape[0], dtype=np.float32)[:, None] * inverse[None, :]
    cosine = np.cos(angle)
    sine = np.sin(angle)
    small = (
        attn_gain,
        ffn_gain,
        jnp.asarray(np.concatenate([cosine, cosine], axis=1), jnp.float32),
        jnp.asarray(np.concatenate([-sine, sine], axis=1), jnp.float32),
        segment_ids,
    )
    (
        query_rot,
        key_rot,
        value_low,
        log_total,
        attended,
        mixed,
        grad_gu,
        grad_down,
        out_own,
        out_sib,
        own_grad,
        sibling_grad,
        first_grad,
        second_grad,
        _,
        _,
        met_gu,
        met_down,
    ) = forward_call(
        small + (table,),
        (
            tokens,
            query_weight,
            key_matrix,
            value_matrix,
            output_weight,
            cotangent,
            expert_gate[0],
            expert_up[0],
            expert_down[0],
        ),
    )
    (
        query_grad,
        extra_grad,
        output_grad,
        tokens_grad,
        gate_grad,
        up_grad,
        down_grad,
        near_sum,
        far_sum,
        _,
    ) = backward_call(
        small + (log_total, key_rot, value_low),
        (
            own_grad,
            sibling_grad,
            first_grad,
            second_grad,
            mixed,
            cotangent,
            attended,
            query_rot,
            tokens,
            output_weight,
            query_weight,
            key_matrix,
            value_matrix,
            grad_gu,
            grad_down,
            out_own,
            out_sib,
            met_gu,
            met_down,
        ),
    )
    total = mixed
    for part in (out_own[0], out_sib[0], near_sum, far_sum):
        total = total + part.astype(jnp.float32)
    layer_out = total.astype(jnp.bfloat16)
    split_k = key_matrix.shape[1]
    split_v = split_k + value_matrix.shape[1]
    gain_sums = extra_grad[:, split_v : split_v + 2] + extra_grad[:, split_v + 2 : split_v + 4]
    return (
        layer_out,
        tokens_grad,
        query_grad,
        extra_grad[:, :split_k],
        extra_grad[:, split_k:split_v],
        output_grad.T,
        gain_sums[:, 0],
        gain_sums[:, 1],
        gate_grad[None],
        up_grad[None],
        down_grad[None],
    )


def solution(mesh):
    in_specs = (
        P(("grp", "ep"), None),
        P(("grp", "ep"), None),
        P(("grp", "ep"), None),
        P(("grp", "ep"), None),
        P(),
        P(),
        P(),
        P(),
        P(),
        P(),
        P("ep", None, None),
        P("ep", None, None),
        P("ep", None, None),
        P(("grp", "ep"), None),
    )
    out_specs = (
        P(("grp", "ep"), None),
        P(("grp", "ep"), None),
        P(("grp", "ep"), None),
        P(("grp", "ep"), None),
        P(("grp", "ep"), None),
        P(None, ("grp", "ep")),
        P(("grp", "ep")),
        P(("grp", "ep")),
        P("ep", "grp", None),
        P("ep", "grp", None),
        P("ep", None, "grp"),
    )
    paired = mesh.shape["grp"] == 4 and mesh.shape["ep"] == 8
    local = local_dense if paired else local_routed
    return jax.shard_map(local, mesh=mesh, in_specs=in_specs, out_specs=out_specs, check_vma=False)
```

```python
import jax
import jax.numpy as jnp
import numpy as np
from jax import lax
from jax.experimental import pallas as pl
from jax.experimental.pallas import tpu as pltpu
from jax.sharding import PartitionSpec as P

HEAD_SIZE = 128


EPS = 1e-06
BASE = 10000.0


def apply_rotary(value_rows, cosine_table, sine_table):
    half = value_rows.shape[-1] // 2
    first = value_rows[..., :half]
    second = value_rows[..., half:]
    return jnp.concatenate(
        [first * cosine_table - second * sine_table, second * cosine_table + first * sine_table],
        axis=-1,
    )


def unrotate(value_rows, cosine_table, sine_table):
    half = value_rows.shape[-1] // 2
    first = value_rows[..., :half]
    second = value_rows[..., half:]
    return jnp.concatenate(
        [first * cosine_table + second * sine_table, second * cosine_table - first * sine_table],
        axis=-1,
    )


def glu_value(gate_val, up_val):
    return jax.nn.gelu(gate_val, approximate=True) * up_val


def scores_of(query_rot, key_rot, allowed):
    score = jnp.einsum(
        "tkgd,skd->kgts", query_rot, key_rot, preferred_element_type=jnp.float32
    ) * HEAD_SIZE ** (-0.5)
    return jnp.where(allowed, score, -1e30)


def local_routed(
    tokens,
    segment_ids,
    routes,
    route_gates,
    attn_gain,
    ffn_gain,
    query_weight,
    key_matrix,
    value_matrix,
    output_weight,
    expert_gate,
    expert_up,
    expert_down,
    cotangent,
):
    length_total, width = tokens.shape
    choose = routes.shape[1]
    local_experts = expert_gate.shape[0]
    owners = lax.axis_size("ep")
    experts = owners * local_experts
    capacity = 3 * length_total * choose // (2 * experts)
    query_heads = query_weight.shape[1] // HEAD_SIZE
    key_heads = key_matrix.shape[1] // HEAD_SIZE
    q_per_kv = query_heads // key_heads
    segment = segment_ids[0]
    padding = segment == jnp.max(segment)
    later = jnp.arange(length_total)[:, None] >= jnp.arange(length_total)[None, :]
    diagonal = jnp.arange(length_total)[:, None] == jnp.arange(length_total)[None, :]
    allowed = (
        later
        & (segment[:, None] == segment[None, :])
        & (jnp.logical_not(padding)[None, :] | diagonal)
    )
    position = jnp.arange(length_total, dtype=jnp.float32)
    inverse = BASE ** (-jnp.arange(HEAD_SIZE // 2, dtype=jnp.float32) * 2.0 / HEAD_SIZE)
    angle = position[:, None] * inverse[None, :]
    cosine_table = jnp.cos(angle)[:, None, :]
    sine_table = jnp.sin(angle)[:, None, :]
    tok_float = tokens.astype(jnp.float32)
    scale_first = lax.rsqrt(jnp.mean(tok_float * tok_float, axis=-1, keepdims=True) + EPS)
    normed_first = tok_float * scale_first
    h_first = (normed_first * attn_gain).astype(jnp.bfloat16)
    query_rows = jnp.dot(h_first, query_weight, preferred_element_type=jnp.float32).reshape(
        length_total, query_heads, HEAD_SIZE
    )
    key_rows = jnp.dot(h_first, key_matrix, preferred_element_type=jnp.float32).reshape(
        length_total, key_heads, HEAD_SIZE
    )
    value_low = jnp.dot(h_first, value_matrix, preferred_element_type=jnp.float32).astype(
        jnp.bfloat16
    )
    value_low = value_low.reshape(length_total, key_heads, HEAD_SIZE)
    query_rot = (
        apply_rotary(query_rows, cosine_table, sine_table)
        .astype(jnp.bfloat16)
        .reshape(length_total, key_heads, q_per_kv, HEAD_SIZE)
    )
    key_rot = apply_rotary(key_rows, cosine_table, sine_table).astype(jnp.bfloat16)
    score = scores_of(query_rot, key_rot, allowed)
    row_max = jnp.max(score, axis=-1, keepdims=True)
    expo = jnp.exp(score - row_max)
    row_sum = jnp.sum(expo, axis=-1, keepdims=True)
    log_total = row_max + jnp.log(row_sum)
    probs_low = (expo / row_sum).astype(jnp.bfloat16)
    attended = jnp.einsum(
        "kgts,skd->tkgd", probs_low, value_low, preferred_element_type=jnp.float32
    )
    attended = attended.reshape(length_total, query_heads * HEAD_SIZE).astype(jnp.bfloat16)
    mixed = tok_float + jnp.dot(attended, output_weight, preferred_element_type=jnp.float32)
    scale_second = lax.rsqrt(jnp.mean(mixed * mixed, axis=-1, keepdims=True) + EPS)
    normed_second = mixed * scale_second
    h_second = (normed_second * ffn_gain).astype(jnp.bfloat16)
    flat_routes = routes.reshape(-1)
    assigns = flat_routes.shape[0]
    onehot = (flat_routes[:, None] == jnp.arange(experts, dtype=jnp.int32)[None, :]).astype(
        jnp.int32
    )
    position_in = jnp.sum(jnp.cumsum(onehot, axis=0) * onehot, axis=1) - 1
    slot_index = flat_routes * capacity + position_in
    source = (
        jnp.full((experts * capacity,), assigns, jnp.int32)
        .at[slot_index]
        .set(jnp.arange(assigns, dtype=jnp.int32))
    )
    token_of = source // choose
    h_ext = jnp.concatenate([h_second, jnp.zeros((1, width), jnp.bfloat16)], axis=0)
    send_rows = h_ext[token_of].reshape(owners, local_experts, capacity, width)
    row_entries = lax.all_to_all(send_rows, "ep", split_axis=0, concat_axis=0, tiled=True)
    gate_val = jnp.einsum(
        "secd,edf->secf", row_entries, expert_gate, preferred_element_type=jnp.float32
    )
    up_val = jnp.einsum(
        "secd,edf->secf", row_entries, expert_up, preferred_element_type=jnp.float32
    )
    act = glu_value(gate_val, up_val).astype(jnp.bfloat16)
    result = jnp.einsum("secf,efd->secd", act, expert_down, preferred_element_type=jnp.float32)
    outputs = (result.astype(jnp.bfloat16), row_entries, gate_val, up_val)
    returned = lax.all_to_all(outputs[0], "ep", split_axis=0, concat_axis=0, tiled=True).reshape(
        experts * capacity, width
    )
    picked = returned[slot_index].reshape(length_total, choose, width).astype(jnp.float32)
    layer_out = (mixed + jnp.sum(route_gates[:, :, None] * picked, axis=1)).astype(jnp.bfloat16)
    grad_out = cotangent.astype(jnp.float32)
    slot_grads = (
        (route_gates[:, :, None] * grad_out[:, None, :])
        .astype(jnp.bfloat16)
        .reshape(assigns, width)
    )
    slot_ext = jnp.concatenate([slot_grads, jnp.zeros((1, width), jnp.bfloat16)], axis=0)
    grad_send = slot_ext[source].reshape(owners, local_experts, capacity, width)
    grad_recv = lax.all_to_all(grad_send, "ep", split_axis=0, concat_axis=0, tiled=True)
    recv_rows = outputs[1]
    gate_val = outputs[2]
    up_val = outputs[3]
    act, act_back = jax.vjp(glu_value, gate_val, up_val)
    act_low = act.astype(jnp.bfloat16)
    down_part = jnp.einsum("secf,secd->efd", act_low, grad_recv, preferred_element_type=jnp.float32)
    act_grad = jnp.einsum(
        "secd,efd->secf", grad_recv, expert_down, preferred_element_type=jnp.float32
    )
    gate_grad_val, up_grad_val = act_back(act_grad)
    gate_low = gate_grad_val.astype(jnp.bfloat16)
    up_low = up_grad_val.astype(jnp.bfloat16)
    gate_part = jnp.einsum(
        "secd,secf->edf", recv_rows, gate_low, preferred_element_type=jnp.float32
    )
    up_part = jnp.einsum("secd,secf->edf", recv_rows, up_low, preferred_element_type=jnp.float32)
    rows_grad = jnp.einsum(
        "secf,edf->secd", gate_low, expert_gate, preferred_element_type=jnp.float32
    )
    rows_grad = rows_grad + jnp.einsum(
        "secf,edf->secd", up_low, expert_up, preferred_element_type=jnp.float32
    )
    rows_back = lax.all_to_all(
        rows_grad.astype(jnp.bfloat16), "ep", split_axis=0, concat_axis=0, tiled=True
    )
    rows_back = rows_back.reshape(experts * capacity, width)
    expert_sums = (
        lax.psum_scatter(
            gate_part.astype(jnp.bfloat16), "grp", scatter_dimension=1, tiled=True
        ).astype(jnp.float32),
        lax.psum_scatter(
            up_part.astype(jnp.bfloat16), "grp", scatter_dimension=1, tiled=True
        ).astype(jnp.float32),
        lax.psum_scatter(
            down_part.astype(jnp.bfloat16), "grp", scatter_dimension=2, tiled=True
        ).astype(jnp.float32),
    )
    second_grad = jnp.sum(
        rows_back[slot_index].reshape(length_total, choose, width).astype(jnp.float32), axis=1
    )
    ffn_gain_part = jnp.sum(second_grad * normed_second, axis=0)
    normed_grad = second_grad * ffn_gain
    mixed_grad = grad_out + scale_second * (
        normed_grad - normed_second * jnp.mean(normed_grad * normed_second, axis=-1, keepdims=True)
    )
    mixed_low = mixed_grad.astype(jnp.bfloat16)
    output_part = jnp.einsum("ti,td->id", attended, mixed_low, preferred_element_type=jnp.float32)
    attended_grad = jnp.einsum(
        "td,id->ti", mixed_low, output_weight, preferred_element_type=jnp.float32
    )
    attended_grad = attended_grad.astype(jnp.bfloat16).reshape(
        length_total, key_heads, q_per_kv, HEAD_SIZE
    )
    probs = jnp.exp(scores_of(query_rot, key_rot, allowed) - log_total)
    probs_again = probs.astype(jnp.bfloat16)
    value_part_grad = jnp.einsum(
        "kgts,tkgd->skd", probs_again, attended_grad, preferred_element_type=jnp.float32
    )
    prob_grad = jnp.einsum(
        "tkgd,skd->kgts", attended_grad, value_low, preferred_element_type=jnp.float32
    )
    inner = jnp.sum(probs * prob_grad, axis=-1, keepdims=True)
    score_grad = (probs * (prob_grad - inner)).astype(jnp.bfloat16)
    qrot_grad = jnp.einsum(
        "kgts,skd->tkgd", score_grad, key_rot, preferred_element_type=jnp.float32
    ) * HEAD_SIZE ** (-0.5)
    krot_grad = jnp.einsum(
        "kgts,tkgd->skd", score_grad, query_rot, preferred_element_type=jnp.float32
    ) * HEAD_SIZE ** (-0.5)
    query_grad_low = unrotate(
        qrot_grad.reshape(length_total, query_heads, HEAD_SIZE), cosine_table, sine_table
    )
    query_grad_low = query_grad_low.astype(jnp.bfloat16).reshape(
        length_total, query_heads * HEAD_SIZE
    )
    key_grad_low = (
        unrotate(krot_grad, cosine_table, sine_table)
        .astype(jnp.bfloat16)
        .reshape(length_total, key_heads * HEAD_SIZE)
    )
    value_grad_low = value_part_grad.astype(jnp.bfloat16).reshape(
        length_total, key_heads * HEAD_SIZE
    )
    query_part = jnp.einsum(
        "td,ti->di", h_first, query_grad_low, preferred_element_type=jnp.float32
    )
    key_part = jnp.einsum("td,ti->di", h_first, key_grad_low, preferred_element_type=jnp.float32)
    value_part = jnp.einsum(
        "td,ti->di", h_first, value_grad_low, preferred_element_type=jnp.float32
    )
    first_grad = jnp.einsum(
        "ti,di->td", query_grad_low, query_weight, preferred_element_type=jnp.float32
    )
    first_grad = first_grad + jnp.einsum(
        "ti,di->td", key_grad_low, key_matrix, preferred_element_type=jnp.float32
    )
    first_grad = first_grad + jnp.einsum(
        "ti,di->td", value_grad_low, value_matrix, preferred_element_type=jnp.float32
    )
    attn_gain_part = jnp.sum(first_grad * normed_first, axis=0)
    normed_first_grad = first_grad * attn_gain
    tokens_grad = mixed_grad + scale_first * (
        normed_first_grad
        - normed_first * jnp.mean(normed_first_grad * normed_first, axis=-1, keepdims=True)
    )
    shared = (
        lax.psum_scatter(query_part, ("grp", "ep"), scatter_dimension=0, tiled=True),
        lax.psum_scatter(key_part, ("grp", "ep"), scatter_dimension=0, tiled=True),
        lax.psum_scatter(value_part, ("grp", "ep"), scatter_dimension=0, tiled=True),
        lax.psum_scatter(output_part, ("grp", "ep"), scatter_dimension=1, tiled=True),
        lax.psum_scatter(attn_gain_part, ("grp", "ep"), scatter_dimension=0, tiled=True),
        lax.psum_scatter(ffn_gain_part, ("grp", "ep"), scatter_dimension=0, tiled=True),
    )
    return (
        layer_out,
        tokens_grad,
        shared[0],
        shared[1],
        shared[2],
        shared[3],
        shared[4],
        shared[5],
        expert_sums[0],
        expert_sums[1],
        expert_sums[2],
    )


def forward_kernel(
    attn_gain_ref, ffn_gain_ref, cos_ref, sin_ref, seg_row_ref, tab_ref, tok_ref,
    wq_ref, wk_ref, wv_ref, wo_ref, dy_ref, gate_ref, up_ref, down_ref,
    query_ref, key_ref, value_ref, lse_ref, att_ref, mixed_ref, grad_gu_ref, grad_down_ref,
    out_own_ref, out_sib_ref, d_own_ref, d_sib_ref, d_first_ref, d_second_ref, part_d_ref,
    part_o_ref, ex_gu_ref, ex_down_ref,
    xb, dyb, tab, w_gu, w_down, sib, far_in, gather_send, gather_recv, tab_send, tab_recv,
    fetch_send, fetch_recv, pass_send, pass_recv, local_sem, part_send, part_recv, keep_sem,
    sum_send, sum_recv, ex_send, ex_recv, store_sem, stage_sem,
):
    f32, bf16 = jnp.float32, jnp.bfloat16
    grp, ep = lax.axis_index("grp"), lax.axis_index("ep")
    core = lax.rem(grp, 2)
    side = grp // 2
    low = lax.rem(ep, 4)
    y, z = lax.rem(low, 2), low // 2
    by_y = ep + 1 - 2 * y
    by_z = ep + 2 - 4 * z
    by_both = by_y + 2 - 4 * z
    by_far = ep + 4 - 8 * (ep // 4)
    first = by_y * (1 - core) + by_z * core
    second = by_z * (1 - core) + by_y * core
    other = grp + 1 - 2 * core
    across = (grp + 2 - 4 * side, ep)
    away = (grp, by_far)
    rows, width = tok_ref.shape
    half = rows // 2
    hidden = gate_ref.shape[1]
    mine = hidden // 2
    head = cos_ref.shape[1]
    heads = width // head
    key_width = wk_ref.shape[1]
    per_key = heads * head // key_width

    def remote(src, dst, send, recv, device):
        return pltpu.make_async_remote_copy(
            src_ref=src, dst_ref=dst, send_sem=send, recv_sem=recv, device_id=device,
            device_id_type=pl.DeviceIdType.MESH,
        )

    members = (
        ((grp, first), 1), ((grp, second), 2), ((grp, by_both), 3), ((other, ep), 4),
        ((other, first), 5), ((other, second), 6), ((other, by_both), 7),
    )
    barrier = pltpu.get_barrier_semaphore()
    for device in [device for device, _ in members] + [across, away]:
        pl.semaphore_signal(barrier, inc=1, device_id=device, device_id_type=pl.DeviceIdType.MESH)
    pl.semaphore_wait(barrier, 9)

    units = pl.ds(pl.multiple_of(core * mine, mine), mine)
    own_weights = (
        (gate_ref.at[:, units], w_gu.at[0, :, pl.ds(0, mine)]),
        (up_ref.at[:, units], w_gu.at[0, :, pl.ds(mine, mine)]),
        (down_ref.at[units, :], w_down.at[0]),
    )
    wide_at = pl.ds(pl.multiple_of(side * (width // 2), width // 2), width // 2)
    deep_at = pl.ds(pl.multiple_of(side * (mine // 2), mine // 2), mine // 2)
    deep_from = pl.ds(pl.multiple_of(core * mine + side * (mine // 2), mine // 2), mine // 2)
    pieces = (
        (gate_ref.at[wide_at, units], w_gu.at[1, wide_at, pl.ds(0, mine)]),
        (up_ref.at[wide_at, units], w_gu.at[1, wide_at, pl.ds(mine, mine)]),
        (down_ref.at[deep_from, :], w_down.at[1, deep_at, :]),
    )

    def fetch_copy(m):
        return remote(*pieces[m], fetch_send.at[m], fetch_recv.at[m], away)

    def pass_copy(m):
        return remote(pieces[m][1], pieces[m][1], pass_send.at[m], pass_recv.at[m], across)

    def load(number, src, dst):
        return pltpu.make_async_copy(src, dst, local_sem.at[number])

    def gather_copy(k, number):
        own, buf = ((xb.at[0], xb), (dy_ref, dyb))[k]
        src, dst, device = (
            (own, 1, (grp, first)), (own, 4, (other, ep)), (own, 2, (grp, second)),
            (buf.at[1], 5, (other, ep)), (buf.at[2], 6, (other, ep)),
            (buf.at[2], 3, (grp, first)), (buf.at[3], 7, (other, ep)),
        )[number]
        if k == 1 and number == 5:
            src, device = buf.at[2 - core], (grp, by_y)
        return remote(
            src, buf.at[dst], gather_send.at[k, number], gather_recv.at[k, number], device
        )

    arrival = {1: 0, 4: 1, 2: 2, 5: 3, 6: 4, 3: 5, 7: 6}

    def start(k, *numbers):
        for number in numbers:
            gather_copy(k, number).start()

    def arrived(k, slot):
        gather_copy(k, arrival[slot]).wait_recv()

    def table_copy(slot):
        device = members[slot - 1][0]
        return remote(tab_ref, tab.at[slot], tab_send.at[slot], tab_recv.at[slot], device)

    fetch_copy(0).start()
    start(1, 0, 1, 2)
    for slot in range(1, 8):
        table_copy(slot).start()
    own_dy = lambda: load(0, dy_ref, dyb.at[0])
    tab[0] = tab_ref[...]

    def dot_nt(a, b):
        return lax.dot_general(a, b, (((1,), (1,)), ((), ())), preferred_element_type=f32)

    def dot_tn(a, b):
        return lax.dot_general(a, b, (((0,), (0,)), ((), ())), preferred_element_type=f32)

    def attention(w_big, w_key, w_value, tok, act, query, key, value, bias, mixed, lse):
        tok_load = load(4, tok_ref, tok)
        query_load = load(5, wq_ref, w_big)
        key_load = load(6, wk_ref, w_key)
        value_load = load(7, wv_ref, w_value)
        for copy in (tok_load, query_load, key_load, value_load):
            copy.start()
        own_dy().start()
        for m, (src, dst) in enumerate(own_weights):
            load(1 + m, src, dst).start()
        segment = jnp.broadcast_to(seg_row_ref[...].astype(f32), (8, rows))
        segment_column = jnp.transpose(segment)[:, :1].astype(jnp.int32)
        position = lax.broadcasted_iota(jnp.int32, (rows, rows), 0)
        other_position = lax.broadcasted_iota(jnp.int32, (rows, rows), 1)
        padding = seg_row_ref[...] == jnp.max(seg_row_ref[...])
        allowed = (
            (other_position <= position)
            & (segment_column == seg_row_ref[...])
            & (jnp.logical_not(padding) | (other_position == position))
        )
        bias[...] = jnp.where(allowed, 0.0, -1e30)
        lse[...] = jnp.zeros_like(lse)
        tok_load.wait()

        @pl.loop(0, rows // 128)
        def _(step):
            at = pl.ds(pl.multiple_of(step * 128, 128), 128)
            entry = tok[at, :].astype(f32)
            factor = lax.rsqrt(jnp.mean(entry * entry, axis=-1, keepdims=True) + EPS)
            act[at, :] = (entry * factor * attn_gain_ref[...][None, :]).astype(bf16)

        def turn(entry, at):
            swapped = pltpu.roll(entry, head // 2, 1)
            return entry * cos_ref[at, :] + swapped * sin_ref[at, :]

        key_load.wait()
        value_load.wait()
        key_rows = jnp.dot(act[...], w_key[...], preferred_element_type=f32)
        for kv in range(key_width // head):
            columns = slice(kv * head, (kv + 1) * head)
            key[:, columns] = turn(key_rows[:, columns], slice(None)).astype(bf16)
        value[...] = jnp.dot(act[...], w_value[...], preferred_element_type=f32).astype(bf16)
        query_load.wait()
        for tile in range(width // 256):
            columns = slice(tile * 256, (tile + 1) * 256)
            entry = jnp.dot(act[...], w_big[:, columns], preferred_element_type=f32)
            for part in range(256 // head):
                columns = slice(part * head, (part + 1) * head)
                to = slice(tile * 256 + part * head, tile * 256 + (part + 1) * head)
                query[:, to] = turn(entry[:, columns], slice(None)).astype(bf16)
        out_load = load(8, wo_ref, w_big)
        out_load.start()
        stores = [
            pltpu.make_async_copy(src, dst, store_sem.at[i])
            for i, (src, dst) in enumerate(((query, query_ref), (key, key_ref), (value, value_ref)))
        ]
        for copy in stores:
            copy.start()
        scale = head ** (-0.5)
        lane = lax.broadcasted_iota(jnp.int32, (half, head), 1)
        for number in range(heads):
            columns = slice(number * head, (number + 1) * head)
            kv = number // per_key
            kv_columns = slice(kv * head, (kv + 1) * head)
            for part in range(2):
                at = slice(part * half, (part + 1) * half)
                seen = slice(0, (part + 1) * half)
                score = dot_nt(query[at, columns], key[seen, kv_columns]) * scale + bias[at, seen]
                top = jnp.max(score, axis=-1, keepdims=True)
                expo = jnp.exp(score - top)
                total = jnp.sum(expo, axis=-1, keepdims=True)
                lse[at, :] = jnp.where(lane == number, top + jnp.log(total), lse[at, :])
                probs = (expo / total).astype(bf16)
                mixed_value = jnp.dot(probs, value[seen, kv_columns], preferred_element_type=f32)
                act[at, columns] = mixed_value.astype(bf16)
        fetch_copy(1).start()
        out_load.wait()
        att_store = pltpu.make_async_copy(act, att_ref, store_sem.at[3])
        att_store.start()
        lse_store = pltpu.make_async_copy(lse, lse_ref, store_sem.at[4])
        lse_store.start()
        for part in range(4):
            at = slice(part * rows // 4, (part + 1) * rows // 4)
            total = tok[at, :].astype(f32) + jnp.dot(
                act[at, :], w_big[...], preferred_element_type=f32
            )
            mixed[at, :] = total
            factor = lax.rsqrt(jnp.mean(total * total, axis=-1, keepdims=True) + EPS)
            xb[0, at, :] = (total * factor * ffn_gain_ref[...][None, :]).astype(bf16)
        start(0, 0, 1, 2)
        mixed_store = pltpu.make_async_copy(mixed, mixed_ref, store_sem.at[5])
        mixed_store.start()
        for copy in stores + [att_store, lse_store, mixed_store]:
            copy.wait()

    vmem = pltpu.VMEM
    pl.run_scoped(
        attention,
        vmem((width, width), bf16),
        vmem((width, key_width), bf16),
        vmem((width, key_width), bf16),
        vmem((rows, width), bf16),
        vmem((rows, width), bf16),
        vmem((rows, width), bf16),
        vmem((rows, key_width), bf16),
        vmem((rows, key_width), bf16),
        vmem((rows, rows), f32),
        vmem((rows, width), f32),
        vmem((rows, head), f32),
    )

    def experts(acc_gu, acc_down, act_s, gu_s, dz_s, stage):
        own_dy().wait()
        for m, (src, dst) in enumerate(own_weights):
            load(1 + m, src, dst).wait()
        for slot in range(1, 8):
            table_copy(slot).wait_send()
            table_copy(slot).wait_recv()
        acc_gu[...] = jnp.zeros_like(acc_gu)
        acc_down[...] = jnp.zeros_like(acc_down)

        def gates(slot, hosted):
            block = jnp.transpose(tab[slot])
            lane = lax.broadcasted_iota(jnp.int32, block.shape, 1)
            return jnp.sum(jnp.where(lane == hosted, block, 0.0), axis=1, keepdims=True)

        c0 = 0.7978845608028654
        c1 = 0.044715

        def work(which, slot, hosted, deliver):
            column = gates(slot, hosted)
            for part in range(2):
                at = pl.ds(part * half, half)
                gate = column[part * half : (part + 1) * half]
                gu = jnp.dot(xb[slot, at, :], w_gu[which], preferred_element_type=f32)
                dz = (gate * dyb[slot, at, :].astype(f32)).astype(bf16)
                dz_s[at, :] = dz
                da = dot_nt(dz, w_down[which])
                g, u = gu[:, :mine], gu[:, mine:]
                square = g * g
                t = jnp.tanh(c0 * (g + c1 * square * g))
                gelu = 0.5 * g * (1.0 + t)
                slope = 0.5 * (1.0 + t) + 0.5 * g * (1.0 - t * t) * (c0 * (1.0 + 3.0 * c1 * square))
                act_s[at, :] = (gelu * u).astype(bf16)
                gu_s[at, :mine] = (da * u * slope).astype(bf16)
                gu_s[at, mine:] = (da * gelu).astype(bf16)
            for part in range(3):
                at = pl.ds(part * (width // 3), width // 3)
                acc_gu[which, at, :] += dot_tn(xb[slot, :, at], gu_s[...])
                acc_down[which, :, at] += dot_tn(act_s[...], dz_s[:, at])
            for part in range(2):
                at = pl.ds(part * half, half)
                gate = column[part * half : (part + 1) * half]
                dx = dot_nt(gu_s[at, :], w_gu[which])
                result = gate * jnp.dot(act_s[at, :], w_down[which], preferred_element_type=f32)
                deliver(at, dx, result)

        def slot_up(step):
            pair, odd = step // 2, lax.rem(step, 2)
            middle = (lax.rem(pair, 2) * (1 - pair // 3) + pair // 2 * (1 - pair // 3))
            turned = core * (1 - odd) + (1 - core) * odd
            swapped = middle * (3 - 2 * pair) * turned
            return pair + swapped + 4 * odd

        def stage_out(k, step):
            buf = lax.rem(step, 2)
            dst = (part_d_ref, part_o_ref)[k].at[slot_up(step)]
            return pltpu.make_async_copy(stage.at[k, buf], dst, stage_sem.at[k, buf])

        @pl.loop(0, 8)
        def _(step):
            def at_step(number):
                return pl.when(step == number)

            @at_step(1)
            def _():
                fetch_copy(2).start()
                arrived(0, 4)
                arrived(1, 4)

            @at_step(2)
            def _():
                arrived(1, 1)
                start(1, 3)
                arrived(1, 2)
                start(1, 5, 4)
                fetch_copy(0).wait_recv()
                pass_copy(0).start()
                @pl.when(core == 0)
                def _():
                    arrived(0, 1)
                    start(0, 3)

                @pl.when(core == 1)
                def _():
                    arrived(0, 2)
                    start(0, 5, 4)


            @at_step(3)
            def _():
                @pl.when(core == 0)
                def _():
                    arrived(0, 6)
                    arrived(1, 6)

                @pl.when(core == 1)
                def _():
                    arrived(0, 5)
                    arrived(1, 5)


            @at_step(4)
            def _():
                @pl.when(core == 0)
                def _():
                    arrived(0, 2)
                    start(0, 5, 4)

                @pl.when(core == 1)
                def _():
                    arrived(0, 1)
                    start(0, 3)

                for m in (1, 2):
                    fetch_copy(m).wait_recv()
                    pass_copy(m).start()

            @at_step(5)
            def _():
                @pl.when(core == 0)
                def _():
                    arrived(0, 5)
                    arrived(1, 5)

                @pl.when(core == 1)
                def _():
                    arrived(0, 6)
                    arrived(1, 6)

                arrived(1, 3)
                start(1, 6)

            @at_step(6)
            def _():
                arrived(0, 3)
                start(0, 6)

            @at_step(7)
            def _():
                arrived(0, 7)
                arrived(1, 7)

            @pl.when(step >= 2)
            def _():
                stage_out(0, step - 2).wait()
                stage_out(1, step - 2).wait()

            buf = lax.rem(step, 2)

            def deliver(at, dx, result):
                stage[0, buf, at, :] = dx.astype(bf16)
                stage[1, buf, at, :] = result.astype(bf16)

            work(0, slot_up(step), ep, deliver)
            stage_out(0, step).start()
            stage_out(1, step).start()

        for k in range(2):
            for step in (6, 7):
                stage_out(k, step).wait()
        for k in range(2):
            for number in range(7):
                gather_copy(k, number).wait_send()

        def grad_copies(which):
            return (
                pltpu.make_async_copy(w_gu.at[which], grad_gu_ref.at[which], store_sem.at[6 + 2 * which]),
                pltpu.make_async_copy(
                    w_down.at[which], grad_down_ref.at[which], store_sem.at[7 + 2 * which]
                ),
            )

        def slot_down(step):
            pair = step // 2
            return 3 - 2 * lax.rem(pair, 2) - pair // 2 + 4 * (1 - lax.rem(step, 2))

        def stage_in(k, step):
            buf = lax.rem(step, 2)
            src = (part_d_ref, part_o_ref)[k].at[slot_down(step)]
            return pltpu.make_async_copy(src, stage.at[k, buf], stage_sem.at[k, buf])

        stage_in(0, 0).start()
        stage_in(1, 0).start()
        def flush(which):
            w_gu[which] = acc_gu[which].astype(bf16)
            w_down[which] = acc_down[which].astype(bf16)
            for copy in grad_copies(which):
                copy.start()

        def exchange(m):
            at = pl.ds(pl.multiple_of((1 - side) * (width // 2), width // 2), width // 2)
            src = w_down.at[0, :, at] if m else w_gu.at[0, at, :]
            return remote(src, (ex_gu_ref, ex_down_ref)[m], ex_send.at[m], ex_recv.at[m], across)

        for m in range(3):
            pass_copy(m).wait()
            fetch_copy(m).wait_send()

        def keep_copy(j):
            return pltpu.make_async_copy(dyb.at[j], out_own_ref.at[j], keep_sem.at[j])

        def grad_part(j):
            dst = d_sib_ref if j == 0 else sib.at[j - 1]
            return remote(xb.at[4 + j], dst, part_send.at[0, j], part_recv.at[0, j], (other, ep))

        def out_part(j):
            return remote(
                dyb.at[4 + j], out_sib_ref.at[j], part_send.at[1, j], part_recv.at[1, j], (other, ep)
            )

        own_grad = lambda: pltpu.make_async_copy(xb.at[0], d_own_ref, keep_sem.at[4])
        send_far = lambda: remote(xb.at[3], far_in, sum_send.at[0], sum_recv.at[0], (grp, first))
        send_first = lambda: remote(
            xb.at[1], d_first_ref, sum_send.at[1], sum_recv.at[1], (grp, first)
        )
        send_second = lambda: remote(
            xb.at[2], d_second_ref, sum_send.at[2], sum_recv.at[2], (grp, second)
        )

        def add_into(dst, *others):
            @pl.loop(0, rows // 128)
            def _(i):
                at = pl.ds(pl.multiple_of(i * 128, 128), 128)
                total = dst[at, :].astype(f32)
                for part in others:
                    total = total + part[at, :].astype(f32)
                dst[at, :] = total.astype(bf16)

        @pl.loop(0, 8)
        def _(step):
            def at_step(number):
                return pl.when(step == number)

            stage_in(0, step).wait()
            stage_in(1, step).wait()

            @pl.when(step < 7)
            def _():
                stage_in(0, step + 1).start()
                stage_in(1, step + 1).start()

            buf = lax.rem(step, 2)
            slot = slot_down(step)

            def deliver(at, dx, result):
                xb[slot, at, :] = (dx + stage[0, buf, at, :].astype(f32)).astype(bf16)
                dyb[slot, at, :] = (result + stage[1, buf, at, :].astype(f32)).astype(bf16)

            work(1, slot, ep + 4 - 8 * (ep // 4), deliver)
            for number, j in enumerate((3, 1, 2, 0)):

                @at_step(2 * number)
                def _(j=j):
                    grad_part(j).start()
                    out_part(j).start()

                @at_step(2 * number + 1)
                def _(j=j):
                    keep_copy(j).start()

            @at_step(1)
            def _():
                grad_part(3).wait_recv()
                add_into(xb.at[3], sib.at[2])
                send_far().start()
                flush(0)
                for m in range(2):
                    exchange(m).start()

            @at_step(3)
            def _():
                grad_part(1).wait_recv()
                add_into(xb.at[1], sib.at[0])
                send_first().start()

            @at_step(5)
            def _():
                grad_part(2).wait_recv()
                send_far().wait_recv()
                add_into(xb.at[2], sib.at[1], far_in)
                send_second().start()

        own_grad().start()
        flush(1)
        for j in range(4):
            grad_part(j).wait_send()
            out_part(j).wait()
            keep_copy(j).wait()
        grad_part(0).wait_recv()
        own_grad().wait()
        send_far().wait_send()
        send_first().wait()
        send_second().wait()
        for which in range(2):
            for copy in grad_copies(which):
                copy.wait()
            exchange(which).wait()

    pl.run_scoped(
        experts,
        vmem((2, width, hidden), f32),
        vmem((2, mine, width), f32),
        vmem((rows, mine), bf16),
        vmem((rows, hidden), bf16),
        vmem((rows, width), bf16),
        vmem((2, 2, rows, width), bf16),
    )


def forward_call(vmem_args, any_args):
    f32, bf16 = jnp.float32, jnp.bfloat16
    rows, width = any_args[0].shape
    head = vmem_args[2].shape[1]
    key_width = any_args[2].shape[1]
    hidden = any_args[6].shape[1]
    anywhere = pl.BlockSpec(memory_space=pl.ANY)
    inside = pl.BlockSpec(memory_space=pltpu.VMEM)
    shape = jax.ShapeDtypeStruct
    dma = pltpu.SemaphoreType.DMA
    vmem = pltpu.VMEM
    chunk = shape((rows, width), bf16)
    four = shape((4, rows, width), bf16)
    eight = shape((8, rows, width), bf16)
    return pl.pallas_call(
        forward_kernel,
        out_shape=(
            chunk,
            shape((rows, key_width), bf16),
            shape((rows, key_width), bf16),
            shape((rows, head), f32),
            chunk,
            shape((rows, width), f32),
            shape((2, width, hidden), bf16),
            shape((2, hidden // 2, width), bf16),
            four,
            four,
            chunk,
            chunk,
            chunk,
            chunk,
            eight,
            eight,
            shape((width // 2, hidden), bf16),
            shape((hidden // 2, width // 2), bf16),
        ),
        in_specs=[inside] * len(vmem_args) + [anywhere] * len(any_args),
        out_specs=(anywhere,) * 18,
        scratch_shapes=[
            vmem((8, rows, width), bf16),
            vmem((8, rows, width), bf16),
            vmem((8,) + vmem_args[5].shape, f32),
            vmem((2, width, hidden), bf16),
            vmem((2, hidden // 2, width), bf16),
            vmem((3, rows, width), bf16),
            vmem((rows, width), bf16),
            dma((2, 7)),
            dma((2, 7)),
            dma((8,)),
            dma((8,)),
            dma((3,)),
            dma((3,)),
            dma((3,)),
            dma((3,)),
            dma((9,)),
            dma((2, 4)),
            dma((2, 4)),
            dma((5,)),
            dma((3,)),
            dma((3,)),
            dma((2,)),
            dma((2,)),
            dma((10,)),
            dma((2, 2)),
        ],
        compiler_params=pltpu.CompilerParams(
            collective_id=0, has_side_effects=True, vmem_limit_bytes=64 * 2**20
        ),
        cost_estimate=pl.CostEstimate(
            flops=160 * rows * width * hidden, bytes_accessed=60 * 2**20, transcendentals=0
        ),
    )(*vmem_args, *any_args)


def backward_kernel(
    attn_gain_ref, ffn_gain_ref, cos_ref, sin_ref, seg_row_ref, lse_ref, key_ref,
    value_ref, second0_ref, second1_ref, second2_ref, second3_ref, mixed_ref, cot_ref, att_ref,
    query_ref, tok_ref, wo_ref, wq_ref, wk_ref, wv_ref, ggu_ref, gd_ref, own_ref, sibling_ref,
    first_gu_ref, first_down_ref,
    query_out, kv_out, out_out, tokens_ref, gate_out, up_out, down_out, ra_ref, rb_ref, rf_ref,
    pool, w_big, w_key, w_value, grad, proj, bias, key_acc, value_acc, gain_acc,
    out_buf, out_land, query_buf, later_buf, query_land, kv_buf, kv_land,
    ex_gu, ex_down, ef_gu, ef_down, ec_gu, ec_down, kept_gu, kept_down, stage, stage_down, load_sem, out_send, out_recv, ex_send, ex_recv, ef_send, ef_recv, ec_send, ec_recv,
    halve_send, halve_recv, free_sem, store_sem,
):
    f32, bf16 = jnp.float32, jnp.bfloat16
    grp, ep = lax.axis_index("grp"), lax.axis_index("ep")
    core = lax.rem(grp, 2)
    x = grp // 2
    y = lax.rem(ep, 2)
    z_low = lax.rem(ep // 2, 2)
    z_high = ep // 4
    by_y = (grp, ep + 1 - 2 * y)
    by_z = (grp, ep + 2 - 4 * z_low)
    by_far = (grp, ep + 4 - 8 * z_high)
    by_core = (grp + 1 - 2 * core, ep)
    by_x = (grp + 2 - 4 * x, ep)
    first = (grp, by_y[1] * (1 - core) + by_z[1] * core)
    second = (grp, by_z[1] * (1 - core) + by_y[1] * core)
    rows, width = grad.shape
    head = cos_ref.shape[1]
    heads = width // head
    key_width = key_ref.shape[1]
    per_key = heads * head // key_width
    block = width // 32

    def remote(src, dst, send, recv, device):
        return pltpu.make_async_remote_copy(
            src_ref=src, dst_ref=dst, send_sem=send, recv_sem=recv, device_id=device,
            device_id_type=pl.DeviceIdType.MESH,
        )

    partners = (by_core, by_y, by_z, by_x, by_far)
    barrier = pltpu.get_barrier_semaphore()
    for device in partners:
        pl.semaphore_signal(barrier, inc=1, device_id=device, device_id_type=pl.DeviceIdType.MESH)
    pl.semaphore_wait(barrier, 5)

    wide_half = width // 2
    quarter = width // 4
    mine = gd_ref.shape[1]
    ex_dst = (ex_gu, ex_down)

    def part(ref, m, index, size):
        at = pl.ds(pl.multiple_of(index * size, size), size)
        return ref.at[:, at] if m == 1 else ref.at[at, :]

    def piece(i):
        at = pl.ds(i * quarter, quarter)
        if i == 2:
            return part(gd_ref.at[1], 1, 1 - x, wide_half), ex_down.at[1], ef_down
        start = pl.multiple_of((1 - x) * wide_half + i * quarter, quarter)
        return ggu_ref.at[1, pl.ds(start, quarter), :], ex_gu.at[1, at, :], ef_gu.at[at, :]

    def ex_copy(i):
        src, dst, _ = piece(i)
        return remote(src, dst, ex_send.at[i], ex_recv.at[i], by_x)

    def ef_copy(i):
        _, src, dst = piece(i)
        return remote(src, dst, ef_send.at[i], ef_recv.at[i], by_far)

    def ec_copy(m):
        src = part(ex_dst[m].at[0], m, 1 - core, quarter)
        return remote(src, (ec_gu, ec_down)[m], ec_send.at[m], ec_recv.at[m], by_core)

    def kept_copy(which, m):
        src = part((ggu_ref, gd_ref)[m].at[which], m, x, wide_half)
        return pltpu.make_async_copy(src, (kept_gu, kept_down)[m], load_sem.at[22 + m])

    def load(number, src, dst):
        return pltpu.make_async_copy(src, dst, load_sem.at[number])

    ex_copy(0).start()
    loads = (
        (own_ref.at[3], pool.at[6]),
        (sibling_ref.at[3], pool.at[9]),
        (own_ref.at[1], pool.at[5]),
        (sibling_ref.at[1], pool.at[8]),
        (second0_ref, pool.at[1]),
        (second1_ref, pool.at[2]),
        (second2_ref, pool.at[3]),
        (second3_ref, pool.at[4]),
        (mixed_ref, grad),
        (cot_ref, pool.at[0]),
        (wo_ref, w_big),
        (own_ref.at[2], pool.at[7]),
    )
    for number, (src, dst) in enumerate(loads):
        load(number, src, dst).start()

    def wait_load(number):
        load(number, *loads[number]).wait()

    def add_into(dst, *others):
        @pl.loop(0, rows // 128)
        def _(step):
            at = pl.ds(pl.multiple_of(step * 128, 128), 128)
            total = dst[at, :].astype(f32)
            for other in others:
                total = total + other[at, :].astype(f32)
            dst[at, :] = total.astype(bf16)

    def merge(dst, other):
        @pl.loop(0, dst.shape[0] // 128)
        def _(step):
            at = pl.ds(pl.multiple_of(step * 128, 128), 128)
            dst[at, :] = (dst[at, :].astype(f32) + other[at, :].astype(f32)).astype(bf16)

    def expert_piece(i):
        if i != 1:
            kept_copy(1, i // 2).wait()
        ex_copy(i).wait_recv()
        merge(piece(i)[1], kept_down if i == 2 else kept_gu.at[pl.ds(i * quarter, quarter), :])
        ef_copy(i).start()
        if i > 0:
            kept_copy(0, i - 1).start()

    def expert_own():
        for m in range(2):
            kept_copy(0, m).wait()
            arrived_copies[m].wait()
            merge(ex_dst[m].at[0], (kept_gu, kept_down)[m])

    def expert_third():
        for i in range(3):
            ef_copy(i).wait_recv()
        for m in range(2):
            merge(ex_dst[m].at[0], (ef_gu, ef_down)[m])
            ec_copy(m).start()
        at = pl.ds(pl.multiple_of(core * quarter, quarter), quarter)
        stage[...] = ex_gu[0, at, :].astype(f32)
        stage_down[...] = ex_down[0, :, at].astype(f32)
        for copy in final_copies(0):
            copy.start()

    far_copy = lambda: remote(pool.at[6], rf_ref, out_send.at[0], out_recv.at[0], first)
    first_copy = lambda: remote(pool.at[5], ra_ref, out_send.at[1], out_recv.at[1], first)
    second_copy = lambda: remote(pool.at[7], rb_ref, out_send.at[2], out_recv.at[2], second)
    wait_load(0)
    wait_load(1)
    add_into(pool.at[6], pool.at[9])
    far_copy().start()
    wait_load(2)
    wait_load(3)
    add_into(pool.at[5], pool.at[8])
    first_copy().start()
    sib2 = lambda: load(12, sibling_ref.at[2], pool.at[8])
    sib2().start()
    arrived_copies = [
        load(20 + m, (first_gu_ref, first_down_ref)[m], ex_dst[m].at[0]) for m in range(2)
    ]
    for m in range(2):
        arrived_copies[m].start()
        kept_copy(1, m).start()

    for number in range(4, 10):
        wait_load(number)
    gain_acc[...] = jnp.zeros_like(gain_acc)

    @pl.loop(0, rows // 128)
    def _(step):
        at = pl.ds(pl.multiple_of(step * 128, 128), 128)
        value = grad[at, :]
        scale = lax.rsqrt(jnp.mean(value * value, axis=-1, keepdims=True) + EPS)
        normed = value * scale
        down = (
            pool[1, at, :].astype(f32)
            + pool[2, at, :].astype(f32)
            + pool[3, at, :].astype(f32)
            + pool[4, at, :].astype(f32)
        )
        product = down * normed
        gain_acc[1:2, :] += jnp.sum(product, axis=0, keepdims=True)
        mean = jnp.mean(product * ffn_gain_ref[...][None, :], axis=-1, keepdims=True)
        result = pool[0, at, :].astype(f32) + scale * (down * ffn_gain_ref[...][None, :] - normed * mean)
        grad[at, :] = result
        pool[3, at, :] = result.astype(bf16)

    att_load = lambda: load(13, att_ref, pool.at[1])
    query_load = lambda: load(14, query_ref, pool.at[2])
    tok_load = lambda: load(15, tok_ref, pool.at[0])
    key_weight_load = lambda: load(16, wk_ref, w_key)
    value_weight_load = lambda: load(17, wv_ref, w_value)
    for copy in (att_load, query_load, tok_load, key_weight_load, value_weight_load):
        copy().start()

    segment = jnp.broadcast_to(seg_row_ref[...].astype(f32), (8, rows))
    segment_column = jnp.transpose(segment)[:, :1].astype(jnp.int32)
    position = lax.broadcasted_iota(jnp.int32, (rows, rows), 0)
    other_position = lax.broadcasted_iota(jnp.int32, (rows, rows), 1)
    padding = seg_row_ref[...] == jnp.max(seg_row_ref[...])
    allowed = (
        (other_position <= position)
        & (segment_column == seg_row_ref[...])
        & (jnp.logical_not(padding) | (other_position == position))
    )
    bias[...] = jnp.where(allowed, 0.0, -1e30)

    def dot_nt(a, b):
        return lax.dot_general(a, b, (((1,), (1,)), ((), ())), preferred_element_type=f32)

    def dot_tn(a, b):
        return lax.dot_general(a, b, (((0,), (0,)), ((), ())), preferred_element_type=f32)

    far_levels = ((z_low, by_z), (z_high, by_far))
    orders = (
        ((core, by_core), (y, by_y), (x, by_x)) + far_levels,
        ((core, by_core), (x, by_x), (y, by_y)) + far_levels,
    )
    offsets = (0, 16, 24, 28, 30)
    places = []
    for levels in orders:
        starts = [0]
        for level, (bit, _) in enumerate(levels):
            starts.append(starts[-1] + bit * (16 >> level))
        places.append(starts)

    def landing(job, land, level):
        size = 16 >> level
        if job in (1, 2):
            columns = pl.ds((job - 1) * (width // 2), width // 2)
            if level > 0:
                return query_land.at[pl.ds(offsets[level] - 16, size), :, columns]
            return out_land.at[pl.ds(0, size), :, columns]
        return land.at[pl.ds(offsets[level], size)]

    def halve_copy(job, buf, land, level):
        bit, device = orders[min(job, 1)][level]
        starts = places[min(job, 1)]
        size = 16 >> level
        return remote(
            buf.at[pl.ds(starts[level] + (1 - bit) * size, size)],
            landing(job, land, level),
            halve_send.at[job, level],
            halve_recv.at[job, level],
            device,
        )

    def absorb(job, buf, land, level, result=None):
        halve_copy(job, buf, land, level).wait_recv()
        starts = places[min(job, 1)]
        size = 16 >> level
        arrivals = landing(job, land, level)
        if result is None:

            @pl.loop(0, size)
            def _(i):
                at = starts[level + 1] + i
                buf[at] = (buf[at].astype(f32) + arrivals[i].astype(f32)).astype(bf16)

        else:
            result[...] = buf[starts[5]].astype(f32) + arrivals[0].astype(f32)
        if job == 0 and level == 0:
            for later in range(2):
                pl.semaphore_signal(
                    free_sem.at[later], inc=1, device_id=by_core,
                    device_id_type=pl.DeviceIdType.MESH,
                )
        if level < 4:
            launch(job, level + 1)

    jobs = (
        (out_buf, out_land), (query_buf, out_land), (later_buf, out_land), (kv_buf, kv_land)
    )

    def launch(job, level):
        if job in (1, 2) and level == 0:
            pl.semaphore_wait(free_sem.at[job - 1], 1)
        halve_copy(job, *jobs[job], level).start()

    def begin(job):
        launch(job, 0)

    def advance(job, level):
        results = (
            out_out,
            query_out.at[:, pl.ds(0, width // 2)],
            query_out.at[:, pl.ds(width // 2, width // 2)],
            kv_out,
        )
        absorb(job, *jobs[job], level, results[job] if level == 4 else None)

    def place(buf, tile, value, columns):
        for b in range(8):
            high, low, odd = b >> 2, (b >> 1) & 1, b & 1
            middle = odd * 2 + (tile >> 1) if buf is out_buf else (tile >> 1) * 2 + odd
            to = (((tile & 1) * 4 + middle) * 2 + low) * 2 + high
            buf[to, :, columns] = value[b * block : (b + 1) * block].astype(bf16)

    ex_copy(1).start()
    att_load().wait()
    for tile in range(4):
        at = slice(tile * 8 * block, (tile + 1) * 8 * block)
        place(out_buf, tile, dot_tn(pool[3, :, at], pool[1]), slice(None))
    begin(0)
    wait_load(10)
    for half in range(2):
        at = slice(half * rows // 2, (half + 1) * rows // 2)
        pool[4, at, :] = dot_nt(pool[3, at, :], w_big[...]).astype(bf16)
    query_weight_load = lambda: load(18, wq_ref, w_big)
    query_weight_load().start()
    ex_copy(2).start()
    expert_piece(0)

    tok_load().wait()

    def first_norm(at):
        value = pool[0, at, :].astype(f32)
        scale = lax.rsqrt(jnp.mean(value * value, axis=-1, keepdims=True) + EPS)
        return scale, value * scale

    @pl.loop(0, rows // 128)
    def _(step):
        at = pl.ds(pl.multiple_of(step * 128, 128), 128)
        pool[1, at, :] = (first_norm(at)[1] * attn_gain_ref[...][None, :]).astype(bf16)

    def send_second():
        wait_load(11)
        sib2().wait()
        far_copy().wait_recv()
        far_load = load(19, rf_ref, pool.at[9])
        far_load.start()
        far_load.wait()
        add_into(pool.at[7], pool.at[8], pool.at[9])
        second_copy().start()

    def final_copies(which):
        own = core * (1 - which) + (1 - core) * which
        units = pl.ds(pl.multiple_of(own * mine, mine), mine)
        pairs = (
            (stage.at[:, pl.ds(0, mine)], gate_out.at[:, units]),
            (stage.at[:, pl.ds(mine, mine)], up_out.at[:, units]),
            (stage_down, down_out.at[units, :]),
        )
        return [
            pltpu.make_async_copy(src, dst, store_sem.at[4 + 3 * which + i])
            for i, (src, dst) in enumerate(pairs)
        ]

    def expert_last():
        for copy in final_copies(0):
            copy.wait()
        for m in range(2):
            ec_copy(m).wait_recv()
        stage[...] = ec_gu[...].astype(f32)
        stage_down[...] = ec_down[...].astype(f32)
        for copy in final_copies(1):
            copy.start()

    def turn_back(value, at):
        swapped = pltpu.roll(value, head // 2, 1)
        return value * cos_ref[at, :] - swapped * sin_ref[at, :]

    scale = head ** (-0.5)
    query_load().wait()
    key_acc[...] = jnp.zeros_like(key_acc)
    value_acc[...] = jnp.zeros_like(value_acc)

    def place_query(part, buf):
        columns = slice(part * width // 2, (part + 1) * width // 2)
        for tile in range(4):
            at = slice(tile * 8 * block, (tile + 1) * 8 * block)
            place(buf, tile, dot_tn(pool[1, :, at], proj[:, columns]), slice(None))
        begin(1 + part)

    def between(number):
        if number == 1:
            advance(0, 0)
        elif number == 3:
            expert_piece(1)
        elif number == 5:
            place_query(0, query_buf)
        elif number == 7:
            send_second()
        elif number == 8:
            advance(1, 0)
        elif number == 10:
            expert_piece(2)

    for number in range(heads):
        columns = slice(number * head, (number + 1) * head)
        kv = number // per_key
        kv_columns = slice(kv * head, (kv + 1) * head)
        for half in range(2):
            at = slice(half * rows // 2, (half + 1) * rows // 2)
            seen = slice(0, (half + 1) * rows // 2)
            q = pool[2, at, columns]
            da = pool[4, at, columns]
            k = key_ref[seen, kv_columns]
            score = dot_nt(q, k) * scale + bias[at, seen]
            probs = jnp.exp(score - lse_ref[at, number : number + 1])
            dprob = dot_nt(da, value_ref[seen, kv_columns])
            inner = jnp.sum(probs * dprob, axis=-1, keepdims=True)
            dscore = (probs * (dprob - inner)).astype(bf16)
            value_acc[seen, kv_columns] += dot_tn(probs.astype(bf16), da)
            key_acc[seen, kv_columns] += dot_tn(dscore, q)
            dq = jnp.dot(dscore, k, preferred_element_type=f32) * scale
            proj[at, columns] = turn_back(dq, at).astype(bf16)
        between(number)

    for kv in range(key_width // head):
        columns = slice(kv * head, (kv + 1) * head)
        to = slice(width + kv * head, width + (kv + 1) * head)
        proj[:, to] = turn_back(key_acc[:, columns] * scale, slice(None)).astype(bf16)
        to = slice(width + key_width + kv * head, width + key_width + (kv + 1) * head)
        proj[:, to] = value_acc[:, columns].astype(bf16)

    place_query(1, later_buf)
    for tile in range(4):
        at = slice(tile * 8 * block, (tile + 1) * 8 * block)
        place(kv_buf, tile, dot_tn(pool[1, :, at], proj[:, width:]), slice(0, 2 * key_width))
    query_weight_load().wait()
    key_weight_load().wait()
    value_weight_load().wait()
    for quarter_step in range(4):
        at = slice(quarter_step * rows // 4, (quarter_step + 1) * rows // 4)
        down = dot_nt(proj[at, :width], w_big[...])
        down = down + dot_nt(proj[at, width : width + key_width], w_key[...])
        down = down + dot_nt(proj[at, width + key_width :], w_value[...])
        factor, normed = first_norm(at)
        product = down * normed
        gain_acc[0:1, :] += jnp.sum(product, axis=0, keepdims=True)
        mean = jnp.mean(product * attn_gain_ref[...][None, :], axis=-1, keepdims=True)
        grad[at, :] = grad[at, :] + factor * (down * attn_gain_ref[...][None, :] - normed * mean)
        if quarter_step == 0:
            advance(2, 0)
        elif quarter_step == 1:
            advance(1, 1)
        elif quarter_step == 2:
            expert_own()
    tokens_store = lambda: pltpu.make_async_copy(grad, tokens_ref, store_sem.at[0])
    tokens_store().start()

    gains = gain_acc[...]
    high = gains.astype(bf16).astype(f32)
    row = lax.broadcasted_iota(jnp.int32, gains.shape, 0)
    lower = pltpu.roll(gains - high, 2, 0)
    both = jnp.transpose(jnp.where(row < 2, high, lower))
    both = jnp.concatenate([both, jnp.zeros((width, head - 8), f32)], axis=1)
    for tile in range(4):
        at = slice(tile * 8 * block, (tile + 1) * 8 * block)
        place(kv_buf, tile, both[at], slice(2 * key_width, 2 * key_width + head))
    begin(3)

    advance(3, 0)
    advance(0, 1)
    advance(2, 1)
    advance(1, 2)
    advance(3, 1)
    advance(0, 2)
    advance(2, 2)
    advance(1, 3)
    advance(3, 2)
    advance(0, 3)
    advance(2, 3)
    advance(3, 3)
    expert_third()

    first_copy().wait_recv()
    second_copy().wait_recv()
    expert_last()
    for job in (1, 0, 2, 3):
        advance(job, 4)

    for copy in (far_copy, first_copy, second_copy):
        copy().wait_send()
    for m in range(2):
        ec_copy(m).wait_send()
    for i in range(3):
        ex_copy(i).wait_send()
        ef_copy(i).wait_send()
    for copy in final_copies(1):
        copy.wait()
    for job in range(4):
        for level in range(5):
            halve_copy(job, *jobs[job], level).wait_send()
    tokens_store().wait()


def backward_call(vmem_args, any_args):
    f32, bf16 = jnp.float32, jnp.bfloat16
    rows, head = vmem_args[2].shape
    key_width = vmem_args[6].shape[1]
    width = vmem_args[0].shape[0]
    hidden = any_args[13].shape[2]
    block = width // 32
    extra = 2 * key_width + head
    anywhere = pl.BlockSpec(memory_space=pl.ANY)
    inside = pl.BlockSpec(memory_space=pltpu.VMEM)
    shape = jax.ShapeDtypeStruct
    dma = pltpu.SemaphoreType.DMA
    vmem = pltpu.VMEM
    return pl.pallas_call(
        backward_kernel,
        out_shape=(
            shape((block, width), f32),
            shape((block, extra), f32),
            shape((block, width), f32),
            shape((rows, width), f32),
            shape((width // 4, hidden), f32),
            shape((width // 4, hidden), f32),
            shape((hidden, width // 4), f32),
            shape((rows, width), bf16),
            shape((rows, width), bf16),
            shape((rows, width), bf16),
        ),
        in_specs=[inside] * len(vmem_args) + [anywhere] * len(any_args),
        out_specs=(inside,) * 3 + (anywhere,) * 7,
        scratch_shapes=[
            vmem((10, rows, width), bf16),
            vmem((width, width), bf16),
            vmem((width, key_width), bf16),
            vmem((width, key_width), bf16),
            vmem((rows, width), f32),
            vmem((rows, width + 2 * key_width), bf16),
            vmem((rows, rows), f32),
            vmem((rows, key_width), f32),
            vmem((rows, key_width), f32),
            vmem((8, width), f32),
            vmem((32, block, width), bf16),
            vmem((31, block, width), bf16),
            vmem((32, block, width // 2), bf16),
            vmem((32, block, width // 2), bf16),
            vmem((15, block, width), bf16),
            vmem((32, block, extra), bf16),
            vmem((31, block, extra), bf16),
            vmem((2, width // 2, hidden), bf16),
            vmem((2, hidden // 2, width // 2), bf16),
            vmem((width // 2, hidden), bf16),
            vmem((hidden // 2, width // 2), bf16),
            vmem((width // 4, hidden), bf16),
            vmem((hidden // 2, width // 4), bf16),
            vmem((width // 2, hidden), bf16),
            vmem((hidden // 2, width // 2), bf16),
            vmem((width // 4, hidden), f32),
            vmem((hidden // 2, width // 4), f32),
            dma((24,)),
            dma((3,)),
            dma((3,)),
            dma((3,)),
            dma((3,)),
            dma((3,)),
            dma((3,)),
            dma((2,)),
            dma((2,)),
            dma((4, 5)),
            dma((4, 5)),
            pltpu.SemaphoreType.REGULAR((2,)),
            dma((10,)),
        ],
        compiler_params=pltpu.CompilerParams(
            collective_id=1, has_side_effects=True, vmem_limit_bytes=64 * 2**20
        ),
        cost_estimate=pl.CostEstimate(
            flops=30 * rows * width * width, bytes_accessed=60 * 2**20, transcendentals=0
        ),
    )(*vmem_args, *any_args)


def local_dense(
    tokens,
    segment_ids,
    routes,
    route_gates,
    attn_gain,
    ffn_gain,
    query_weight,
    key_matrix,
    value_matrix,
    output_weight,
    expert_gate,
    expert_up,
    expert_down,
    cotangent,
):
    experts = lax.axis_size("ep")
    table = jnp.sum(
        jnp.where(
            routes.T[None, :, :] == jnp.arange(experts, dtype=jnp.int32)[:, None, None],
            route_gates.T[None, :, :],
            0.0,
        ),
        axis=1,
    )
    power = -np.arange(HEAD_SIZE // 2, dtype=np.float32) * np.float32(2.0 / HEAD_SIZE)
    inverse = np.float32(BASE) ** power
    angle = np.arange(tokens.shape[0], dtype=np.float32)[:, None] * inverse[None, :]
    cosine = np.cos(angle)
    sine = np.sin(angle)
    small = (
        attn_gain,
        ffn_gain,
        jnp.asarray(np.concatenate([cosine, cosine], axis=1), jnp.float32),
        jnp.asarray(np.concatenate([-sine, sine], axis=1), jnp.float32),
        segment_ids,
    )
    (
        query_rot,
        key_rot,
        value_low,
        log_total,
        attended,
        mixed,
        grad_gu,
        grad_down,
        out_own,
        out_sib,
        own_grad,
        sibling_grad,
        first_grad,
        second_grad,
        _,
        _,
        met_gu,
        met_down,
    ) = forward_call(
        small + (table,),
        (
            tokens,
            query_weight,
            key_matrix,
            value_matrix,
            output_weight,
            cotangent,
            expert_gate[0],
            expert_up[0],
            expert_down[0],
        ),
    )
    (
        query_grad,
        extra_grad,
        output_grad,
        tokens_grad,
        gate_grad,
        up_grad,
        down_grad,
        near_sum,
        far_sum,
        _,
    ) = backward_call(
        small + (log_total, key_rot, value_low),
        (
            own_grad,
            sibling_grad,
            first_grad,
            second_grad,
            mixed,
            cotangent,
            attended,
            query_rot,
            tokens,
            output_weight,
            query_weight,
            key_matrix,
            value_matrix,
            grad_gu,
            grad_down,
            out_own,
            out_sib,
            met_gu,
            met_down,
        ),
    )
    total = mixed
    for part in (out_own[0], out_sib[0], near_sum, far_sum):
        total = total + part.astype(jnp.float32)
    layer_out = total.astype(jnp.bfloat16)
    split_k = key_matrix.shape[1]
    split_v = split_k + value_matrix.shape[1]
    gain_sums = extra_grad[:, split_v : split_v + 2] + extra_grad[:, split_v + 2 : split_v + 4]
    return (
        layer_out,
        tokens_grad,
        query_grad,
        extra_grad[:, :split_k],
        extra_grad[:, split_k:split_v],
        output_grad.T,
        gain_sums[:, 0],
        gain_sums[:, 1],
        gate_grad[None],
        up_grad[None],
        down_grad[None],
    )


def solution(mesh):
    in_specs = (
        P(("grp", "ep"), None),
        P(("grp", "ep"), None),
        P(("grp", "ep"), None),
        P(("grp", "ep"), None),
        P(),
        P(),
        P(),
        P(),
        P(),
        P(),
        P("ep", None, None),
        P("ep", None, None),
        P("ep", None, None),
        P(("grp", "ep"), None),
    )
    out_specs = (
        P(("grp", "ep"), None),
        P(("grp", "ep"), None),
        P(("grp", "ep"), None),
        P(("grp", "ep"), None),
        P(("grp", "ep"), None),
        P(None, ("grp", "ep")),
        P(("grp", "ep")),
        P(("grp", "ep")),
        P("ep", "grp", None),
        P("ep", "grp", None),
        P("ep", None, "grp"),
    )
    paired = mesh.shape["grp"] == 4 and mesh.shape["ep"] == 8
    local = local_dense if paired else local_routed
    return jax.shard_map(local, mesh=mesh, in_specs=in_specs, out_specs=out_specs, check_vma=False)
```
